32 devices in a mesh: freq: 16 (over z, x, core), mz: 2 (over y).
Axes of the slice: x: 2, y: 2, z: 4, core: 2. Of those that a mesh axis runs over, the one named last changes fastest.
Arguments:
- intensity: bfloat16 [8, 6144, 4096], P(None, 'freq', 'mz'), may hold values from -6 to 6
- elution: float32 [6144, 64], P(('freq', 'mz')), may hold values from -6 to 6
- loadings: float32 [8, 64], replicated, may hold values from 0.0005 to 0.01
- shifts: int32 [8, 64], replicated, may hold values from 0 to 255
- bin_weight: float32 [6144], replicated, may hold values from 0.25 to 4
Outputs:
- spectral: float32 [64, 4096], P(None, ('mz', 'freq'))
The draws below stay inside these ranges and needn't reach their ends.
All inputs are finite; a program needn't handle non-finite values.
Results may differ from the reference program's by a relative error of at most 0.0003.
Values may be sent and summed in bfloat16 or wider, within the bound.
No kernel may reach another device: no remote copies, remote signals or barrier semaphores. Data moves between devices by JAX's collectives and lax.ppermute only.
A program may use at most 64 MiB of HBM per device.

```python
import math
import jax
import jax.numpy as jnp
from jax import lax

T_SIZE = 6144
M = 4096
R = 64
K = 8
N_FREQ = 16


def plant(entries, stream_key, smallest, largest):
    spot = [jax.random.randint(jax.random.fold_in(stream_key, axis), (), 0, length) for axis, length in enumerate(entries.shape)]
    longest = entries.shape.index(max(entries.shape))
    neighbour = spot[:longest] + [(spot[longest] + 1) % entries.shape[longest]] + spot[longest + 1:]
    return entries.at[tuple(spot)].set(smallest).at[tuple(neighbour)].set(largest)


def level_of(key, extent, pieces, low, top_value):
    def one(dim, blocks):
        draws = jax.random.uniform(jax.random.fold_in(jax.random.fold_in(key, 6), dim), (blocks,), jnp.float32, low / len(pieces), top_value / len(pieces))
        return jnp.repeat(jnp.exp(draws), extent[dim] // blocks).reshape((-1,) + (1,) * (len(extent) - dim - 1))

    level = one(*pieces[0])
    for cut in pieces[1:]:
        level = level * one(*cut)
    return level


def normal_values(key, extent, deviation, reach, cuts=(), held_as=jnp.bfloat16):
    values = jax.random.normal(key, extent, jnp.float32) * deviation
    if len(cuts) > 0:
        values = level_of(key, extent, cuts, -0.22, 0.18) * values
    return jnp.clip(values, min=-reach, max=reach).astype(held_as)


def setup_inputs(seed: int = 0) -> dict:
    seeds = jax.random.split(jax.random.key(seed), 6)
    intensity = normal_values(seeds[0], (K, T_SIZE, M), 1.0, 6.0, ((1, 16), (2, 2)))
    elution = normal_values(seeds[1], (T_SIZE, R), 1.0, 6.0, ((0, 32),), jnp.float32)
    loadings = jnp.clip(jnp.exp(jax.random.uniform(seeds[2], (K, R), jnp.float32, math.log(0.0005), math.log(0.01))), 0.0005, 0.01)
    shifts = plant(jax.random.randint(seeds[3], (K, R), 0, 256), jax.random.fold_in(seeds[3], 1), 0, 255).astype(jnp.int32)
    bin_weight = jnp.clip(jnp.exp(jax.random.uniform(seeds[4], (T_SIZE,), jnp.float32, math.log(0.25), math.log(4.0))), 0.25, 4.0)
    return dict(intensity=intensity, elution=elution, loadings=loadings, shifts=shifts, bin_weight=bin_weight)


PRECISE = lax.Precision.HIGHEST

def turn_angle(product, length):
    return 2.0 * math.pi / length * (product % length).astype(jnp.float32)

def cholesky_solve(gram_matrix, numerator):
    factor = jnp.linalg.cholesky(gram_matrix)
    middle = lax.linalg.triangular_solve(factor, numerator, left_side=True, lower=True)
    return lax.linalg.triangular_solve(factor, middle, left_side=True, lower=True, transpose_a=True)

def reference(intensity, elution, loadings, shifts, bin_weight):
    freq_count = N_FREQ
    bin_count = T_SIZE // freq_count
    norm_scale = 1.0 / math.sqrt(T_SIZE)
    dev_ids = jnp.arange(freq_count, dtype=jnp.int32)
    bin_ids = jnp.arange(bin_count, dtype=jnp.int32)
    dev_angle = turn_angle(dev_ids[:, None] * dev_ids[None, :], freq_count)
    cos_dev = jnp.cos(dev_angle)
    sin_dev = jnp.sin(dev_angle)
    twiddle = turn_angle(dev_ids[:, None] * bin_ids[None, :], T_SIZE)
    twid_cos = jnp.cos(twiddle)[:, :, None]
    twid_sin = jnp.sin(twiddle)[:, :, None]
    bin_angle = turn_angle(bin_ids[:, None] * bin_ids[None, :], bin_count)
    cos_bin = jnp.cos(bin_angle)
    sin_bin = jnp.sin(bin_angle)
    stacked = elution.reshape(freq_count, bin_count * R)
    part_re = jnp.dot(cos_dev, stacked, precision=PRECISE).reshape(freq_count, bin_count, R)
    part_im = -jnp.dot(sin_dev, stacked, precision=PRECISE).reshape(freq_count, bin_count, R)
    turn_re = part_re * twid_cos + part_im * twid_sin
    turn_im = part_im * twid_cos - part_re * twid_sin
    spec_re = (jnp.einsum('bq,aqr->abr', cos_bin, turn_re, precision=PRECISE) + jnp.einsum('bq,aqr->abr', sin_bin, turn_im, precision=PRECISE)) * norm_scale
    spec_im = (jnp.einsum('bq,aqr->abr', cos_bin, turn_im, precision=PRECISE) - jnp.einsum('bq,aqr->abr', sin_bin, turn_re, precision=PRECISE)) * norm_scale
    weights_grid = bin_weight.reshape(bin_count, freq_count).T[:, :, None]
    freq_index = dev_ids[:, None] + freq_count * bin_ids[None, :]

    def one_run(totals, inputs):
        run_data, run_amp, run_lag = inputs
        phase = turn_angle(freq_index[:, :, None] * run_lag[None, None, :], T_SIZE)
        phase_cos = jnp.cos(phase)
        phase_sin = jnp.sin(phase)
        model_re = run_amp * (spec_re * phase_cos + spec_im * phase_sin)
        model_im = run_amp * (spec_im * phase_cos - spec_re * phase_sin)
        wmod_re = weights_grid * model_re
        wmod_im = weights_grid * model_im
        gram_part = jnp.einsum('abr,abs->rs', wmod_re, model_re, precision=PRECISE) + jnp.einsum('abr,abs->rs', wmod_im, model_im, precision=PRECISE)
        back_re = jnp.einsum('abr,bq->aqr', wmod_re, cos_bin, precision=PRECISE) - jnp.einsum('abr,bq->aqr', wmod_im, sin_bin, precision=PRECISE)
        back_im = jnp.einsum('abr,bq->aqr', wmod_re, sin_bin, precision=PRECISE) + jnp.einsum('abr,bq->aqr', wmod_im, cos_bin, precision=PRECISE)
        samples = run_data.astype(jnp.float32).reshape(freq_count, bin_count * M)
        raw_re = jnp.dot(cos_dev, samples, precision=PRECISE).reshape(freq_count, bin_count, M)
        raw_im = -jnp.dot(sin_dev, samples, precision=PRECISE).reshape(freq_count, bin_count, M)
        half_re = raw_re * twid_cos + raw_im * twid_sin
        half_im = raw_im * twid_cos - raw_re * twid_sin
        num_part = jnp.dot(back_re.reshape(T_SIZE, R).T, half_re.reshape(T_SIZE, M), precision=PRECISE) + jnp.dot(back_im.reshape(T_SIZE, R).T, half_im.reshape(T_SIZE, M), precision=PRECISE)
        return ((totals[0] + num_part, totals[1] + gram_part), None)
    start = (jnp.zeros((R, M), jnp.float32), jnp.zeros((R, R), jnp.float32))
    (numerator, gram_matrix), _ = lax.scan(one_run, start, (intensity, loadings, shifts))
    numerator = numerator * norm_scale
    return cholesky_solve(gram_matrix, numerator)
```

```python
import functools
import math

import jax
import jax.numpy as jnp
import numpy as np
from jax import lax
from jax.experimental import pallas as pl
from jax.experimental.pallas import tpu as pltpu
from jax.sharding import PartitionSpec as P

PRECISE = lax.Precision.HIGHEST
LANES = 128
REACH = 256
MIB = 1024 * 1024


def f32_dot(a, b, dims=(((1,), (0,)), ((), ()))):
    return lax.dot_general(a, b, dims, precision=PRECISE, preferred_element_type=jnp.float32)


def two_terms(x):
    high = x.astype(jnp.bfloat16)
    low = (x - high.astype(jnp.float32)).astype(jnp.bfloat16)
    return high, low


def vmem(count):
    return [pl.BlockSpec(memory_space=pltpu.VMEM)] * count


def pack_kernel(x_ref, o_ref):
    high, low = two_terms(x_ref[...])
    o_ref[...] = jnp.concatenate([high, low], axis=1)


def pack(elution):
    rows, components = elution.shape
    return pl.pallas_call(
        pack_kernel,
        out_shape=jax.ShapeDtypeStruct((rows, 2 * components), jnp.bfloat16),
        in_specs=vmem(1),
        out_specs=vmem(1)[0],
        name="pack_elution",
    )(elution)


def circulant_kernel(w_ref, lane_ref, twid_ref, row_ref, u_ref):
    rows = w_ref.shape[1]
    w = w_ref[...]
    over_lanes = (((0,), (0,)), ((), ()))
    a_re = f32_dot(w, lane_ref[0], over_lanes)
    a_im = -f32_dot(w, lane_ref[1], over_lanes)
    b_re = a_re * twid_ref[0] + a_im * twid_ref[1]
    b_im = a_im * twid_ref[0] - a_re * twid_ref[1]
    c = f32_dot(row_ref[0], b_re) + f32_dot(row_ref[1], b_im)
    sub = lax.broadcasted_iota(jnp.int32, (LANES, LANES), 0)
    lane = lax.broadcasted_iota(jnp.int32, (LANES, LANES), 1)

    def turned(row):
        return pltpu.roll(jnp.broadcast_to(c[row : row + 1], (LANES, LANES)), 0, 1, stride=1, stride_axis=0)

    before = turned(rows - 1)
    for row in range(rows):
        now = turned(row)
        high, low = two_terms(jnp.where(lane >= sub, now, before))
        u_ref[0:LANES, row * LANES : (row + 1) * LANES] = high
        u_ref[LANES:, row * LANES : (row + 1) * LANES] = low
        before = now


def circulant(bin_weight):
    length = bin_weight.shape[0]
    rows = length // LANES

    def tables(a, b, period):
        angle = 2.0 * math.pi / period * ((a[:, None] * b[None, :]) % period)
        return np.stack([np.cos(angle), np.sin(angle)])

    lane_ids, row_ids = np.arange(LANES), np.arange(rows)
    lane_table = tables(lane_ids, lane_ids, LANES).astype(np.float32)
    twid_table = tables(row_ids, lane_ids, length).astype(np.float32)
    row_table = (tables(row_ids, row_ids, rows) / length).astype(np.float32)
    return pl.pallas_call(
        circulant_kernel,
        out_shape=jax.ShapeDtypeStruct((2 * LANES, length), jnp.bfloat16),
        in_specs=vmem(4),
        out_specs=vmem(1)[0],
        cost_estimate=pl.CostEstimate(flops=2_000_000_000, bytes_accessed=4 * MIB, transcendentals=0),
        name="circulant_block",
    )(bin_weight.reshape(LANES, rows), lane_table, twid_table, row_table)


def product_kernel(
    places, order, packed, i_ref, e_ref, u_ref, amp_ref, lag_ref, num_ref, gram_ref, wide, terms, held, sems
):
    run_count, bin_count, local_mz = i_ref.shape
    components = amp_ref.shape[0]
    length = u_ref.shape[1]
    chunk = held.shape[2] // sems.shape[0]
    chunks = sems.shape[0]
    copies = []
    for n in range(chunks):
        part = pl.ds(n * chunk, chunk)
        copies.append(pltpu.make_async_copy(i_ref.at[:, :, part], held.at[:, :, part], sems.at[n]))
        copies[-1].start()

    freq_rank = lax.axis_index("freq")
    me = freq_rank * lax.axis_size("mz") + lax.axis_index("mz")
    start = lax.rem(freq_rank * bin_count + length - REACH, length)
    step = math.gcd(math.gcd(bin_count, LANES), e_ref.shape[1])
    per_shard = e_ref.shape[1] // step
    steps = length // step

    def bring(j, carry):
        at = lax.rem(start // step + j, steps)
        shard = at // per_shard
        if order is not None:
            turned = lax.bitwise_xor(shard, me)
            place = 0
            for bit, value in enumerate(order):
                place = place + (lax.rem(turned // value, 2) << bit)
            shard = place
        row = pl.multiple_of(lax.rem(at, per_shard) * step, step)
        block = e_ref[pl.ds(shard, 1), pl.ds(row, step), :][0]
        to = pl.multiple_of(j * step, step)
        wide[pl.ds(to + LANES, step), 0:LANES] = block
        wide[pl.ds(to, step), LANES:] = block
        return carry

    extra = (wide.shape[0] - length) // step
    lax.fori_loop(0, steps + extra - LANES // step, bring, 0)

    u = u_ref[...]
    pieces, windows = [], []
    for a in range(0, places, 2):
        rows = wide[LANES + a * LANES : LANES + a * LANES + length, :]
        made = lax.dot_general(
            u, rows, (((1,), (0,)), ((), ())), preferred_element_type=jnp.float32
        )
        made = made[:LANES] + made[LANES:]
        for half in range(min(2, places - a)):
            piece = made[:, half * LANES : (half + 1) * LANES].T
            pieces.append(piece[:components] + piece[components:])
    for a in range(places):
        piece = wide[LANES + a * LANES : 2 * LANES + a * LANES, 0:LANES].astype(jnp.float32).T
        windows.append(piece[:components] + piece[components:])
    base = jnp.concatenate(
        [jnp.concatenate(pieces, axis=1), jnp.concatenate(windows, axis=1)], axis=0
    )
    span = -(-bin_count // LANES) * LANES
    for k in range(run_count):
        lag = lag_ref[:, k : k + 1]
        left = REACH - 1 - jnp.concatenate([lag, lag], axis=0)
        y = base
        for bit in (7, 6, 5, 4, 3, 2, 1, 0):
            move = 1 << bit
            y = jnp.where(
                lax.rem(left // move, 2) == 1, pltpu.roll(y, y.shape[1] - move, 1), y
            )
            if move == LANES:
                y = y[:, : span + LANES]
        y = pltpu.roll(y, y.shape[1] - 1, 1)[:, :bin_count]
        amp = amp_ref[:, k : k + 1]
        high, low = two_terms(y * jnp.concatenate([amp, amp], axis=0))
        terms[0:components, k * bin_count : (k + 1) * bin_count] = high[:components]
        terms[components : 2 * components, k * bin_count : (k + 1) * bin_count] = low[:components]
        terms[2 * components : 3 * components, k * bin_count : (k + 1) * bin_count] = high[components:]
        terms[3 * components :, k * bin_count : (k + 1) * bin_count] = low[components:]
    model = terms[0 : 2 * components, :]
    gram = lax.dot_general(
        model, terms[2 * components :, :], (((1,), (1,)), ((), ())), preferred_element_type=jnp.float32
    )
    gram = gram[:components] + gram[components:]
    gram = gram[:, :components] + gram[:, components:]
    if packed:
        half = components // 2
        gram = jnp.concatenate([gram[:half], gram[half:]], axis=1)
        for n in range(num_ref.shape[0]):
            num_ref[n, components:, :] = gram
    gram_ref[...] = gram

    for n in range(chunks):
        copies[n].wait()
        data = held[:, :, n * chunk : (n + 1) * chunk].reshape(run_count * bin_count, chunk)
        made = jnp.dot(model, data, preferred_element_type=jnp.float32)
        made = made[:components] + made[components:]
        if packed:
            for part in range(chunk // LANES):
                num_ref[n * (chunk // LANES) + part, 0:components, :] = made[
                    :, part * LANES : (part + 1) * LANES
                ]
        else:
            num_ref[:, n * chunk : (n + 1) * chunk] = made


def product(intensity, gathered, order, u, loadings, shifts, packed):
    run_count, bin_count, local_mz = intensity.shape
    components = loadings.shape[1]
    length = u.shape[1]
    places = -(-(bin_count + REACH) // LANES)
    chunk = 256
    num_shape = (local_mz // LANES, components + components // 2, LANES) if packed else (components, local_mz)
    gram_shape = (components // 2, LANES) if packed else (components, components)
    scratch_rows = LANES + length + 2 * LANES * ((places - 1) // 2)
    return pl.pallas_call(
        functools.partial(product_kernel, places, order, packed),
        out_shape=(
            jax.ShapeDtypeStruct(num_shape, jnp.float32),
            jax.ShapeDtypeStruct(gram_shape, jnp.float32),
        ),
        in_specs=[pl.BlockSpec(memory_space=pl.ANY)] + vmem(4),
        out_specs=tuple(vmem(2)),
        scratch_shapes=[
            pltpu.VMEM((scratch_rows, 2 * LANES), jnp.bfloat16),
            pltpu.VMEM((4 * components, run_count * bin_count), jnp.bfloat16),
            pltpu.VMEM(intensity.shape, jnp.bfloat16),
            pltpu.SemaphoreType.DMA((local_mz // chunk,)),
        ],
        compiler_params=pltpu.CompilerParams(vmem_limit_bytes=48 * MIB),
        cost_estimate=pl.CostEstimate(
            flops=8_000_000_000, bytes_accessed=2 * intensity.size, transcendentals=0
        ),
        name="model_products",
    )(intensity, gathered, u, loadings.T, shifts.T)


def eliminate(gram, right):
    components = gram.shape[0]
    row_id = lax.broadcasted_iota(jnp.int32, (components, 1), 0)
    for j in range(components):
        pivot = 1.0 / gram[j : j + 1, j : j + 1]
        factor = jnp.where(row_id == j, 0.0, gram[:, j : j + 1] * pivot)
        gram, right = gram - factor * gram[j : j + 1, :], right - factor * right[j : j + 1, :]
    eye = row_id == lax.broadcasted_iota(jnp.int32, gram.shape, 1)
    return right / jnp.sum(jnp.where(eye, gram, 0.0), axis=1, keepdims=True)


def solve_packed_kernel(x_ref, o_ref):
    components = o_ref.shape[0]
    half = components // 2
    total = x_ref[0]
    for n in range(1, x_ref.shape[0]):
        total = total + x_ref[n]
    tail = total[components:]
    gram = jnp.concatenate([tail[:, :components], tail[:, components:]], axis=0)
    o_ref[...] = eliminate(gram, total[:components])


def solve_kernel(g_ref, n_ref, o_ref):
    o_ref[...] = eliminate(g_ref[...], n_ref[...])


def solve_call(kernel, out_shape, *args):
    return pl.pallas_call(
        kernel,
        out_shape=jax.ShapeDtypeStruct(out_shape, jnp.float32),
        in_specs=vmem(len(args)),
        out_specs=vmem(1)[0],
        compiler_params=pltpu.CompilerParams(vmem_limit_bytes=32 * MIB),
        name="solve",
    )(*args)


def doubling_gather(mine, axes, count, order):
    held = mine[None]
    for value in order:
        came = lax.ppermute(held, axes, [(i, i ^ value) for i in range(count)])
        held = jnp.concatenate([held, came], axis=0)
    return held


def on_device(intensity, elution, loadings, shifts, bin_weight):
    freq_count = lax.axis_size("freq")
    mz_count = lax.axis_size("mz")
    count = freq_count * mz_count
    components = loadings.shape[1]
    axes = ("freq", "mz")
    mine = pack(elution)
    own = intensity.shape[2] // freq_count
    packed = own == LANES and 2 * components == LANES
    order = None
    if count & (count - 1) == 0 and elution.shape[0] % 64 == 0:
        bits = [1 << b for b in range(count.bit_length() - 1)]
        order = tuple(bits[::-1][: len(bits) - 2] + [bits[0], bits[1]])
        gathered = doubling_gather(mine, axes, count, order)
    else:
        gathered = lax.all_gather(mine, axes, axis=0).reshape(-1, math.gcd(intensity.shape[1], LANES), LANES)
    u = circulant(bin_weight)
    numerator, gram = product(intensity, gathered, order, u, loadings, shifts, packed)
    if packed:
        spread = lax.all_to_all(numerator, "freq", 0, 0)
        return solve_call(solve_packed_kernel, (components, own), spread)
    gram = lax.psum(gram, "freq")
    owned = lax.psum_scatter(numerator, "freq", scatter_dimension=1, tiled=True)
    return solve_call(solve_kernel, (components, own), gram, owned)


def solution(mesh):
    in_specs = (P(None, "freq", "mz"), P(("freq", "mz"), None), P(), P(), P())
    out_specs = P(None, ("mz", "freq"))
    return jax.shard_map(on_device, mesh=mesh, in_specs=in_specs, out_specs=out_specs, check_vma=False)
```

```python
import functools
import math

import jax
import jax.numpy as jnp
import numpy as np
from jax import lax
from jax.experimental import pallas as pl
from jax.experimental.pallas import tpu as pltpu
from jax.sharding import PartitionSpec as P

PRECISE = lax.Precision.HIGHEST
LANES = 128
REACH = 256
MIB = 1024 * 1024


def f32_dot(a, b, dims=(((1,), (0,)), ((), ()))):
    return lax.dot_general(a, b, dims, precision=PRECISE, preferred_element_type=jnp.float32)


def two_terms(x):
    high = x.astype(jnp.bfloat16)
    low = (x - high.astype(jnp.float32)).astype(jnp.bfloat16)
    return high, low


def vmem(count):
    return [pl.BlockSpec(memory_space=pltpu.VMEM)] * count


def pack_kernel(x_ref, o_ref):
    x = x_ref[...]
    components, rows = x.shape
    pad = -rows % LANES
    if pad:
        x = jnp.concatenate([x, jnp.zeros((components, pad), x.dtype)], axis=1)
    high, low = two_terms(x.T[:rows])
    o_ref[...] = jnp.concatenate([high, low], axis=1)


def pack(elution):
    rows, components = elution.shape
    return pl.pallas_call(
        pack_kernel,
        out_shape=jax.ShapeDtypeStruct((rows, 2 * components), jnp.bfloat16),
        in_specs=vmem(1),
        out_specs=vmem(1)[0],
        name="pack_elution",
    )(elution.T)


def circulant_kernel(w_ref, lane_ref, twid_ref, row_ref, u_ref):
    rows = w_ref.shape[1]
    w = w_ref[...]
    over_lanes = (((0,), (0,)), ((), ()))
    a_re = f32_dot(w, lane_ref[0], over_lanes)
    a_im = -f32_dot(w, lane_ref[1], over_lanes)
    b_re = a_re * twid_ref[0] + a_im * twid_ref[1]
    b_im = a_im * twid_ref[0] - a_re * twid_ref[1]
    c = f32_dot(row_ref[0], b_re) + f32_dot(row_ref[1], b_im)
    sub = lax.broadcasted_iota(jnp.int32, (LANES, LANES), 0)
    lane = lax.broadcasted_iota(jnp.int32, (LANES, LANES), 1)

    def turned(row):
        return pltpu.roll(jnp.broadcast_to(c[row : row + 1], (LANES, LANES)), 0, 1, stride=1, stride_axis=0)

    before = turned(rows - 1)
    for row in range(rows):
        now = turned(row)
        high, low = two_terms(jnp.where(lane >= sub, now, before))
        u_ref[0:LANES, row * LANES : (row + 1) * LANES] = high
        u_ref[LANES:, row * LANES : (row + 1) * LANES] = low
        before = now


def circulant(bin_weight):
    length = bin_weight.shape[0]
    rows = length // LANES

    def tables(a, b, period):
        angle = 2.0 * math.pi / period * ((a[:, None] * b[None, :]) % period)
        return np.stack([np.cos(angle), np.sin(angle)])

    lane_ids, row_ids = np.arange(LANES), np.arange(rows)
    lane_table = tables(lane_ids, lane_ids, LANES).astype(np.float32)
    twid_table = tables(row_ids, lane_ids, length).astype(np.float32)
    row_table = (tables(row_ids, row_ids, rows) / length).astype(np.float32)
    return pl.pallas_call(
        circulant_kernel,
        out_shape=jax.ShapeDtypeStruct((2 * LANES, length), jnp.bfloat16),
        in_specs=vmem(4),
        out_specs=vmem(1)[0],
        cost_estimate=pl.CostEstimate(flops=2_000_000_000, bytes_accessed=4 * MIB, transcendentals=0),
        name="circulant_block",
    )(bin_weight.reshape(LANES, rows), lane_table, twid_table, row_table)


def product_kernel(places, doubled, *refs):
    if doubled:
        i_ref, own_ref, other_ref, u_hbm, amp_ref, lag_ref, keep_ref, send_ref = refs[:8]
    else:
        i_ref, own_ref, u_hbm, amp_ref, lag_ref, num_ref, gram_ref = refs[:7]
    u_ref, wide, terms, held, sems = refs[-5:]
    run_count, bin_count, local_mz = i_ref.shape
    components = amp_ref.shape[1]
    length = u_ref.shape[1]
    chunks = sems.shape[0] - 1
    chunk = local_mz // chunks
    u_copy = pltpu.make_async_copy(u_hbm, u_ref, sems.at[chunks])
    u_copy.start()
    copies = []
    for n in range(chunks):
        part = pl.ds(n * chunk, chunk)
        copies.append(pltpu.make_async_copy(i_ref.at[:, :, part], held.at[:, :, part], sems.at[n]))
        copies[-1].start()

    freq_rank = lax.axis_index("freq")
    if doubled:
        mz_rank = lax.axis_index("mz")
        freq_count = own_ref.shape[0]
        rows = own_ref.shape[1]
        for block in range(-1, freq_count + 1):
            apart = lax.bitwise_xor((freq_rank + block) & (freq_count - 1), freq_rank)
            place = 0
            for bit in range(freq_count.bit_length() - 1):
                place = place * 2 + ((apart >> bit) & 1)
            for ref, half in ((own_ref, mz_rank), (other_ref, 1 - mz_rank)):
                values = ref[pl.ds(place, 1)][0]
                to = pl.multiple_of(2 * REACH + block * bin_count + half * rows, 64)
                wide[pl.ds(to, rows), 0:LANES] = values
                wide[pl.ds(pl.multiple_of(to - LANES, 64), rows), LANES:] = values
    else:
        step = own_ref.shape[1]
        steps = length // step
        first = lax.rem(freq_rank * bin_count + length - REACH, length) // step

        def bring(j, carry):
            values = own_ref[pl.ds(lax.rem(first + j, steps), 1)][0]
            to = pl.multiple_of(REACH + j * step, step)
            wide[pl.ds(to, step), 0:LANES] = values
            wide[pl.ds(pl.multiple_of(to - LANES, step), step), LANES:] = values
            return carry

        lax.fori_loop(0, (wide.shape[0] - REACH) // step, bring, 0)

    u_copy.wait()
    pieces, windows = [], []
    for a in range(0, places, 2):
        at = REACH + a * LANES
        made = jnp.dot(u_ref[...], wide[at : at + length, :], preferred_element_type=jnp.float32)
        made = made[:LANES] + made[LANES:]
        for half in range(min(2, places - a)):
            piece = made[:, half * LANES : (half + 1) * LANES].T
            pieces.append(piece[:components] + piece[components:])
    for a in range(places):
        at = REACH + a * LANES
        piece = wide[at : at + LANES, 0:LANES].astype(jnp.float32).T
        windows.append(piece[:components] + piece[components:])
    base = jnp.concatenate(
        [jnp.concatenate(pieces, axis=1), jnp.concatenate(windows, axis=1)], axis=0
    )
    span = -(-bin_count // LANES) * LANES
    amps, lags = amp_ref[...].T, lag_ref[...].T
    for k in range(run_count):
        lag = lags[:, k : k + 1]
        left = REACH - 1 - jnp.concatenate([lag, lag], axis=0)
        y = base
        for bit in (7, 6, 5, 4, 3, 2, 1, 0):
            move = 1 << bit
            y = jnp.where((left & move) != 0, pltpu.roll(y, y.shape[1] - move, 1), y)
            if move == LANES:
                y = y[:, : span + LANES]
        y = pltpu.roll(y, y.shape[1] - 1, 1)[:, :bin_count]
        amp = amps[:, k : k + 1]
        high, low = two_terms(y * jnp.concatenate([amp, amp], axis=0))
        part = slice(k * bin_count, (k + 1) * bin_count)
        terms[0:components, part] = high[:components]
        terms[components : 2 * components, part] = low[:components]
        terms[2 * components : 3 * components, part] = high[components:]
        terms[3 * components :, part] = low[components:]
    gram = lax.dot_general(
        terms[0 : 2 * components, :],
        terms[2 * components :, :],
        (((1,), (1,)), ((), ())),
        preferred_element_type=jnp.float32,
    )
    gram = gram[:components] + gram[components:]
    gram = gram[:, :components] + gram[:, components:]
    if doubled:
        half = components // 2
        gram = jnp.concatenate([gram[:half], gram[half:]], axis=1)
        keep_ref[chunks * components :, :] = gram
        send_ref[chunks * components :, :] = gram
    else:
        gram_ref[...] = gram

    for n in range(chunks):
        copies[n].wait()
        data = held[:, :, n * chunk : (n + 1) * chunk].reshape(run_count * bin_count, chunk)
        made = jnp.dot(terms[0 : 2 * components, :], data, preferred_element_type=jnp.float32)
        made = made[:components] + made[components:]
        if doubled:
            core = freq_rank & 1
            apart = lax.bitwise_xor(freq_rank >> 1, n)
            place = 0
            for bit, value in enumerate(halving_order(freq_count)[1:][::-1]):
                place = place + (((apart >> (value.bit_length() - 2)) & 1) << bit)
            at = pl.ds(pl.multiple_of(place * components, components), components)
            even, odd = made[:, :LANES], made[:, LANES:]
            keep_ref[at, :] = jnp.where(core == 0, even, odd)
            send_ref[at, :] = jnp.where(core == 0, odd, even)
        else:
            num_ref[:, n * chunk : (n + 1) * chunk] = made


def halving_order(freq_count):
    bits = [1 << b for b in range(freq_count.bit_length() - 1)]
    return tuple(bits[:2] + bits[2:][::-1])


def product(intensity, gathered, u, loadings, shifts):
    run_count, bin_count, local_mz = intensity.shape
    components = loadings.shape[1]
    length = u.shape[1]
    places = -(-(bin_count + REACH) // LANES)
    chunk = 2 * LANES
    chunks = local_mz // chunk
    doubled = len(gathered) == 2
    if doubled:
        out_shapes = [(chunks * components + components // 2, LANES)] * 2
        wide_rows = 2 * REACH + length + bin_count
    else:
        out_shapes = [(components, local_mz), (components, components)]
        wide_rows = REACH + length + 2 * LANES * ((places - 1) // 2)
    return pl.pallas_call(
        functools.partial(product_kernel, places, doubled),
        out_shape=tuple(jax.ShapeDtypeStruct(shape, jnp.float32) for shape in out_shapes),
        in_specs=[pl.BlockSpec(memory_space=pl.ANY)]
        + vmem(len(gathered))
        + [pl.BlockSpec(memory_space=pl.ANY)]
        + vmem(2),
        out_specs=tuple(vmem(2)),
        scratch_shapes=[
            pltpu.VMEM(u.shape, jnp.bfloat16),
            pltpu.VMEM((wide_rows, 2 * LANES), jnp.bfloat16),
            pltpu.VMEM((4 * components, run_count * bin_count), jnp.bfloat16),
            pltpu.VMEM(intensity.shape, jnp.bfloat16),
            pltpu.SemaphoreType.DMA((chunks + 1,)),
        ],
        compiler_params=pltpu.CompilerParams(vmem_limit_bytes=48 * MIB),
        cost_estimate=pl.CostEstimate(
            flops=8_000_000_000, bytes_accessed=2 * intensity.size, transcendentals=0
        ),
        name="model_products",
    )(intensity, *gathered, u, loadings, shifts)


def eliminate(gram, right):
    components = gram.shape[0]
    row_id = lax.broadcasted_iota(jnp.int32, (components, 1), 0)
    for j in range(0, components, 2):
        first = jnp.broadcast_to(gram[:, j : j + 1], gram.shape)
        second = jnp.broadcast_to(gram[:, j + 1 : j + 2], gram.shape)
        a, b, d = first[j : j + 1], second[j : j + 1], second[j + 1 : j + 2]
        scale = 1.0 / (a * d - b * b)
        away = (row_id != j) & (row_id != j + 1)
        f1 = jnp.where(away, first * (d * scale) - second * (b * scale), 0.0)
        f2 = jnp.where(away, second * (a * scale) - first * (b * scale), 0.0)
        gram, right = (
            gram - f1 * gram[j : j + 1] - f2 * gram[j + 1 : j + 2],
            right - f1[:, : right.shape[1]] * right[j : j + 1] - f2[:, : right.shape[1]] * right[j + 1 : j + 2],
        )
    lane = lax.broadcasted_iota(jnp.int32, gram.shape, 1)
    even = row_id % 2 == 0

    def across(x):
        return jnp.where(even, pltpu.roll(x, components - 1, 0), pltpu.roll(x, 1, 0))

    own = jnp.sum(jnp.where(lane == row_id, gram, 0.0), axis=1, keepdims=True) + jnp.zeros_like(right)
    off = jnp.sum(jnp.where(lane == (row_id ^ 1), gram, 0.0), axis=1, keepdims=True)
    other = across(own)
    return (other * right - off * across(right)) / (other * own - off * off)


def summed(refs, rows, tail):
    total = refs[0][0:rows] + refs[1][0:rows]
    gram = refs[0][refs[0].shape[0] - tail :] + refs[1][refs[1].shape[0] - tail :]
    for ref in refs[2:]:
        total = total + ref[0:rows]
        gram = gram + ref[ref.shape[0] - tail :]
    return total, gram


def stage_kernel(tail, *refs):
    o_ref = refs[-1]
    half = o_ref.shape[0] - tail
    total, gram = summed(refs[:-1], 2 * half, tail)
    o_ref[0:half, :] = total[half:]
    o_ref[half:, :] = gram


def solve_doubled_kernel(tail, *refs):
    o_ref = refs[-1]
    total, gram = summed(refs[:-1], o_ref.shape[0], tail)
    gram = jnp.concatenate([gram, pltpu.roll(gram, gram.shape[1] // 2, 1)], axis=0)
    o_ref[...] = eliminate(gram, total)


def solve_kernel(g_ref, n_ref, o_ref):
    components = o_ref.shape[0]
    gram = jnp.concatenate([g_ref[...], jnp.zeros((components, LANES - components), jnp.float32)], axis=1)
    o_ref[...] = eliminate(gram, n_ref[...])


def small_call(kernel, out_shape, name, *args):
    return pl.pallas_call(
        kernel,
        out_shape=jax.ShapeDtypeStruct(out_shape, jnp.float32),
        in_specs=vmem(len(args)),
        out_specs=vmem(1)[0],
        compiler_params=pltpu.CompilerParams(vmem_limit_bytes=32 * MIB),
        name=name,
    )(*args)


def swap(x, axes, count, value):
    return lax.ppermute(x, axes, [(i, i ^ value) for i in range(count)])


def on_device(intensity, elution, loadings, shifts, bin_weight):
    freq_count = lax.axis_size("freq")
    mz_count = lax.axis_size("mz")
    components = loadings.shape[1]
    axes = ("freq", "mz")
    mine = pack(elution)
    own = intensity.shape[2] // freq_count
    doubled = (
        own == LANES
        and 2 * components == LANES
        and mz_count == 2
        and freq_count & (freq_count - 1) == 0
        and freq_count >= 4
        and elution.shape[0] % 64 == 0
        and intensity.shape[1] % LANES == 0
    )
    if not doubled:
        gathered = lax.all_gather(mine, axes, axis=0).reshape(-1, math.gcd(intensity.shape[1], LANES), LANES)
        numerator, gram = product(intensity, (gathered,), circulant(bin_weight), loadings, shifts)
        gram = lax.psum(gram, "freq")
        owned = lax.psum_scatter(numerator, "freq", scatter_dimension=1, tiled=True)
        return small_call(solve_kernel, (components, own), "solve", gram, owned)
    held = mine[None]
    for bit in reversed(range(freq_count.bit_length() - 1)):
        held = jnp.concatenate([held, swap(held, "freq", freq_count, 1 << bit)], axis=0)
    other = swap(held, "mz", mz_count, 1)
    u = circulant(bin_weight)
    keep, send = product(intensity, (held, other), u, loadings, shifts)
    tail = components // 2
    parts = [keep]
    stages = halving_order(freq_count)
    rows = keep.shape[0] - tail
    for index, value in enumerate(stages):
        parts.append(swap(send, "freq", freq_count, value))
        if index + 1 < len(stages):
            rows = rows // 2
            send = small_call(
                functools.partial(stage_kernel, tail), (rows + tail, LANES), "reduce_stage", *parts
            )
    return small_call(functools.partial(solve_doubled_kernel, tail), (components, own), "solve", *parts)


def solution(mesh):
    in_specs = (P(None, "freq", "mz"), P(("freq", "mz"), None), P(), P(), P())
    out_specs = P(None, ("mz", "freq"))
    return jax.shard_map(on_device, mesh=mesh, in_specs=in_specs, out_specs=out_specs, check_vma=False)
```

```python
import functools
import math

import jax
import jax.numpy as jnp
import numpy as np
from jax import lax
from jax.experimental import pallas as pl
from jax.experimental.pallas import tpu as pltpu
from jax.sharding import PartitionSpec as P

PRECISE = lax.Precision.HIGHEST
LANES = 128
REACH = 256
MIB = 1024 * 1024


def f32_dot(a, b, dims=(((1,), (0,)), ((), ()))):
    return lax.dot_general(a, b, dims, precision=PRECISE, preferred_element_type=jnp.float32)


def two_terms(x):
    high = x.astype(jnp.bfloat16)
    low = (x - high.astype(jnp.float32)).astype(jnp.bfloat16)
    return high, low


def vmem(count):
    return [pl.BlockSpec(memory_space=pltpu.VMEM)] * count


def pack_kernel(x_ref, o_ref):
    x = x_ref[...]
    components, rows = x.shape
    pad = -rows % LANES
    if pad:
        x = jnp.concatenate([x, jnp.zeros((components, pad), x.dtype)], axis=1)
    high, low = two_terms(x.T[:rows])
    o_ref[...] = jnp.concatenate([high, low], axis=1)


def pack(elution):
    rows, components = elution.shape
    return pl.pallas_call(
        pack_kernel,
        out_shape=jax.ShapeDtypeStruct((rows, 2 * components), jnp.bfloat16),
        in_specs=vmem(1),
        out_specs=vmem(1)[0],
        compiler_params=pltpu.CompilerParams(vmem_limit_bytes=8 * MIB),
        name="pack_elution",
    )(elution.T)


def circulant_kernel(w_ref, lane_ref, twid_ref, row_ref, u_ref):
    rows = w_ref.shape[1]
    w = w_ref[...]
    over_lanes = (((0,), (0,)), ((), ()))
    a_re = f32_dot(w, lane_ref[0], over_lanes)
    a_im = -f32_dot(w, lane_ref[1], over_lanes)
    b_re = a_re * twid_ref[0] + a_im * twid_ref[1]
    b_im = a_im * twid_ref[0] - a_re * twid_ref[1]
    c = f32_dot(row_ref[0], b_re) + f32_dot(row_ref[1], b_im)
    sub = lax.broadcasted_iota(jnp.int32, (LANES, LANES), 0)
    lane = lax.broadcasted_iota(jnp.int32, (LANES, LANES), 1)

    def turned(row):
        return pltpu.roll(jnp.broadcast_to(c[row : row + 1], (LANES, LANES)), 0, 1, stride=1, stride_axis=0)

    before = turned(rows - 1)
    for row in range(rows):
        now = turned(row)
        high, low = two_terms(jnp.where(lane >= sub, now, before))
        u_ref[0:LANES, row * LANES : (row + 1) * LANES] = high
        u_ref[LANES:, row * LANES : (row + 1) * LANES] = low
        before = now


def circulant(bin_weight):
    length = bin_weight.shape[0]
    rows = length // LANES

    def tables(a, b, period):
        angle = 2.0 * math.pi / period * ((a[:, None] * b[None, :]) % period)
        return np.stack([np.cos(angle), np.sin(angle)])

    lane_ids, row_ids = np.arange(LANES), np.arange(rows)
    lane_table = tables(lane_ids, lane_ids, LANES).astype(np.float32)
    twid_table = tables(row_ids, lane_ids, length).astype(np.float32)
    row_table = (tables(row_ids, row_ids, rows) / length).astype(np.float32)
    return pl.pallas_call(
        circulant_kernel,
        out_shape=jax.ShapeDtypeStruct((2 * LANES, length), jnp.bfloat16),
        in_specs=vmem(4),
        out_specs=vmem(1)[0],
        compiler_params=pltpu.CompilerParams(vmem_limit_bytes=16 * MIB),
        cost_estimate=pl.CostEstimate(flops=2_000_000_000, bytes_accessed=4 * MIB, transcendentals=0),
        name="circulant_block",
    )(bin_weight.reshape(LANES, rows), lane_table, twid_table, row_table)


def model_kernel(places, planes, *refs):
    u_ref, g_ref, wide = refs[-3:]
    length = u_ref.shape[1]
    components = g_ref.shape[0]
    freq_rank = lax.axis_index("freq")
    if planes:
        own_ref, came_ref = refs[:2]
        mz_rank = lax.axis_index("mz")
        freq_count = 2 * own_ref.shape[0]
        rows = own_ref.shape[1]
        empty = jnp.zeros((rows, LANES), jnp.bfloat16)
        for block in range(-1, freq_count + 1):
            apart = lax.bitwise_xor((freq_rank + block) & (freq_count - 1), freq_rank)
            ref = came_ref if block % 2 else own_ref
            values = ref[pl.ds(block_place(apart, freq_count), 1)][0]
            for here, half in ((values, mz_rank), (empty, 1 - mz_rank)):
                to = pl.multiple_of(2 * REACH + (2 * block + half) * rows, 64)
                wide[pl.ds(to, rows), 0:LANES] = here
                wide[pl.ds(pl.multiple_of(to - LANES, 64), rows), LANES:] = here
    else:
        own_ref = refs[0]
        step = own_ref.shape[1]
        steps = length // step
        bin_count = length // lax.axis_size("freq")
        first = lax.rem(freq_rank * bin_count + length - REACH, length) // step

        def bring(j, carry):
            values = own_ref[pl.ds(lax.rem(first + j, steps), 1)][0]
            to = pl.multiple_of(REACH + j * step, step)
            wide[pl.ds(to, step), 0:LANES] = values
            wide[pl.ds(pl.multiple_of(to - LANES, step), step), LANES:] = values
            return carry

        lax.fori_loop(0, (wide.shape[0] - REACH) // step, bring, 0)
    for a in range(0, places, 2):
        at = REACH + a * LANES
        made = jnp.dot(u_ref[...], wide[at : at + length, :], preferred_element_type=jnp.float32)
        made = made[:LANES] + made[LANES:]
        for half in range(min(2, places - a)):
            piece = made[:, half * LANES : (half + 1) * LANES].T
            g_ref[:, (a + half) * LANES : (a + half + 1) * LANES] = piece[:components] + piece[components:]


def block_place(apart, freq_count):
    return (apart >> 2) + ((apart >> 1) & 1) * (freq_count // 4)


def partial_model(gathered, u, bin_count, components):
    length = u.shape[1]
    places = -(-(bin_count + REACH) // LANES)
    planes = len(gathered) == 2
    wide_rows = 2 * REACH + length + bin_count if planes else REACH + length + 2 * LANES * ((places - 1) // 2)
    return pl.pallas_call(
        functools.partial(model_kernel, places, planes),
        out_shape=jax.ShapeDtypeStruct((components, places * LANES), jnp.float32),
        in_specs=vmem(len(gathered) + 1),
        out_specs=vmem(1)[0],
        scratch_shapes=[pltpu.VMEM((wide_rows, 2 * LANES), jnp.bfloat16)],
        compiler_params=pltpu.CompilerParams(vmem_limit_bytes=24 * MIB),
        cost_estimate=pl.CostEstimate(flops=2_000_000_000, bytes_accessed=4 * MIB, transcendentals=0),
        name="partial_model",
    )(*gathered, u)


def product_kernel(parts, planes, *refs):
    i_ref = refs[0]
    g_refs = refs[1 : 1 + parts]
    if planes:
        mine_ref, came_ref, near_ref, far_ref, amp_ref, lag_ref, keep_ref, send_ref = refs[1 + parts : 9 + parts]
    else:
        own_ref, amp_ref, lag_ref, num_ref, gram_ref = refs[1 + parts : 6 + parts]
    window, terms, held, sems = refs[-4:]
    run_count, bin_count, local_mz = i_ref.shape
    components = amp_ref.shape[1]
    chunks = sems.shape[0]
    chunk = local_mz // chunks
    copies = []
    for n in range(chunks):
        part = pl.ds(n * chunk, chunk)
        copies.append(pltpu.make_async_copy(i_ref.at[:, :, part], held.at[:, :, part], sems.at[n]))
        copies[-1].start()

    freq_rank = lax.axis_index("freq")
    if planes:
        mz_rank = lax.axis_index("mz")
        freq_count = 2 * came_ref.shape[0]
        rows = mine_ref.shape[0]
        apart = lax.bitwise_xor((freq_rank - 1) & (freq_count - 1), freq_rank)
        before = came_ref[pl.ds(block_place(apart, freq_count), 1)][0]
        skip = bin_count - REACH
        for block, half, values in (
            (0, mz_rank, before),
            (0, 1 - mz_rank, far_ref[...]),
            (1, mz_rank, mine_ref[...]),
            (1, 1 - mz_rank, near_ref[...]),
        ):
            window[pl.ds(pl.multiple_of((2 * block + half) * rows, 64), rows), :] = values
    else:
        step = own_ref.shape[1]
        steps = own_ref.shape[0]
        first = lax.rem(freq_rank * bin_count + steps * step - REACH, steps * step) // step
        skip = 0
        for j in range(window.shape[0] // step):
            window[j * step : (j + 1) * step, :] = own_ref[pl.ds(lax.rem(first + j, steps), 1)][0]
    g = g_refs[0][...]
    for ref in g_refs[1:]:
        g = g + ref[...]
    pieces = []
    for a in range(g.shape[1] // LANES):
        piece = window[skip + a * LANES : skip + (a + 1) * LANES, :].astype(jnp.float32).T
        pieces.append(piece[:components] + piece[components:])
    base = jnp.concatenate([g, jnp.concatenate(pieces, axis=1)], axis=0)
    span = -(-bin_count // LANES) * LANES
    amps, lags = amp_ref[...].T, lag_ref[...].T
    for k in range(run_count):
        lag = lags[:, k : k + 1]
        left = REACH - 1 - jnp.concatenate([lag, lag], axis=0)
        y = base
        for bit in (7, 6, 5, 4, 3, 2, 1, 0):
            move = 1 << bit
            y = jnp.where((left & move) != 0, pltpu.roll(y, y.shape[1] - move, 1), y)
            if move == LANES:
                y = y[:, : span + LANES]
        y = pltpu.roll(y, y.shape[1] - 1, 1)[:, :bin_count]
        amp = amps[:, k : k + 1]
        high, low = two_terms(y * jnp.concatenate([amp, amp], axis=0))
        part = slice(k * bin_count, (k + 1) * bin_count)
        terms[0:components, part] = high[:components]
        terms[components : 2 * components, part] = low[:components]
        terms[2 * components : 3 * components, part] = high[components:]
        terms[3 * components :, part] = low[components:]
    gram = lax.dot_general(
        terms[0 : 2 * components, :],
        terms[2 * components :, :],
        (((1,), (1,)), ((), ())),
        preferred_element_type=jnp.float32,
    )
    gram = gram[:components] + gram[components:]
    gram = gram[:, :components] + gram[:, components:]
    if planes:
        half = components // 2
        gram = jnp.concatenate([gram[:half], gram[half:]], axis=1)
        keep_ref[chunks * components :, :] = gram
        send_ref[chunks * components :, :] = gram
    else:
        gram_ref[...] = gram

    for n in range(chunks):
        copies[n].wait()
        data = held[:, :, n * chunk : (n + 1) * chunk].reshape(run_count * bin_count, chunk)
        made = jnp.dot(terms[0 : 2 * components, :], data, preferred_element_type=jnp.float32)
        made = made[:components] + made[components:]
        if planes:
            core = freq_rank & 1
            place = block_place(lax.bitwise_xor(freq_rank, 2 * n + core), freq_count)
            at = pl.ds(pl.multiple_of(place * components, components), components)
            even, odd = made[:, :LANES], made[:, LANES:]
            keep_ref[at, :] = jnp.where(core == 0, even, odd)
            send_ref[at, :] = jnp.where(core == 0, odd, even)
        else:
            num_ref[:, n * chunk : (n + 1) * chunk] = made


def product(intensity, models, elutions, loadings, shifts):
    run_count, bin_count, local_mz = intensity.shape
    components = loadings.shape[1]
    chunk = 2 * LANES
    chunks = local_mz // chunk
    planes = len(elutions) > 1
    if planes:
        out_shapes = [(chunks * components + components // 2, LANES)] * 2
        window_rows = 2 * bin_count
    else:
        out_shapes = [(components, local_mz), (components, components)]
        window_rows = models[0].shape[1]
    return pl.pallas_call(
        functools.partial(product_kernel, len(models), planes),
        out_shape=tuple(jax.ShapeDtypeStruct(shape, jnp.float32) for shape in out_shapes),
        in_specs=[pl.BlockSpec(memory_space=pl.ANY)] + vmem(len(models) + len(elutions) + 2),
        out_specs=tuple(vmem(2)),
        scratch_shapes=[
            pltpu.VMEM((window_rows, LANES), jnp.bfloat16),
            pltpu.VMEM((4 * components, run_count * bin_count), jnp.bfloat16),
            pltpu.VMEM(intensity.shape, jnp.bfloat16),
            pltpu.SemaphoreType.DMA((chunks,)),
        ],
        compiler_params=pltpu.CompilerParams(vmem_limit_bytes=48 * MIB),
        cost_estimate=pl.CostEstimate(
            flops=8_000_000_000, bytes_accessed=2 * intensity.size, transcendentals=0
        ),
        name="model_products",
    )(intensity, *models, *elutions, loadings, shifts)


def eliminate(gram, right):
    components = gram.shape[0]
    row_id = lax.broadcasted_iota(jnp.int32, (components, 1), 0)
    for j in range(0, components, 2):
        first = jnp.broadcast_to(gram[:, j : j + 1], gram.shape)
        second = jnp.broadcast_to(gram[:, j + 1 : j + 2], gram.shape)
        a, b, d = first[j : j + 1], second[j : j + 1], second[j + 1 : j + 2]
        scale = 1.0 / (a * d - b * b)
        away = (row_id != j) & (row_id != j + 1)
        f1 = jnp.where(away, first * (d * scale) - second * (b * scale), 0.0)
        f2 = jnp.where(away, second * (a * scale) - first * (b * scale), 0.0)
        gram, right = (
            gram - f1 * gram[j : j + 1] - f2 * gram[j + 1 : j + 2],
            right - f1[:, : right.shape[1]] * right[j : j + 1] - f2[:, : right.shape[1]] * right[j + 1 : j + 2],
        )
    lane = lax.broadcasted_iota(jnp.int32, gram.shape, 1)
    even = row_id % 2 == 0

    def across(x):
        return jnp.where(even, pltpu.roll(x, components - 1, 0), pltpu.roll(x, 1, 0))

    own = jnp.sum(jnp.where(lane == row_id, gram, 0.0), axis=1, keepdims=True) + jnp.zeros_like(right)
    off = jnp.sum(jnp.where(lane == (row_id ^ 1), gram, 0.0), axis=1, keepdims=True)
    other = across(own)
    return (other * right - off * across(right)) / (other * own - off * off)


def summed(refs, rows, tail):
    total = refs[0][0:rows] + refs[1][0:rows]
    gram = refs[0][refs[0].shape[0] - tail :] + refs[1][refs[1].shape[0] - tail :]
    for ref in refs[2:]:
        total = total + ref[0:rows]
        gram = gram + ref[ref.shape[0] - tail :]
    return total, gram


def stage_kernel(tail, count, *refs):
    outs = refs[-count:]
    rows = outs[0].shape[0] - tail
    total, gram = summed(refs[:-count], (count + 1) * rows, tail)
    for n, o_ref in enumerate(outs):
        o_ref[0:rows, :] = total[(n + 1) * rows : (n + 2) * rows]
        o_ref[rows:, :] = gram


def solve_planes_kernel(tail, *refs):
    o_ref = refs[-1]
    total, gram = summed(refs[:-1], o_ref.shape[0], tail)
    gram = jnp.concatenate([gram, pltpu.roll(gram, gram.shape[1] // 2, 1)], axis=0)
    o_ref[...] = eliminate(gram, total)


def solve_kernel(g_ref, n_ref, o_ref):
    components = o_ref.shape[0]
    gram = jnp.concatenate([g_ref[...], jnp.zeros((components, LANES - components), jnp.float32)], axis=1)
    o_ref[...] = eliminate(gram, n_ref[...])


def small_call(kernel, out_shape, name, *args, count=1):
    outs = pl.pallas_call(
        kernel,
        out_shape=(jax.ShapeDtypeStruct(out_shape, jnp.float32),) * count,
        in_specs=vmem(len(args)),
        out_specs=tuple(vmem(count)),
        compiler_params=pltpu.CompilerParams(vmem_limit_bytes=8 * MIB),
        name=name,
    )(*args)
    return outs


def swap(x, axes, count, value):
    return lax.ppermute(x, axes, [(i, i ^ value) for i in range(count)])


def on_device(intensity, elution, loadings, shifts, bin_weight):
    freq_count = lax.axis_size("freq")
    mz_count = lax.axis_size("mz")
    components = loadings.shape[1]
    bin_count = intensity.shape[1]
    axes = ("freq", "mz")
    mine = pack(elution)
    own = intensity.shape[2] // freq_count
    planes = (
        own == LANES
        and 2 * components == LANES
        and mz_count == 2
        and freq_count & (freq_count - 1) == 0
        and freq_count >= 8
        and elution.shape[0] % 64 == 0
        and bin_count % LANES == 0
        and bin_count >= REACH
    )
    if not planes:
        gathered = lax.all_gather(mine, axes, axis=0).reshape(-1, math.gcd(bin_count, LANES), LANES)
        g = partial_model((gathered,), circulant(bin_weight), bin_count, components)
        numerator, gram = product(intensity, (g,), (gathered,), loadings, shifts)
        gram = lax.psum(gram, "freq")
        owned = lax.psum_scatter(numerator, "freq", scatter_dimension=1, tiled=True)
        return small_call(solve_kernel, (components, own), "solve", gram, owned)[0]
    z_steps = range(4, freq_count, 4)
    held = jnp.stack([mine] + [swap(mine, "freq", freq_count, step) for step in z_steps])
    held = jnp.concatenate([held, swap(held, "freq", freq_count, 2)], axis=0)
    u = circulant(bin_weight)
    held, u = lax.optimization_barrier((held, u))
    came = swap(held, "freq", freq_count, 1)
    near = swap(mine, "mz", mz_count, 1)
    onward = [
        (f * mz_count + y, (f + 1) % freq_count * mz_count + 1 - y)
        for f in range(freq_count)
        for y in range(mz_count)
    ]
    far = lax.ppermute(mine, axes, onward)
    g = partial_model((held, came), u, bin_count, components)
    models = (g, swap(g, "mz", mz_count, 1))
    keep, send = product(intensity, models, (mine, came, near, far), loadings, shifts)
    tail = components // 2
    quarter = freq_count // 4 * components
    parts = [keep, swap(send, "freq", freq_count, 1)]
    (send,) = small_call(
        functools.partial(stage_kernel, tail, 1), (quarter + tail, LANES), "reduce_stage", *parts
    )
    parts.append(swap(send, "freq", freq_count, 2))
    count = len(z_steps)
    sends = small_call(
        functools.partial(stage_kernel, tail, count), (components + tail, LANES), "reduce_stage", *parts, count=count
    )
    parts += [swap(send, "freq", freq_count, step) for send, step in zip(sends, z_steps)]
    return small_call(functools.partial(solve_planes_kernel, tail), (components, own), "solve", *parts)[0]


def solution(mesh):
    in_specs = (P(None, "freq", "mz"), P(("freq", "mz"), None), P(), P(), P())
    out_specs = P(None, ("mz", "freq"))
    return jax.shard_map(on_device, mesh=mesh, in_specs=in_specs, out_specs=out_specs, check_vma=False)
```

```python
import functools
import math

import jax
import jax.numpy as jnp
import numpy as np
from jax import lax
from jax.experimental import pallas as pl
from jax.experimental.pallas import tpu as pltpu
from jax.sharding import PartitionSpec as P

PRECISE = lax.Precision.HIGHEST
LANES = 128
REACH = 256
MIB = 1024 * 1024


def f32_dot(a, b, dims=(((1,), (0,)), ((), ()))):
    return lax.dot_general(a, b, dims, precision=PRECISE, preferred_element_type=jnp.float32)


def two_terms(x):
    high = x.astype(jnp.bfloat16)
    low = (x - high.astype(jnp.float32)).astype(jnp.bfloat16)
    return high, low


def vmem(count):
    return [pl.BlockSpec(memory_space=pltpu.VMEM)] * count


def pack_kernel(x_ref, o_ref):
    x = x_ref[...]
    components, rows = x.shape
    pad = -rows % LANES
    if pad:
        x = jnp.concatenate([x, jnp.zeros((components, pad), x.dtype)], axis=1)
    high, low = two_terms(x.T[:rows])
    o_ref[...] = jnp.concatenate([high, low], axis=1)


def pack(elution):
    rows, components = elution.shape
    return pl.pallas_call(
        pack_kernel,
        out_shape=jax.ShapeDtypeStruct((rows, 2 * components), jnp.bfloat16),
        in_specs=vmem(1),
        out_specs=vmem(1)[0],
        compiler_params=pltpu.CompilerParams(vmem_limit_bytes=8 * MIB),
        name="pack_elution",
    )(elution.T)


def circulant_kernel(w_ref, table_ref, u_ref):
    rows = w_ref.shape[1]
    w = w_ref[...]
    over_lanes = (((0,), (0,)), ((), ()))

    def table(at, height, width):
        return table_ref[at : at + height, :width], table_ref[at + height : at + 2 * height, :width]

    lane_cos, lane_sin = table(0, LANES, LANES)
    twid_cos, twid_sin = table(2 * LANES, rows, LANES)
    row_cos, row_sin = table(2 * LANES + 2 * rows, rows, rows)
    a_re = f32_dot(w, lane_cos, over_lanes)
    a_im = -f32_dot(w, lane_sin, over_lanes)
    b_re = a_re * twid_cos + a_im * twid_sin
    b_im = a_im * twid_cos - a_re * twid_sin
    c = f32_dot(row_cos, b_re) + f32_dot(row_sin, b_im)
    sub = lax.broadcasted_iota(jnp.int32, (LANES, LANES), 0)
    lane = lax.broadcasted_iota(jnp.int32, (LANES, LANES), 1)

    def turned(row):
        return pltpu.roll(jnp.broadcast_to(c[row : row + 1], (LANES, LANES)), 0, 1, stride=1, stride_axis=0)

    before = turned(rows - 1)
    for row in range(rows):
        now = turned(row)
        high, low = two_terms(jnp.where(lane >= sub, now, before))
        u_ref[0:LANES, row * LANES : (row + 1) * LANES] = high
        u_ref[LANES:, row * LANES : (row + 1) * LANES] = low
        before = now


def circulant(bin_weight):
    length = bin_weight.shape[0]
    rows = length // LANES

    def tables(a, b, period):
        angle = 2.0 * math.pi / period * ((a[:, None] * b[None, :]) % period)
        return np.pad(np.concatenate([np.cos(angle), np.sin(angle)]), ((0, 0), (0, LANES - b.size)))

    lane_ids, row_ids = np.arange(LANES), np.arange(rows)
    table = np.concatenate(
        [
            tables(lane_ids, lane_ids, LANES),
            tables(row_ids, lane_ids, length),
            tables(row_ids, row_ids, rows) / length,
        ]
    ).astype(np.float32)
    return pl.pallas_call(
        circulant_kernel,
        out_shape=jax.ShapeDtypeStruct((2 * LANES, length), jnp.bfloat16),
        in_specs=vmem(2),
        out_specs=vmem(1)[0],
        compiler_params=pltpu.CompilerParams(vmem_limit_bytes=16 * MIB),
        cost_estimate=pl.CostEstimate(flops=2_000_000_000, bytes_accessed=4 * MIB, transcendentals=0),
        name="circulant_block",
    )(bin_weight.reshape(LANES, rows), table)


def model_kernel(places, planes, *refs):
    u_ref, g_ref, wide = refs[-3:]
    length = u_ref.shape[1]
    components = g_ref.shape[0]
    freq_rank = lax.axis_index("freq")
    if planes:
        own_ref, came_ref = refs[:2]
        mz_rank = lax.axis_index("mz")
        freq_count = 2 * own_ref.shape[0]
        rows = own_ref.shape[1]
        empty = jnp.zeros((rows, LANES), jnp.bfloat16)
        for block in range(-1, freq_count + 1):
            apart = lax.bitwise_xor((freq_rank + block) & (freq_count - 1), freq_rank)
            ref = came_ref if block % 2 else own_ref
            values = ref[pl.ds(block_place(apart, freq_count), 1)][0]
            for here, half in ((values, mz_rank), (empty, 1 - mz_rank)):
                to = pl.multiple_of(2 * REACH + (2 * block + half) * rows, 64)
                wide[pl.ds(to, rows), 0:LANES] = here
                wide[pl.ds(pl.multiple_of(to - LANES, 64), rows), LANES:] = here
    else:
        own_ref = refs[0]
        step = own_ref.shape[1]
        steps = length // step
        bin_count = length // lax.axis_size("freq")
        first = lax.rem(freq_rank * bin_count + length - REACH, length) // step

        def bring(j, carry):
            values = own_ref[pl.ds(lax.rem(first + j, steps), 1)][0]
            to = pl.multiple_of(REACH + j * step, step)
            wide[pl.ds(to, step), 0:LANES] = values
            wide[pl.ds(pl.multiple_of(to - LANES, step), step), LANES:] = values
            return carry

        lax.fori_loop(0, (wide.shape[0] - REACH) // step, bring, 0)
    for a in range(0, places, 2):
        at = REACH + a * LANES
        made = jnp.dot(u_ref[...], wide[at : at + length, :], preferred_element_type=jnp.float32)
        made = made[:LANES] + made[LANES:]
        for half in range(min(2, places - a)):
            piece = made[:, half * LANES : (half + 1) * LANES].T
            g_ref[:, (a + half) * LANES : (a + half + 1) * LANES] = piece[:components] + piece[components:]


def block_place(apart, freq_count):
    return (apart >> 2) + ((apart >> 1) & 1) * (freq_count // 4)


def partial_model(gathered, u, bin_count, components):
    length = u.shape[1]
    places = -(-(bin_count + REACH) // LANES)
    planes = len(gathered) == 2
    wide_rows = 2 * REACH + length + bin_count if planes else REACH + length + 2 * LANES * ((places - 1) // 2)
    return pl.pallas_call(
        functools.partial(model_kernel, places, planes),
        out_shape=jax.ShapeDtypeStruct((components, places * LANES), jnp.float32),
        in_specs=vmem(len(gathered) + 1),
        out_specs=vmem(1)[0],
        scratch_shapes=[pltpu.VMEM((wide_rows, 2 * LANES), jnp.bfloat16)],
        compiler_params=pltpu.CompilerParams(vmem_limit_bytes=24 * MIB),
        cost_estimate=pl.CostEstimate(flops=2_000_000_000, bytes_accessed=4 * MIB, transcendentals=0),
        name="partial_model",
    )(*gathered, u)


def shifted_terms(x, amps, lags, bin_count, terms):
    components = x.shape[0]
    out_count = -(-bin_count // LANES)
    x = pltpu.roll(x, x.shape[1] - 1, 1)
    height = 16
    lane = lax.broadcasted_iota(jnp.int32, (height, LANES), 1)
    for at in range(0, components, height):
        vectors = [x[at : at + height, v * LANES : (v + 1) * LANES] for v in range(out_count + 2)]
        for k in range(amps.shape[1]):
            left = REACH - 1 - jnp.broadcast_to(lags[at : at + height, k : k + 1], lane.shape)
            amp = jnp.broadcast_to(amps[at : at + height, k : k + 1], lane.shape)
            source = lane + (left & (LANES - 1))
            index = source & (LANES - 1)
            far, same = left >= LANES, source < LANES
            turned = [jnp.take_along_axis(v, index, axis=1, mode="promise_in_bounds") for v in vectors]
            turned = [jnp.where(far, turned[v + 1], turned[v]) for v in range(out_count + 1)]
            for v in range(out_count):
                high, low = two_terms(amp * jnp.where(same, turned[v], turned[v + 1]))
                width = min(LANES, bin_count - v * LANES)
                to = slice(k * bin_count + v * LANES, k * bin_count + v * LANES + width)
                terms[at : at + height, to] = high[:, :width]
                terms[components + at : components + at + height, to] = low[:, :width]


def elution_kernel(planes, *refs):
    amp_ref, lag_ref, terms, window = refs[-4:]
    components = amp_ref.shape[1]
    bin_count = terms.shape[1] // amp_ref.shape[0]
    freq_rank = lax.axis_index("freq")
    if planes:
        mine_ref, came_ref, near_ref, far_ref = refs[:4]
        mz_rank = lax.axis_index("mz")
        freq_count = 2 * came_ref.shape[0]
        rows = mine_ref.shape[0]
        apart = lax.bitwise_xor((freq_rank - 1) & (freq_count - 1), freq_rank)
        before = came_ref[pl.ds(block_place(apart, freq_count), 1)][0]
        skip = bin_count - REACH
        for block, half, values in (
            (0, mz_rank, before),
            (0, 1 - mz_rank, far_ref[...]),
            (1, mz_rank, mine_ref[...]),
            (1, 1 - mz_rank, near_ref[...]),
        ):
            window[pl.ds(pl.multiple_of((2 * block + half) * rows, 64), rows), :] = values
    else:
        own_ref = refs[0]
        step = own_ref.shape[1]
        steps = own_ref.shape[0]
        first = lax.rem(freq_rank * bin_count + steps * step - REACH, steps * step) // step
        skip = 0
        for j in range(window.shape[0] // step):
            window[j * step : (j + 1) * step, :] = own_ref[pl.ds(lax.rem(first + j, steps), 1)][0]
    pieces = []
    for at in range(skip, window.shape[0], LANES):
        piece = window[at : at + LANES, :].astype(jnp.float32).T
        pieces.append(piece[:components] + piece[components:])
    shifted_terms(jnp.concatenate(pieces, axis=1), amp_ref[...].T, lag_ref[...].T, bin_count, terms)


def elution_terms(elutions, loadings, shifts, bin_count):
    run_count, components = loadings.shape
    places = -(-(bin_count + REACH) // LANES)
    planes = len(elutions) > 1
    return pl.pallas_call(
        functools.partial(elution_kernel, planes),
        out_shape=jax.ShapeDtypeStruct((2 * components, run_count * bin_count), jnp.bfloat16),
        in_specs=vmem(len(elutions) + 2),
        out_specs=vmem(1)[0],
        scratch_shapes=[pltpu.VMEM((2 * bin_count if planes else places * LANES, LANES), jnp.bfloat16)],
        compiler_params=pltpu.CompilerParams(vmem_limit_bytes=12 * MIB),
        cost_estimate=pl.CostEstimate(flops=1_000_000_000, bytes_accessed=2 * MIB, transcendentals=0),
        name="elution_terms",
    )(*elutions, loadings, shifts)


def product_kernel(parts, planes, *refs):
    i_ref = refs[0]
    g_refs = refs[1 : 1 + parts]
    elution_ref, amp_ref, lag_ref, num_ref, other_ref, terms, held, sems = refs[1 + parts :]
    run_count, bin_count, local_mz = i_ref.shape
    components = amp_ref.shape[1]
    chunks = sems.shape[0]
    chunk = local_mz // chunks
    copies = []
    for n in range(chunks):
        part = pl.ds(n * chunk, chunk)
        copies.append(pltpu.make_async_copy(i_ref.at[:, :, part], held.at[:, :, part], sems.at[n]))
        copies[-1].start()

    g = g_refs[0][...]
    for ref in g_refs[1:]:
        g = g + ref[...]
    shifted_terms(g, amp_ref[...].T, lag_ref[...].T, bin_count, terms)
    gram = lax.dot_general(
        terms[...], elution_ref[...], (((1,), (1,)), ((), ())), preferred_element_type=jnp.float32
    )
    gram = gram[:components] + gram[components:]
    gram = gram[:, :components] + gram[:, components:]
    if planes:
        keep_ref, send_ref = num_ref, other_ref
        half = components // 2
        gram = jnp.concatenate([gram[:half], gram[half:]], axis=1)
        keep_ref[chunks * components :, :] = gram
        send_ref[chunks * components :, :] = gram
    else:
        other_ref[...] = gram

    for n in range(chunks):
        copies[n].wait()
        data = held[:, :, n * chunk : (n + 1) * chunk].reshape(run_count * bin_count, chunk)
        made = jnp.dot(terms[...], data, preferred_element_type=jnp.float32)
        made = made[:components] + made[components:]
        if planes:
            freq_rank = lax.axis_index("freq")
            core = freq_rank & 1
            place = block_place(lax.bitwise_xor(freq_rank, 2 * n + core), 2 * chunks)
            at = pl.ds(pl.multiple_of(place * components, components), components)
            even, odd = made[:, :LANES], made[:, LANES:]
            keep_ref[at, :] = jnp.where(core == 0, even, odd)
            send_ref[at, :] = jnp.where(core == 0, odd, even)
        else:
            num_ref[:, n * chunk : (n + 1) * chunk] = made


def product(intensity, models, elution, loadings, shifts, planes):
    run_count, bin_count, local_mz = intensity.shape
    components = loadings.shape[1]
    chunk = 2 * LANES
    chunks = local_mz // chunk
    if planes:
        out_shapes = [(chunks * components + components // 2, LANES)] * 2
    else:
        out_shapes = [(components, local_mz), (components, components)]
    return pl.pallas_call(
        functools.partial(product_kernel, len(models), planes),
        out_shape=tuple(jax.ShapeDtypeStruct(shape, jnp.float32) for shape in out_shapes),
        in_specs=[pl.BlockSpec(memory_space=pl.ANY)] + vmem(len(models) + 3),
        out_specs=tuple(vmem(2)),
        scratch_shapes=[
            pltpu.VMEM((2 * components, run_count * bin_count), jnp.bfloat16),
            pltpu.VMEM(intensity.shape, jnp.bfloat16),
            pltpu.SemaphoreType.DMA((chunks,)),
        ],
        compiler_params=pltpu.CompilerParams(vmem_limit_bytes=48 * MIB),
        cost_estimate=pl.CostEstimate(
            flops=8_000_000_000, bytes_accessed=2 * intensity.size, transcendentals=0
        ),
        name="model_products",
    )(intensity, *models, elution, loadings, shifts)


def eliminate(gram, right):
    components = gram.shape[0]
    row_id = lax.broadcasted_iota(jnp.int32, (components, 1), 0)
    for j in range(0, components, 2):
        first = jnp.broadcast_to(gram[:, j : j + 1], gram.shape)
        second = jnp.broadcast_to(gram[:, j + 1 : j + 2], gram.shape)
        a, b, d = first[j : j + 1], second[j : j + 1], second[j + 1 : j + 2]
        scale = 1.0 / (a * d - b * b)
        away = (row_id != j) & (row_id != j + 1)
        f1 = jnp.where(away, first * (d * scale) - second * (b * scale), 0.0)
        f2 = jnp.where(away, second * (a * scale) - first * (b * scale), 0.0)
        gram, right = (
            gram - f1 * gram[j : j + 1] - f2 * gram[j + 1 : j + 2],
            right - f1[:, : right.shape[1]] * right[j : j + 1] - f2[:, : right.shape[1]] * right[j + 1 : j + 2],
        )
    lane = lax.broadcasted_iota(jnp.int32, gram.shape, 1)
    even = row_id % 2 == 0

    def across(x):
        return jnp.where(even, pltpu.roll(x, components - 1, 0), pltpu.roll(x, 1, 0))

    own = jnp.sum(jnp.where(lane == row_id, gram, 0.0), axis=1, keepdims=True) + jnp.zeros_like(right)
    off = jnp.sum(jnp.where(lane == (row_id ^ 1), gram, 0.0), axis=1, keepdims=True)
    other = across(own)
    return (other * right - off * across(right)) / (other * own - off * off)


def summed(refs, rows, tail):
    total = refs[0][0:rows] + refs[1][0:rows]
    gram = refs[0][refs[0].shape[0] - tail :] + refs[1][refs[1].shape[0] - tail :]
    for ref in refs[2:]:
        total = total + ref[0:rows]
        gram = gram + ref[ref.shape[0] - tail :]
    return total, gram


def stage_kernel(tail, count, *refs):
    outs = refs[-count:]
    rows = outs[0].shape[0] - tail
    total, gram = summed(refs[:-count], (count + 1) * rows, tail)
    for n, o_ref in enumerate(outs):
        o_ref[0:rows, :] = total[(n + 1) * rows : (n + 2) * rows]
        o_ref[rows:, :] = gram


def solve_planes_kernel(tail, *refs):
    o_ref = refs[-1]
    total, gram = summed(refs[:-1], o_ref.shape[0], tail)
    gram = jnp.concatenate([gram, pltpu.roll(gram, gram.shape[1] // 2, 1)], axis=0)
    o_ref[...] = eliminate(gram, total)


def solve_kernel(g_ref, n_ref, o_ref):
    components = o_ref.shape[0]
    gram = jnp.concatenate([g_ref[...], jnp.zeros((components, LANES - components), jnp.float32)], axis=1)
    o_ref[...] = eliminate(gram, n_ref[...])


def small_call(kernel, out_shape, name, *args, count=1):
    outs = pl.pallas_call(
        kernel,
        out_shape=(jax.ShapeDtypeStruct(out_shape, jnp.float32),) * count,
        in_specs=vmem(len(args)),
        out_specs=tuple(vmem(count)),
        compiler_params=pltpu.CompilerParams(vmem_limit_bytes=8 * MIB),
        name=name,
    )(*args)
    return outs


def swap(x, axes, count, value):
    return lax.ppermute(x, axes, [(i, i ^ value) for i in range(count)])


def on_device(intensity, elution, loadings, shifts, bin_weight):
    freq_count = lax.axis_size("freq")
    mz_count = lax.axis_size("mz")
    components = loadings.shape[1]
    bin_count = intensity.shape[1]
    axes = ("freq", "mz")
    mine = pack(elution)
    own = intensity.shape[2] // freq_count
    planes = (
        own == LANES
        and 2 * components == LANES
        and mz_count == 2
        and freq_count & (freq_count - 1) == 0
        and freq_count >= 8
        and elution.shape[0] % 64 == 0
        and bin_count % LANES == 0
        and bin_count >= REACH
    )
    if not planes:
        gathered = lax.all_gather(mine, axes, axis=0).reshape(-1, math.gcd(bin_count, LANES), LANES)
        g = partial_model((gathered,), circulant(bin_weight), bin_count, components)
        shifted = elution_terms((gathered,), loadings, shifts, bin_count)
        numerator, gram = product(intensity, (g,), shifted, loadings, shifts, planes)
        gram = lax.psum(gram, "freq")
        owned = lax.psum_scatter(numerator, "freq", scatter_dimension=1, tiled=True)
        return small_call(solve_kernel, (components, own), "solve", gram, owned)[0]
    near = swap(mine, "mz", mz_count, 1)
    onward = [
        (f * mz_count + y, (f + 1) % freq_count * mz_count + 1 - y)
        for f in range(freq_count)
        for y in range(mz_count)
    ]
    far = lax.ppermute(mine, axes, onward)
    z_steps = range(4, freq_count, 4)
    held = jnp.stack([mine] + [swap(mine, "freq", freq_count, step) for step in z_steps])
    held, near, far, bin_weight = lax.optimization_barrier((held, near, far, bin_weight))
    held = jnp.concatenate([held, swap(held, "freq", freq_count, 2)], axis=0)
    u = circulant(bin_weight)
    held, u = lax.optimization_barrier((held, u))
    came = swap(held, "freq", freq_count, 1)
    g = partial_model((held, came), u, bin_count, components)
    models = (g, swap(g, "mz", mz_count, 1))
    shifted = elution_terms((mine, came, near, far), loadings, shifts, bin_count)
    keep, send = product(intensity, models, shifted, loadings, shifts, planes)
    tail = components // 2
    quarter = freq_count // 4 * components
    parts = [keep, swap(send, "freq", freq_count, 1)]
    (send,) = small_call(
        functools.partial(stage_kernel, tail, 1), (quarter + tail, LANES), "reduce_stage", *parts
    )
    parts.append(swap(send, "freq", freq_count, 2))
    count = len(z_steps)
    sends = small_call(
        functools.partial(stage_kernel, tail, count), (components + tail, LANES), "reduce_stage", *parts, count=count
    )
    parts += [swap(send, "freq", freq_count, step) for send, step in zip(sends, z_steps)]
    return small_call(functools.partial(solve_planes_kernel, tail), (components, own), "solve", *parts)[0]


def solution(mesh):
    in_specs = (P(None, "freq", "mz"), P(("freq", "mz"), None), P(), P(), P())
    out_specs = P(None, ("mz", "freq"))
    return jax.shard_map(on_device, mesh=mesh, in_specs=in_specs, out_specs=out_specs, check_vma=False)
```

```python
import functools
import math

import jax
import jax.numpy as jnp
import numpy as np
from jax import lax
from jax.experimental import pallas as pl
from jax.experimental.pallas import tpu as pltpu
from jax.sharding import PartitionSpec as P

PRECISE = lax.Precision.HIGHEST
LANES = 128
REACH = 256
MIB = 1024 * 1024


def f32_dot(a, b, dims=(((1,), (0,)), ((), ()))):
    return lax.dot_general(a, b, dims, precision=PRECISE, preferred_element_type=jnp.float32)


def two_terms(x):
    high = x.astype(jnp.bfloat16)
    low = (x - high.astype(jnp.float32)).astype(jnp.bfloat16)
    return high, low


def vmem(count):
    return [pl.BlockSpec(memory_space=pltpu.VMEM)] * count


def pack_kernel(x_ref, o_ref):
    x = x_ref[...]
    components, rows = x.shape
    pad = -rows % LANES
    if pad:
        x = jnp.concatenate([x, jnp.zeros((components, pad), x.dtype)], axis=1)
    high, low = two_terms(x.T[:rows])
    o_ref[...] = jnp.concatenate([high, low], axis=1)


def pack(elution):
    rows, components = elution.shape
    return pl.pallas_call(
        pack_kernel,
        out_shape=jax.ShapeDtypeStruct((rows, 2 * components), jnp.bfloat16),
        in_specs=vmem(1),
        out_specs=vmem(1)[0],
        compiler_params=pltpu.CompilerParams(vmem_limit_bytes=8 * MIB),
        name="pack_elution",
    )(elution.T)


def circulant_kernel(w_ref, table_ref, u_ref):
    rows = w_ref.shape[1]
    w = w_ref[...]
    over_lanes = (((0,), (0,)), ((), ()))

    def table(at, height, width):
        return table_ref[at : at + height, :width], table_ref[at + height : at + 2 * height, :width]

    lane_cos, lane_sin = table(0, LANES, LANES)
    twid_cos, twid_sin = table(2 * LANES, rows, LANES)
    row_cos, row_sin = table(2 * LANES + 2 * rows, rows, rows)
    a_re = f32_dot(w, lane_cos, over_lanes)
    a_im = -f32_dot(w, lane_sin, over_lanes)
    b_re = a_re * twid_cos + a_im * twid_sin
    b_im = a_im * twid_cos - a_re * twid_sin
    c = f32_dot(row_cos, b_re) + f32_dot(row_sin, b_im)
    sub = lax.broadcasted_iota(jnp.int32, (LANES, LANES), 0)
    lane = lax.broadcasted_iota(jnp.int32, (LANES, LANES), 1)

    def turned(row):
        return pltpu.roll(jnp.broadcast_to(c[row : row + 1], (LANES, LANES)), 0, 1, stride=1, stride_axis=0)

    before = turned(rows - 1)
    for row in range(rows):
        now = turned(row)
        high, low = two_terms(jnp.where(lane >= sub, now, before))
        u_ref[0:LANES, row * LANES : (row + 1) * LANES] = high
        u_ref[LANES:, row * LANES : (row + 1) * LANES] = low
        before = now


def circulant(weights):
    length = weights.size
    rows = length // LANES

    def tables(a, b, period):
        angle = 2.0 * math.pi / period * ((a[:, None] * b[None, :]) % period)
        return np.pad(np.concatenate([np.cos(angle), np.sin(angle)]), ((0, 0), (0, LANES - b.size)))

    lane_ids, row_ids = np.arange(LANES), np.arange(rows)
    table = np.concatenate(
        [
            tables(lane_ids, lane_ids, LANES),
            tables(row_ids, lane_ids, length),
            tables(row_ids, row_ids, rows) / length,
        ]
    ).astype(np.float32)
    return pl.pallas_call(
        circulant_kernel,
        out_shape=jax.ShapeDtypeStruct((2 * LANES, length), jnp.bfloat16),
        in_specs=vmem(2),
        out_specs=vmem(1)[0],
        compiler_params=pltpu.CompilerParams(vmem_limit_bytes=16 * MIB),
        cost_estimate=pl.CostEstimate(flops=2_000_000_000, bytes_accessed=4 * MIB, transcendentals=0),
        name="circulant_block",
    )(weights, table)


def model_kernel(places, planes, *refs):
    u_ref, g_ref, wide = refs[-3:]
    length = u_ref.shape[1]
    components = g_ref.shape[0]
    freq_rank = lax.axis_index("freq")
    if planes:
        own_ref, came_ref = refs[:2]
        mz_rank = lax.axis_index("mz")
        freq_count = 2 * own_ref.shape[0]
        rows = own_ref.shape[1]
        empty = jnp.zeros((rows, LANES), jnp.bfloat16)
        for block in range(-1, freq_count + 1):
            apart = lax.bitwise_xor((freq_rank + block) & (freq_count - 1), freq_rank)
            ref = came_ref if block % 2 else own_ref
            values = ref[pl.ds(block_place(apart, freq_count), 1)][0]
            for here, half in ((values, mz_rank), (empty, 1 - mz_rank)):
                to = pl.multiple_of(2 * REACH + (2 * block + half) * rows, 64)
                wide[pl.ds(to, rows), 0:LANES] = here
                wide[pl.ds(pl.multiple_of(to - LANES, 64), rows), LANES:] = here
    else:
        own_ref = refs[0]
        step = own_ref.shape[1]
        steps = length // step
        bin_count = length // lax.axis_size("freq")
        first = lax.rem(freq_rank * bin_count + length - REACH, length) // step

        def bring(j, carry):
            values = own_ref[pl.ds(lax.rem(first + j, steps), 1)][0]
            to = pl.multiple_of(REACH + j * step, step)
            wide[pl.ds(to, step), 0:LANES] = values
            wide[pl.ds(pl.multiple_of(to - LANES, step), step), LANES:] = values
            return carry

        lax.fori_loop(0, (wide.shape[0] - REACH) // step, bring, 0)
    for a in range(0, places, 2):
        at = REACH + a * LANES
        made = jnp.dot(u_ref[...], wide[at : at + length, :], preferred_element_type=jnp.float32)
        made = made[:LANES] + made[LANES:]
        for half in range(min(2, places - a)):
            piece = made[:, half * LANES : (half + 1) * LANES].T
            g_ref[:, (a + half) * LANES : (a + half + 1) * LANES] = piece[:components] + piece[components:]


def block_place(apart, freq_count):
    return (apart >> 2) + ((apart >> 1) & 1) * (freq_count // 4)


def partial_model(gathered, u, bin_count, components):
    length = u.shape[1]
    places = -(-(bin_count + REACH) // LANES)
    planes = len(gathered) == 2
    wide_rows = 2 * REACH + length + bin_count if planes else REACH + length + 2 * LANES * ((places - 1) // 2)
    return pl.pallas_call(
        functools.partial(model_kernel, places, planes),
        out_shape=jax.ShapeDtypeStruct((components, places * LANES), jnp.float32),
        in_specs=vmem(len(gathered) + 1),
        out_specs=vmem(1)[0],
        scratch_shapes=[pltpu.VMEM((wide_rows, 2 * LANES), jnp.bfloat16)],
        compiler_params=pltpu.CompilerParams(vmem_limit_bytes=24 * MIB),
        cost_estimate=pl.CostEstimate(flops=2_000_000_000, bytes_accessed=4 * MIB, transcendentals=0),
        name="partial_model",
    )(*gathered, u)


def shifted_terms(x, amps, lags, bin_count, terms):
    components = x.shape[0]
    out_count = -(-bin_count // LANES)
    x = pltpu.roll(x, x.shape[1] - 1, 1)
    height = 16
    lane = lax.broadcasted_iota(jnp.int32, (height, LANES), 1)
    for at in range(0, components, height):
        vectors = [x[at : at + height, v * LANES : (v + 1) * LANES] for v in range(out_count + 2)]
        for k in range(amps.shape[1]):
            left = REACH - 1 - jnp.broadcast_to(lags[at : at + height, k : k + 1], lane.shape)
            amp = jnp.broadcast_to(amps[at : at + height, k : k + 1], lane.shape)
            source = lane + (left & (LANES - 1))
            index = source & (LANES - 1)
            far, same = left >= LANES, source < LANES
            turned = [jnp.take_along_axis(v, index, axis=1, mode="promise_in_bounds") for v in vectors]
            turned = [jnp.where(far, turned[v + 1], turned[v]) for v in range(out_count + 1)]
            for v in range(out_count):
                high, low = two_terms(amp * jnp.where(same, turned[v], turned[v + 1]))
                width = min(LANES, bin_count - v * LANES)
                to = slice(k * bin_count + v * LANES, k * bin_count + v * LANES + width)
                terms[at : at + height, to] = high[:, :width]
                terms[components + at : components + at + height, to] = low[:, :width]


def elution_kernel(planes, *refs):
    amp_ref, lag_ref, terms, window = refs[-4:]
    components = amp_ref.shape[1]
    bin_count = terms.shape[1] // amp_ref.shape[0]
    freq_rank = lax.axis_index("freq")
    if planes:
        mine_ref, came_ref, near_ref, far_ref = refs[:4]
        mz_rank = lax.axis_index("mz")
        freq_count = 2 * came_ref.shape[0]
        rows = mine_ref.shape[0]
        apart = lax.bitwise_xor((freq_rank - 1) & (freq_count - 1), freq_rank)
        before = came_ref[pl.ds(block_place(apart, freq_count), 1)][0]
        skip = bin_count - REACH
        for block, half, values in (
            (0, mz_rank, before),
            (0, 1 - mz_rank, far_ref[...]),
            (1, mz_rank, mine_ref[...]),
            (1, 1 - mz_rank, near_ref[...]),
        ):
            window[pl.ds(pl.multiple_of((2 * block + half) * rows, 64), rows), :] = values
    else:
        own_ref = refs[0]
        step = own_ref.shape[1]
        steps = own_ref.shape[0]
        first = lax.rem(freq_rank * bin_count + steps * step - REACH, steps * step) // step
        skip = 0
        for j in range(window.shape[0] // step):
            window[j * step : (j + 1) * step, :] = own_ref[pl.ds(lax.rem(first + j, steps), 1)][0]
    pieces = []
    for at in range(skip, window.shape[0], LANES):
        piece = window[at : at + LANES, :].astype(jnp.float32).T
        pieces.append(piece[:components] + piece[components:])
    shifted_terms(jnp.concatenate(pieces, axis=1), amp_ref[...].T, lag_ref[...].T, bin_count, terms)


def elution_terms(elutions, loadings, shifts, bin_count):
    run_count, components = loadings.shape
    places = -(-(bin_count + REACH) // LANES)
    planes = len(elutions) > 1
    return pl.pallas_call(
        functools.partial(elution_kernel, planes),
        out_shape=jax.ShapeDtypeStruct((2 * components, run_count * bin_count), jnp.bfloat16),
        in_specs=vmem(len(elutions) + 2),
        out_specs=vmem(1)[0],
        scratch_shapes=[pltpu.VMEM((2 * bin_count if planes else places * LANES, LANES), jnp.bfloat16)],
        compiler_params=pltpu.CompilerParams(vmem_limit_bytes=12 * MIB),
        cost_estimate=pl.CostEstimate(flops=1_000_000_000, bytes_accessed=2 * MIB, transcendentals=0),
        name="elution_terms",
    )(*elutions, loadings, shifts)


def product_kernel(parts, planes, *refs):
    i_ref = refs[0]
    g_refs = refs[1 : 1 + parts]
    elution_ref, amp_ref, lag_ref, num_ref, other_ref, terms = refs[1 + parts :]
    run_count, bin_count, local_mz = i_ref.shape
    components = amp_ref.shape[1]
    chunk = 2 * LANES
    chunks = local_mz // chunk
    g = g_refs[0][...]
    for ref in g_refs[1:]:
        g = g + ref[...]
    shifted_terms(g, amp_ref[...].T, lag_ref[...].T, bin_count, terms)
    gram = lax.dot_general(
        terms[...], elution_ref[...], (((1,), (1,)), ((), ())), preferred_element_type=jnp.float32
    )
    gram = gram[:components] + gram[components:]
    gram = gram[:, :components] + gram[:, components:]
    if planes:
        keep_ref, send_ref = num_ref, other_ref
        half = components // 2
        gram = jnp.concatenate([gram[:half], gram[half:]], axis=1)
        keep_ref[chunks * components :, :] = gram
        send_ref[chunks * components :, :] = gram
    else:
        other_ref[...] = gram

    for n in range(chunks):
        data = i_ref[:, :, n * chunk : (n + 1) * chunk].reshape(run_count * bin_count, chunk)
        made = jnp.dot(terms[...], data, preferred_element_type=jnp.float32)
        made = made[:components] + made[components:]
        if planes:
            freq_rank = lax.axis_index("freq")
            core = freq_rank & 1
            place = block_place(lax.bitwise_xor(freq_rank, 2 * n + core), 2 * chunks)
            at = pl.ds(pl.multiple_of(place * components, components), components)
            even, odd = made[:, :LANES], made[:, LANES:]
            keep_ref[at, :] = jnp.where(core == 0, even, odd)
            send_ref[at, :] = jnp.where(core == 0, odd, even)
        else:
            num_ref[:, n * chunk : (n + 1) * chunk] = made


def product(intensity, models, elution, loadings, shifts, planes):
    run_count, bin_count, local_mz = intensity.shape
    components = loadings.shape[1]
    chunk = 2 * LANES
    chunks = local_mz // chunk
    if planes:
        out_shapes = [(chunks * components + components // 2, LANES)] * 2
    else:
        out_shapes = [(components, local_mz), (components, components)]
    return pl.pallas_call(
        functools.partial(product_kernel, len(models), planes),
        out_shape=tuple(jax.ShapeDtypeStruct(shape, jnp.float32) for shape in out_shapes),
        in_specs=vmem(len(models) + 4),
        out_specs=tuple(vmem(2)),
        scratch_shapes=[pltpu.VMEM((2 * components, run_count * bin_count), jnp.bfloat16)],
        compiler_params=pltpu.CompilerParams(vmem_limit_bytes=24 * MIB),
        cost_estimate=pl.CostEstimate(
            flops=8_000_000_000, bytes_accessed=2 * intensity.size, transcendentals=0
        ),
        name="model_products",
    )(intensity, *models, elution, loadings, shifts)


def inverse2(a, b, d):
    scale = 1.0 / (a * d - b * b)
    return d * scale, -b * scale, a * scale


def eliminate(gram, right):
    components = gram.shape[0]
    row_id = lax.broadcasted_iota(jnp.int32, gram.shape, 0)
    for j in range(0, components, 4):
        columns = [jnp.broadcast_to(gram[:, j + n : j + n + 1], gram.shape) for n in range(4)]
        pivot = [[columns[n][j + m : j + m + 1] for n in range(4)] for m in range(4)]
        a00, a01, a11 = inverse2(pivot[0][0], pivot[0][1], pivot[1][1])
        b00, b01, b10, b11 = pivot[0][2], pivot[0][3], pivot[1][2], pivot[1][3]
        w00, w01 = a00 * b00 + a01 * b10, a00 * b01 + a01 * b11
        w10, w11 = a01 * b00 + a11 * b10, a01 * b01 + a11 * b11
        s00, s01, s11 = inverse2(
            pivot[2][2] - (b00 * w00 + b10 * w10),
            pivot[2][3] - (b00 * w01 + b10 * w11),
            pivot[3][3] - (b01 * w01 + b11 * w11),
        )
        away = (row_id < j) | (row_id >= j + 4)
        c0, c1, c2, c3 = (
            jnp.where(away, column, jnp.where(row_id == j + n, -1.0, 0.0)) for n, column in enumerate(columns)
        )
        t2, t3 = c2 - c0 * w00 - c1 * w10, c3 - c0 * w01 - c1 * w11
        f2, f3 = t2 * s00 + t3 * s01, t2 * s01 + t3 * s11
        f0 = c0 * a00 + c1 * a01 - f2 * w00 - f3 * w01
        f1 = c0 * a01 + c1 * a11 - f2 * w10 - f3 * w11
        factors = (f0, f1, f2, f3)

        def reduced(x):
            out = jnp.where(away[:, : x.shape[1]], x, 0.0)
            for n, factor in enumerate(factors):
                out = out - factor[:, : x.shape[1]] * x[j + n : j + n + 1]
            return out

        gram, right = reduced(gram), reduced(right)
    return right


def summed(refs, rows, tail):
    total = refs[0][0:rows] + refs[1][0:rows]
    gram = refs[0][refs[0].shape[0] - tail :] + refs[1][refs[1].shape[0] - tail :]
    for ref in refs[2:]:
        total = total + ref[0:rows]
        gram = gram + ref[ref.shape[0] - tail :]
    return total, gram


def stage_kernel(tail, count, *refs):
    outs = refs[-count:]
    rows = outs[0].shape[0] - tail
    total, gram = summed(refs[:-count], (count + 1) * rows, tail)
    for n, o_ref in enumerate(outs):
        o_ref[0:rows, :] = total[(n + 1) * rows : (n + 2) * rows]
        o_ref[rows:, :] = gram


def solve_planes_kernel(tail, *refs):
    o_ref = refs[-1]
    total, gram = summed(refs[:-1], o_ref.shape[0], tail)
    gram = jnp.concatenate([gram, pltpu.roll(gram, gram.shape[1] // 2, 1)], axis=0)
    o_ref[...] = eliminate(gram, total)


def solve_kernel(g_ref, n_ref, o_ref):
    components = o_ref.shape[0]
    gram = jnp.concatenate([g_ref[...], jnp.zeros((components, LANES - components), jnp.float32)], axis=1)
    o_ref[...] = eliminate(gram, n_ref[...])


def small_call(kernel, out_shape, name, *args, count=1):
    outs = pl.pallas_call(
        kernel,
        out_shape=(jax.ShapeDtypeStruct(out_shape, jnp.float32),) * count,
        in_specs=vmem(len(args)),
        out_specs=tuple(vmem(count)),
        compiler_params=pltpu.CompilerParams(vmem_limit_bytes=8 * MIB),
        name=name,
    )(*args)
    return outs


def swap(x, axes, count, value):
    return lax.ppermute(x, axes, [(i, i ^ value) for i in range(count)])


def on_device(intensity, elution, loadings, shifts, bin_weight):
    freq_count = lax.axis_size("freq")
    mz_count = lax.axis_size("mz")
    components = loadings.shape[1]
    bin_count = intensity.shape[1]
    axes = ("freq", "mz")
    mine = pack(elution)
    own = intensity.shape[2] // freq_count
    planes = (
        own == LANES
        and 2 * components == LANES
        and mz_count == 2
        and freq_count & (freq_count - 1) == 0
        and freq_count >= 8
        and elution.shape[0] % 64 == 0
        and bin_count % LANES == 0
        and bin_count >= REACH
    )
    if not planes:
        gathered = lax.all_gather(mine, axes, axis=0).reshape(-1, math.gcd(bin_count, LANES), LANES)
        g = partial_model((gathered,), circulant(bin_weight.reshape(LANES, -1)), bin_count, components)
        shifted = elution_terms((gathered,), loadings, shifts, bin_count)
        numerator, gram = product(intensity, (g,), shifted, loadings, shifts, planes)
        gram = lax.psum(gram, "freq")
        owned = lax.psum_scatter(numerator, "freq", scatter_dimension=1, tiled=True)
        return small_call(solve_kernel, (components, own), "solve", gram, owned)[0]
    z_steps = range(4, freq_count, 4)
    held = jnp.stack([mine] + [swap(mine, "freq", freq_count, step) for step in z_steps])
    weights = bin_weight.reshape(LANES, -1)
    held, weights, later = lax.optimization_barrier((held, weights, mine))
    near = swap(later, "mz", mz_count, 1)
    onward = [
        (f * mz_count + y, (f + 1) % freq_count * mz_count + 1 - y)
        for f in range(freq_count)
        for y in range(mz_count)
    ]
    far = lax.ppermute(later, axes, onward)
    held = jnp.concatenate([held, swap(held, "freq", freq_count, 2)], axis=0)
    u = circulant(weights)
    held, u, near, far = lax.optimization_barrier((held, u, near, far))
    came = swap(held, "freq", freq_count, 1)
    g = partial_model((held, came), u, bin_count, components)
    models = (g, swap(g, "mz", mz_count, 1))
    shifted = elution_terms((mine, came, near, far), loadings, shifts, bin_count)
    keep, send = product(intensity, models, shifted, loadings, shifts, planes)
    tail = components // 2
    quarter = freq_count // 4 * components
    parts = [keep, swap(send, "freq", freq_count, 1)]
    (send,) = small_call(
        functools.partial(stage_kernel, tail, 1), (quarter + tail, LANES), "reduce_stage", *parts
    )
    parts.append(swap(send, "freq", freq_count, 2))
    count = len(z_steps)
    sends = small_call(
        functools.partial(stage_kernel, tail, count), (components + tail, LANES), "reduce_stage", *parts, count=count
    )
    parts += [swap(send, "freq", freq_count, step) for send, step in zip(sends, z_steps)]
    return small_call(functools.partial(solve_planes_kernel, tail), (components, own), "solve", *parts)[0]


def solution(mesh):
    in_specs = (P(None, "freq", "mz"), P(("freq", "mz"), None), P(), P(), P())
    out_specs = P(None, ("mz", "freq"))
    return jax.shard_map(on_device, mesh=mesh, in_specs=in_specs, out_specs=out_specs, check_vma=False)
```

```python
import functools
import math

import jax
import jax.numpy as jnp
import numpy as np
from jax import lax
from jax.experimental import pallas as pl
from jax.experimental.pallas import tpu as pltpu
from jax.sharding import PartitionSpec as P

PRECISE = lax.Precision.HIGHEST
LANES = 128
REACH = 256
MIB = 1024 * 1024


def f32_dot(a, b, dims=(((1,), (0,)), ((), ()))):
    return lax.dot_general(a, b, dims, precision=PRECISE, preferred_element_type=jnp.float32)


def two_terms(x):
    high = x.astype(jnp.bfloat16)
    low = (x - high.astype(jnp.float32)).astype(jnp.bfloat16)
    return high, low


def vmem(count):
    return [pl.BlockSpec(memory_space=pltpu.VMEM)] * count


def pack_kernel(x_ref, o_ref):
    x = x_ref[...]
    components, rows = x.shape
    pad = -rows % LANES
    if pad:
        x = jnp.concatenate([x, jnp.zeros((components, pad), x.dtype)], axis=1)
    high, low = two_terms(x.T[:rows])
    o_ref[...] = jnp.concatenate([high, low], axis=1)


def pack(elution):
    rows, components = elution.shape
    return pl.pallas_call(
        pack_kernel,
        out_shape=jax.ShapeDtypeStruct((rows, 2 * components), jnp.bfloat16),
        in_specs=vmem(1),
        out_specs=vmem(1)[0],
        compiler_params=pltpu.CompilerParams(vmem_limit_bytes=8 * MIB),
        name="pack_elution",
    )(elution.T)


def circulant_kernel(w_ref, table_ref, u_ref):
    rows = w_ref.shape[1]
    w = w_ref[...]
    over_lanes = (((0,), (0,)), ((), ()))

    def table(at, height, width):
        return table_ref[at : at + height, :width], table_ref[at + height : at + 2 * height, :width]

    lane_cos, lane_sin = table(0, LANES, LANES)
    twid_cos, twid_sin = table(2 * LANES, rows, LANES)
    row_cos, row_sin = table(2 * LANES + 2 * rows, rows, rows)
    a_re = f32_dot(w, lane_cos, over_lanes)
    a_im = -f32_dot(w, lane_sin, over_lanes)
    b_re = a_re * twid_cos + a_im * twid_sin
    b_im = a_im * twid_cos - a_re * twid_sin
    c = f32_dot(row_cos, b_re) + f32_dot(row_sin, b_im)
    sub = lax.broadcasted_iota(jnp.int32, (LANES, LANES), 0)
    lane = lax.broadcasted_iota(jnp.int32, (LANES, LANES), 1)

    def turned(row):
        return pltpu.roll(jnp.broadcast_to(c[row : row + 1], (LANES, LANES)), 0, 1, stride=1, stride_axis=0)

    before = turned(rows - 1)
    for row in range(rows):
        now = turned(row)
        high, low = two_terms(jnp.where(lane >= sub, now, before))
        u_ref[0:LANES, row * LANES : (row + 1) * LANES] = high
        u_ref[LANES:, row * LANES : (row + 1) * LANES] = low
        before = now


def circulant(weights):
    length = weights.size
    rows = length // LANES

    def tables(a, b, period):
        angle = 2.0 * math.pi / period * ((a[:, None] * b[None, :]) % period)
        return np.pad(np.concatenate([np.cos(angle), np.sin(angle)]), ((0, 0), (0, LANES - b.size)))

    lane_ids, row_ids = np.arange(LANES), np.arange(rows)
    table = np.concatenate(
        [
            tables(lane_ids, lane_ids, LANES),
            tables(row_ids, lane_ids, length),
            tables(row_ids, row_ids, rows) / length,
        ]
    ).astype(np.float32)
    return pl.pallas_call(
        circulant_kernel,
        out_shape=jax.ShapeDtypeStruct((2 * LANES, length), jnp.bfloat16),
        in_specs=vmem(2),
        out_specs=vmem(1)[0],
        compiler_params=pltpu.CompilerParams(vmem_limit_bytes=16 * MIB),
        cost_estimate=pl.CostEstimate(flops=2_000_000_000, bytes_accessed=4 * MIB, transcendentals=0),
        name="circulant_block",
    )(weights, table)


def model_kernel(places, planes, *refs):
    u_ref, g_ref, wide = refs[-3:]
    length = u_ref.shape[1]
    components = g_ref.shape[0]
    freq_rank = lax.axis_index("freq")
    if planes:
        own_ref, came_ref = refs[:2]
        mz_rank = lax.axis_index("mz")
        freq_count = 2 * own_ref.shape[0]
        rows = own_ref.shape[1]
        empty = jnp.zeros((rows, LANES), jnp.bfloat16)
        for block in range(-1, freq_count + 1):
            apart = lax.bitwise_xor((freq_rank + block) & (freq_count - 1), freq_rank)
            ref = came_ref if block % 2 else own_ref
            values = ref[pl.ds(block_place(apart, freq_count), 1)][0]
            for here, half in ((values, mz_rank), (empty, 1 - mz_rank)):
                to = pl.multiple_of(2 * REACH + (2 * block + half) * rows, 64)
                wide[pl.ds(to, rows), 0:LANES] = here
                wide[pl.ds(pl.multiple_of(to - LANES, 64), rows), LANES:] = here
    else:
        own_ref = refs[0]
        step = own_ref.shape[1]
        steps = length // step
        bin_count = length // lax.axis_size("freq")
        first = lax.rem(freq_rank * bin_count + length - REACH, length) // step

        def bring(j, carry):
            values = own_ref[pl.ds(lax.rem(first + j, steps), 1)][0]
            to = pl.multiple_of(REACH + j * step, step)
            wide[pl.ds(to, step), 0:LANES] = values
            wide[pl.ds(pl.multiple_of(to - LANES, step), step), LANES:] = values
            return carry

        lax.fori_loop(0, (wide.shape[0] - REACH) // step, bring, 0)
    for a in range(0, places, 2):
        at = REACH + a * LANES
        made = jnp.dot(u_ref[...], wide[at : at + length, :], preferred_element_type=jnp.float32)
        made = made[:LANES] + made[LANES:]
        for half in range(min(2, places - a)):
            piece = made[:, half * LANES : (half + 1) * LANES].T
            g_ref[:, (a + half) * LANES : (a + half + 1) * LANES] = piece[:components] + piece[components:]


def block_place(apart, freq_count):
    return (apart >> 2) + ((apart >> 1) & 1) * (freq_count // 4)


def partial_model(gathered, u, bin_count, components):
    length = u.shape[1]
    places = -(-(bin_count + REACH) // LANES)
    planes = len(gathered) == 2
    wide_rows = 2 * REACH + length + bin_count if planes else REACH + length + 2 * LANES * ((places - 1) // 2)
    return pl.pallas_call(
        functools.partial(model_kernel, places, planes),
        out_shape=jax.ShapeDtypeStruct((components, places * LANES), jnp.float32),
        in_specs=vmem(len(gathered) + 1),
        out_specs=vmem(1)[0],
        scratch_shapes=[pltpu.VMEM((wide_rows, 2 * LANES), jnp.bfloat16)],
        compiler_params=pltpu.CompilerParams(vmem_limit_bytes=24 * MIB),
        cost_estimate=pl.CostEstimate(flops=2_000_000_000, bytes_accessed=4 * MIB, transcendentals=0),
        name="partial_model",
    )(*gathered, u)


def shifted_terms(x, amps, lags, bin_count, terms):
    components = x.shape[0]
    out_count = -(-bin_count // LANES)
    x = pltpu.roll(x, x.shape[1] - 1, 1)
    height = 16
    lane = lax.broadcasted_iota(jnp.int32, (height, LANES), 1)
    for at in range(0, components, height):
        vectors = [x[at : at + height, v * LANES : (v + 1) * LANES] for v in range(out_count + 2)]
        for k in range(amps.shape[1]):
            left = REACH - 1 - jnp.broadcast_to(lags[at : at + height, k : k + 1], lane.shape)
            amp = jnp.broadcast_to(amps[at : at + height, k : k + 1], lane.shape)
            source = lane + (left & (LANES - 1))
            index = source & (LANES - 1)
            far, same = left >= LANES, source < LANES
            turned = [jnp.take_along_axis(v, index, axis=1, mode="promise_in_bounds") for v in vectors]
            turned = [jnp.where(far, turned[v + 1], turned[v]) for v in range(out_count + 1)]
            for v in range(out_count):
                high, low = two_terms(amp * jnp.where(same, turned[v], turned[v + 1]))
                width = min(LANES, bin_count - v * LANES)
                to = slice(k * bin_count + v * LANES, k * bin_count + v * LANES + width)
                terms[at : at + height, to] = high[:, :width]
                terms[components + at : components + at + height, to] = low[:, :width]


def elution_kernel(planes, *refs):
    amp_ref, lag_ref, terms, window = refs[-4:]
    components = amp_ref.shape[1]
    bin_count = terms.shape[1] // amp_ref.shape[0]
    freq_rank = lax.axis_index("freq")
    if planes:
        mine_ref, came_ref, near_ref, far_ref = refs[:4]
        mz_rank = lax.axis_index("mz")
        freq_count = 2 * came_ref.shape[0]
        rows = mine_ref.shape[0]
        apart = lax.bitwise_xor((freq_rank - 1) & (freq_count - 1), freq_rank)
        before = came_ref[pl.ds(block_place(apart, freq_count), 1)][0]
        skip = bin_count - REACH
        for block, half, values in (
            (0, mz_rank, before),
            (0, 1 - mz_rank, far_ref[...]),
            (1, mz_rank, mine_ref[...]),
            (1, 1 - mz_rank, near_ref[...]),
        ):
            window[pl.ds(pl.multiple_of((2 * block + half) * rows, 64), rows), :] = values
    else:
        own_ref = refs[0]
        step = own_ref.shape[1]
        steps = own_ref.shape[0]
        first = lax.rem(freq_rank * bin_count + steps * step - REACH, steps * step) // step
        skip = 0
        for j in range(window.shape[0] // step):
            window[j * step : (j + 1) * step, :] = own_ref[pl.ds(lax.rem(first + j, steps), 1)][0]
    pieces = []
    for at in range(skip, window.shape[0], LANES):
        piece = window[at : at + LANES, :].astype(jnp.float32).T
        pieces.append(piece[:components] + piece[components:])
    shifted_terms(jnp.concatenate(pieces, axis=1), amp_ref[...].T, lag_ref[...].T, bin_count, terms)


def elution_terms(elutions, loadings, shifts, bin_count):
    run_count, components = loadings.shape
    places = -(-(bin_count + REACH) // LANES)
    planes = len(elutions) > 1
    return pl.pallas_call(
        functools.partial(elution_kernel, planes),
        out_shape=jax.ShapeDtypeStruct((2 * components, run_count * bin_count), jnp.bfloat16),
        in_specs=vmem(len(elutions) + 2),
        out_specs=vmem(1)[0],
        scratch_shapes=[pltpu.VMEM((2 * bin_count if planes else places * LANES, LANES), jnp.bfloat16)],
        compiler_params=pltpu.CompilerParams(vmem_limit_bytes=12 * MIB),
        cost_estimate=pl.CostEstimate(flops=1_000_000_000, bytes_accessed=2 * MIB, transcendentals=0),
        name="elution_terms",
    )(*elutions, loadings, shifts)


def product_kernel(parts, planes, *refs):
    i_ref = refs[0]
    g_refs = refs[1 : 1 + parts]
    elution_ref, amp_ref, lag_ref, num_ref, other_ref, terms = refs[1 + parts :]
    run_count, bin_count, local_mz = i_ref.shape
    components = amp_ref.shape[1]
    chunk = 2 * LANES
    chunks = local_mz // chunk
    g = g_refs[0][...]
    for ref in g_refs[1:]:
        g = g + ref[...]
    shifted_terms(g, amp_ref[...].T, lag_ref[...].T, bin_count, terms)
    gram = lax.dot_general(
        terms[...], elution_ref[...], (((1,), (1,)), ((), ())), preferred_element_type=jnp.float32
    )
    gram = gram[:components] + gram[components:]
    gram = gram[:, :components] + gram[:, components:]
    if planes:
        keep_ref, send_ref = num_ref, other_ref
        half = components // 2
        gram = jnp.concatenate([gram[:half], gram[half:]], axis=1)
        keep_ref[chunks * components :, :] = gram
        send_ref[chunks * components :, :] = gram
    else:
        other_ref[...] = gram

    for n in range(chunks):
        data = i_ref[:, :, n * chunk : (n + 1) * chunk].reshape(run_count * bin_count, chunk)
        made = jnp.dot(terms[...], data, preferred_element_type=jnp.float32)
        made = made[:components] + made[components:]
        if planes:
            freq_rank = lax.axis_index("freq")
            core = freq_rank & 1
            place = block_place(lax.bitwise_xor(freq_rank, 2 * n + core), 2 * chunks)
            at = pl.ds(pl.multiple_of(place * components, components), components)
            even, odd = made[:, :LANES], made[:, LANES:]
            keep_ref[at, :] = jnp.where(core == 0, even, odd)
            send_ref[at, :] = jnp.where(core == 0, odd, even)
        else:
            num_ref[:, n * chunk : (n + 1) * chunk] = made


def product(intensity, models, elution, loadings, shifts, planes):
    run_count, bin_count, local_mz = intensity.shape
    components = loadings.shape[1]
    chunk = 2 * LANES
    chunks = local_mz // chunk
    if planes:
        out_shapes = [(chunks * components + components // 2, LANES)] * 2
    else:
        out_shapes = [(components, local_mz), (components, components)]
    return pl.pallas_call(
        functools.partial(product_kernel, len(models), planes),
        out_shape=tuple(jax.ShapeDtypeStruct(shape, jnp.float32) for shape in out_shapes),
        in_specs=vmem(len(models) + 4),
        out_specs=tuple(vmem(2)),
        scratch_shapes=[pltpu.VMEM((2 * components, run_count * bin_count), jnp.bfloat16)],
        compiler_params=pltpu.CompilerParams(vmem_limit_bytes=24 * MIB),
        cost_estimate=pl.CostEstimate(
            flops=8_000_000_000, bytes_accessed=2 * intensity.size, transcendentals=0
        ),
        name="model_products",
    )(intensity, *models, elution, loadings, shifts)


def inverse2(a, b, d):
    scale = 1.0 / (a * d - b * b)
    return d * scale, -b * scale, a * scale


def eliminate(gram, right):
    components = gram.shape[0]
    row_id = lax.broadcasted_iota(jnp.int32, gram.shape, 0)
    for j in range(0, components, 4):
        columns = [jnp.broadcast_to(gram[:, j + n : j + n + 1], gram.shape) for n in range(4)]
        pivot = [[columns[n][j + m : j + m + 1] for n in range(4)] for m in range(4)]
        a00, a01, a11 = inverse2(pivot[0][0], pivot[0][1], pivot[1][1])
        b00, b01, b10, b11 = pivot[0][2], pivot[0][3], pivot[1][2], pivot[1][3]
        w00, w01 = a00 * b00 + a01 * b10, a00 * b01 + a01 * b11
        w10, w11 = a01 * b00 + a11 * b10, a01 * b01 + a11 * b11
        s00, s01, s11 = inverse2(
            pivot[2][2] - (b00 * w00 + b10 * w10),
            pivot[2][3] - (b00 * w01 + b10 * w11),
            pivot[3][3] - (b01 * w01 + b11 * w11),
        )
        away = (row_id < j) | (row_id >= j + 4)
        c0, c1, c2, c3 = (
            jnp.where(away, column, jnp.where(row_id == j + n, -1.0, 0.0)) for n, column in enumerate(columns)
        )
        t2, t3 = c2 - c0 * w00 - c1 * w10, c3 - c0 * w01 - c1 * w11
        f2, f3 = t2 * s00 + t3 * s01, t2 * s01 + t3 * s11
        f0 = c0 * a00 + c1 * a01 - f2 * w00 - f3 * w01
        f1 = c0 * a01 + c1 * a11 - f2 * w10 - f3 * w11
        factors = (f0, f1, f2, f3)

        def reduced(x):
            out = jnp.where(away[:, : x.shape[1]], x, 0.0)
            for n, factor in enumerate(factors):
                out = out - factor[:, : x.shape[1]] * x[j + n : j + n + 1]
            return out

        gram, right = reduced(gram), reduced(right)
    return right


def total_of(refs, at, rows):
    total = refs[0][at : at + rows]
    for ref in refs[1:]:
        total = total + ref[at : at + rows]
    return total


def halve_kernel(tail, a_ref, b_ref, o_ref, gram_ref):
    rows = o_ref.shape[0]
    o_ref[...] = total_of((a_ref, b_ref), rows, rows)
    gram_ref[...] = total_of((a_ref, b_ref), 2 * rows, tail)


def spread_kernel(*refs):
    ins, outs = refs[:3], refs[3:]
    rows = outs[0].shape[0]
    for n, o_ref in enumerate(outs):
        o_ref[...] = total_of(ins, (n + 1) * rows, rows)


def sum_kernel(*refs):
    refs[-1][...] = total_of(refs[:-1], 0, refs[-1].shape[0])


def invert_kernel(*refs):
    o_ref = refs[-1]
    gram = total_of(refs[:-1], 0, refs[0].shape[0])
    gram = jnp.concatenate([gram, pltpu.roll(gram, gram.shape[1] // 2, 1)], axis=0)
    row_id = lax.broadcasted_iota(jnp.int32, gram.shape, 0)
    eye = jnp.where(row_id == lax.broadcasted_iota(jnp.int32, gram.shape, 1), 1.0, 0.0)
    o_ref[...] = eliminate(gram, eye)


def finish_kernel(inverse_ref, *refs):
    o_ref = refs[-1]
    components = o_ref.shape[0]
    o_ref[...] = f32_dot(inverse_ref[:, :components], total_of(refs[:-1], 0, components))


def solve_kernel(g_ref, n_ref, o_ref):
    components = o_ref.shape[0]
    gram = jnp.concatenate([g_ref[...], jnp.zeros((components, LANES - components), jnp.float32)], axis=1)
    o_ref[...] = eliminate(gram, n_ref[...])


def small_call(kernel, shapes, name, *args, flops=1_000_000):
    outs = pl.pallas_call(
        kernel,
        out_shape=tuple(jax.ShapeDtypeStruct(shape, jnp.float32) for shape in shapes),
        in_specs=vmem(len(args)),
        out_specs=tuple(vmem(len(shapes))),
        compiler_params=pltpu.CompilerParams(vmem_limit_bytes=8 * MIB),
        cost_estimate=pl.CostEstimate(flops=flops, bytes_accessed=1024, transcendentals=0),
        name=name,
    )(*args)
    return outs


def swap(x, axes, count, value):
    return lax.ppermute(x, axes, [(i, i ^ value) for i in range(count)])


def on_device(intensity, elution, loadings, shifts, bin_weight):
    freq_count = lax.axis_size("freq")
    mz_count = lax.axis_size("mz")
    components = loadings.shape[1]
    bin_count = intensity.shape[1]
    axes = ("freq", "mz")
    mine = pack(elution)
    own = intensity.shape[2] // freq_count
    planes = (
        own == LANES
        and 2 * components == LANES
        and mz_count == 2
        and freq_count & (freq_count - 1) == 0
        and freq_count >= 8
        and elution.shape[0] % 64 == 0
        and bin_count % LANES == 0
        and bin_count >= REACH
    )
    if not planes:
        gathered = lax.all_gather(mine, axes, axis=0).reshape(-1, math.gcd(bin_count, LANES), LANES)
        g = partial_model((gathered,), circulant(bin_weight.reshape(LANES, -1)), bin_count, components)
        shifted = elution_terms((gathered,), loadings, shifts, bin_count)
        numerator, gram = product(intensity, (g,), shifted, loadings, shifts, planes)
        gram = lax.psum(gram, "freq")
        owned = lax.psum_scatter(numerator, "freq", scatter_dimension=1, tiled=True)
        return small_call(solve_kernel, [(components, own)], "solve", gram, owned)[0]
    z_steps = range(4, freq_count, 4)
    held = jnp.stack([mine] + [swap(mine, "freq", freq_count, step) for step in z_steps])
    weights = bin_weight.reshape(LANES, -1)
    held, weights, later = lax.optimization_barrier((held, weights, mine))
    near = swap(later, "mz", mz_count, 1)
    onward = [
        (f * mz_count + y, (f + 1) % freq_count * mz_count + 1 - y)
        for f in range(freq_count)
        for y in range(mz_count)
    ]
    far = lax.ppermute(later, axes, onward)
    held = jnp.concatenate([held, swap(held, "freq", freq_count, 2)], axis=0)
    u = circulant(weights)
    held, u, near, far = lax.optimization_barrier((held, u, near, far))
    came = swap(held, "freq", freq_count, 1)
    g = partial_model((held, came), u, bin_count, components)
    models = (g, swap(g, "mz", mz_count, 1))
    shifted = elution_terms((mine, came, near, far), loadings, shifts, bin_count)
    keep, send = product(intensity, models, shifted, loadings, shifts, planes)
    tail = components // 2
    came = swap(send, "freq", freq_count, 1)
    send, gram = small_call(
        functools.partial(halve_kernel, tail),
        [(freq_count // 4 * components, LANES), (tail, LANES)],
        "reduce_cores",
        keep,
        came,
    )
    across = swap(send, "freq", freq_count, 2)
    grams = [swap(gram, "freq", freq_count, step) for step in z_steps]
    (gram,) = small_call(sum_kernel, [(tail, LANES)], "reduce_gram", gram, *grams)
    gram_across = swap(gram, "freq", freq_count, 2)
    sends = small_call(spread_kernel, [(components, LANES)] * len(z_steps), "reduce_x", keep, came, across)
    parts = [swap(part, "freq", freq_count, step) for part, step in zip(sends, z_steps)]
    (inverse,) = small_call(
        invert_kernel, [(components, LANES)], "invert_gram", gram, gram_across, flops=3_000_000_000
    )
    return small_call(finish_kernel, [(components, own)], "finish", inverse, keep, came, across, *parts)[0]


def solution(mesh):
    in_specs = (P(None, "freq", "mz"), P(("freq", "mz"), None), P(), P(), P())
    out_specs = P(None, ("mz", "freq"))
    return jax.shard_map(on_device, mesh=mesh, in_specs=in_specs, out_specs=out_specs, check_vma=False)
```

```python
import functools
import math

import jax
import jax.numpy as jnp
import numpy as np
from jax import lax
from jax.experimental import pallas as pl
from jax.experimental.pallas import tpu as pltpu
from jax.sharding import PartitionSpec as P

PRECISE = lax.Precision.HIGHEST
LANES = 128
REACH = 256
MIB = 1024 * 1024


def f32_dot(a, b, dims=(((1,), (0,)), ((), ()))):
    return lax.dot_general(a, b, dims, precision=PRECISE, preferred_element_type=jnp.float32)


def two_terms(x):
    high = x.astype(jnp.bfloat16)
    low = (x - high.astype(jnp.float32)).astype(jnp.bfloat16)
    return high, low


def vmem(count):
    return [pl.BlockSpec(memory_space=pltpu.VMEM)] * count


def pack_kernel(x_ref, o_ref):
    x = x_ref[...]
    components, rows = x.shape
    pad = -rows % LANES
    if pad:
        x = jnp.concatenate([x, jnp.zeros((components, pad), x.dtype)], axis=1)
    high, low = two_terms(x.T[:rows])
    o_ref[...] = jnp.concatenate([high, low], axis=1)


def pack(elution):
    rows, components = elution.shape
    return pl.pallas_call(
        pack_kernel,
        out_shape=jax.ShapeDtypeStruct((rows, 2 * components), jnp.bfloat16),
        in_specs=vmem(1),
        out_specs=vmem(1)[0],
        compiler_params=pltpu.CompilerParams(vmem_limit_bytes=8 * MIB),
        name="pack_elution",
    )(elution.T)


def circulant_kernel(turn, w_ref, table_ref, u_ref):
    rows = w_ref.shape[1]
    w = w_ref[...]
    over_lanes = (((0,), (0,)), ((), ()))

    def table(at, height, width):
        return table_ref[at : at + height, :width], table_ref[at + height : at + 2 * height, :width]

    lane_cos, lane_sin = table(0, LANES, LANES)
    twid_cos, twid_sin = table(2 * LANES, rows, LANES)
    row_cos, row_sin = table(2 * LANES + 2 * rows, rows, rows)
    a_re = f32_dot(w, lane_cos, over_lanes)
    a_im = -f32_dot(w, lane_sin, over_lanes)
    b_re = a_re * twid_cos + a_im * twid_sin
    b_im = a_im * twid_cos - a_re * twid_sin
    c = f32_dot(row_cos, b_re) + f32_dot(row_sin, b_im)
    sub = lax.broadcasted_iota(jnp.int32, (LANES, LANES), 0)
    lane = lax.broadcasted_iota(jnp.int32, (LANES, LANES), 1)

    if turn:
        part = LANES - turn % LANES
        near, after = (
            pltpu.roll(jnp.concatenate([c[n:], c[:n]], axis=0), part % LANES, 1)
            for n in (turn // LANES, turn // LANES + 1)
        )
        moved = jnp.where(lax.broadcasted_iota(jnp.int32, c.shape, 1) < part, near, after)
        c = jnp.where(lax.axis_index("mz") == 1, moved, c)

    def turned(row):
        return pltpu.roll(jnp.broadcast_to(c[row : row + 1], (LANES, LANES)), 0, 1, stride=1, stride_axis=0)

    before = turned(rows - 1)
    for row in range(rows):
        now = turned(row)
        high, low = two_terms(jnp.where(lane >= sub, now, before))
        u_ref[0:LANES, row * LANES : (row + 1) * LANES] = high
        u_ref[LANES:, row * LANES : (row + 1) * LANES] = low
        before = now


def circulant(weights, turn):
    length = weights.size
    rows = length // LANES

    def tables(a, b, period):
        angle = 2.0 * math.pi / period * ((a[:, None] * b[None, :]) % period)
        return np.pad(np.concatenate([np.cos(angle), np.sin(angle)]), ((0, 0), (0, LANES - b.size)))

    lane_ids, row_ids = np.arange(LANES), np.arange(rows)
    table = np.concatenate(
        [
            tables(lane_ids, lane_ids, LANES),
            tables(row_ids, lane_ids, length),
            tables(row_ids, row_ids, rows) / length,
        ]
    ).astype(np.float32)
    return pl.pallas_call(
        functools.partial(circulant_kernel, turn),
        out_shape=jax.ShapeDtypeStruct((2 * LANES, length), jnp.bfloat16),
        in_specs=vmem(2),
        out_specs=vmem(1)[0],
        compiler_params=pltpu.CompilerParams(vmem_limit_bytes=16 * MIB),
        cost_estimate=pl.CostEstimate(flops=2_000_000_000, bytes_accessed=4 * MIB, transcendentals=0),
        name="circulant_block",
    )(weights, table)


def model_kernel(places, planes, *refs):
    u_ref, g_ref, wide = refs[-3:]
    length = u_ref.shape[1]
    components = g_ref.shape[0]
    freq_rank = lax.axis_index("freq")
    if planes:
        own_ref, came_ref = refs[:2]
        freq_count = 2 * own_ref.shape[0]
        rows = own_ref.shape[1]
        padded = wide.shape[0] // freq_count
        for block in range(freq_count):
            apart = lax.bitwise_xor((freq_rank + block) & (freq_count - 1), freq_rank)
            ref = came_ref if block % 2 else own_ref
            values = ref[pl.ds(block_place(apart, freq_count), 1)][0]
            at, before = block * padded, (block - 1) % freq_count * padded
            wide[at : at + rows, 0:LANES] = values
            wide[before : before + rows, LANES:] = values
            wide[at + rows : at + padded, :] = jnp.zeros((padded - rows, 2 * LANES), jnp.bfloat16)
        period = length // freq_count // LANES
        for a in range(min(period, places)):
            columns = []
            for block in range(freq_count):
                first = REACH // LANES + period * block - a
                for n in range(first, first + padded // LANES):
                    at = n % (length // LANES) * LANES
                    columns.append(u_ref[:, at : at + LANES])
            width = 2 * LANES if a + period < places else LANES
            made = jnp.dot(
                jnp.concatenate(columns, axis=1), wide[:, :width], preferred_element_type=jnp.float32
            )
            made = made[:LANES] + made[LANES:]
            for half in range(width // LANES):
                piece = made[:, half * LANES : (half + 1) * LANES].T
                to = (a + half * period) * LANES
                g_ref[:, to : to + LANES] = piece[:components] + piece[components:]
        return
    own_ref = refs[0]
    step = own_ref.shape[1]
    steps = length // step
    bin_count = length // lax.axis_size("freq")
    first = lax.rem(freq_rank * bin_count + length - REACH, length) // step

    def bring(j, carry):
        values = own_ref[pl.ds(lax.rem(first + j, steps), 1)][0]
        to = pl.multiple_of(REACH + j * step, step)
        wide[pl.ds(to, step), 0:LANES] = values
        wide[pl.ds(pl.multiple_of(to - LANES, step), step), LANES:] = values
        return carry

    lax.fori_loop(0, (wide.shape[0] - REACH) // step, bring, 0)
    for a in range(0, places, 2):
        at = REACH + a * LANES
        made = jnp.dot(u_ref[...], wide[at : at + length, :], preferred_element_type=jnp.float32)
        made = made[:LANES] + made[LANES:]
        for half in range(min(2, places - a)):
            piece = made[:, half * LANES : (half + 1) * LANES].T
            g_ref[:, (a + half) * LANES : (a + half + 1) * LANES] = piece[:components] + piece[components:]


def block_place(apart, freq_count):
    return (apart >> 2) + ((apart >> 1) & 1) * (freq_count // 4)


def partial_model(gathered, u, bin_count, components):
    length = u.shape[1]
    places = -(-(bin_count + REACH) // LANES)
    planes = len(gathered) == 2
    if planes:
        own = gathered[0]
        wide_rows = 2 * own.shape[0] * (-(-own.shape[1] // LANES) * LANES)
    else:
        wide_rows = REACH + length + 2 * LANES * ((places - 1) // 2)
    return pl.pallas_call(
        functools.partial(model_kernel, places, planes),
        out_shape=jax.ShapeDtypeStruct((components, places * LANES), jnp.float32),
        in_specs=vmem(len(gathered) + 1),
        out_specs=vmem(1)[0],
        scratch_shapes=[pltpu.VMEM((wide_rows, 2 * LANES), jnp.bfloat16)],
        compiler_params=pltpu.CompilerParams(vmem_limit_bytes=24 * MIB),
        cost_estimate=pl.CostEstimate(flops=2_000_000_000, bytes_accessed=4 * MIB, transcendentals=0),
        name="partial_model",
    )(*gathered, u)


def shifted_terms(x, amps, lags, bin_count, terms):
    components = x.shape[0]
    out_count = -(-bin_count // LANES)
    x = pltpu.roll(x, x.shape[1] - 1, 1)
    height = 16
    lane = lax.broadcasted_iota(jnp.int32, (height, LANES), 1)
    for at in range(0, components, height):
        vectors = [x[at : at + height, v * LANES : (v + 1) * LANES] for v in range(out_count + 2)]
        for k in range(amps.shape[1]):
            left = REACH - 1 - jnp.broadcast_to(lags[at : at + height, k : k + 1], lane.shape)
            amp = jnp.broadcast_to(amps[at : at + height, k : k + 1], lane.shape)
            source = lane + (left & (LANES - 1))
            index = source & (LANES - 1)
            far, same = left >= LANES, source < LANES
            turned = [jnp.take_along_axis(v, index, axis=1, mode="promise_in_bounds") for v in vectors]
            turned = [jnp.where(far, turned[v + 1], turned[v]) for v in range(out_count + 1)]
            for v in range(out_count):
                high, low = two_terms(amp * jnp.where(same, turned[v], turned[v + 1]))
                width = min(LANES, bin_count - v * LANES)
                to = slice(k * bin_count + v * LANES, k * bin_count + v * LANES + width)
                terms[at : at + height, to] = high[:, :width]
                terms[components + at : components + at + height, to] = low[:, :width]


def pair_kernel(mine_ref, came_ref, o_ref):
    rows = mine_ref.shape[0]
    freq_count = 2 * came_ref.shape[0]
    freq_rank = lax.axis_index("freq")
    apart = lax.bitwise_xor((freq_rank - 1) & (freq_count - 1), freq_rank)
    o_ref[0:rows, :] = came_ref[pl.ds(block_place(apart, freq_count), 1)][0]
    o_ref[rows:, :] = mine_ref[...]


def window_pair(mine, came):
    return pl.pallas_call(
        pair_kernel,
        out_shape=jax.ShapeDtypeStruct((2 * mine.shape[0], mine.shape[1]), mine.dtype),
        in_specs=vmem(2),
        out_specs=vmem(1)[0],
        compiler_params=pltpu.CompilerParams(vmem_limit_bytes=8 * MIB),
        name="window_pair",
    )(mine, came)


def elution_kernel(planes, *refs):
    amp_ref, lag_ref, terms, window = refs[-4:]
    components = amp_ref.shape[1]
    bin_count = terms.shape[1] // amp_ref.shape[0]
    freq_rank = lax.axis_index("freq")
    if planes:
        pair_ref, other_ref = refs[:2]
        mz_rank = lax.axis_index("mz")
        rows = pair_ref.shape[0] // 2
        skip = bin_count - REACH
        for ref, half in ((pair_ref, mz_rank), (other_ref, 1 - mz_rank)):
            for block in range(2):
                to = pl.multiple_of((2 * block + half) * rows, 64)
                window[pl.ds(to, rows), :] = ref[block * rows : (block + 1) * rows, :]
    else:
        own_ref = refs[0]
        step = own_ref.shape[1]
        steps = own_ref.shape[0]
        first = lax.rem(freq_rank * bin_count + steps * step - REACH, steps * step) // step
        skip = 0
        for j in range(window.shape[0] // step):
            window[j * step : (j + 1) * step, :] = own_ref[pl.ds(lax.rem(first + j, steps), 1)][0]
    pieces = []
    for at in range(skip, window.shape[0], LANES):
        piece = window[at : at + LANES, :].astype(jnp.float32).T
        pieces.append(piece[:components] + piece[components:])
    shifted_terms(jnp.concatenate(pieces, axis=1), amp_ref[...].T, lag_ref[...].T, bin_count, terms)


def elution_terms(elutions, loadings, shifts, bin_count):
    run_count, components = loadings.shape
    places = -(-(bin_count + REACH) // LANES)
    planes = len(elutions) > 1
    return pl.pallas_call(
        functools.partial(elution_kernel, planes),
        out_shape=jax.ShapeDtypeStruct((2 * components, run_count * bin_count), jnp.bfloat16),
        in_specs=vmem(len(elutions) + 2),
        out_specs=vmem(1)[0],
        scratch_shapes=[pltpu.VMEM((2 * bin_count if planes else places * LANES, LANES), jnp.bfloat16)],
        compiler_params=pltpu.CompilerParams(vmem_limit_bytes=12 * MIB),
        cost_estimate=pl.CostEstimate(flops=1_000_000_000, bytes_accessed=2 * MIB, transcendentals=0),
        name="elution_terms",
    )(*elutions, loadings, shifts)


def product_kernel(parts, planes, *refs):
    i_ref = refs[0]
    g_refs = refs[1 : 1 + parts]
    elution_ref, amp_ref, lag_ref, num_ref, other_ref, terms = refs[1 + parts :]
    run_count, bin_count, local_mz = i_ref.shape
    components = amp_ref.shape[1]
    chunk = 2 * LANES
    chunks = local_mz // chunk
    g = g_refs[0][...]
    for ref in g_refs[1:]:
        g = g + ref[...]
    shifted_terms(g, amp_ref[...].T, lag_ref[...].T, bin_count, terms)
    gram = lax.dot_general(
        terms[...], elution_ref[...], (((1,), (1,)), ((), ())), preferred_element_type=jnp.float32
    )
    gram = gram[:components] + gram[components:]
    gram = gram[:, :components] + gram[:, components:]
    if planes:
        keep_ref, send_ref = num_ref, other_ref
        half = components // 2
        gram = jnp.concatenate([gram[:half], gram[half:]], axis=1)
        keep_ref[chunks * components :, :] = gram
        send_ref[chunks * components :, :] = gram
    else:
        other_ref[...] = gram

    for n in range(chunks):
        data = i_ref[:, :, n * chunk : (n + 1) * chunk].reshape(run_count * bin_count, chunk)
        made = jnp.dot(terms[...], data, preferred_element_type=jnp.float32)
        made = made[:components] + made[components:]
        if planes:
            freq_rank = lax.axis_index("freq")
            core = freq_rank & 1
            place = n // 2 + ((lax.bitwise_xor(freq_rank, 2 * n) >> 1) & 1) * (chunks // 2)
            at = pl.ds(pl.multiple_of(place * components, components), components)
            even, odd = made[:, :LANES], made[:, LANES:]
            keep_ref[at, :] = jnp.where(core == 0, even, odd)
            send_ref[at, :] = jnp.where(core == 0, odd, even)
        else:
            num_ref[:, n * chunk : (n + 1) * chunk] = made


def product(intensity, models, elution, loadings, shifts, planes):
    run_count, bin_count, local_mz = intensity.shape
    components = loadings.shape[1]
    chunk = 2 * LANES
    chunks = local_mz // chunk
    if planes:
        out_shapes = [(chunks * components + components // 2, LANES)] * 2
    else:
        out_shapes = [(components, local_mz), (components, components)]
    return pl.pallas_call(
        functools.partial(product_kernel, len(models), planes),
        out_shape=tuple(jax.ShapeDtypeStruct(shape, jnp.float32) for shape in out_shapes),
        in_specs=vmem(len(models) + 4),
        out_specs=tuple(vmem(2)),
        scratch_shapes=[pltpu.VMEM((2 * components, run_count * bin_count), jnp.bfloat16)],
        compiler_params=pltpu.CompilerParams(vmem_limit_bytes=24 * MIB),
        cost_estimate=pl.CostEstimate(
            flops=8_000_000_000, bytes_accessed=2 * intensity.size, transcendentals=0
        ),
        name="model_products",
    )(intensity, *models, elution, loadings, shifts)


def inverse2(a, b, d):
    scale = 1.0 / (a * d - b * b)
    return d * scale, -b * scale, a * scale


def eliminate(gram, right):
    components = gram.shape[0]
    row_id = lax.broadcasted_iota(jnp.int32, gram.shape, 0)
    for j in range(0, components, 4):
        columns = [jnp.broadcast_to(gram[:, j + n : j + n + 1], gram.shape) for n in range(4)]
        pivot = [[columns[n][j + m : j + m + 1] for n in range(4)] for m in range(4)]
        a00, a01, a11 = inverse2(pivot[0][0], pivot[0][1], pivot[1][1])
        b00, b01, b10, b11 = pivot[0][2], pivot[0][3], pivot[1][2], pivot[1][3]
        w00, w01 = a00 * b00 + a01 * b10, a00 * b01 + a01 * b11
        w10, w11 = a01 * b00 + a11 * b10, a01 * b01 + a11 * b11
        s00, s01, s11 = inverse2(
            pivot[2][2] - (b00 * w00 + b10 * w10),
            pivot[2][3] - (b00 * w01 + b10 * w11),
            pivot[3][3] - (b01 * w01 + b11 * w11),
        )
        away = (row_id < j) | (row_id >= j + 4)
        c0, c1, c2, c3 = (
            jnp.where(away, column, jnp.where(row_id == j + n, -1.0, 0.0)) for n, column in enumerate(columns)
        )
        t2, t3 = c2 - c0 * w00 - c1 * w10, c3 - c0 * w01 - c1 * w11
        f2, f3 = t2 * s00 + t3 * s01, t2 * s01 + t3 * s11
        f0 = c0 * a00 + c1 * a01 - f2 * w00 - f3 * w01
        f1 = c0 * a01 + c1 * a11 - f2 * w10 - f3 * w11
        factors = (f0, f1, f2, f3)

        def reduced(x):
            out = jnp.where(away[:, : x.shape[1]], x, 0.0)
            for n, factor in enumerate(factors):
                out = out - factor[:, : x.shape[1]] * x[j + n : j + n + 1]
            return out

        gram, right = reduced(gram), reduced(right)
    return right


def total_of(refs, at, rows):
    total = refs[0][at : at + rows]
    for ref in refs[1:]:
        total = total + ref[at : at + rows]
    return total


def halve_kernel(tail, a_ref, b_ref, o_ref):
    rows = o_ref.shape[0] - tail
    o_ref[...] = total_of((a_ref, b_ref), rows, rows + tail)


def spread_kernel(tail, a_ref, b_ref, c_ref, o_ref):
    rows = o_ref.shape[1] - tail
    count = o_ref.shape[0]
    gram = total_of((a_ref, b_ref), 2 * count * rows, tail) + c_ref[count * rows :, :]
    for n in range(count):
        o_ref[n, 0:rows, :] = total_of((a_ref, b_ref, c_ref), n * rows, rows)
        o_ref[n, rows:, :] = gram


def solve_planes_kernel(x_ref, o_ref):
    components = o_ref.shape[0]
    total = x_ref[0]
    for n in range(1, x_ref.shape[0]):
        total = total + x_ref[n]
    gram = total[components:]
    gram = jnp.concatenate([gram, pltpu.roll(gram, gram.shape[1] // 2, 1)], axis=0)
    o_ref[...] = eliminate(gram, total[:components])


def solve_kernel(g_ref, n_ref, o_ref):
    components = o_ref.shape[0]
    gram = jnp.concatenate([g_ref[...], jnp.zeros((components, LANES - components), jnp.float32)], axis=1)
    o_ref[...] = eliminate(gram, n_ref[...])


def small_call(kernel, shape, name, *args):
    return pl.pallas_call(
        kernel,
        out_shape=jax.ShapeDtypeStruct(shape, jnp.float32),
        in_specs=vmem(len(args)),
        out_specs=vmem(1)[0],
        compiler_params=pltpu.CompilerParams(vmem_limit_bytes=8 * MIB),
        name=name,
    )(*args)


def swap(x, axes, count, value):
    return lax.ppermute(x, axes, [(i, i ^ value) for i in range(count)])


def on_device(intensity, elution, loadings, shifts, bin_weight):
    freq_count = lax.axis_size("freq")
    mz_count = lax.axis_size("mz")
    components = loadings.shape[1]
    bin_count = intensity.shape[1]
    axes = ("freq", "mz")
    mine = pack(elution)
    own = intensity.shape[2] // freq_count
    planes = (
        own == LANES
        and 2 * components == LANES
        and mz_count == 2
        and freq_count & (freq_count - 1) == 0
        and freq_count >= 8
        and elution.shape[0] % 64 == 0
        and bin_count % LANES == 0
        and bin_count >= REACH
    )
    if not planes:
        gathered = lax.all_gather(mine, axes, axis=0).reshape(-1, math.gcd(bin_count, LANES), LANES)
        g = partial_model((gathered,), circulant(bin_weight.reshape(LANES, -1), 0), bin_count, components)
        shifted = elution_terms((gathered,), loadings, shifts, bin_count)
        numerator, gram = product(intensity, (g,), shifted, loadings, shifts, planes)
        gram = lax.psum(gram, "freq")
        owned = lax.psum_scatter(numerator, "freq", scatter_dimension=1, tiled=True)
        return small_call(solve_kernel, (components, own), "solve", gram, owned)
    z_steps = range(4, freq_count, 4)
    held = jnp.stack([mine] + [swap(mine, "freq", freq_count, step) for step in z_steps])
    weights = bin_weight.reshape(LANES, -1)
    held, weights = lax.optimization_barrier((held, weights))
    held = jnp.concatenate([held, swap(held, "freq", freq_count, 2)], axis=0)
    u = circulant(weights, elution.shape[0])
    held, u = lax.optimization_barrier((held, u))
    came = swap(held, "freq", freq_count, 1)
    pair = window_pair(mine, came)
    other = swap(pair, "mz", mz_count, 1)
    g = partial_model((held, came), u, bin_count, components)
    g, other = lax.optimization_barrier((g, other))
    models = (g, swap(g, "mz", mz_count, 1))
    shifted = elution_terms((pair, other), loadings, shifts, bin_count)
    keep, send = product(intensity, models, shifted, loadings, shifts, planes)
    tail = components // 2
    chips = freq_count // 4
    came = swap(send, "freq", freq_count, 1)
    send = small_call(
        functools.partial(halve_kernel, tail), (chips * components + tail, LANES), "reduce_cores", keep, came
    )
    across = swap(send, "freq", freq_count, 2)
    send = small_call(
        functools.partial(spread_kernel, tail), (chips, components + tail, LANES), "reduce_x", keep, came, across
    )
    groups = [[4 * z + chip for z in range(chips)] for chip in range(4)]
    spread = lax.all_to_all(send, "freq", 0, 0, axis_index_groups=groups)
    return small_call(solve_planes_kernel, (components, own), "solve", spread)


def solution(mesh):
    in_specs = (P(None, "freq", "mz"), P(("freq", "mz"), None), P(), P(), P())
    out_specs = P(None, ("mz", "freq"))
    return jax.shard_map(on_device, mesh=mesh, in_specs=in_specs, out_specs=out_specs, check_vma=False)
```

```python
import functools
import math

import jax
import jax.numpy as jnp
import numpy as np
from jax import lax
from jax.experimental import pallas as pl
from jax.experimental.pallas import tpu as pltpu
from jax.sharding import PartitionSpec as P

PRECISE = lax.Precision.HIGHEST
LANES = 128
REACH = 256
MIB = 1024 * 1024


def f32_dot(a, b, dims=(((1,), (0,)), ((), ()))):
    return lax.dot_general(a, b, dims, precision=PRECISE, preferred_element_type=jnp.float32)


def two_terms(x):
    high = x.astype(jnp.bfloat16)
    low = (x - high.astype(jnp.float32)).astype(jnp.bfloat16)
    return high, low


def vmem(count):
    return [pl.BlockSpec(memory_space=pltpu.VMEM)] * count


def pack_kernel(x_ref, o_ref):
    x = x_ref[...]
    components, rows = x.shape
    pad = -rows % LANES
    if pad:
        x = jnp.concatenate([x, jnp.zeros((components, pad), x.dtype)], axis=1)
    high, low = two_terms(x.T[:rows])
    o_ref[...] = jnp.concatenate([high, low], axis=1)


def pack(elution):
    rows, components = elution.shape
    return pl.pallas_call(
        pack_kernel,
        out_shape=jax.ShapeDtypeStruct((rows, 2 * components), jnp.bfloat16),
        in_specs=vmem(1),
        out_specs=vmem(1)[0],
        compiler_params=pltpu.CompilerParams(vmem_limit_bytes=8 * MIB),
        name="pack_elution",
    )(elution.T)


def circulant_kernel(turn, w_ref, table_ref, u_ref):
    rows = w_ref.shape[1]
    w = w_ref[...]
    over_lanes = (((0,), (0,)), ((), ()))

    def table(at, height, width):
        return table_ref[at : at + height, :width], table_ref[at + height : at + 2 * height, :width]

    lane_cos, lane_sin = table(0, LANES, LANES)
    twid_cos, twid_sin = table(2 * LANES, rows, LANES)
    row_cos, row_sin = table(2 * LANES + 2 * rows, rows, rows)
    a_re = f32_dot(w, lane_cos, over_lanes)
    a_im = -f32_dot(w, lane_sin, over_lanes)
    b_re = a_re * twid_cos + a_im * twid_sin
    b_im = a_im * twid_cos - a_re * twid_sin
    c = f32_dot(row_cos, b_re) + f32_dot(row_sin, b_im)
    sub = lax.broadcasted_iota(jnp.int32, (LANES, LANES), 0)
    lane = lax.broadcasted_iota(jnp.int32, (LANES, LANES), 1)

    if turn:
        part = LANES - turn % LANES
        near, after = (
            pltpu.roll(jnp.concatenate([c[n:], c[:n]], axis=0), part % LANES, 1)
            for n in (turn // LANES, turn // LANES + 1)
        )
        moved = jnp.where(lax.broadcasted_iota(jnp.int32, c.shape, 1) < part, near, after)
        c = jnp.where(lax.axis_index("mz") == 1, moved, c)

    def turned(row):
        return pltpu.roll(jnp.broadcast_to(c[row : row + 1], (LANES, LANES)), 0, 1, stride=1, stride_axis=0)

    before = turned(rows - 1)
    for row in range(rows):
        now = turned(row)
        high, low = two_terms(jnp.where(lane >= sub, now, before))
        u_ref[0:LANES, row * LANES : (row + 1) * LANES] = high
        u_ref[LANES:, row * LANES : (row + 1) * LANES] = low
        before = now


def circulant(weights, turn):
    length = weights.size
    rows = length // LANES

    def tables(a, b, period):
        angle = 2.0 * math.pi / period * ((a[:, None] * b[None, :]) % period)
        return np.pad(np.concatenate([np.cos(angle), np.sin(angle)]), ((0, 0), (0, LANES - b.size)))

    lane_ids, row_ids = np.arange(LANES), np.arange(rows)
    table = np.concatenate(
        [
            tables(lane_ids, lane_ids, LANES),
            tables(row_ids, lane_ids, length),
            tables(row_ids, row_ids, rows) / length,
        ]
    ).astype(np.float32)
    return pl.pallas_call(
        functools.partial(circulant_kernel, turn),
        out_shape=jax.ShapeDtypeStruct((2 * LANES, length), jnp.bfloat16),
        in_specs=vmem(2),
        out_specs=vmem(1)[0],
        compiler_params=pltpu.CompilerParams(vmem_limit_bytes=16 * MIB),
        cost_estimate=pl.CostEstimate(flops=2_000_000_000, bytes_accessed=4 * MIB, transcendentals=0),
        name="circulant_block",
    )(weights, table)


def model_kernel(places, planes, *refs):
    u_ref, g_ref, wide = refs[-3:]
    length = u_ref.shape[1]
    components = g_ref.shape[0]
    freq_rank = lax.axis_index("freq")
    if planes:
        own_ref, came_ref = refs[:2]
        freq_count = 2 * own_ref.shape[0]
        rows = own_ref.shape[1]
        padded = wide.shape[0] // freq_count
        for block in range(freq_count):
            apart = lax.bitwise_xor((freq_rank + block) & (freq_count - 1), freq_rank)
            ref = came_ref if block % 2 else own_ref
            values = ref[pl.ds(block_place(apart, freq_count), 1)][0]
            at, before = block * padded, (block - 1) % freq_count * padded
            wide[at : at + rows, 0:LANES] = values
            wide[before : before + rows, LANES:] = values
            wide[at + rows : at + padded, :] = jnp.zeros((padded - rows, 2 * LANES), jnp.bfloat16)
        period = length // freq_count // LANES
        for a in range(min(period, places)):
            columns = []
            for block in range(freq_count):
                first = REACH // LANES + period * block - a
                for n in range(first, first + padded // LANES):
                    at = n % (length // LANES) * LANES
                    columns.append(u_ref[:, at : at + LANES])
            width = 2 * LANES if a + period < places else LANES
            made = jnp.dot(
                jnp.concatenate(columns, axis=1), wide[:, :width], preferred_element_type=jnp.float32
            )
            made = made[:LANES] + made[LANES:]
            for half in range(width // LANES):
                piece = made[:, half * LANES : (half + 1) * LANES].T
                to = (a + half * period) * LANES
                g_ref[:, to : to + LANES] = piece[:components] + piece[components:]
        return
    own_ref = refs[0]
    step = own_ref.shape[1]
    steps = length // step
    bin_count = length // lax.axis_size("freq")
    first = lax.rem(freq_rank * bin_count + length - REACH, length) // step

    def bring(j, carry):
        values = own_ref[pl.ds(lax.rem(first + j, steps), 1)][0]
        to = pl.multiple_of(REACH + j * step, step)
        wide[pl.ds(to, step), 0:LANES] = values
        wide[pl.ds(pl.multiple_of(to - LANES, step), step), LANES:] = values
        return carry

    lax.fori_loop(0, (wide.shape[0] - REACH) // step, bring, 0)
    for a in range(0, places, 2):
        at = REACH + a * LANES
        made = jnp.dot(u_ref[...], wide[at : at + length, :], preferred_element_type=jnp.float32)
        made = made[:LANES] + made[LANES:]
        for half in range(min(2, places - a)):
            piece = made[:, half * LANES : (half + 1) * LANES].T
            g_ref[:, (a + half) * LANES : (a + half + 1) * LANES] = piece[:components] + piece[components:]


def block_place(apart, freq_count):
    return (apart >> 2) + ((apart >> 1) & 1) * (freq_count // 4)


def partial_model(gathered, u, bin_count, components):
    length = u.shape[1]
    places = -(-(bin_count + REACH) // LANES)
    planes = len(gathered) == 2
    if planes:
        own = gathered[0]
        wide_rows = 2 * own.shape[0] * (-(-own.shape[1] // LANES) * LANES)
    else:
        wide_rows = REACH + length + 2 * LANES * ((places - 1) // 2)
    return pl.pallas_call(
        functools.partial(model_kernel, places, planes),
        out_shape=jax.ShapeDtypeStruct((components, places * LANES), jnp.float32),
        in_specs=vmem(len(gathered) + 1),
        out_specs=vmem(1)[0],
        scratch_shapes=[pltpu.VMEM((wide_rows, 2 * LANES), jnp.bfloat16)],
        compiler_params=pltpu.CompilerParams(vmem_limit_bytes=24 * MIB),
        cost_estimate=pl.CostEstimate(flops=2_000_000_000, bytes_accessed=4 * MIB, transcendentals=0),
        name="partial_model",
    )(*gathered, u)


def shifted_terms(x, amps, lags, bin_count, terms):
    components = x.shape[0]
    out_count = -(-bin_count // LANES)
    x = pltpu.roll(x, x.shape[1] - 1, 1)
    height = 16
    lane = lax.broadcasted_iota(jnp.int32, (height, LANES), 1)
    for at in range(0, components, height):
        vectors = [x[at : at + height, v * LANES : (v + 1) * LANES] for v in range(out_count + 2)]
        for k in range(amps.shape[1]):
            left = REACH - 1 - jnp.broadcast_to(lags[at : at + height, k : k + 1], lane.shape)
            amp = jnp.broadcast_to(amps[at : at + height, k : k + 1], lane.shape)
            source = lane + (left & (LANES - 1))
            index = source & (LANES - 1)
            far, same = left >= LANES, source < LANES
            turned = [jnp.take_along_axis(v, index, axis=1, mode="promise_in_bounds") for v in vectors]
            turned = [jnp.where(far, turned[v + 1], turned[v]) for v in range(out_count + 1)]
            for v in range(out_count):
                high, low = two_terms(amp * jnp.where(same, turned[v], turned[v + 1]))
                width = min(LANES, bin_count - v * LANES)
                to = slice(k * bin_count + v * LANES, k * bin_count + v * LANES + width)
                terms[at : at + height, to] = high[:, :width]
                terms[components + at : components + at + height, to] = low[:, :width]


def pair_kernel(mine_ref, came_ref, o_ref):
    rows = mine_ref.shape[0]
    freq_count = 2 * came_ref.shape[0]
    freq_rank = lax.axis_index("freq")
    apart = lax.bitwise_xor((freq_rank - 1) & (freq_count - 1), freq_rank)
    o_ref[0:rows, :] = came_ref[pl.ds(block_place(apart, freq_count), 1)][0]
    o_ref[rows:, :] = mine_ref[...]


def window_pair(mine, came):
    return pl.pallas_call(
        pair_kernel,
        out_shape=jax.ShapeDtypeStruct((2 * mine.shape[0], mine.shape[1]), mine.dtype),
        in_specs=vmem(2),
        out_specs=vmem(1)[0],
        compiler_params=pltpu.CompilerParams(vmem_limit_bytes=8 * MIB),
        name="window_pair",
    )(mine, came)


def elution_kernel(planes, *refs):
    amp_ref, lag_ref, terms, window = refs[-4:]
    components = amp_ref.shape[1]
    bin_count = terms.shape[1] // amp_ref.shape[0]
    freq_rank = lax.axis_index("freq")
    if planes:
        pair_ref, other_ref = refs[:2]
        mz_rank = lax.axis_index("mz")
        rows = pair_ref.shape[0] // 2
        skip = bin_count - REACH
        for ref, half in ((pair_ref, mz_rank), (other_ref, 1 - mz_rank)):
            for block in range(2):
                to = pl.multiple_of((2 * block + half) * rows, 64)
                window[pl.ds(to, rows), :] = ref[block * rows : (block + 1) * rows, :]
    else:
        own_ref = refs[0]
        step = own_ref.shape[1]
        steps = own_ref.shape[0]
        first = lax.rem(freq_rank * bin_count + steps * step - REACH, steps * step) // step
        skip = 0
        for j in range(window.shape[0] // step):
            window[j * step : (j + 1) * step, :] = own_ref[pl.ds(lax.rem(first + j, steps), 1)][0]
    pieces = []
    for at in range(skip, window.shape[0], LANES):
        piece = window[at : at + LANES, :].astype(jnp.float32).T
        pieces.append(piece[:components] + piece[components:])
    shifted_terms(jnp.concatenate(pieces, axis=1), amp_ref[...].T, lag_ref[...].T, bin_count, terms)


def elution_terms(elutions, loadings, shifts, bin_count):
    run_count, components = loadings.shape
    places = -(-(bin_count + REACH) // LANES)
    planes = len(elutions) > 1
    return pl.pallas_call(
        functools.partial(elution_kernel, planes),
        out_shape=jax.ShapeDtypeStruct((2 * components, run_count * bin_count), jnp.bfloat16),
        in_specs=vmem(len(elutions) + 2),
        out_specs=vmem(1)[0],
        scratch_shapes=[pltpu.VMEM((2 * bin_count if planes else places * LANES, LANES), jnp.bfloat16)],
        compiler_params=pltpu.CompilerParams(vmem_limit_bytes=12 * MIB),
        cost_estimate=pl.CostEstimate(flops=1_000_000_000, bytes_accessed=2 * MIB, transcendentals=0),
        name="elution_terms",
    )(*elutions, loadings, shifts)


def product_kernel(parts, planes, *refs):
    i_ref = refs[0]
    g_refs = refs[1 : 1 + parts]
    elution_ref, amp_ref, lag_ref, num_ref, other_ref, terms = refs[1 + parts :]
    run_count, bin_count, local_mz = i_ref.shape
    components = amp_ref.shape[1]
    chunk = 2 * LANES
    chunks = local_mz // chunk
    g = g_refs[0][...]
    for ref in g_refs[1:]:
        g = g + ref[...]
    shifted_terms(g, amp_ref[...].T, lag_ref[...].T, bin_count, terms)
    gram = lax.dot_general(
        terms[...], elution_ref[...], (((1,), (1,)), ((), ())), preferred_element_type=jnp.float32
    )
    gram = gram[:components] + gram[components:]
    gram = gram[:, :components] + gram[:, components:]
    if planes:
        keep_ref, send_ref = num_ref, other_ref
        half = components // 2
        gram = jnp.concatenate([gram[:half], gram[half:]], axis=1)
        keep_ref[chunks * components :, :] = gram
        send_ref[chunks * components :, :] = gram
    else:
        other_ref[...] = gram

    for n in range(chunks):
        data = i_ref[:, :, n * chunk : (n + 1) * chunk].reshape(run_count * bin_count, chunk)
        made = jnp.dot(terms[...], data, preferred_element_type=jnp.float32)
        made = made[:components] + made[components:]
        if planes:
            freq_rank = lax.axis_index("freq")
            core = freq_rank & 1
            place = block_place(lax.bitwise_xor(freq_rank, 2 * n + core), 2 * chunks)
            at = pl.ds(pl.multiple_of(place * components, components), components)
            even, odd = made[:, :LANES], made[:, LANES:]
            keep_ref[at, :] = jnp.where(core == 0, even, odd)
            send_ref[at, :] = jnp.where(core == 0, odd, even)
        else:
            num_ref[:, n * chunk : (n + 1) * chunk] = made


def product(intensity, models, elution, loadings, shifts, planes):
    run_count, bin_count, local_mz = intensity.shape
    components = loadings.shape[1]
    chunk = 2 * LANES
    chunks = local_mz // chunk
    if planes:
        out_shapes = [(chunks * components + components // 2, LANES)] * 2
    else:
        out_shapes = [(components, local_mz), (components, components)]
    return pl.pallas_call(
        functools.partial(product_kernel, len(models), planes),
        out_shape=tuple(jax.ShapeDtypeStruct(shape, jnp.float32) for shape in out_shapes),
        in_specs=vmem(len(models) + 4),
        out_specs=tuple(vmem(2)),
        scratch_shapes=[pltpu.VMEM((2 * components, run_count * bin_count), jnp.bfloat16)],
        compiler_params=pltpu.CompilerParams(vmem_limit_bytes=24 * MIB),
        cost_estimate=pl.CostEstimate(
            flops=8_000_000_000, bytes_accessed=2 * intensity.size, transcendentals=0
        ),
        name="model_products",
    )(intensity, *models, elution, loadings, shifts)


def inverse2(a, b, d):
    scale = 1.0 / (a * d - b * b)
    return d * scale, -b * scale, a * scale


def eliminate(gram, right):
    components = gram.shape[0]
    row_id = lax.broadcasted_iota(jnp.int32, gram.shape, 0)
    for j in range(0, components, 4):
        columns = [jnp.broadcast_to(gram[:, j + n : j + n + 1], gram.shape) for n in range(4)]
        pivot = [[columns[n][j + m : j + m + 1] for n in range(4)] for m in range(4)]
        a00, a01, a11 = inverse2(pivot[0][0], pivot[0][1], pivot[1][1])
        b00, b01, b10, b11 = pivot[0][2], pivot[0][3], pivot[1][2], pivot[1][3]
        w00, w01 = a00 * b00 + a01 * b10, a00 * b01 + a01 * b11
        w10, w11 = a01 * b00 + a11 * b10, a01 * b01 + a11 * b11
        s00, s01, s11 = inverse2(
            pivot[2][2] - (b00 * w00 + b10 * w10),
            pivot[2][3] - (b00 * w01 + b10 * w11),
            pivot[3][3] - (b01 * w01 + b11 * w11),
        )
        away = (row_id < j) | (row_id >= j + 4)
        c0, c1, c2, c3 = (
            jnp.where(away, column, jnp.where(row_id == j + n, -1.0, 0.0)) for n, column in enumerate(columns)
        )
        t2, t3 = c2 - c0 * w00 - c1 * w10, c3 - c0 * w01 - c1 * w11
        f2, f3 = t2 * s00 + t3 * s01, t2 * s01 + t3 * s11
        f0 = c0 * a00 + c1 * a01 - f2 * w00 - f3 * w01
        f1 = c0 * a01 + c1 * a11 - f2 * w10 - f3 * w11
        factors = (f0, f1, f2, f3)

        def reduced(x):
            out = jnp.where(away[:, : x.shape[1]], x, 0.0)
            for n, factor in enumerate(factors):
                out = out - factor[:, : x.shape[1]] * x[j + n : j + n + 1]
            return out

        gram, right = reduced(gram), reduced(right)
    return right


def total_of(refs, at, rows):
    total = refs[0][at : at + rows]
    for ref in refs[1:]:
        total = total + ref[at : at + rows]
    return total


def halve_kernel(tail, a_ref, b_ref, o_ref):
    rows = o_ref.shape[0] - tail
    o_ref[...] = total_of((a_ref, b_ref), rows, rows + tail)


def spread_kernel(tail, a_ref, b_ref, c_ref, *outs):
    rows = outs[0].shape[0] - tail
    count = len(outs)
    gram = total_of((a_ref, b_ref), 2 * count * rows, tail) + c_ref[count * rows :, :]
    for n, o_ref in enumerate(outs):
        o_ref[0:rows, :] = total_of((a_ref, b_ref, c_ref), n * rows, rows)
        o_ref[rows:, :] = gram


def solve_planes_kernel(*refs):
    o_ref = refs[-1]
    components = o_ref.shape[0]
    total = total_of(refs[:-1], 0, refs[0].shape[0])
    gram = total[components:]
    gram = jnp.concatenate([gram, pltpu.roll(gram, gram.shape[1] // 2, 1)], axis=0)
    o_ref[...] = eliminate(gram, total[:components])


def solve_kernel(g_ref, n_ref, o_ref):
    components = o_ref.shape[0]
    gram = jnp.concatenate([g_ref[...], jnp.zeros((components, LANES - components), jnp.float32)], axis=1)
    o_ref[...] = eliminate(gram, n_ref[...])


def small_call(kernel, shape, name, *args, count=1):
    return pl.pallas_call(
        kernel,
        out_shape=(jax.ShapeDtypeStruct(shape, jnp.float32),) * count,
        in_specs=vmem(len(args)),
        out_specs=tuple(vmem(count)),
        compiler_params=pltpu.CompilerParams(vmem_limit_bytes=8 * MIB),
        name=name,
    )(*args)


def swap(x, axes, count, value):
    return lax.ppermute(x, axes, [(i, i ^ value) for i in range(count)])


def on_device(intensity, elution, loadings, shifts, bin_weight):
    freq_count = lax.axis_size("freq")
    mz_count = lax.axis_size("mz")
    components = loadings.shape[1]
    bin_count = intensity.shape[1]
    axes = ("freq", "mz")
    mine = pack(elution)
    own = intensity.shape[2] // freq_count
    planes = (
        own == LANES
        and 2 * components == LANES
        and mz_count == 2
        and freq_count & (freq_count - 1) == 0
        and freq_count >= 8
        and elution.shape[0] % 64 == 0
        and bin_count % LANES == 0
        and bin_count >= REACH
    )
    if not planes:
        gathered = lax.all_gather(mine, axes, axis=0).reshape(-1, math.gcd(bin_count, LANES), LANES)
        g = partial_model((gathered,), circulant(bin_weight.reshape(LANES, -1), 0), bin_count, components)
        shifted = elution_terms((gathered,), loadings, shifts, bin_count)
        numerator, gram = product(intensity, (g,), shifted, loadings, shifts, planes)
        gram = lax.psum(gram, "freq")
        owned = lax.psum_scatter(numerator, "freq", scatter_dimension=1, tiled=True)
        return small_call(solve_kernel, (components, own), "solve", gram, owned)[0]
    z_steps = range(4, freq_count, 4)
    held = jnp.stack([mine] + [swap(mine, "freq", freq_count, step) for step in z_steps])
    weights = bin_weight.reshape(LANES, -1)
    held, weights = lax.optimization_barrier((held, weights))
    held = jnp.concatenate([held, swap(held, "freq", freq_count, 2)], axis=0)
    u = circulant(weights, elution.shape[0])
    held, u = lax.optimization_barrier((held, u))
    came = swap(held, "freq", freq_count, 1)
    pair = window_pair(mine, came)
    other = swap(pair, "mz", mz_count, 1)
    g = partial_model((held, came), u, bin_count, components)
    models = (g, swap(g, "mz", mz_count, 1))
    shifted = elution_terms((pair, other), loadings, shifts, bin_count)
    keep, send = product(intensity, models, shifted, loadings, shifts, planes)
    tail = components // 2
    chips = freq_count // 4
    came = swap(send, "freq", freq_count, 1)
    (send,) = small_call(
        functools.partial(halve_kernel, tail), (chips * components + tail, LANES), "reduce_cores", keep, came
    )
    across = swap(send, "freq", freq_count, 2)
    own_part, *sends = small_call(
        functools.partial(spread_kernel, tail), (components + tail, LANES), "reduce_x", keep, came, across, count=chips
    )
    parts = [swap(send, "freq", freq_count, step) for send, step in zip(sends, z_steps)]
    return small_call(solve_planes_kernel, (components, own), "solve", own_part, *parts)[0]


def solution(mesh):
    in_specs = (P(None, "freq", "mz"), P(("freq", "mz"), None), P(), P(), P())
    out_specs = P(None, ("mz", "freq"))
    return jax.shard_map(on_device, mesh=mesh, in_specs=in_specs, out_specs=out_specs, check_vma=False)
```

```python
import functools
import math

import jax
import jax.numpy as jnp
import numpy as np
from jax import lax
from jax.experimental import pallas as pl
from jax.experimental.pallas import tpu as pltpu
from jax.sharding import PartitionSpec as P

PRECISE = lax.Precision.HIGHEST
LANES = 128
REACH = 256
MIB = 1024 * 1024
FULL = 32767.0


def f32_dot(a, b, dims=(((1,), (0,)), ((), ()))):
    return lax.dot_general(a, b, dims, precision=PRECISE, preferred_element_type=jnp.float32)


def two_terms(x):
    high = x.astype(jnp.bfloat16)
    low = (x - high.astype(jnp.float32)).astype(jnp.bfloat16)
    return high, low


def vmem(count):
    return [pl.BlockSpec(memory_space=pltpu.VMEM)] * count


def pack_kernel(x_ref, o_ref):
    x = x_ref[...]
    components, rows = x.shape
    pad = -rows % LANES
    if pad:
        x = jnp.concatenate([x, jnp.zeros((components, pad), x.dtype)], axis=1)
    high, low = two_terms(x.T[:rows])
    o_ref[...] = jnp.concatenate([high, low], axis=1)


def pack(elution):
    rows, components = elution.shape
    return pl.pallas_call(
        pack_kernel,
        out_shape=jax.ShapeDtypeStruct((rows, 2 * components), jnp.bfloat16),
        in_specs=vmem(1),
        out_specs=vmem(1)[0],
        compiler_params=pltpu.CompilerParams(vmem_limit_bytes=8 * MIB),
        name="pack_elution",
    )(elution.T)


def encode_kernel(x_ref, o_ref):
    components, rows = x_ref.shape
    half = rows // 2
    x = x_ref[...]
    pad = -rows % LANES
    x = jnp.concatenate([x, jnp.zeros((components, pad), x.dtype)], axis=1).T[:rows]
    peak = jnp.maximum(jnp.max(jnp.abs(x), axis=0, keepdims=True), 1e-30)
    level = jnp.floor(256.0 / math.log(2.0) * jnp.log(peak)) + 1.0
    x = x * (FULL / scale_of(level))
    x = jnp.clip(jnp.floor(x + 0.5), -FULL, FULL).astype(jnp.int32).astype(jnp.int16)
    o_ref[0:half, :] = jnp.concatenate([x[:half], x[half:]], axis=1)
    level = jnp.broadcast_to(level, (16, components)).astype(jnp.int32).astype(jnp.int16)
    o_ref[half:, :] = jnp.concatenate([level, level], axis=1)


def scale_of(level):
    return jnp.exp(math.log(2.0) / 256.0 * level)


def decoded(x):
    half = x.shape[0] - 16
    x = x.astype(jnp.int32).astype(jnp.float32)
    x = x[:half] * (scale_of(x[half : half + 1]) * (1.0 / FULL))
    high = x.astype(jnp.bfloat16).astype(jnp.float32)
    low = x - high
    left = lax.broadcasted_iota(jnp.int32, x.shape, 1) < LANES // 2
    top = jnp.where(left, high, pltpu.roll(low, LANES // 2, 1))
    bottom = jnp.where(left, pltpu.roll(high, LANES // 2, 1), low)
    return jnp.concatenate([top, bottom], axis=0).astype(jnp.bfloat16)


def encode(elution):
    rows, components = elution.shape
    return pl.pallas_call(
        encode_kernel,
        out_shape=jax.ShapeDtypeStruct((rows // 2 + 16, 2 * components), jnp.int16),
        in_specs=vmem(1),
        out_specs=vmem(1)[0],
        compiler_params=pltpu.CompilerParams(vmem_limit_bytes=8 * MIB),
        name="encode_elution",
    )(elution.T)


def circulant_kernel(turn, w_ref, table_ref, u_ref):
    rows = w_ref.shape[1]
    w = w_ref[...]
    over_lanes = (((0,), (0,)), ((), ()))

    def table(at, height, width):
        return table_ref[at : at + height, :width], table_ref[at + height : at + 2 * height, :width]

    lane_cos, lane_sin = table(0, LANES, LANES)
    twid_cos, twid_sin = table(2 * LANES, rows, LANES)
    row_cos, row_sin = table(2 * LANES + 2 * rows, rows, rows)
    a_re = f32_dot(w, lane_cos, over_lanes)
    a_im = -f32_dot(w, lane_sin, over_lanes)
    b_re = a_re * twid_cos + a_im * twid_sin
    b_im = a_im * twid_cos - a_re * twid_sin
    c = f32_dot(row_cos, b_re) + f32_dot(row_sin, b_im)
    sub = lax.broadcasted_iota(jnp.int32, (LANES, LANES), 0)
    lane = lax.broadcasted_iota(jnp.int32, (LANES, LANES), 1)

    if turn:
        part = LANES - turn % LANES
        near, after = (
            pltpu.roll(jnp.concatenate([c[n:], c[:n]], axis=0), part % LANES, 1)
            for n in (turn // LANES, turn // LANES + 1)
        )
        moved = jnp.where(lax.broadcasted_iota(jnp.int32, c.shape, 1) < part, near, after)
        c = jnp.where(lax.axis_index("mz") == 1, moved, c)

    def turned(row):
        return pltpu.roll(jnp.broadcast_to(c[row : row + 1], (LANES, LANES)), 0, 1, stride=1, stride_axis=0)

    before = turned(rows - 1)
    for row in range(rows):
        now = turned(row)
        high, low = two_terms(jnp.where(lane >= sub, now, before))
        u_ref[0:LANES, row * LANES : (row + 1) * LANES] = high
        u_ref[LANES:, row * LANES : (row + 1) * LANES] = low
        before = now


def circulant(weights, turn):
    length = weights.size
    rows = length // LANES

    def tables(a, b, period):
        angle = 2.0 * math.pi / period * ((a[:, None] * b[None, :]) % period)
        return np.pad(np.concatenate([np.cos(angle), np.sin(angle)]), ((0, 0), (0, LANES - b.size)))

    lane_ids, row_ids = np.arange(LANES), np.arange(rows)
    table = np.concatenate(
        [
            tables(lane_ids, lane_ids, LANES),
            tables(row_ids, lane_ids, length),
            tables(row_ids, row_ids, rows) / length,
        ]
    ).astype(np.float32)
    return pl.pallas_call(
        functools.partial(circulant_kernel, turn),
        out_shape=jax.ShapeDtypeStruct((2 * LANES, length), jnp.bfloat16),
        in_specs=vmem(2),
        out_specs=vmem(1)[0],
        compiler_params=pltpu.CompilerParams(vmem_limit_bytes=16 * MIB),
        cost_estimate=pl.CostEstimate(flops=2_000_000_000, bytes_accessed=4 * MIB, transcendentals=0),
        name="circulant_block",
    )(weights, table)


def model_kernel(places, planes, *refs):
    u_ref, g_ref, wide = refs[-3:]
    length = u_ref.shape[1]
    components = g_ref.shape[0]
    freq_rank = lax.axis_index("freq")
    if planes:
        own_ref, came_ref = refs[:2]
        freq_count = 2 * own_ref.shape[0]
        rows = 2 * (own_ref.shape[1] - 16)
        padded = wide.shape[0] // freq_count
        for block in range(freq_count):
            apart = lax.bitwise_xor((freq_rank + block) & (freq_count - 1), freq_rank)
            ref = came_ref if block % 2 else own_ref
            values = decoded(ref[pl.ds(block_place(apart, freq_count), 1)][0])
            at, before = block * padded, (block - 1) % freq_count * padded
            wide[at : at + rows, 0:LANES] = values
            wide[before : before + rows, LANES:] = values
            wide[at + rows : at + padded, :] = jnp.zeros((padded - rows, 2 * LANES), jnp.bfloat16)
        period = length // freq_count // LANES
        for a in range(min(period, places)):
            columns = []
            for block in range(freq_count):
                first = REACH // LANES + period * block - a
                for n in range(first, first + padded // LANES):
                    at = n % (length // LANES) * LANES
                    columns.append(u_ref[:, at : at + LANES])
            width = 2 * LANES if a + period < places else LANES
            made = jnp.dot(
                jnp.concatenate(columns, axis=1), wide[:, :width], preferred_element_type=jnp.float32
            )
            made = made[:LANES] + made[LANES:]
            for half in range(width // LANES):
                piece = made[:, half * LANES : (half + 1) * LANES].T
                to = (a + half * period) * LANES
                g_ref[:, to : to + LANES] = piece[:components] + piece[components:]
        return
    own_ref = refs[0]
    step = own_ref.shape[1]
    steps = length // step
    bin_count = length // lax.axis_size("freq")
    first = lax.rem(freq_rank * bin_count + length - REACH, length) // step

    def bring(j, carry):
        values = own_ref[pl.ds(lax.rem(first + j, steps), 1)][0]
        to = pl.multiple_of(REACH + j * step, step)
        wide[pl.ds(to, step), 0:LANES] = values
        wide[pl.ds(pl.multiple_of(to - LANES, step), step), LANES:] = values
        return carry

    lax.fori_loop(0, (wide.shape[0] - REACH) // step, bring, 0)
    for a in range(0, places, 2):
        at = REACH + a * LANES
        made = jnp.dot(u_ref[...], wide[at : at + length, :], preferred_element_type=jnp.float32)
        made = made[:LANES] + made[LANES:]
        for half in range(min(2, places - a)):
            piece = made[:, half * LANES : (half + 1) * LANES].T
            g_ref[:, (a + half) * LANES : (a + half + 1) * LANES] = piece[:components] + piece[components:]


def block_place(apart, freq_count):
    return (apart >> 2) + ((apart >> 1) & 1) * (freq_count // 4)


def partial_model(gathered, u, bin_count, components):
    length = u.shape[1]
    places = -(-(bin_count + REACH) // LANES)
    planes = len(gathered) == 2
    if planes:
        own = gathered[0]
        wide_rows = 2 * own.shape[0] * (-(-2 * (own.shape[1] - 16) // LANES) * LANES)
    else:
        wide_rows = REACH + length + 2 * LANES * ((places - 1) // 2)
    return pl.pallas_call(
        functools.partial(model_kernel, places, planes),
        out_shape=jax.ShapeDtypeStruct((components, places * LANES), jnp.float32),
        in_specs=vmem(len(gathered) + 1),
        out_specs=vmem(1)[0],
        scratch_shapes=[pltpu.VMEM((wide_rows, 2 * LANES), jnp.bfloat16)],
        compiler_params=pltpu.CompilerParams(vmem_limit_bytes=24 * MIB),
        cost_estimate=pl.CostEstimate(flops=2_000_000_000, bytes_accessed=4 * MIB, transcendentals=0),
        name="partial_model",
    )(*gathered, u)


def shifted_terms(x, amps, lags, bin_count, terms):
    components = x.shape[0]
    out_count = -(-bin_count // LANES)
    x = pltpu.roll(x, x.shape[1] - 1, 1)
    height = 16
    lane = lax.broadcasted_iota(jnp.int32, (height, LANES), 1)
    for at in range(0, components, height):
        vectors = [x[at : at + height, v * LANES : (v + 1) * LANES] for v in range(out_count + 2)]
        for k in range(amps.shape[1]):
            left = REACH - 1 - jnp.broadcast_to(lags[at : at + height, k : k + 1], lane.shape)
            amp = jnp.broadcast_to(amps[at : at + height, k : k + 1], lane.shape)
            source = lane + (left & (LANES - 1))
            index = source & (LANES - 1)
            far, same = left >= LANES, source < LANES
            turned = [jnp.take_along_axis(v, index, axis=1, mode="promise_in_bounds") for v in vectors]
            turned = [jnp.where(far, turned[v + 1], turned[v]) for v in range(out_count + 1)]
            for v in range(out_count):
                high, low = two_terms(amp * jnp.where(same, turned[v], turned[v + 1]))
                width = min(LANES, bin_count - v * LANES)
                to = slice(k * bin_count + v * LANES, k * bin_count + v * LANES + width)
                terms[at : at + height, to] = high[:, :width]
                terms[components + at : components + at + height, to] = low[:, :width]


def pair_kernel(mine_ref, came_ref, o_ref):
    rows = mine_ref.shape[0]
    freq_count = 2 * came_ref.shape[0]
    freq_rank = lax.axis_index("freq")
    apart = lax.bitwise_xor((freq_rank - 1) & (freq_count - 1), freq_rank)
    o_ref[0:rows, :] = came_ref[pl.ds(block_place(apart, freq_count), 1)][0]
    o_ref[rows:, :] = mine_ref[...]


def window_pair(mine, came):
    return pl.pallas_call(
        pair_kernel,
        out_shape=jax.ShapeDtypeStruct((2 * mine.shape[0], mine.shape[1]), mine.dtype),
        in_specs=vmem(2),
        out_specs=vmem(1)[0],
        compiler_params=pltpu.CompilerParams(vmem_limit_bytes=8 * MIB),
        name="window_pair",
    )(mine, came)


def elution_kernel(planes, *refs):
    amp_ref, lag_ref, terms, window = refs[-4:]
    components = amp_ref.shape[1]
    bin_count = terms.shape[1] // amp_ref.shape[0]
    freq_rank = lax.axis_index("freq")
    if planes:
        pair_ref, other_ref = refs[:2]
        mz_rank = lax.axis_index("mz")
        coded = pair_ref.shape[0] // 2
        rows = 2 * (coded - 16)
        skip = bin_count - REACH
        for ref, half in ((pair_ref, mz_rank), (other_ref, 1 - mz_rank)):
            for block in range(2):
                to = pl.multiple_of((2 * block + half) * rows, 64)
                window[pl.ds(to, rows), :] = decoded(ref[block * coded : (block + 1) * coded, :])
    else:
        own_ref = refs[0]
        step = own_ref.shape[1]
        steps = own_ref.shape[0]
        first = lax.rem(freq_rank * bin_count + steps * step - REACH, steps * step) // step
        skip = 0
        for j in range(window.shape[0] // step):
            window[j * step : (j + 1) * step, :] = own_ref[pl.ds(lax.rem(first + j, steps), 1)][0]
    pieces = []
    for at in range(skip, window.shape[0], LANES):
        piece = window[at : at + LANES, :].astype(jnp.float32).T
        pieces.append(piece[:components] + piece[components:])
    shifted_terms(jnp.concatenate(pieces, axis=1), amp_ref[...].T, lag_ref[...].T, bin_count, terms)


def elution_terms(elutions, loadings, shifts, bin_count):
    run_count, components = loadings.shape
    places = -(-(bin_count + REACH) // LANES)
    planes = len(elutions) > 1
    return pl.pallas_call(
        functools.partial(elution_kernel, planes),
        out_shape=jax.ShapeDtypeStruct((2 * components, run_count * bin_count), jnp.bfloat16),
        in_specs=vmem(len(elutions) + 2),
        out_specs=vmem(1)[0],
        scratch_shapes=[pltpu.VMEM((2 * bin_count if planes else places * LANES, LANES), jnp.bfloat16)],
        compiler_params=pltpu.CompilerParams(vmem_limit_bytes=12 * MIB),
        cost_estimate=pl.CostEstimate(flops=1_000_000_000, bytes_accessed=2 * MIB, transcendentals=0),
        name="elution_terms",
    )(*elutions, loadings, shifts)


def product_kernel(parts, planes, *refs):
    i_ref = refs[0]
    g_refs = refs[1 : 1 + parts]
    elution_ref, amp_ref, lag_ref, num_ref, other_ref, terms = refs[1 + parts :]
    run_count, bin_count, local_mz = i_ref.shape
    components = amp_ref.shape[1]
    chunk = 2 * LANES
    chunks = local_mz // chunk
    g = g_refs[0][...]
    for ref in g_refs[1:]:
        g = g + ref[...]
    shifted_terms(g, amp_ref[...].T, lag_ref[...].T, bin_count, terms)
    gram = lax.dot_general(
        terms[...], elution_ref[...], (((1,), (1,)), ((), ())), preferred_element_type=jnp.float32
    )
    gram = gram[:components] + gram[components:]
    gram = gram[:, :components] + gram[:, components:]
    if planes:
        keep_ref, send_ref = num_ref, other_ref
        half = components // 2
        gram = jnp.concatenate([gram[:half], gram[half:]], axis=1)
        keep_ref[chunks * components :, :] = gram
        send_ref[chunks * components :, :] = gram
    else:
        other_ref[...] = gram

    for n in range(chunks):
        data = i_ref[:, :, n * chunk : (n + 1) * chunk].reshape(run_count * bin_count, chunk)
        made = jnp.dot(terms[...], data, preferred_element_type=jnp.float32)
        made = made[:components] + made[components:]
        if planes:
            freq_rank = lax.axis_index("freq")
            core = freq_rank & 1
            place = block_place(lax.bitwise_xor(freq_rank, 2 * n + core), 2 * chunks)
            at = pl.ds(pl.multiple_of(place * components, components), components)
            even, odd = made[:, :LANES], made[:, LANES:]
            keep_ref[at, :] = jnp.where(core == 0, even, odd)
            send_ref[at, :] = jnp.where(core == 0, odd, even)
        else:
            num_ref[:, n * chunk : (n + 1) * chunk] = made


def product(intensity, models, elution, loadings, shifts, planes):
    run_count, bin_count, local_mz = intensity.shape
    components = loadings.shape[1]
    chunk = 2 * LANES
    chunks = local_mz // chunk
    if planes:
        out_shapes = [(chunks * components + components // 2, LANES)] * 2
    else:
        out_shapes = [(components, local_mz), (components, components)]
    return pl.pallas_call(
        functools.partial(product_kernel, len(models), planes),
        out_shape=tuple(jax.ShapeDtypeStruct(shape, jnp.float32) for shape in out_shapes),
        in_specs=vmem(len(models) + 4),
        out_specs=tuple(vmem(2)),
        scratch_shapes=[pltpu.VMEM((2 * components, run_count * bin_count), jnp.bfloat16)],
        compiler_params=pltpu.CompilerParams(vmem_limit_bytes=24 * MIB),
        cost_estimate=pl.CostEstimate(
            flops=8_000_000_000, bytes_accessed=2 * intensity.size, transcendentals=0
        ),
        name="model_products",
    )(intensity, *models, elution, loadings, shifts)


def inverse2(a, b, d):
    scale = 1.0 / (a * d - b * b)
    return d * scale, -b * scale, a * scale


def eliminate(gram, right):
    components = gram.shape[0]
    row_id = lax.broadcasted_iota(jnp.int32, gram.shape, 0)
    for j in range(0, components, 4):
        columns = [jnp.broadcast_to(gram[:, j + n : j + n + 1], gram.shape) for n in range(4)]
        pivot = [[columns[n][j + m : j + m + 1] for n in range(4)] for m in range(4)]
        a00, a01, a11 = inverse2(pivot[0][0], pivot[0][1], pivot[1][1])
        b00, b01, b10, b11 = pivot[0][2], pivot[0][3], pivot[1][2], pivot[1][3]
        w00, w01 = a00 * b00 + a01 * b10, a00 * b01 + a01 * b11
        w10, w11 = a01 * b00 + a11 * b10, a01 * b01 + a11 * b11
        s00, s01, s11 = inverse2(
            pivot[2][2] - (b00 * w00 + b10 * w10),
            pivot[2][3] - (b00 * w01 + b10 * w11),
            pivot[3][3] - (b01 * w01 + b11 * w11),
        )
        away = (row_id < j) | (row_id >= j + 4)
        c0, c1, c2, c3 = (
            jnp.where(away, column, jnp.where(row_id == j + n, -1.0, 0.0)) for n, column in enumerate(columns)
        )
        t2, t3 = c2 - c0 * w00 - c1 * w10, c3 - c0 * w01 - c1 * w11
        f2, f3 = t2 * s00 + t3 * s01, t2 * s01 + t3 * s11
        f0 = c0 * a00 + c1 * a01 - f2 * w00 - f3 * w01
        f1 = c0 * a01 + c1 * a11 - f2 * w10 - f3 * w11
        factors = (f0, f1, f2, f3)

        def reduced(x):
            out = jnp.where(away[:, : x.shape[1]], x, 0.0)
            for n, factor in enumerate(factors):
                out = out - factor[:, : x.shape[1]] * x[j + n : j + n + 1]
            return out

        gram, right = reduced(gram), reduced(right)
    return right


def total_of(refs, at, rows):
    total = refs[0][at : at + rows]
    for ref in refs[1:]:
        total = total + ref[at : at + rows]
    return total


def halve_kernel(tail, a_ref, b_ref, o_ref):
    rows = o_ref.shape[0] - tail
    o_ref[...] = total_of((a_ref, b_ref), rows, rows + tail)


def spread_kernel(tail, a_ref, b_ref, c_ref, *outs):
    rows = outs[0].shape[0] - tail
    count = len(outs)
    gram = total_of((a_ref, b_ref), 2 * count * rows, tail) + c_ref[count * rows :, :]
    for n, o_ref in enumerate(outs):
        o_ref[0:rows, :] = total_of((a_ref, b_ref, c_ref), n * rows, rows)
        o_ref[rows:, :] = gram


def solve_planes_kernel(*refs):
    o_ref = refs[-1]
    components = o_ref.shape[0]
    total = total_of(refs[:-1], 0, refs[0].shape[0])
    gram = total[components:]
    gram = jnp.concatenate([gram, pltpu.roll(gram, gram.shape[1] // 2, 1)], axis=0)
    o_ref[...] = eliminate(gram, total[:components])


def solve_kernel(g_ref, n_ref, o_ref):
    components = o_ref.shape[0]
    gram = jnp.concatenate([g_ref[...], jnp.zeros((components, LANES - components), jnp.float32)], axis=1)
    o_ref[...] = eliminate(gram, n_ref[...])


def small_call(kernel, shape, name, *args, count=1):
    return pl.pallas_call(
        kernel,
        out_shape=(jax.ShapeDtypeStruct(shape, jnp.float32),) * count,
        in_specs=vmem(len(args)),
        out_specs=tuple(vmem(count)),
        compiler_params=pltpu.CompilerParams(vmem_limit_bytes=8 * MIB),
        name=name,
    )(*args)


def swap(x, axes, count, value):
    return lax.ppermute(x, axes, [(i, i ^ value) for i in range(count)])


def on_device(intensity, elution, loadings, shifts, bin_weight):
    freq_count = lax.axis_size("freq")
    mz_count = lax.axis_size("mz")
    components = loadings.shape[1]
    bin_count = intensity.shape[1]
    axes = ("freq", "mz")
    own = intensity.shape[2] // freq_count
    planes = (
        own == LANES
        and 2 * components == LANES
        and mz_count == 2
        and freq_count & (freq_count - 1) == 0
        and freq_count >= 8
        and elution.shape[0] % 64 == 0
        and bin_count % LANES == 0
        and bin_count >= REACH
    )
    if not planes:
        mine = pack(elution)
        gathered = lax.all_gather(mine, axes, axis=0).reshape(-1, math.gcd(bin_count, LANES), LANES)
        g = partial_model((gathered,), circulant(bin_weight.reshape(LANES, -1), 0), bin_count, components)
        shifted = elution_terms((gathered,), loadings, shifts, bin_count)
        numerator, gram = product(intensity, (g,), shifted, loadings, shifts, planes)
        gram = lax.psum(gram, "freq")
        owned = lax.psum_scatter(numerator, "freq", scatter_dimension=1, tiled=True)
        return small_call(solve_kernel, (components, own), "solve", gram, owned)[0]
    mine = encode(elution)
    z_steps = range(4, freq_count, 4)
    held = jnp.stack([mine] + [swap(mine, "freq", freq_count, step) for step in z_steps])
    weights = bin_weight.reshape(LANES, -1)
    held, weights = lax.optimization_barrier((held, weights))
    held = jnp.concatenate([held, swap(held, "freq", freq_count, 2)], axis=0)
    u = circulant(weights, elution.shape[0])
    held, u = lax.optimization_barrier((held, u))
    came = swap(held, "freq", freq_count, 1)
    pair = window_pair(mine, came)
    other = swap(pair, "mz", mz_count, 1)
    g = partial_model((held, came), u, bin_count, components)
    g, other = lax.optimization_barrier((g, other))
    models = (g, swap(g, "mz", mz_count, 1))
    shifted = elution_terms((pair, other), loadings, shifts, bin_count)
    keep, send = product(intensity, models, shifted, loadings, shifts, planes)
    tail = components // 2
    chips = freq_count // 4
    came = swap(send, "freq", freq_count, 1)
    (send,) = small_call(
        functools.partial(halve_kernel, tail), (chips * components + tail, LANES), "reduce_cores", keep, came
    )
    across = swap(send, "freq", freq_count, 2)
    own_part, *sends = small_call(
        functools.partial(spread_kernel, tail), (components + tail, LANES), "reduce_x", keep, came, across, count=chips
    )
    parts = [swap(send, "freq", freq_count, step) for send, step in zip(sends, z_steps)][::-1]
    return small_call(solve_planes_kernel, (components, own), "solve", own_part, *parts)[0]


def solution(mesh):
    in_specs = (P(None, "freq", "mz"), P(("freq", "mz"), None), P(), P(), P())
    out_specs = P(None, ("mz", "freq"))
    return jax.shard_map(on_device, mesh=mesh, in_specs=in_specs, out_specs=out_specs, check_vma=False)
```

```python
import functools
import math

import jax
import jax.numpy as jnp
import numpy as np
from jax import lax
from jax.experimental import pallas as pl
from jax.experimental.pallas import tpu as pltpu
from jax.sharding import PartitionSpec as P

PRECISE = lax.Precision.HIGHEST
LANES = 128
REACH = 256
MIB = 1024 * 1024
FULL = 32767.0


def f32_dot(a, b, dims=(((1,), (0,)), ((), ()))):
    return lax.dot_general(a, b, dims, precision=PRECISE, preferred_element_type=jnp.float32)


def two_terms(x):
    high = x.astype(jnp.bfloat16)
    low = (x - high.astype(jnp.float32)).astype(jnp.bfloat16)
    return high, low


def vmem(count):
    return [pl.BlockSpec(memory_space=pltpu.VMEM)] * count


def pack_kernel(x_ref, o_ref):
    x = x_ref[...]
    components, rows = x.shape
    pad = -rows % LANES
    if pad:
        x = jnp.concatenate([x, jnp.zeros((components, pad), x.dtype)], axis=1)
    high, low = two_terms(x.T[:rows])
    o_ref[...] = jnp.concatenate([high, low], axis=1)


def pack(elution):
    rows, components = elution.shape
    return pl.pallas_call(
        pack_kernel,
        out_shape=jax.ShapeDtypeStruct((rows, 2 * components), jnp.bfloat16),
        in_specs=vmem(1),
        out_specs=vmem(1)[0],
        compiler_params=pltpu.CompilerParams(vmem_limit_bytes=8 * MIB),
        name="pack_elution",
    )(elution.T)


def encode_kernel(x_ref, o_ref):
    components, rows = x_ref.shape
    half = rows // 2
    x = x_ref[...]
    pad = -rows % LANES
    x = jnp.concatenate([x, jnp.zeros((components, pad), x.dtype)], axis=1).T[:rows]
    peak = jnp.maximum(jnp.max(jnp.abs(x), axis=0, keepdims=True), 1e-30)
    level = jnp.floor(256.0 / math.log(2.0) * jnp.log(peak)) + 1.0
    x = x * (FULL / scale_of(level))
    x = jnp.clip(jnp.floor(x + 0.5), -FULL, FULL).astype(jnp.int32).astype(jnp.int16)
    o_ref[0:half, :] = jnp.concatenate([x[:half], x[half:]], axis=1)
    level = jnp.broadcast_to(level, (16, components)).astype(jnp.int32).astype(jnp.int16)
    o_ref[half:, :] = jnp.concatenate([level, level], axis=1)


def scale_of(level):
    return jnp.exp(math.log(2.0) / 256.0 * level)


def decoded(x):
    half = x.shape[0] - 16
    x = x.astype(jnp.int32).astype(jnp.float32)
    x = x[:half] * (scale_of(x[half : half + 1]) * (1.0 / FULL))
    high = x.astype(jnp.bfloat16).astype(jnp.float32)
    low = x - high
    left = lax.broadcasted_iota(jnp.int32, x.shape, 1) < LANES // 2
    top = jnp.where(left, high, pltpu.roll(low, LANES // 2, 1))
    bottom = jnp.where(left, pltpu.roll(high, LANES // 2, 1), low)
    return jnp.concatenate([top, bottom], axis=0).astype(jnp.bfloat16)


def encode(elution):
    rows, components = elution.shape
    return pl.pallas_call(
        encode_kernel,
        out_shape=jax.ShapeDtypeStruct((rows // 2 + 16, 2 * components), jnp.int16),
        in_specs=vmem(1),
        out_specs=vmem(1)[0],
        compiler_params=pltpu.CompilerParams(vmem_limit_bytes=8 * MIB),
        name="encode_elution",
    )(elution.T)


def circulant_kernel(turn, w_ref, table_ref, u_ref):
    rows = w_ref.shape[1]
    w = w_ref[...]
    over_lanes = (((0,), (0,)), ((), ()))

    def table(at, height, width):
        return table_ref[at : at + height, :width], table_ref[at + height : at + 2 * height, :width]

    lane_cos, lane_sin = table(0, LANES, LANES)
    twid_cos, twid_sin = table(2 * LANES, rows, LANES)
    row_cos, row_sin = table(2 * LANES + 2 * rows, rows, rows)
    a_re = f32_dot(w, lane_cos, over_lanes)
    a_im = -f32_dot(w, lane_sin, over_lanes)
    b_re = a_re * twid_cos + a_im * twid_sin
    b_im = a_im * twid_cos - a_re * twid_sin
    c = f32_dot(row_cos, b_re) + f32_dot(row_sin, b_im)
    sub = lax.broadcasted_iota(jnp.int32, (LANES, LANES), 0)
    lane = lax.broadcasted_iota(jnp.int32, (LANES, LANES), 1)

    if turn:
        part = LANES - turn % LANES
        near, after = (
            pltpu.roll(jnp.concatenate([c[n:], c[:n]], axis=0), part % LANES, 1)
            for n in (turn // LANES, turn // LANES + 1)
        )
        moved = jnp.where(lax.broadcasted_iota(jnp.int32, c.shape, 1) < part, near, after)
        c = jnp.where(lax.axis_index("mz") == 1, moved, c)

    def turned(row):
        return pltpu.roll(jnp.broadcast_to(c[row : row + 1], (LANES, LANES)), 0, 1, stride=1, stride_axis=0)

    before = turned(rows - 1)
    for row in range(rows):
        now = turned(row)
        high, low = two_terms(jnp.where(lane >= sub, now, before))
        u_ref[0:LANES, row * LANES : (row + 1) * LANES] = high
        u_ref[LANES:, row * LANES : (row + 1) * LANES] = low
        before = now


def circulant(weights, turn):
    length = weights.size
    rows = length // LANES

    def tables(a, b, period):
        angle = 2.0 * math.pi / period * ((a[:, None] * b[None, :]) % period)
        return np.pad(np.concatenate([np.cos(angle), np.sin(angle)]), ((0, 0), (0, LANES - b.size)))

    lane_ids, row_ids = np.arange(LANES), np.arange(rows)
    table = np.concatenate(
        [
            tables(lane_ids, lane_ids, LANES),
            tables(row_ids, lane_ids, length),
            tables(row_ids, row_ids, rows) / length,
        ]
    ).astype(np.float32)
    return pl.pallas_call(
        functools.partial(circulant_kernel, turn),
        out_shape=jax.ShapeDtypeStruct((2 * LANES, length), jnp.bfloat16),
        in_specs=vmem(2),
        out_specs=vmem(1)[0],
        compiler_params=pltpu.CompilerParams(vmem_limit_bytes=16 * MIB),
        cost_estimate=pl.CostEstimate(flops=2_000_000_000, bytes_accessed=4 * MIB, transcendentals=0),
        name="circulant_block",
    )(weights, table)


def model_kernel(places, planes, *refs):
    u_ref, g_ref, wide = refs[-3:]
    length = u_ref.shape[1]
    components = g_ref.shape[0]
    freq_rank = lax.axis_index("freq")
    if planes:
        own_ref, came_ref = refs[:2]
        freq_count = 2 * own_ref.shape[0]
        rows = 2 * (own_ref.shape[1] - 16)
        padded = wide.shape[0] // freq_count
        for block in range(freq_count):
            apart = lax.bitwise_xor((freq_rank + block) & (freq_count - 1), freq_rank)
            ref = came_ref if block % 2 else own_ref
            values = decoded(ref[pl.ds(block_place(apart, freq_count), 1)][0])
            at, before = block * padded, (block - 1) % freq_count * padded
            wide[at : at + rows, 0:LANES] = values
            wide[before : before + rows, LANES:] = values
            wide[at + rows : at + padded, :] = jnp.zeros((padded - rows, 2 * LANES), jnp.bfloat16)
        period = length // freq_count // LANES
        for a in range(min(period, places)):
            columns = []
            for block in range(freq_count):
                first = REACH // LANES + period * block - a
                for n in range(first, first + padded // LANES):
                    at = n % (length // LANES) * LANES
                    columns.append(u_ref[:, at : at + LANES])
            width = 2 * LANES if a + period < places else LANES
            made = jnp.dot(
                jnp.concatenate(columns, axis=1), wide[:, :width], preferred_element_type=jnp.float32
            )
            made = made[:LANES] + made[LANES:]
            for half in range(width // LANES):
                piece = made[:, half * LANES : (half + 1) * LANES].T
                to = (a + half * period) * LANES
                g_ref[:, to : to + LANES] = piece[:components] + piece[components:]
        return
    own_ref = refs[0]
    step = own_ref.shape[1]
    steps = length // step
    bin_count = length // lax.axis_size("freq")
    first = lax.rem(freq_rank * bin_count + length - REACH, length) // step

    def bring(j, carry):
        values = own_ref[pl.ds(lax.rem(first + j, steps), 1)][0]
        to = pl.multiple_of(REACH + j * step, step)
        wide[pl.ds(to, step), 0:LANES] = values
        wide[pl.ds(pl.multiple_of(to - LANES, step), step), LANES:] = values
        return carry

    lax.fori_loop(0, (wide.shape[0] - REACH) // step, bring, 0)
    for a in range(0, places, 2):
        at = REACH + a * LANES
        made = jnp.dot(u_ref[...], wide[at : at + length, :], preferred_element_type=jnp.float32)
        made = made[:LANES] + made[LANES:]
        for half in range(min(2, places - a)):
            piece = made[:, half * LANES : (half + 1) * LANES].T
            g_ref[:, (a + half) * LANES : (a + half + 1) * LANES] = piece[:components] + piece[components:]


def block_place(apart, freq_count):
    return (apart >> 2) + ((apart >> 1) & 1) * (freq_count // 4)


def partial_model(gathered, u, bin_count, components):
    length = u.shape[1]
    places = -(-(bin_count + REACH) // LANES)
    planes = len(gathered) == 2
    if planes:
        own = gathered[0]
        wide_rows = 2 * own.shape[0] * (-(-2 * (own.shape[1] - 16) // LANES) * LANES)
    else:
        wide_rows = REACH + length + 2 * LANES * ((places - 1) // 2)
    return pl.pallas_call(
        functools.partial(model_kernel, places, planes),
        out_shape=jax.ShapeDtypeStruct((components, places * LANES), jnp.float32),
        in_specs=vmem(len(gathered) + 1),
        out_specs=vmem(1)[0],
        scratch_shapes=[pltpu.VMEM((wide_rows, 2 * LANES), jnp.bfloat16)],
        compiler_params=pltpu.CompilerParams(vmem_limit_bytes=24 * MIB),
        cost_estimate=pl.CostEstimate(flops=2_000_000_000, bytes_accessed=4 * MIB, transcendentals=0),
        name="partial_model",
    )(*gathered, u)


def shifted_terms(x, amps, lags, bin_count, terms):
    components = x.shape[0]
    out_count = -(-bin_count // LANES)
    x = pltpu.roll(x, x.shape[1] - 1, 1)
    height = 16
    lane = lax.broadcasted_iota(jnp.int32, (height, LANES), 1)
    for at in range(0, components, height):
        vectors = [x[at : at + height, v * LANES : (v + 1) * LANES] for v in range(out_count + 2)]
        for k in range(amps.shape[1]):
            left = REACH - 1 - jnp.broadcast_to(lags[at : at + height, k : k + 1], lane.shape)
            amp = jnp.broadcast_to(amps[at : at + height, k : k + 1], lane.shape)
            source = lane + (left & (LANES - 1))
            index = source & (LANES - 1)
            far, same = left >= LANES, source < LANES
            turned = [jnp.take_along_axis(v, index, axis=1, mode="promise_in_bounds") for v in vectors]
            turned = [jnp.where(far, turned[v + 1], turned[v]) for v in range(out_count + 1)]
            for v in range(out_count):
                high, low = two_terms(amp * jnp.where(same, turned[v], turned[v + 1]))
                width = min(LANES, bin_count - v * LANES)
                to = slice(k * bin_count + v * LANES, k * bin_count + v * LANES + width)
                terms[at : at + height, to] = high[:, :width]
                terms[components + at : components + at + height, to] = low[:, :width]


def pair_kernel(mine_ref, came_ref, o_ref):
    rows = mine_ref.shape[0]
    freq_count = 2 * came_ref.shape[0]
    freq_rank = lax.axis_index("freq")
    apart = lax.bitwise_xor((freq_rank - 1) & (freq_count - 1), freq_rank)
    o_ref[0:rows, :] = came_ref[pl.ds(block_place(apart, freq_count), 1)][0]
    o_ref[rows:, :] = mine_ref[...]


def window_pair(mine, came):
    return pl.pallas_call(
        pair_kernel,
        out_shape=jax.ShapeDtypeStruct((2 * mine.shape[0], mine.shape[1]), mine.dtype),
        in_specs=vmem(2),
        out_specs=vmem(1)[0],
        compiler_params=pltpu.CompilerParams(vmem_limit_bytes=8 * MIB),
        name="window_pair",
    )(mine, came)


def elution_kernel(planes, *refs):
    amp_ref, lag_ref, terms, window = refs[-4:]
    components = amp_ref.shape[1]
    bin_count = terms.shape[1] // amp_ref.shape[0]
    freq_rank = lax.axis_index("freq")
    if planes:
        pair_ref, other_ref = refs[:2]
        mz_rank = lax.axis_index("mz")
        coded = pair_ref.shape[0] // 2
        rows = 2 * (coded - 16)
        skip = bin_count - REACH
        for ref, half in ((pair_ref, mz_rank), (other_ref, 1 - mz_rank)):
            for block in range(2):
                to = pl.multiple_of((2 * block + half) * rows, 64)
                window[pl.ds(to, rows), :] = decoded(ref[block * coded : (block + 1) * coded, :])
    else:
        own_ref = refs[0]
        step = own_ref.shape[1]
        steps = own_ref.shape[0]
        first = lax.rem(freq_rank * bin_count + steps * step - REACH, steps * step) // step
        skip = 0
        for j in range(window.shape[0] // step):
            window[j * step : (j + 1) * step, :] = own_ref[pl.ds(lax.rem(first + j, steps), 1)][0]
    pieces = []
    for at in range(skip, window.shape[0], LANES):
        piece = window[at : at + LANES, :].astype(jnp.float32).T
        pieces.append(piece[:components] + piece[components:])
    shifted_terms(jnp.concatenate(pieces, axis=1), amp_ref[...].T, lag_ref[...].T, bin_count, terms)


def elution_terms(elutions, loadings, shifts, bin_count):
    run_count, components = loadings.shape
    places = -(-(bin_count + REACH) // LANES)
    planes = len(elutions) > 1
    return pl.pallas_call(
        functools.partial(elution_kernel, planes),
        out_shape=jax.ShapeDtypeStruct((2 * components, run_count * bin_count), jnp.bfloat16),
        in_specs=vmem(len(elutions) + 2),
        out_specs=vmem(1)[0],
        scratch_shapes=[pltpu.VMEM((2 * bin_count if planes else places * LANES, LANES), jnp.bfloat16)],
        compiler_params=pltpu.CompilerParams(vmem_limit_bytes=12 * MIB),
        cost_estimate=pl.CostEstimate(flops=1_000_000_000, bytes_accessed=2 * MIB, transcendentals=0),
        name="elution_terms",
    )(*elutions, loadings, shifts)


def product_kernel(parts, planes, *refs):
    i_ref = refs[0]
    g_refs = refs[1 : 1 + parts]
    elution_ref, amp_ref, lag_ref, num_ref, other_ref, terms = refs[1 + parts :]
    run_count, bin_count, local_mz = i_ref.shape
    components = amp_ref.shape[1]
    chunk = 2 * LANES
    chunks = local_mz // chunk
    g = g_refs[0][...]
    for ref in g_refs[1:]:
        g = g + ref[...]
    shifted_terms(g, amp_ref[...].T, lag_ref[...].T, bin_count, terms)
    gram = lax.dot_general(
        terms[...], elution_ref[...], (((1,), (1,)), ((), ())), preferred_element_type=jnp.float32
    )
    gram = gram[:components] + gram[components:]
    gram = gram[:, :components] + gram[:, components:]
    if planes:
        keep_ref, send_ref = num_ref, other_ref
        half = components // 2
        gram = jnp.concatenate([gram[:half], gram[half:]], axis=1)
        keep_ref[chunks * components :, :] = gram
        send_ref[chunks * components :, :] = gram
    else:
        other_ref[...] = gram

    for n in range(chunks):
        data = i_ref[:, :, n * chunk : (n + 1) * chunk].reshape(run_count * bin_count, chunk)
        made = jnp.dot(terms[...], data, preferred_element_type=jnp.float32)
        made = made[:components] + made[components:]
        if planes:
            freq_rank = lax.axis_index("freq")
            core = freq_rank & 1
            place = block_place(lax.bitwise_xor(freq_rank, 2 * n + core), 2 * chunks)
            at = pl.ds(pl.multiple_of(place * components, components), components)
            even, odd = made[:, :LANES], made[:, LANES:]
            keep_ref[at, :] = jnp.where(core == 0, even, odd)
            send_ref[at, :] = jnp.where(core == 0, odd, even)
        else:
            num_ref[:, n * chunk : (n + 1) * chunk] = made


def product(intensity, models, elution, loadings, shifts, planes):
    run_count, bin_count, local_mz = intensity.shape
    components = loadings.shape[1]
    chunk = 2 * LANES
    chunks = local_mz // chunk
    if planes:
        out_shapes = [(chunks * components + components // 2, LANES)] * 2
    else:
        out_shapes = [(components, local_mz), (components, components)]
    return pl.pallas_call(
        functools.partial(product_kernel, len(models), planes),
        out_shape=tuple(jax.ShapeDtypeStruct(shape, jnp.float32) for shape in out_shapes),
        in_specs=vmem(len(models) + 4),
        out_specs=tuple(vmem(2)),
        scratch_shapes=[pltpu.VMEM((2 * components, run_count * bin_count), jnp.bfloat16)],
        compiler_params=pltpu.CompilerParams(vmem_limit_bytes=24 * MIB),
        cost_estimate=pl.CostEstimate(
            flops=8_000_000_000, bytes_accessed=2 * intensity.size, transcendentals=0
        ),
        name="model_products",
    )(intensity, *models, elution, loadings, shifts)


def inverse2(a, b, d):
    scale = 1.0 / (a * d - b * b)
    return d * scale, -b * scale, a * scale


def eliminate(gram, right):
    components = gram.shape[0]
    row_id = lax.broadcasted_iota(jnp.int32, gram.shape, 0)
    for j in range(0, components, 4):
        columns = [jnp.broadcast_to(gram[:, j + n : j + n + 1], gram.shape) for n in range(4)]
        pivot = [[columns[n][j + m : j + m + 1] for n in range(4)] for m in range(4)]
        a00, a01, a11 = inverse2(pivot[0][0], pivot[0][1], pivot[1][1])
        b00, b01, b10, b11 = pivot[0][2], pivot[0][3], pivot[1][2], pivot[1][3]
        w00, w01 = a00 * b00 + a01 * b10, a00 * b01 + a01 * b11
        w10, w11 = a01 * b00 + a11 * b10, a01 * b01 + a11 * b11
        s00, s01, s11 = inverse2(
            pivot[2][2] - (b00 * w00 + b10 * w10),
            pivot[2][3] - (b00 * w01 + b10 * w11),
            pivot[3][3] - (b01 * w01 + b11 * w11),
        )
        away = (row_id < j) | (row_id >= j + 4)
        c0, c1, c2, c3 = (
            jnp.where(away, column, jnp.where(row_id == j + n, -1.0, 0.0)) for n, column in enumerate(columns)
        )
        t2, t3 = c2 - c0 * w00 - c1 * w10, c3 - c0 * w01 - c1 * w11
        f2, f3 = t2 * s00 + t3 * s01, t2 * s01 + t3 * s11
        f0 = c0 * a00 + c1 * a01 - f2 * w00 - f3 * w01
        f1 = c0 * a01 + c1 * a11 - f2 * w10 - f3 * w11
        factors = (f0, f1, f2, f3)

        def reduced(x):
            out = jnp.where(away[:, : x.shape[1]], x, 0.0)
            for n, factor in enumerate(factors):
                out = out - factor[:, : x.shape[1]] * x[j + n : j + n + 1]
            return out

        gram, right = reduced(gram), reduced(right)
    return right


def total_of(refs, at, rows):
    total = refs[0][at : at + rows]
    for ref in refs[1:]:
        total = total + ref[at : at + rows]
    return total


def fixed_point(x, full):
    return jnp.clip(jnp.floor(x + 0.5), -full, full)


def as_int16(x):
    return x.astype(jnp.int32).astype(jnp.int16)


def row_level(x):
    peak = jnp.maximum(jnp.max(jnp.abs(x), axis=1, keepdims=True), 1e-30)
    return jnp.floor(256.0 / math.log(2.0) * jnp.log(peak)) + 1.0


def diagonal(x, rows):
    shape = (rows, LANES)
    on = lax.broadcasted_iota(jnp.int32, shape, 0) == lax.broadcasted_iota(jnp.int32, shape, 1)
    return jnp.where(on, jnp.broadcast_to(x, shape), 0.0)


def encode_rows(x, gram, o_ref):
    rows, tail = x.shape[0], gram.shape[0]
    parts = [x[at : at + LANES] for at in range(0, rows, LANES)]
    levels = [row_level(part) for part in parts] + [row_level(gram)]
    at = 0
    for part, level in zip(parts, levels):
        o_ref[at : at + part.shape[0], :] = as_int16(fixed_point(part * (FULL / scale_of(level)), FULL))
        at += part.shape[0]
    scaled = gram * (FULL / scale_of(levels[-1]))
    high = fixed_point(scaled, FULL)
    o_ref[at : at + tail, :] = as_int16(high)
    o_ref[at + tail : at + 2 * tail, :] = as_int16(fixed_point((scaled - high) * (2 * FULL), FULL))
    row_id = lax.broadcasted_iota(jnp.int32, (16, LANES), 0)
    block = jnp.zeros((16, LANES), jnp.float32)
    for n, level in enumerate(levels):
        lanes = jnp.sum(diagonal(level, level.shape[0]), axis=0, keepdims=True)
        block = jnp.where(row_id == n, lanes, block)
    o_ref[at + 2 * tail :, :] = as_int16(block)


def decode_rows(ref, tail):
    rows = ref.shape[0] - 2 * tail - 16
    x = ref[...].astype(jnp.int32).astype(jnp.float32)

    def scale(n, count):
        at = rows + 2 * tail + n
        return scale_of(jnp.sum(diagonal(x[at : at + 1], count), axis=1, keepdims=True)) * (1.0 / FULL)

    parts = []
    for n, at in enumerate(range(0, rows, LANES)):
        count = min(LANES, rows - at)
        parts.append(x[at : at + count] * scale(n, count))
    gram = x[rows : rows + tail] + x[rows + tail : rows + 2 * tail] * (0.5 / FULL)
    return jnp.concatenate(parts, axis=0), gram * scale(len(parts), tail)


def halve_kernel(tail, a_ref, b_ref, o_ref):
    rows = o_ref.shape[0] - 2 * tail - 16
    total = total_of((a_ref, b_ref), rows, rows + tail)
    encode_rows(total[:rows], total[rows:], o_ref)


def spread_kernel(tail, a_ref, b_ref, c_ref, own_ref, *outs):
    rows = own_ref.shape[0] - tail
    count = len(outs) + 1
    total, gram = decode_rows(c_ref, tail)
    total = total + total_of((a_ref, b_ref), 0, count * rows)
    gram = gram + total_of((a_ref, b_ref), 2 * count * rows, tail)
    own_ref[0:rows, :] = total[:rows]
    own_ref[rows:, :] = gram
    for n, o_ref in enumerate(outs):
        encode_rows(total[(n + 1) * rows : (n + 2) * rows], gram, o_ref)


def solve_planes_kernel(own_ref, *refs):
    o_ref = refs[-1]
    components = o_ref.shape[0]
    total, gram = own_ref[:components], own_ref[components:]
    for ref in refs[:-1]:
        part, gram_part = decode_rows(ref, gram.shape[0])
        total, gram = total + part, gram + gram_part
    gram = jnp.concatenate([gram, pltpu.roll(gram, gram.shape[1] // 2, 1)], axis=0)
    o_ref[...] = eliminate(gram, total)


def solve_kernel(g_ref, n_ref, o_ref):
    components = o_ref.shape[0]
    gram = jnp.concatenate([g_ref[...], jnp.zeros((components, LANES - components), jnp.float32)], axis=1)
    o_ref[...] = eliminate(gram, n_ref[...])


def small_call(kernel, outs, name, *args):
    return pl.pallas_call(
        kernel,
        out_shape=tuple(jax.ShapeDtypeStruct(shape, dtype) for shape, dtype in outs),
        in_specs=vmem(len(args)),
        out_specs=tuple(vmem(len(outs))),
        compiler_params=pltpu.CompilerParams(vmem_limit_bytes=8 * MIB),
        name=name,
    )(*args)


def swap(x, axes, count, value):
    return lax.ppermute(x, axes, [(i, i ^ value) for i in range(count)])


def on_device(intensity, elution, loadings, shifts, bin_weight):
    freq_count = lax.axis_size("freq")
    mz_count = lax.axis_size("mz")
    components = loadings.shape[1]
    bin_count = intensity.shape[1]
    axes = ("freq", "mz")
    own = intensity.shape[2] // freq_count
    planes = (
        own == LANES
        and 2 * components == LANES
        and mz_count == 2
        and freq_count & (freq_count - 1) == 0
        and freq_count >= 8
        and elution.shape[0] % 64 == 0
        and bin_count % LANES == 0
        and bin_count >= REACH
    )
    if not planes:
        mine = pack(elution)
        gathered = lax.all_gather(mine, axes, axis=0).reshape(-1, math.gcd(bin_count, LANES), LANES)
        g = partial_model((gathered,), circulant(bin_weight.reshape(LANES, -1), 0), bin_count, components)
        shifted = elution_terms((gathered,), loadings, shifts, bin_count)
        numerator, gram = product(intensity, (g,), shifted, loadings, shifts, planes)
        gram = lax.psum(gram, "freq")
        owned = lax.psum_scatter(numerator, "freq", scatter_dimension=1, tiled=True)
        return small_call(solve_kernel, [((components, own), jnp.float32)], "solve", gram, owned)[0]
    mine = encode(elution)
    z_steps = range(4, freq_count, 4)
    held = jnp.stack([mine] + [swap(mine, "freq", freq_count, step) for step in z_steps])
    weights = bin_weight.reshape(LANES, -1)
    held, weights = lax.optimization_barrier((held, weights))
    held = jnp.concatenate([held, swap(held, "freq", freq_count, 2)], axis=0)
    u = circulant(weights, elution.shape[0])
    held, u = lax.optimization_barrier((held, u))
    came = swap(held, "freq", freq_count, 1)
    pair = window_pair(mine, came)
    other = swap(pair, "mz", mz_count, 1)
    g = partial_model((held, came), u, bin_count, components)
    g, other = lax.optimization_barrier((g, other))
    models = (g, swap(g, "mz", mz_count, 1))
    shifted = elution_terms((pair, other), loadings, shifts, bin_count)
    keep, send = product(intensity, models, shifted, loadings, shifts, planes)
    tail = components // 2
    chips = freq_count // 4
    came = swap(send, "freq", freq_count, 1)
    coded = 2 * tail + 16
    (send,) = small_call(
        functools.partial(halve_kernel, tail),
        [((chips * components + coded, LANES), jnp.int16)],
        "reduce_cores",
        keep,
        came,
    )
    across = swap(send, "freq", freq_count, 2)
    own_part, *sends = small_call(
        functools.partial(spread_kernel, tail),
        [((components + tail, LANES), jnp.float32)] + [((components + coded, LANES), jnp.int16)] * (chips - 1),
        "reduce_x",
        keep,
        came,
        across,
    )
    parts = [swap(send, "freq", freq_count, step) for send, step in zip(sends, z_steps)][::-1]
    return small_call(
        solve_planes_kernel, [((components, own), jnp.float32)], "solve", own_part, *parts
    )[0]


def solution(mesh):
    in_specs = (P(None, "freq", "mz"), P(("freq", "mz"), None), P(), P(), P())
    out_specs = P(None, ("mz", "freq"))
    return jax.shard_map(on_device, mesh=mesh, in_specs=in_specs, out_specs=out_specs, check_vma=False)
```

```python
import functools
import math

import jax
import jax.numpy as jnp
import numpy as np
from jax import lax
from jax.experimental import pallas as pl
from jax.experimental.pallas import tpu as pltpu
from jax.sharding import PartitionSpec as P

PRECISE = lax.Precision.HIGHEST
LANES = 128
REACH = 256
MIB = 1024 * 1024
FULL = 32767.0


def f32_dot(a, b, dims=(((1,), (0,)), ((), ()))):
    return lax.dot_general(a, b, dims, precision=PRECISE, preferred_element_type=jnp.float32)


def two_terms(x):
    high = x.astype(jnp.bfloat16)
    low = (x - high.astype(jnp.float32)).astype(jnp.bfloat16)
    return high, low


def vmem(count):
    return [pl.BlockSpec(memory_space=pltpu.VMEM)] * count


def pack_kernel(x_ref, o_ref):
    x = x_ref[...]
    components, rows = x.shape
    pad = -rows % LANES
    if pad:
        x = jnp.concatenate([x, jnp.zeros((components, pad), x.dtype)], axis=1)
    high, low = two_terms(x.T[:rows])
    o_ref[...] = jnp.concatenate([high, low], axis=1)


def pack(elution):
    rows, components = elution.shape
    return pl.pallas_call(
        pack_kernel,
        out_shape=jax.ShapeDtypeStruct((rows, 2 * components), jnp.bfloat16),
        in_specs=vmem(1),
        out_specs=vmem(1)[0],
        compiler_params=pltpu.CompilerParams(vmem_limit_bytes=8 * MIB),
        name="pack_elution",
    )(elution.T)


def encode_kernel(x_ref, o_ref):
    components, rows = x_ref.shape
    half = rows // 2
    x = x_ref[...]
    pad = -rows % LANES
    x = jnp.concatenate([x, jnp.zeros((components, pad), x.dtype)], axis=1).T[:rows]
    peak = jnp.maximum(jnp.max(jnp.abs(x), axis=0, keepdims=True), 1e-30)
    level = jnp.floor(256.0 / math.log(2.0) * jnp.log(peak)) + 1.0
    x = x * (FULL / scale_of(level))
    x = jnp.clip(jnp.floor(x + 0.5), -FULL, FULL).astype(jnp.int32).astype(jnp.int16)
    o_ref[0:half, :] = jnp.concatenate([x[:half], x[half:]], axis=1)
    level = jnp.broadcast_to(level, (16, components)).astype(jnp.int32).astype(jnp.int16)
    o_ref[half:, :] = jnp.concatenate([level, level], axis=1)


def encode_columns(x, o_ref):
    rows = x.shape[0]
    peak = jnp.maximum(jnp.max(jnp.abs(x), axis=0, keepdims=True), 1e-30)
    level = jnp.floor(256.0 / math.log(2.0) * jnp.log(peak)) + 1.0
    x = jnp.clip(jnp.floor(x * (FULL / scale_of(level)) + 0.5), -FULL, FULL)
    o_ref[0:rows, :] = x.astype(jnp.int32).astype(jnp.int16)
    o_ref[rows:, :] = jnp.broadcast_to(level, (16, x.shape[1])).astype(jnp.int32).astype(jnp.int16)


def scale_of(level):
    return jnp.exp(math.log(2.0) / 256.0 * level)


def decoded(x):
    half = x.shape[0] - 16
    x = x.astype(jnp.int32).astype(jnp.float32)
    return x[:half] * (scale_of(x[half : half + 1]) * (1.0 / FULL))


def decoded_terms(x):
    x = decoded(x)
    high = x.astype(jnp.bfloat16).astype(jnp.float32)
    low = x - high
    left = lax.broadcasted_iota(jnp.int32, x.shape, 1) < LANES // 2
    top = jnp.where(left, high, pltpu.roll(low, LANES // 2, 1))
    bottom = jnp.where(left, pltpu.roll(high, LANES // 2, 1), low)
    return jnp.concatenate([top, bottom], axis=0).astype(jnp.bfloat16)


def encode(elution):
    rows, components = elution.shape
    return pl.pallas_call(
        encode_kernel,
        out_shape=jax.ShapeDtypeStruct((rows // 2 + 16, 2 * components), jnp.int16),
        in_specs=vmem(1),
        out_specs=vmem(1)[0],
        compiler_params=pltpu.CompilerParams(vmem_limit_bytes=8 * MIB),
        name="encode_elution",
    )(elution.T)


def circulant_kernel(turn, w_ref, table_ref, u_ref):
    rows = w_ref.shape[1]
    w = w_ref[...]
    over_lanes = (((0,), (0,)), ((), ()))

    def table(at, height, width):
        return table_ref[at : at + height, :width], table_ref[at + height : at + 2 * height, :width]

    lane_cos, lane_sin = table(0, LANES, LANES)
    twid_cos, twid_sin = table(2 * LANES, rows, LANES)
    row_cos, row_sin = table(2 * LANES + 2 * rows, rows, rows)
    a_re = f32_dot(w, lane_cos, over_lanes)
    a_im = -f32_dot(w, lane_sin, over_lanes)
    b_re = a_re * twid_cos + a_im * twid_sin
    b_im = a_im * twid_cos - a_re * twid_sin
    c = f32_dot(row_cos, b_re) + f32_dot(row_sin, b_im)
    sub = lax.broadcasted_iota(jnp.int32, (LANES, LANES), 0)
    lane = lax.broadcasted_iota(jnp.int32, (LANES, LANES), 1)

    if turn:
        part = LANES - turn % LANES
        near, after = (
            pltpu.roll(jnp.concatenate([c[n:], c[:n]], axis=0), part % LANES, 1)
            for n in (turn // LANES, turn // LANES + 1)
        )
        moved = jnp.where(lax.broadcasted_iota(jnp.int32, c.shape, 1) < part, near, after)
        c = jnp.where(lax.axis_index("mz") == 1, moved, c)

    def turned(row):
        return pltpu.roll(jnp.broadcast_to(c[row : row + 1], (LANES, LANES)), 0, 1, stride=1, stride_axis=0)

    before = turned(rows - 1)
    for row in range(rows):
        now = turned(row)
        high, low = two_terms(jnp.where(lane >= sub, now, before))
        u_ref[0:LANES, row * LANES : (row + 1) * LANES] = high
        u_ref[LANES:, row * LANES : (row + 1) * LANES] = low
        before = now


def circulant(weights, turn):
    length = weights.size
    rows = length // LANES

    def tables(a, b, period):
        angle = 2.0 * math.pi / period * ((a[:, None] * b[None, :]) % period)
        return np.pad(np.concatenate([np.cos(angle), np.sin(angle)]), ((0, 0), (0, LANES - b.size)))

    lane_ids, row_ids = np.arange(LANES), np.arange(rows)
    table = np.concatenate(
        [
            tables(lane_ids, lane_ids, LANES),
            tables(row_ids, lane_ids, length),
            tables(row_ids, row_ids, rows) / length,
        ]
    ).astype(np.float32)
    return pl.pallas_call(
        functools.partial(circulant_kernel, turn),
        out_shape=jax.ShapeDtypeStruct((2 * LANES, length), jnp.bfloat16),
        in_specs=vmem(2),
        out_specs=vmem(1)[0],
        compiler_params=pltpu.CompilerParams(vmem_limit_bytes=16 * MIB),
        cost_estimate=pl.CostEstimate(flops=2_000_000_000, bytes_accessed=4 * MIB, transcendentals=0),
        name="circulant_block",
    )(weights, table)


def model_kernel(places, planes, *refs):
    if planes:
        u_ref, g_ref, coded_ref, wide = refs[-4:]
    else:
        u_ref, g_ref, wide = refs[-3:]
    length = u_ref.shape[1]
    components = g_ref.shape[0]
    freq_rank = lax.axis_index("freq")
    if planes:
        own_ref, came_ref = refs[:2]
        freq_count = 2 * own_ref.shape[0]
        rows = 2 * (own_ref.shape[1] - 16)
        padded = wide.shape[0] // freq_count
        for block in range(freq_count):
            apart = lax.bitwise_xor((freq_rank + block) & (freq_count - 1), freq_rank)
            ref = came_ref if block % 2 else own_ref
            values = decoded_terms(ref[pl.ds(block_place(apart, freq_count), 1)][0])
            at, before = block * padded, (block - 1) % freq_count * padded
            wide[at : at + rows, 0:LANES] = values
            wide[before : before + rows, LANES:] = values
            wide[at + rows : at + padded, :] = jnp.zeros((padded - rows, 2 * LANES), jnp.bfloat16)
        period = length // freq_count // LANES
        left = lax.broadcasted_iota(jnp.int32, (LANES, LANES), 1) < components
        sides = []
        for a in range(period):
            columns = []
            for block in range(freq_count):
                first = REACH // LANES + period * block - a
                for n in range(first, first + padded // LANES):
                    at = n % (length // LANES) * LANES
                    columns.append(u_ref[:, at : at + LANES])
            width = 2 * LANES if a + period < places else LANES
            made = jnp.dot(
                jnp.concatenate(columns, axis=1), wide[:, :width], preferred_element_type=jnp.float32
            )
            made = made[:LANES] + made[LANES:]
            tiles = []
            for half in range(width // LANES):
                tile = made[:, half * LANES : (half + 1) * LANES]
                tiles.append(tile + pltpu.roll(tile, components, 1))
                to = (a + half * period) * LANES
                g_ref[:, to : to + LANES] = tiles[-1].T[:components]
            if len(tiles) == 1:
                half = LANES // 2
                sides.append(jnp.where(left[:half], tiles[0][:half], tiles[0][half:]))
            else:
                sides.append(jnp.where(left, tiles[0], tiles[1]))
        encode_columns(jnp.concatenate(sides, axis=0), coded_ref)
        return
    own_ref = refs[0]
    step = own_ref.shape[1]
    steps = length // step
    bin_count = length // lax.axis_size("freq")
    first = lax.rem(freq_rank * bin_count + length - REACH, length) // step

    def bring(j, carry):
        values = own_ref[pl.ds(lax.rem(first + j, steps), 1)][0]
        to = pl.multiple_of(REACH + j * step, step)
        wide[pl.ds(to, step), 0:LANES] = values
        wide[pl.ds(pl.multiple_of(to - LANES, step), step), LANES:] = values
        return carry

    lax.fori_loop(0, (wide.shape[0] - REACH) // step, bring, 0)
    for a in range(0, places, 2):
        at = REACH + a * LANES
        made = jnp.dot(u_ref[...], wide[at : at + length, :], preferred_element_type=jnp.float32)
        made = made[:LANES] + made[LANES:]
        for half in range(min(2, places - a)):
            piece = made[:, half * LANES : (half + 1) * LANES].T
            g_ref[:, (a + half) * LANES : (a + half + 1) * LANES] = piece[:components] + piece[components:]


def block_place(apart, freq_count):
    return (apart >> 2) + ((apart >> 1) & 1) * (freq_count // 4)


def partial_model(gathered, u, bin_count, components):
    length = u.shape[1]
    places = -(-(bin_count + REACH) // LANES)
    planes = len(gathered) == 2
    if planes:
        own = gathered[0]
        wide_rows = 2 * own.shape[0] * (-(-2 * (own.shape[1] - 16) // LANES) * LANES)
    else:
        wide_rows = REACH + length + 2 * LANES * ((places - 1) // 2)
    outs = [jax.ShapeDtypeStruct((components, places * LANES), jnp.float32)]
    if planes:
        outs.append(jax.ShapeDtypeStruct((places * LANES // 2 + 16, LANES), jnp.int16))
    return pl.pallas_call(
        functools.partial(model_kernel, places, planes),
        out_shape=tuple(outs),
        in_specs=vmem(len(gathered) + 1),
        out_specs=tuple(vmem(len(outs))),
        scratch_shapes=[pltpu.VMEM((wide_rows, 2 * LANES), jnp.bfloat16)],
        compiler_params=pltpu.CompilerParams(vmem_limit_bytes=24 * MIB),
        cost_estimate=pl.CostEstimate(flops=2_000_000_000, bytes_accessed=4 * MIB, transcendentals=0),
        name="partial_model",
    )(*gathered, u)


def shifted_terms(x, amps, lags, bin_count, terms):
    components = x.shape[0]
    out_count = -(-bin_count // LANES)
    x = pltpu.roll(x, x.shape[1] - 1, 1)
    height = 16
    lane = lax.broadcasted_iota(jnp.int32, (height, LANES), 1)
    for at in range(0, components, height):
        vectors = [x[at : at + height, v * LANES : (v + 1) * LANES] for v in range(out_count + 2)]
        for k in range(amps.shape[1]):
            left = REACH - 1 - jnp.broadcast_to(lags[at : at + height, k : k + 1], lane.shape)
            amp = jnp.broadcast_to(amps[at : at + height, k : k + 1], lane.shape)
            source = lane + (left & (LANES - 1))
            index = source & (LANES - 1)
            far, same = left >= LANES, source < LANES
            turned = [jnp.take_along_axis(v, index, axis=1, mode="promise_in_bounds") for v in vectors]
            turned = [jnp.where(far, turned[v + 1], turned[v]) for v in range(out_count + 1)]
            for v in range(out_count):
                high, low = two_terms(amp * jnp.where(same, turned[v], turned[v + 1]))
                width = min(LANES, bin_count - v * LANES)
                to = slice(k * bin_count + v * LANES, k * bin_count + v * LANES + width)
                terms[at : at + height, to] = high[:, :width]
                terms[components + at : components + at + height, to] = low[:, :width]


def pair_kernel(mine_ref, came_ref, o_ref):
    rows = mine_ref.shape[0]
    freq_count = 2 * came_ref.shape[0]
    freq_rank = lax.axis_index("freq")
    apart = lax.bitwise_xor((freq_rank - 1) & (freq_count - 1), freq_rank)
    o_ref[0:rows, :] = came_ref[pl.ds(block_place(apart, freq_count), 1)][0]
    o_ref[rows:, :] = mine_ref[...]


def window_pair(mine, came):
    return pl.pallas_call(
        pair_kernel,
        out_shape=jax.ShapeDtypeStruct((2 * mine.shape[0], mine.shape[1]), mine.dtype),
        in_specs=vmem(2),
        out_specs=vmem(1)[0],
        compiler_params=pltpu.CompilerParams(vmem_limit_bytes=8 * MIB),
        name="window_pair",
    )(mine, came)


def elution_kernel(planes, *refs):
    amp_ref, lag_ref, terms, window = refs[-4:]
    components = amp_ref.shape[1]
    bin_count = terms.shape[1] // amp_ref.shape[0]
    freq_rank = lax.axis_index("freq")
    if planes:
        pair_ref, other_ref = refs[:2]
        mz_rank = lax.axis_index("mz")
        coded = pair_ref.shape[0] // 2
        rows = 2 * (coded - 16)
        skip = bin_count - REACH
        for ref, half in ((pair_ref, mz_rank), (other_ref, 1 - mz_rank)):
            for block in range(2):
                to = pl.multiple_of((2 * block + half) * rows, 64)
                values = decoded(ref[block * coded : (block + 1) * coded, :])
                half_rows = rows // 2
                window[pl.ds(to, half_rows), :] = values
                window[pl.ds(pl.multiple_of(to + half_rows, 32), half_rows), :] = pltpu.roll(values, LANES // 2, 1)
    else:
        own_ref = refs[0]
        step = own_ref.shape[1]
        steps = own_ref.shape[0]
        first = lax.rem(freq_rank * bin_count + steps * step - REACH, steps * step) // step
        skip = 0
        for j in range(window.shape[0] // step):
            window[j * step : (j + 1) * step, :] = own_ref[pl.ds(lax.rem(first + j, steps), 1)][0]
    pieces = []
    for at in range(skip, window.shape[0], LANES):
        piece = window[at : at + LANES, :].astype(jnp.float32).T
        pieces.append(piece[:components] if planes else piece[:components] + piece[components:])
    shifted_terms(jnp.concatenate(pieces, axis=1), amp_ref[...].T, lag_ref[...].T, bin_count, terms)


def elution_terms(elutions, loadings, shifts, bin_count):
    run_count, components = loadings.shape
    places = -(-(bin_count + REACH) // LANES)
    planes = len(elutions) > 1
    return pl.pallas_call(
        functools.partial(elution_kernel, planes),
        out_shape=jax.ShapeDtypeStruct((2 * components, run_count * bin_count), jnp.bfloat16),
        in_specs=vmem(len(elutions) + 2),
        out_specs=vmem(1)[0],
        scratch_shapes=[
            pltpu.VMEM((2 * bin_count, LANES), jnp.float32)
            if planes
            else pltpu.VMEM((places * LANES, LANES), jnp.bfloat16)
        ],
        compiler_params=pltpu.CompilerParams(vmem_limit_bytes=12 * MIB),
        cost_estimate=pl.CostEstimate(flops=1_000_000_000, bytes_accessed=2 * MIB, transcendentals=0),
        name="elution_terms",
    )(*elutions, loadings, shifts)


def product_kernel(parts, planes, *refs):
    i_ref = refs[0]
    g_refs = refs[1 : 1 + parts]
    elution_ref, amp_ref, lag_ref, num_ref, other_ref, terms = refs[1 + parts :]
    run_count, bin_count, local_mz = i_ref.shape
    components = amp_ref.shape[1]
    chunk = 2 * LANES
    chunks = local_mz // chunk
    g = g_refs[0][...]
    if planes:
        period = bin_count // LANES
        x = decoded(g_refs[1][...])
        first, second, at = [], [], 0
        for a in range(period):
            if a + period < g.shape[1] // LANES:
                tile = x[at : at + LANES].T
                second.append(tile[components:])
                at += LANES
            else:
                half = x[at : at + LANES // 2]
                tile = jnp.concatenate([half, pltpu.roll(half, components, 1)], axis=0).T
                at += LANES // 2
            first.append(tile[:components])
        g = g + jnp.concatenate(first + second, axis=1)
    shifted_terms(g, amp_ref[...].T, lag_ref[...].T, bin_count, terms)
    gram = lax.dot_general(
        terms[...], elution_ref[...], (((1,), (1,)), ((), ())), preferred_element_type=jnp.float32
    )
    gram = gram[:components] + gram[components:]
    gram = gram[:, :components] + gram[:, components:]
    if planes:
        keep_ref, send_ref = num_ref, other_ref
        half = components // 2
        gram = jnp.concatenate([gram[:half], gram[half:]], axis=1)
        keep_ref[chunks * components :, :] = gram
        send_ref[chunks * components :, :] = gram
    else:
        other_ref[...] = gram

    for n in range(chunks):
        data = i_ref[:, :, n * chunk : (n + 1) * chunk].reshape(run_count * bin_count, chunk)
        made = jnp.dot(terms[...], data, preferred_element_type=jnp.float32)
        made = made[:components] + made[components:]
        if planes:
            freq_rank = lax.axis_index("freq")
            core = freq_rank & 1
            place = block_place(lax.bitwise_xor(freq_rank, 2 * n + core), 2 * chunks)
            at = pl.ds(pl.multiple_of(place * components, components), components)
            even, odd = made[:, :LANES], made[:, LANES:]
            keep_ref[at, :] = jnp.where(core == 0, even, odd)
            send_ref[at, :] = jnp.where(core == 0, odd, even)
        else:
            num_ref[:, n * chunk : (n + 1) * chunk] = made


def product(intensity, models, elution, loadings, shifts, planes):
    run_count, bin_count, local_mz = intensity.shape
    components = loadings.shape[1]
    chunk = 2 * LANES
    chunks = local_mz // chunk
    if planes:
        out_shapes = [(chunks * components + components // 2, LANES)] * 2
    else:
        out_shapes = [(components, local_mz), (components, components)]
    return pl.pallas_call(
        functools.partial(product_kernel, len(models), planes),
        out_shape=tuple(jax.ShapeDtypeStruct(shape, jnp.float32) for shape in out_shapes),
        in_specs=vmem(len(models) + 4),
        out_specs=tuple(vmem(2)),
        scratch_shapes=[pltpu.VMEM((2 * components, run_count * bin_count), jnp.bfloat16)],
        compiler_params=pltpu.CompilerParams(vmem_limit_bytes=24 * MIB),
        cost_estimate=pl.CostEstimate(
            flops=8_000_000_000, bytes_accessed=2 * intensity.size, transcendentals=0
        ),
        name="model_products",
    )(intensity, *models, elution, loadings, shifts)


def inverse2(a, b, d):
    det = a * d - b * b
    scale = pl.reciprocal(det, approx=True)
    for _ in range(2):
        scale = scale * (2.0 - det * scale)
    return d * scale, -b * scale, a * scale


def eliminate(gram, right):
    components = gram.shape[0]
    row_id = lax.broadcasted_iota(jnp.int32, gram.shape, 0)
    for j in range(0, components, 4):
        columns = [jnp.broadcast_to(gram[:, j + n : j + n + 1], gram.shape) for n in range(4)]
        pivot = [[columns[n][j + m : j + m + 1] for n in range(4)] for m in range(4)]
        a00, a01, a11 = inverse2(pivot[0][0], pivot[0][1], pivot[1][1])
        b00, b01, b10, b11 = pivot[0][2], pivot[0][3], pivot[1][2], pivot[1][3]
        w00, w01 = a00 * b00 + a01 * b10, a00 * b01 + a01 * b11
        w10, w11 = a01 * b00 + a11 * b10, a01 * b01 + a11 * b11
        s00, s01, s11 = inverse2(
            pivot[2][2] - (b00 * w00 + b10 * w10),
            pivot[2][3] - (b00 * w01 + b10 * w11),
            pivot[3][3] - (b01 * w01 + b11 * w11),
        )
        away = (row_id < j) | (row_id >= j + 4)
        c0, c1, c2, c3 = (
            jnp.where(away, column, jnp.where(row_id == j + n, -1.0, 0.0)) for n, column in enumerate(columns)
        )
        t2, t3 = c2 - c0 * w00 - c1 * w10, c3 - c0 * w01 - c1 * w11
        f2, f3 = t2 * s00 + t3 * s01, t2 * s01 + t3 * s11
        f0 = c0 * a00 + c1 * a01 - f2 * w00 - f3 * w01
        f1 = c0 * a01 + c1 * a11 - f2 * w10 - f3 * w11
        factors = (f0, f1, f2, f3)

        def reduced(x):
            out = jnp.where(away[:, : x.shape[1]], x, 0.0)
            for n, factor in enumerate(factors):
                out = out - factor[:, : x.shape[1]] * x[j + n : j + n + 1]
            return out

        gram, right = reduced(gram), reduced(right)
    return right


def total_of(refs, at, rows):
    total = refs[0][at : at + rows]
    for ref in refs[1:]:
        total = total + ref[at : at + rows]
    return total


def fixed_point(x, full):
    return jnp.clip(jnp.floor(x + 0.5), -full, full)


def as_int16(x):
    return x.astype(jnp.int32).astype(jnp.int16)


def row_level(x):
    peak = jnp.maximum(jnp.max(jnp.abs(x), axis=1, keepdims=True), 1e-30)
    return jnp.floor(256.0 / math.log(2.0) * jnp.log(peak)) + 1.0


def diagonal(x, rows):
    shape = (rows, LANES)
    on = lax.broadcasted_iota(jnp.int32, shape, 0) == lax.broadcasted_iota(jnp.int32, shape, 1)
    return jnp.where(on, jnp.broadcast_to(x, shape), 0.0)


def encode_rows(x, gram, o_ref):
    rows, tail = x.shape[0], gram.shape[0]
    parts = [x[at : at + LANES] for at in range(0, rows, LANES)]
    levels = [row_level(part) for part in parts] + [row_level(gram)]
    at = 0
    for part, level in zip(parts, levels):
        o_ref[at : at + part.shape[0], :] = as_int16(fixed_point(part * (FULL / scale_of(level)), FULL))
        at += part.shape[0]
    scaled = gram * (FULL / scale_of(levels[-1]))
    high = fixed_point(scaled, FULL)
    o_ref[at : at + tail, :] = as_int16(high)
    o_ref[at + tail : at + 2 * tail, :] = as_int16(fixed_point((scaled - high) * (2 * FULL), FULL))
    row_id = lax.broadcasted_iota(jnp.int32, (16, LANES), 0)
    block = jnp.zeros((16, LANES), jnp.float32)
    for n, level in enumerate(levels):
        lanes = jnp.sum(diagonal(level, level.shape[0]), axis=0, keepdims=True)
        block = jnp.where(row_id == n, lanes, block)
    o_ref[at + 2 * tail :, :] = as_int16(block)


def decode_rows(ref, tail):
    rows = ref.shape[0] - 2 * tail - 16
    x = ref[...].astype(jnp.int32).astype(jnp.float32)

    def scale(n, count):
        at = rows + 2 * tail + n
        return scale_of(jnp.sum(diagonal(x[at : at + 1], count), axis=1, keepdims=True)) * (1.0 / FULL)

    parts = []
    for n, at in enumerate(range(0, rows, LANES)):
        count = min(LANES, rows - at)
        parts.append(x[at : at + count] * scale(n, count))
    gram = x[rows : rows + tail] + x[rows + tail : rows + 2 * tail] * (0.5 / FULL)
    return jnp.concatenate(parts, axis=0), gram * scale(len(parts), tail)


def halve_kernel(tail, a_ref, b_ref, o_ref):
    rows = o_ref.shape[0] - 2 * tail - 16
    total = total_of((a_ref, b_ref), rows, rows + tail)
    encode_rows(total[:rows], total[rows:], o_ref)


def spread_kernel(tail, a_ref, b_ref, c_ref, own_ref, *outs):
    rows = own_ref.shape[0] - tail
    count = len(outs) + 1
    total, gram = decode_rows(c_ref, tail)
    total = total + total_of((a_ref, b_ref), 0, count * rows)
    gram = gram + total_of((a_ref, b_ref), 2 * count * rows, tail)
    own_ref[0:rows, :] = total[:rows]
    own_ref[rows:, :] = gram
    for n, o_ref in enumerate(outs):
        encode_rows(total[(n + 1) * rows : (n + 2) * rows], gram, o_ref)


def solve_planes_kernel(own_ref, *refs):
    o_ref = refs[-1]
    components = o_ref.shape[0]
    total, gram = own_ref[:components], own_ref[components:]
    for ref in refs[:-1]:
        part, gram_part = decode_rows(ref, gram.shape[0])
        total, gram = total + part, gram + gram_part
    gram = jnp.concatenate([gram, pltpu.roll(gram, gram.shape[1] // 2, 1)], axis=0)
    o_ref[...] = eliminate(gram, total)


def solve_kernel(g_ref, n_ref, o_ref):
    components = o_ref.shape[0]
    gram = jnp.concatenate([g_ref[...], jnp.zeros((components, LANES - components), jnp.float32)], axis=1)
    o_ref[...] = eliminate(gram, n_ref[...])


def small_call(kernel, outs, name, *args):
    return pl.pallas_call(
        kernel,
        out_shape=tuple(jax.ShapeDtypeStruct(shape, dtype) for shape, dtype in outs),
        in_specs=vmem(len(args)),
        out_specs=tuple(vmem(len(outs))),
        compiler_params=pltpu.CompilerParams(vmem_limit_bytes=8 * MIB),
        name=name,
    )(*args)


def swap(x, axes, count, value):
    return lax.ppermute(x, axes, [(i, i ^ value) for i in range(count)])


def on_device(intensity, elution, loadings, shifts, bin_weight):
    freq_count = lax.axis_size("freq")
    mz_count = lax.axis_size("mz")
    components = loadings.shape[1]
    bin_count = intensity.shape[1]
    axes = ("freq", "mz")
    own = intensity.shape[2] // freq_count
    planes = (
        own == LANES
        and 2 * components == LANES
        and mz_count == 2
        and freq_count & (freq_count - 1) == 0
        and freq_count >= 8
        and elution.shape[0] % 64 == 0
        and bin_count % LANES == 0
        and bin_count >= REACH
    )
    if not planes:
        mine = pack(elution)
        gathered = lax.all_gather(mine, axes, axis=0).reshape(-1, math.gcd(bin_count, LANES), LANES)
        (g,) = partial_model((gathered,), circulant(bin_weight.reshape(LANES, -1), 0), bin_count, components)
        shifted = elution_terms((gathered,), loadings, shifts, bin_count)
        numerator, gram = product(intensity, (g,), shifted, loadings, shifts, planes)
        gram = lax.psum(gram, "freq")
        owned = lax.psum_scatter(numerator, "freq", scatter_dimension=1, tiled=True)
        return small_call(solve_kernel, [((components, own), jnp.float32)], "solve", gram, owned)[0]
    mine = encode(elution)
    z_steps = range(4, freq_count, 4)
    held = jnp.stack([mine] + [swap(mine, "freq", freq_count, step) for step in z_steps])
    weights = bin_weight.reshape(LANES, -1)
    held, weights = lax.optimization_barrier((held, weights))
    held = jnp.concatenate([held, swap(held, "freq", freq_count, 2)], axis=0)
    u = circulant(weights, elution.shape[0])
    held, u = lax.optimization_barrier((held, u))
    came = swap(held, "freq", freq_count, 1)
    pair = window_pair(mine, came)
    other = swap(pair, "mz", mz_count, 1)
    g, coded = partial_model((held, came), u, bin_count, components)
    coded, other = lax.optimization_barrier((coded, other))
    models = (g, swap(coded, "mz", mz_count, 1))
    shifted = elution_terms((pair, other), loadings, shifts, bin_count)
    keep, send = product(intensity, models, shifted, loadings, shifts, planes)
    tail = components // 2
    chips = freq_count // 4
    came = swap(send, "freq", freq_count, 1)
    coded = 2 * tail + 16
    (send,) = small_call(
        functools.partial(halve_kernel, tail),
        [((chips * components + coded, LANES), jnp.int16)],
        "reduce_cores",
        keep,
        came,
    )
    across = swap(send, "freq", freq_count, 2)
    own_part, *sends = small_call(
        functools.partial(spread_kernel, tail),
        [((components + tail, LANES), jnp.float32)] + [((components + coded, LANES), jnp.int16)] * (chips - 1),
        "reduce_x",
        keep,
        came,
        across,
    )
    parts = [swap(send, "freq", freq_count, step) for send, step in zip(sends, z_steps)][::-1]
    return small_call(
        solve_planes_kernel, [((components, own), jnp.float32)], "solve", own_part, *parts
    )[0]


def solution(mesh):
    in_specs = (P(None, "freq", "mz"), P(("freq", "mz"), None), P(), P(), P())
    out_specs = P(None, ("mz", "freq"))
    return jax.shard_map(on_device, mesh=mesh, in_specs=in_specs, out_specs=out_specs, check_vma=False)
```

```python
import functools
import math

import jax
import jax.numpy as jnp
import numpy as np
from jax import lax
from jax.experimental import pallas as pl
from jax.experimental.pallas import tpu as pltpu
from jax.sharding import PartitionSpec as P

PRECISE = lax.Precision.HIGHEST
LANES = 128
REACH = 256
MIB = 1024 * 1024
FULL = 32767.0


def f32_dot(a, b, dims=(((1,), (0,)), ((), ()))):
    return lax.dot_general(a, b, dims, precision=PRECISE, preferred_element_type=jnp.float32)


def two_terms(x):
    high = x.astype(jnp.bfloat16)
    low = (x - high.astype(jnp.float32)).astype(jnp.bfloat16)
    return high, low


def vmem(count):
    return [pl.BlockSpec(memory_space=pltpu.VMEM)] * count


def pack_kernel(x_ref, o_ref):
    x = x_ref[...]
    components, rows = x.shape
    pad = -rows % LANES
    if pad:
        x = jnp.concatenate([x, jnp.zeros((components, pad), x.dtype)], axis=1)
    high, low = two_terms(x.T[:rows])
    o_ref[...] = jnp.concatenate([high, low], axis=1)


def pack(elution):
    rows, components = elution.shape
    return pl.pallas_call(
        pack_kernel,
        out_shape=jax.ShapeDtypeStruct((rows, 2 * components), jnp.bfloat16),
        in_specs=vmem(1),
        out_specs=vmem(1)[0],
        compiler_params=pltpu.CompilerParams(vmem_limit_bytes=8 * MIB),
        name="pack_elution",
    )(elution.T)


def encode_kernel(x_ref, o_ref):
    components, rows = x_ref.shape
    half = rows // 2
    x = x_ref[...]
    pad = -rows % LANES
    x = jnp.concatenate([x, jnp.zeros((components, pad), x.dtype)], axis=1).T[:rows]
    peak = jnp.maximum(jnp.max(jnp.abs(x), axis=0, keepdims=True), 1e-30)
    level = jnp.floor(256.0 / math.log(2.0) * jnp.log(peak)) + 1.0
    x = x * (FULL / scale_of(level))
    x = jnp.clip(jnp.floor(x + 0.5), -FULL, FULL).astype(jnp.int32).astype(jnp.int16)
    o_ref[0:half, :] = jnp.concatenate([x[:half], x[half:]], axis=1)
    level = jnp.broadcast_to(level, (16, components)).astype(jnp.int32).astype(jnp.int16)
    o_ref[half:, :] = jnp.concatenate([level, level], axis=1)


def encode_columns(x, o_ref):
    rows = x.shape[0]
    peak = jnp.maximum(jnp.max(jnp.abs(x), axis=0, keepdims=True), 1e-30)
    level = jnp.floor(256.0 / math.log(2.0) * jnp.log(peak)) + 1.0
    x = jnp.clip(jnp.floor(x * (FULL / scale_of(level)) + 0.5), -FULL, FULL)
    o_ref[0:rows, :] = x.astype(jnp.int32).astype(jnp.int16)
    o_ref[rows:, :] = jnp.broadcast_to(level, (16, x.shape[1])).astype(jnp.int32).astype(jnp.int16)


def scale_of(level):
    return jnp.exp(math.log(2.0) / 256.0 * level)


def decoded(x):
    half = x.shape[0] - 16
    x = x.astype(jnp.int32).astype(jnp.float32)
    return x[:half] * (scale_of(x[half : half + 1]) * (1.0 / FULL))


def decoded_terms(x):
    x = decoded(x)
    high = x.astype(jnp.bfloat16).astype(jnp.float32)
    low = x - high
    left = lax.broadcasted_iota(jnp.int32, x.shape, 1) < LANES // 2
    top = jnp.where(left, high, pltpu.roll(low, LANES // 2, 1))
    bottom = jnp.where(left, pltpu.roll(high, LANES // 2, 1), low)
    return jnp.concatenate([top, bottom], axis=0).astype(jnp.bfloat16)


def encode(elution):
    rows, components = elution.shape
    return pl.pallas_call(
        encode_kernel,
        out_shape=jax.ShapeDtypeStruct((rows // 2 + 16, 2 * components), jnp.int16),
        in_specs=vmem(1),
        out_specs=vmem(1)[0],
        compiler_params=pltpu.CompilerParams(vmem_limit_bytes=8 * MIB),
        name="encode_elution",
    )(elution.T)


def circulant_kernel(turn, w_ref, table_ref, u_ref):
    rows = w_ref.shape[1]
    w = w_ref[...]
    over_lanes = (((0,), (0,)), ((), ()))

    def table(at, height, width):
        return table_ref[at : at + height, :width], table_ref[at + height : at + 2 * height, :width]

    lane_cos, lane_sin = table(0, LANES, LANES)
    twid_cos, twid_sin = table(2 * LANES, rows, LANES)
    row_cos, row_sin = table(2 * LANES + 2 * rows, rows, rows)
    a_re = f32_dot(w, lane_cos, over_lanes)
    a_im = -f32_dot(w, lane_sin, over_lanes)
    b_re = a_re * twid_cos + a_im * twid_sin
    b_im = a_im * twid_cos - a_re * twid_sin
    c = f32_dot(row_cos, b_re) + f32_dot(row_sin, b_im)
    sub = lax.broadcasted_iota(jnp.int32, (LANES, LANES), 0)
    lane = lax.broadcasted_iota(jnp.int32, (LANES, LANES), 1)

    if turn:
        part = LANES - turn % LANES
        near, after = (
            pltpu.roll(jnp.concatenate([c[n:], c[:n]], axis=0), part % LANES, 1)
            for n in (turn // LANES, turn // LANES + 1)
        )
        moved = jnp.where(lax.broadcasted_iota(jnp.int32, c.shape, 1) < part, near, after)
        c = jnp.where(lax.axis_index("mz") == 1, moved, c)

    def turned(row):
        return pltpu.roll(jnp.broadcast_to(c[row : row + 1], (LANES, LANES)), 0, 1, stride=1, stride_axis=0)

    before = turned(rows - 1)
    for row in range(rows):
        now = turned(row)
        high, low = two_terms(jnp.where(lane >= sub, now, before))
        u_ref[0:LANES, row * LANES : (row + 1) * LANES] = high
        u_ref[LANES:, row * LANES : (row + 1) * LANES] = low
        before = now


def circulant(weights, turn):
    length = weights.size
    rows = length // LANES

    def tables(a, b, period):
        angle = 2.0 * math.pi / period * ((a[:, None] * b[None, :]) % period)
        return np.pad(np.concatenate([np.cos(angle), np.sin(angle)]), ((0, 0), (0, LANES - b.size)))

    lane_ids, row_ids = np.arange(LANES), np.arange(rows)
    table = np.concatenate(
        [
            tables(lane_ids, lane_ids, LANES),
            tables(row_ids, lane_ids, length),
            tables(row_ids, row_ids, rows) / length,
        ]
    ).astype(np.float32)
    return pl.pallas_call(
        functools.partial(circulant_kernel, turn),
        out_shape=jax.ShapeDtypeStruct((2 * LANES, length), jnp.bfloat16),
        in_specs=vmem(2),
        out_specs=vmem(1)[0],
        compiler_params=pltpu.CompilerParams(vmem_limit_bytes=16 * MIB),
        cost_estimate=pl.CostEstimate(flops=2_000_000_000, bytes_accessed=4 * MIB, transcendentals=0),
        name="circulant_block",
    )(weights, table)


def model_kernel(places, planes, *refs):
    if planes:
        u_ref, g_ref, coded_ref, wide = refs[-4:]
    else:
        u_ref, g_ref, wide = refs[-3:]
    length = u_ref.shape[1]
    components = g_ref.shape[0]
    freq_rank = lax.axis_index("freq")
    if planes:
        own_ref, came_ref = refs[:2]
        freq_count = 2 * own_ref.shape[0]
        rows = 2 * (own_ref.shape[1] - 16)
        padded = wide.shape[0] // freq_count
        for block in range(freq_count):
            apart = lax.bitwise_xor((freq_rank + block) & (freq_count - 1), freq_rank)
            ref = came_ref if block % 2 else own_ref
            values = decoded_terms(ref[pl.ds(block_place(apart, freq_count), 1)][0])
            at, before = block * padded, (block - 1) % freq_count * padded
            wide[at : at + rows, 0:LANES] = values
            wide[before : before + rows, LANES:] = values
            wide[at + rows : at + padded, :] = jnp.zeros((padded - rows, 2 * LANES), jnp.bfloat16)
        period = length // freq_count // LANES
        left = lax.broadcasted_iota(jnp.int32, (LANES, LANES), 1) < components
        sides = []
        for a in range(period):
            columns = []
            for block in range(freq_count):
                first = REACH // LANES + period * block - a
                for n in range(first, first + padded // LANES):
                    at = n % (length // LANES) * LANES
                    columns.append(u_ref[:, at : at + LANES])
            width = 2 * LANES if a + period < places else LANES
            made = jnp.dot(
                jnp.concatenate(columns, axis=1), wide[:, :width], preferred_element_type=jnp.float32
            )
            made = made[:LANES] + made[LANES:]
            tiles = []
            for half in range(width // LANES):
                tile = made[:, half * LANES : (half + 1) * LANES]
                tiles.append(tile + pltpu.roll(tile, components, 1))
                to = (a + half * period) * LANES
                g_ref[:, to : to + LANES] = tiles[-1].T[:components]
            if len(tiles) == 1:
                half = LANES // 2
                sides.append(jnp.where(left[:half], tiles[0][:half], tiles[0][half:]))
            else:
                sides.append(jnp.where(left, tiles[0], tiles[1]))
        encode_columns(jnp.concatenate(sides, axis=0), coded_ref)
        return
    own_ref = refs[0]
    step = own_ref.shape[1]
    steps = length // step
    bin_count = length // lax.axis_size("freq")
    first = lax.rem(freq_rank * bin_count + length - REACH, length) // step

    def bring(j, carry):
        values = own_ref[pl.ds(lax.rem(first + j, steps), 1)][0]
        to = pl.multiple_of(REACH + j * step, step)
        wide[pl.ds(to, step), 0:LANES] = values
        wide[pl.ds(pl.multiple_of(to - LANES, step), step), LANES:] = values
        return carry

    lax.fori_loop(0, (wide.shape[0] - REACH) // step, bring, 0)
    for a in range(0, places, 2):
        at = REACH + a * LANES
        made = jnp.dot(u_ref[...], wide[at : at + length, :], preferred_element_type=jnp.float32)
        made = made[:LANES] + made[LANES:]
        for half in range(min(2, places - a)):
            piece = made[:, half * LANES : (half + 1) * LANES].T
            g_ref[:, (a + half) * LANES : (a + half + 1) * LANES] = piece[:components] + piece[components:]


def block_place(apart, freq_count):
    return (apart >> 2) + ((apart >> 1) & 1) * (freq_count // 4)


def partial_model(gathered, u, bin_count, components):
    length = u.shape[1]
    places = -(-(bin_count + REACH) // LANES)
    planes = len(gathered) == 2
    if planes:
        own = gathered[0]
        wide_rows = 2 * own.shape[0] * (-(-2 * (own.shape[1] - 16) // LANES) * LANES)
    else:
        wide_rows = REACH + length + 2 * LANES * ((places - 1) // 2)
    outs = [jax.ShapeDtypeStruct((components, places * LANES), jnp.float32)]
    if planes:
        outs.append(jax.ShapeDtypeStruct((places * LANES // 2 + 16, LANES), jnp.int16))
    return pl.pallas_call(
        functools.partial(model_kernel, places, planes),
        out_shape=tuple(outs),
        in_specs=vmem(len(gathered) + 1),
        out_specs=tuple(vmem(len(outs))),
        scratch_shapes=[pltpu.VMEM((wide_rows, 2 * LANES), jnp.bfloat16)],
        compiler_params=pltpu.CompilerParams(vmem_limit_bytes=24 * MIB),
        cost_estimate=pl.CostEstimate(flops=2_000_000_000, bytes_accessed=4 * MIB, transcendentals=0),
        name="partial_model",
    )(*gathered, u)


def shifted_terms(x, amps, lags, bin_count, terms):
    components = x.shape[0]
    out_count = -(-bin_count // LANES)
    x = pltpu.roll(x, x.shape[1] - 1, 1)
    height = 16
    lane = lax.broadcasted_iota(jnp.int32, (height, LANES), 1)
    for at in range(0, components, height):
        vectors = [x[at : at + height, v * LANES : (v + 1) * LANES] for v in range(out_count + 2)]
        for k in range(amps.shape[1]):
            left = REACH - 1 - jnp.broadcast_to(lags[at : at + height, k : k + 1], lane.shape)
            amp = jnp.broadcast_to(amps[at : at + height, k : k + 1], lane.shape)
            inside = left & (LANES - 1)
            index = (lane + inside) & (LANES - 1)
            far, same = left >= LANES, lane >= inside
            near = [jnp.where(far, vectors[v + 1], vectors[v]) for v in range(out_count + 1)]
            for v in range(out_count):
                joined = jnp.where(same, near[v], near[v + 1])
                turned = jnp.take_along_axis(joined, index, axis=1, mode="promise_in_bounds")
                high, low = two_terms(amp * turned)
                width = min(LANES, bin_count - v * LANES)
                to = slice(k * bin_count + v * LANES, k * bin_count + v * LANES + width)
                terms[at : at + height, to] = high[:, :width]
                terms[components + at : components + at + height, to] = low[:, :width]


def pair_kernel(mine_ref, came_ref, o_ref):
    rows = mine_ref.shape[0]
    freq_count = 2 * came_ref.shape[0]
    freq_rank = lax.axis_index("freq")
    apart = lax.bitwise_xor((freq_rank - 1) & (freq_count - 1), freq_rank)
    o_ref[0:rows, :] = came_ref[pl.ds(block_place(apart, freq_count), 1)][0]
    o_ref[rows:, :] = mine_ref[...]


def window_pair(mine, came):
    return pl.pallas_call(
        pair_kernel,
        out_shape=jax.ShapeDtypeStruct((2 * mine.shape[0], mine.shape[1]), mine.dtype),
        in_specs=vmem(2),
        out_specs=vmem(1)[0],
        compiler_params=pltpu.CompilerParams(vmem_limit_bytes=8 * MIB),
        name="window_pair",
    )(mine, came)


def elution_kernel(planes, *refs):
    amp_ref, lag_ref, terms, window = refs[-4:]
    components = amp_ref.shape[1]
    bin_count = terms.shape[1] // amp_ref.shape[0]
    freq_rank = lax.axis_index("freq")
    if planes:
        pair_ref, other_ref = refs[:2]
        mz_rank = lax.axis_index("mz")
        coded = pair_ref.shape[0] // 2
        rows = 2 * (coded - 16)
        skip = bin_count - REACH
        for ref, half in ((pair_ref, mz_rank), (other_ref, 1 - mz_rank)):
            for block in range(2):
                to = pl.multiple_of((2 * block + half) * rows, 64)
                values = decoded(ref[block * coded : (block + 1) * coded, :])
                half_rows = rows // 2
                window[pl.ds(to, half_rows), :] = values
                window[pl.ds(pl.multiple_of(to + half_rows, 32), half_rows), :] = pltpu.roll(values, LANES // 2, 1)
    else:
        own_ref = refs[0]
        step = own_ref.shape[1]
        steps = own_ref.shape[0]
        first = lax.rem(freq_rank * bin_count + steps * step - REACH, steps * step) // step
        skip = 0
        for j in range(window.shape[0] // step):
            window[j * step : (j + 1) * step, :] = own_ref[pl.ds(lax.rem(first + j, steps), 1)][0]
    pieces = []
    for at in range(skip, window.shape[0], LANES):
        piece = window[at : at + LANES, :].astype(jnp.float32).T
        pieces.append(piece[:components] if planes else piece[:components] + piece[components:])
    shifted_terms(jnp.concatenate(pieces, axis=1), amp_ref[...].T, lag_ref[...].T, bin_count, terms)


def elution_terms(elutions, loadings, shifts, bin_count):
    run_count, components = loadings.shape
    places = -(-(bin_count + REACH) // LANES)
    planes = len(elutions) > 1
    return pl.pallas_call(
        functools.partial(elution_kernel, planes),
        out_shape=jax.ShapeDtypeStruct((2 * components, run_count * bin_count), jnp.bfloat16),
        in_specs=vmem(len(elutions) + 2),
        out_specs=vmem(1)[0],
        scratch_shapes=[
            pltpu.VMEM((2 * bin_count, LANES), jnp.float32)
            if planes
            else pltpu.VMEM((places * LANES, LANES), jnp.bfloat16)
        ],
        compiler_params=pltpu.CompilerParams(vmem_limit_bytes=12 * MIB),
        cost_estimate=pl.CostEstimate(flops=1_000_000_000, bytes_accessed=2 * MIB, transcendentals=0),
        name="elution_terms",
    )(*elutions, loadings, shifts)


def product_kernel(parts, planes, *refs):
    i_ref = refs[0]
    g_refs = refs[1 : 1 + parts]
    elution_ref, amp_ref, lag_ref, num_ref, other_ref, terms = refs[1 + parts :]
    run_count, bin_count, local_mz = i_ref.shape
    components = amp_ref.shape[1]
    chunk = 2 * LANES
    chunks = local_mz // chunk
    g = g_refs[0][...]
    if planes:
        period = bin_count // LANES
        x = decoded(g_refs[1][...])
        first, second, at = [], [], 0
        for a in range(period):
            if a + period < g.shape[1] // LANES:
                tile = x[at : at + LANES].T
                second.append(tile[components:])
                at += LANES
            else:
                half = x[at : at + LANES // 2]
                tile = jnp.concatenate([half, pltpu.roll(half, components, 1)], axis=0).T
                at += LANES // 2
            first.append(tile[:components])
        g = g + jnp.concatenate(first + second, axis=1)
    shifted_terms(g, amp_ref[...].T, lag_ref[...].T, bin_count, terms)
    gram = lax.dot_general(
        terms[...], elution_ref[...], (((1,), (1,)), ((), ())), preferred_element_type=jnp.float32
    )
    gram = gram[:components] + gram[components:]
    gram = gram[:, :components] + gram[:, components:]
    if planes:
        keep_ref, send_ref = num_ref, other_ref
        half = components // 2
        gram = jnp.concatenate([gram[:half], gram[half:]], axis=1)
        keep_ref[chunks * components :, :] = gram
        send_ref[chunks * components :, :] = gram
    else:
        other_ref[...] = gram

    for n in range(chunks):
        data = i_ref[:, :, n * chunk : (n + 1) * chunk].reshape(run_count * bin_count, chunk)
        made = jnp.dot(terms[...], data, preferred_element_type=jnp.float32)
        made = made[:components] + made[components:]
        if planes:
            freq_rank = lax.axis_index("freq")
            core = freq_rank & 1
            place = block_place(lax.bitwise_xor(freq_rank, 2 * n + core), 2 * chunks)
            at = pl.ds(pl.multiple_of(place * components, components), components)
            even, odd = made[:, :LANES], made[:, LANES:]
            keep_ref[at, :] = jnp.where(core == 0, even, odd)
            send_ref[at, :] = jnp.where(core == 0, odd, even)
        else:
            num_ref[:, n * chunk : (n + 1) * chunk] = made


def product(intensity, models, elution, loadings, shifts, planes):
    run_count, bin_count, local_mz = intensity.shape
    components = loadings.shape[1]
    chunk = 2 * LANES
    chunks = local_mz // chunk
    if planes:
        out_shapes = [(chunks * components + components // 2, LANES)] * 2
    else:
        out_shapes = [(components, local_mz), (components, components)]
    return pl.pallas_call(
        functools.partial(product_kernel, len(models), planes),
        out_shape=tuple(jax.ShapeDtypeStruct(shape, jnp.float32) for shape in out_shapes),
        in_specs=vmem(len(models) + 4),
        out_specs=tuple(vmem(2)),
        scratch_shapes=[pltpu.VMEM((2 * components, run_count * bin_count), jnp.bfloat16)],
        compiler_params=pltpu.CompilerParams(vmem_limit_bytes=24 * MIB),
        cost_estimate=pl.CostEstimate(
            flops=8_000_000_000, bytes_accessed=2 * intensity.size, transcendentals=0
        ),
        name="model_products",
    )(intensity, *models, elution, loadings, shifts)


def inverse2(a, b, d):
    scale = 1.0 / (a * d - b * b)
    return d * scale, -b * scale, a * scale


def eliminate(gram, right):
    components = gram.shape[0]
    height = 8
    shape = (height, gram.shape[1])
    row_id = lax.broadcasted_iota(jnp.int32, shape, 0)
    starts = range(0, components, height)
    gram = [gram[at : at + height] for at in starts]
    right = [right[at : at + height] for at in starts]
    for j in range(0, components, 4):
        here, r = j // height, j % height
        columns = [[jnp.broadcast_to(tile[:, j + n : j + n + 1], shape) for tile in gram] for n in range(4)]
        pivot = [[columns[n][here][r + m : r + m + 1] for n in range(4)] for m in range(4)]
        a00, a01, a11 = inverse2(pivot[0][0], pivot[0][1], pivot[1][1])
        b00, b01, b10, b11 = pivot[0][2], pivot[0][3], pivot[1][2], pivot[1][3]
        w00, w01 = a00 * b00 + a01 * b10, a00 * b01 + a01 * b11
        w10, w11 = a01 * b00 + a11 * b10, a01 * b01 + a11 * b11
        s00, s01, s11 = inverse2(
            pivot[2][2] - (b00 * w00 + b10 * w10),
            pivot[2][3] - (b00 * w01 + b10 * w11),
            pivot[3][3] - (b01 * w01 + b11 * w11),
        )
        away = (row_id < r) | (row_id >= r + 4)
        for n in range(4):
            columns[n][here] = jnp.where(away, columns[n][here], jnp.where(row_id == r + n, -1.0, 0.0))
        gram_rows = [gram[here][r + n : r + n + 1] for n in range(4)]
        right_rows = [right[here][r + n : r + n + 1] for n in range(4)]
        gram[here] = jnp.where(away, gram[here], 0.0)
        right[here] = jnp.where(away[:, : right[here].shape[1]], right[here], 0.0)
        for t in range(len(gram)):
            c0, c1, c2, c3 = (columns[n][t] for n in range(4))
            t2, t3 = c2 - c0 * w00 - c1 * w10, c3 - c0 * w01 - c1 * w11
            f2, f3 = t2 * s00 + t3 * s01, t2 * s01 + t3 * s11
            f0 = c0 * a00 + c1 * a01 - f2 * w00 - f3 * w01
            f1 = c0 * a01 + c1 * a11 - f2 * w10 - f3 * w11
            for n, factor in enumerate((f0, f1, f2, f3)):
                gram[t] = gram[t] - factor * gram_rows[n]
                right[t] = right[t] - factor[:, : right[t].shape[1]] * right_rows[n]
    return jnp.concatenate(right, axis=0)


def total_of(refs, at, rows):
    total = refs[0][at : at + rows]
    for ref in refs[1:]:
        total = total + ref[at : at + rows]
    return total


def fixed_point(x, full):
    return jnp.clip(jnp.floor(x + 0.5), -full, full)


def as_int16(x):
    return x.astype(jnp.int32).astype(jnp.int16)


def row_level(x):
    peak = jnp.maximum(jnp.max(jnp.abs(x), axis=1, keepdims=True), 1e-30)
    return jnp.floor(256.0 / math.log(2.0) * jnp.log(peak)) + 1.0


def diagonal(x, rows):
    shape = (rows, LANES)
    on = lax.broadcasted_iota(jnp.int32, shape, 0) == lax.broadcasted_iota(jnp.int32, shape, 1)
    return jnp.where(on, jnp.broadcast_to(x, shape), 0.0)


def encode_rows(x, gram, o_ref):
    rows, tail = x.shape[0], gram.shape[0]
    parts = [x[at : at + LANES] for at in range(0, rows, LANES)]
    levels = [row_level(part) for part in parts] + [row_level(gram)]
    at = 0
    for part, level in zip(parts, levels):
        o_ref[at : at + part.shape[0], :] = as_int16(fixed_point(part * (FULL / scale_of(level)), FULL))
        at += part.shape[0]
    scaled = gram * (FULL / scale_of(levels[-1]))
    high = fixed_point(scaled, FULL)
    o_ref[at : at + tail, :] = as_int16(high)
    o_ref[at + tail : at + 2 * tail, :] = as_int16(fixed_point((scaled - high) * (2 * FULL), FULL))
    row_id = lax.broadcasted_iota(jnp.int32, (16, LANES), 0)
    block = jnp.zeros((16, LANES), jnp.float32)
    for n, level in enumerate(levels):
        lanes = jnp.sum(diagonal(level, level.shape[0]), axis=0, keepdims=True)
        block = jnp.where(row_id == n, lanes, block)
    o_ref[at + 2 * tail :, :] = as_int16(block)


def decode_rows(ref, tail):
    rows = ref.shape[0] - 2 * tail - 16
    x = ref[...].astype(jnp.int32).astype(jnp.float32)

    def scale(n, count):
        at = rows + 2 * tail + n
        return scale_of(jnp.sum(diagonal(x[at : at + 1], count), axis=1, keepdims=True)) * (1.0 / FULL)

    parts = []
    for n, at in enumerate(range(0, rows, LANES)):
        count = min(LANES, rows - at)
        parts.append(x[at : at + count] * scale(n, count))
    gram = x[rows : rows + tail] + x[rows + tail : rows + 2 * tail] * (0.5 / FULL)
    return jnp.concatenate(parts, axis=0), gram * scale(len(parts), tail)


def halve_kernel(tail, a_ref, b_ref, o_ref):
    rows = o_ref.shape[0] - 2 * tail - 16
    total = total_of((a_ref, b_ref), rows, rows + tail)
    encode_rows(total[:rows], total[rows:], o_ref)


def spread_kernel(tail, a_ref, b_ref, c_ref, own_ref, *outs):
    rows = own_ref.shape[0] - tail
    count = len(outs) + 1
    total, gram = decode_rows(c_ref, tail)
    total = total + total_of((a_ref, b_ref), 0, count * rows)
    gram = gram + total_of((a_ref, b_ref), 2 * count * rows, tail)
    own_ref[0:rows, :] = total[:rows]
    own_ref[rows:, :] = gram
    for n, o_ref in enumerate(outs):
        encode_rows(total[(n + 1) * rows : (n + 2) * rows], gram, o_ref)


def solve_planes_kernel(own_ref, *refs):
    o_ref = refs[-1]
    components = o_ref.shape[0]
    total, gram = own_ref[:components], own_ref[components:]
    for ref in refs[:-1]:
        part, gram_part = decode_rows(ref, gram.shape[0])
        total, gram = total + part, gram + gram_part
    gram = jnp.concatenate([gram, pltpu.roll(gram, gram.shape[1] // 2, 1)], axis=0)
    o_ref[...] = eliminate(gram, total)


def solve_kernel(g_ref, n_ref, o_ref):
    components = o_ref.shape[0]
    gram = jnp.concatenate([g_ref[...], jnp.zeros((components, LANES - components), jnp.float32)], axis=1)
    o_ref[...] = eliminate(gram, n_ref[...])


def small_call(kernel, outs, name, *args):
    return pl.pallas_call(
        kernel,
        out_shape=tuple(jax.ShapeDtypeStruct(shape, dtype) for shape, dtype in outs),
        in_specs=vmem(len(args)),
        out_specs=tuple(vmem(len(outs))),
        compiler_params=pltpu.CompilerParams(vmem_limit_bytes=8 * MIB),
        name=name,
    )(*args)


def swap(x, axes, count, value):
    return lax.ppermute(x, axes, [(i, i ^ value) for i in range(count)])


def on_device(intensity, elution, loadings, shifts, bin_weight):
    freq_count = lax.axis_size("freq")
    mz_count = lax.axis_size("mz")
    components = loadings.shape[1]
    bin_count = intensity.shape[1]
    axes = ("freq", "mz")
    own = intensity.shape[2] // freq_count
    planes = (
        own == LANES
        and 2 * components == LANES
        and mz_count == 2
        and freq_count & (freq_count - 1) == 0
        and freq_count >= 8
        and elution.shape[0] % 64 == 0
        and bin_count % LANES == 0
        and bin_count >= REACH
    )
    if not planes:
        mine = pack(elution)
        gathered = lax.all_gather(mine, axes, axis=0).reshape(-1, math.gcd(bin_count, LANES), LANES)
        (g,) = partial_model((gathered,), circulant(bin_weight.reshape(LANES, -1), 0), bin_count, components)
        shifted = elution_terms((gathered,), loadings, shifts, bin_count)
        numerator, gram = product(intensity, (g,), shifted, loadings, shifts, planes)
        gram = lax.psum(gram, "freq")
        owned = lax.psum_scatter(numerator, "freq", scatter_dimension=1, tiled=True)
        return small_call(solve_kernel, [((components, own), jnp.float32)], "solve", gram, owned)[0]
    mine = encode(elution)
    z_steps = range(4, freq_count, 4)
    held = jnp.stack([mine] + [swap(mine, "freq", freq_count, step) for step in z_steps])
    weights = bin_weight.reshape(LANES, -1)
    held, weights = lax.optimization_barrier((held, weights))
    held = jnp.concatenate([held, swap(held, "freq", freq_count, 2)], axis=0)
    u = circulant(weights, elution.shape[0])
    held, u = lax.optimization_barrier((held, u))
    came = swap(held, "freq", freq_count, 1)
    pair = window_pair(mine, came)
    other = swap(pair, "mz", mz_count, 1)
    g, coded = partial_model((held, came), u, bin_count, components)
    coded, other = lax.optimization_barrier((coded, other))
    models = (g, swap(coded, "mz", mz_count, 1))
    shifted = elution_terms((pair, other), loadings, shifts, bin_count)
    keep, send = product(intensity, models, shifted, loadings, shifts, planes)
    tail = components // 2
    chips = freq_count // 4
    came = swap(send, "freq", freq_count, 1)
    coded = 2 * tail + 16
    (send,) = small_call(
        functools.partial(halve_kernel, tail),
        [((chips * components + coded, LANES), jnp.int16)],
        "reduce_cores",
        keep,
        came,
    )
    across = swap(send, "freq", freq_count, 2)
    own_part, *sends = small_call(
        functools.partial(spread_kernel, tail),
        [((components + tail, LANES), jnp.float32)] + [((components + coded, LANES), jnp.int16)] * (chips - 1),
        "reduce_x",
        keep,
        came,
        across,
    )
    parts = [swap(send, "freq", freq_count, step) for send, step in zip(sends, z_steps)][::-1]
    return small_call(
        solve_planes_kernel, [((components, own), jnp.float32)], "solve", own_part, *parts
    )[0]


def solution(mesh):
    in_specs = (P(None, "freq", "mz"), P(("freq", "mz"), None), P(), P(), P())
    out_specs = P(None, ("mz", "freq"))
    return jax.shard_map(on_device, mesh=mesh, in_specs=in_specs, out_specs=out_specs, check_vma=False)
```

```python
import functools
import math

import jax
import jax.numpy as jnp
import numpy as np
from jax import lax
from jax.experimental import pallas as pl
from jax.experimental.pallas import tpu as pltpu
from jax.sharding import PartitionSpec as P

PRECISE = lax.Precision.HIGHEST
LANES = 128
REACH = 256
MIB = 1024 * 1024
FULL = 32767.0


def f32_dot(a, b, dims=(((1,), (0,)), ((), ()))):
    return lax.dot_general(a, b, dims, precision=PRECISE, preferred_element_type=jnp.float32)


def two_terms(x):
    high = x.astype(jnp.bfloat16)
    low = (x - high.astype(jnp.float32)).astype(jnp.bfloat16)
    return high, low


def vmem(count):
    return [pl.BlockSpec(memory_space=pltpu.VMEM)] * count


def pack_kernel(x_ref, o_ref):
    x = x_ref[...]
    components, rows = x.shape
    pad = -rows % LANES
    if pad:
        x = jnp.concatenate([x, jnp.zeros((components, pad), x.dtype)], axis=1)
    high, low = two_terms(x.T[:rows])
    o_ref[...] = jnp.concatenate([high, low], axis=1)


def pack(elution):
    rows, components = elution.shape
    return pl.pallas_call(
        pack_kernel,
        out_shape=jax.ShapeDtypeStruct((rows, 2 * components), jnp.bfloat16),
        in_specs=vmem(1),
        out_specs=vmem(1)[0],
        compiler_params=pltpu.CompilerParams(vmem_limit_bytes=8 * MIB),
        name="pack_elution",
    )(elution.T)


def encode_kernel(x_ref, o_ref):
    components, rows = x_ref.shape
    half = rows // 2
    x = x_ref[...]
    pad = -rows % LANES
    x = jnp.concatenate([x, jnp.zeros((components, pad), x.dtype)], axis=1).T[:rows]
    peak = jnp.maximum(jnp.max(jnp.abs(x), axis=0, keepdims=True), 1e-30)
    level = jnp.floor(256.0 / math.log(2.0) * jnp.log(peak)) + 1.0
    x = x * (FULL / scale_of(level))
    x = jnp.clip(jnp.floor(x + 0.5), -FULL, FULL).astype(jnp.int32).astype(jnp.int16)
    o_ref[0:half, :] = jnp.concatenate([x[:half], x[half:]], axis=1)
    level = jnp.broadcast_to(level, (16, components)).astype(jnp.int32).astype(jnp.int16)
    o_ref[half:, :] = jnp.concatenate([level, level], axis=1)


def encode_columns(x, o_ref):
    rows = x.shape[0]
    peak = jnp.maximum(jnp.max(jnp.abs(x), axis=0, keepdims=True), 1e-30)
    level = jnp.floor(256.0 / math.log(2.0) * jnp.log(peak)) + 1.0
    x = jnp.clip(jnp.floor(x * (FULL / scale_of(level)) + 0.5), -FULL, FULL)
    o_ref[0:rows, :] = x.astype(jnp.int32).astype(jnp.int16)
    o_ref[rows:, :] = jnp.broadcast_to(level, (16, x.shape[1])).astype(jnp.int32).astype(jnp.int16)


def scale_of(level):
    return jnp.exp(math.log(2.0) / 256.0 * level)


def decoded(x):
    half = x.shape[0] - 16
    x = x.astype(jnp.int32).astype(jnp.float32)
    return x[:half] * (scale_of(x[half : half + 1]) * (1.0 / FULL))


def decoded_terms(x):
    x = decoded(x)
    high = x.astype(jnp.bfloat16).astype(jnp.float32)
    low = x - high
    left = lax.broadcasted_iota(jnp.int32, x.shape, 1) < LANES // 2
    top = jnp.where(left, high, pltpu.roll(low, LANES // 2, 1))
    bottom = jnp.where(left, pltpu.roll(high, LANES // 2, 1), low)
    return jnp.concatenate([top, bottom], axis=0).astype(jnp.bfloat16)


def encode(elution):
    rows, components = elution.shape
    return pl.pallas_call(
        encode_kernel,
        out_shape=jax.ShapeDtypeStruct((rows // 2 + 16, 2 * components), jnp.int16),
        in_specs=vmem(1),
        out_specs=vmem(1)[0],
        compiler_params=pltpu.CompilerParams(vmem_limit_bytes=8 * MIB),
        name="encode_elution",
    )(elution.T)


def circulant_kernel(turn, w_ref, table_ref, u_ref):
    rows = w_ref.shape[1]
    w = w_ref[...]
    over_lanes = (((0,), (0,)), ((), ()))

    def table(at, height, width):
        return table_ref[at : at + height, :width], table_ref[at + height : at + 2 * height, :width]

    lane_cos, lane_sin = table(0, LANES, LANES)
    twid_cos, twid_sin = table(2 * LANES, rows, LANES)
    row_cos, row_sin = table(2 * LANES + 2 * rows, rows, rows)
    a_re = f32_dot(w, lane_cos, over_lanes)
    a_im = -f32_dot(w, lane_sin, over_lanes)
    b_re = a_re * twid_cos + a_im * twid_sin
    b_im = a_im * twid_cos - a_re * twid_sin
    c = f32_dot(row_cos, b_re) + f32_dot(row_sin, b_im)
    sub = lax.broadcasted_iota(jnp.int32, (LANES, LANES), 0)
    lane = lax.broadcasted_iota(jnp.int32, (LANES, LANES), 1)

    if turn:
        part = LANES - turn % LANES
        near, after = (
            pltpu.roll(jnp.concatenate([c[n:], c[:n]], axis=0), part % LANES, 1)
            for n in (turn // LANES, turn // LANES + 1)
        )
        moved = jnp.where(lax.broadcasted_iota(jnp.int32, c.shape, 1) < part, near, after)
        c = jnp.where(lax.axis_index("mz") == 1, moved, c)

    def turned(row):
        return pltpu.roll(jnp.broadcast_to(c[row : row + 1], (LANES, LANES)), 0, 1, stride=1, stride_axis=0)

    before = turned(rows - 1)
    for row in range(rows):
        now = turned(row)
        high, low = two_terms(jnp.where(lane >= sub, now, before))
        u_ref[0:LANES, row * LANES : (row + 1) * LANES] = high
        u_ref[LANES:, row * LANES : (row + 1) * LANES] = low
        before = now


def circulant(weights, turn):
    length = weights.size
    rows = length // LANES

    def tables(a, b, period):
        angle = 2.0 * math.pi / period * ((a[:, None] * b[None, :]) % period)
        return np.pad(np.concatenate([np.cos(angle), np.sin(angle)]), ((0, 0), (0, LANES - b.size)))

    lane_ids, row_ids = np.arange(LANES), np.arange(rows)
    table = np.concatenate(
        [
            tables(lane_ids, lane_ids, LANES),
            tables(row_ids, lane_ids, length),
            tables(row_ids, row_ids, rows) / length,
        ]
    ).astype(np.float32)
    return pl.pallas_call(
        functools.partial(circulant_kernel, turn),
        out_shape=jax.ShapeDtypeStruct((2 * LANES, length), jnp.bfloat16),
        in_specs=vmem(2),
        out_specs=vmem(1)[0],
        compiler_params=pltpu.CompilerParams(vmem_limit_bytes=16 * MIB),
        cost_estimate=pl.CostEstimate(flops=2_000_000_000, bytes_accessed=4 * MIB, transcendentals=0),
        name="circulant_block",
    )(weights, table)


def model_kernel(places, planes, *refs):
    if planes:
        u_ref, g_ref, coded_ref, wide = refs[-4:]
    else:
        u_ref, g_ref, wide = refs[-3:]
    length = u_ref.shape[1]
    components = g_ref.shape[0]
    freq_rank = lax.axis_index("freq")
    if planes:
        own_ref, came_ref = refs[:2]
        freq_count = 2 * own_ref.shape[0]
        rows = 2 * (own_ref.shape[1] - 16)
        padded = wide.shape[0] // freq_count
        for block in range(freq_count):
            apart = lax.bitwise_xor((freq_rank + block) & (freq_count - 1), freq_rank)
            ref = came_ref if block % 2 else own_ref
            values = decoded_terms(ref[pl.ds(block_place(apart, freq_count), 1)][0])
            at, before = block * padded, (block - 1) % freq_count * padded
            wide[at : at + rows, 0:LANES] = values
            wide[before : before + rows, LANES:] = values
            wide[at + rows : at + padded, :] = jnp.zeros((padded - rows, 2 * LANES), jnp.bfloat16)
        period = length // freq_count // LANES
        left = lax.broadcasted_iota(jnp.int32, (LANES, LANES), 1) < components
        sides = []
        for a in range(period):
            columns = []
            for block in range(freq_count):
                first = REACH // LANES + period * block - a
                for n in range(first, first + padded // LANES):
                    at = n % (length // LANES) * LANES
                    columns.append(u_ref[:, at : at + LANES])
            width = 2 * LANES if a + period < places else LANES
            made = jnp.dot(
                jnp.concatenate(columns, axis=1), wide[:, :width], preferred_element_type=jnp.float32
            )
            made = made[:LANES] + made[LANES:]
            tiles = []
            for half in range(width // LANES):
                tile = made[:, half * LANES : (half + 1) * LANES]
                tiles.append(tile + pltpu.roll(tile, components, 1))
                to = (a + half * period) * LANES
                g_ref[:, to : to + LANES] = tiles[-1].T[:components]
            if len(tiles) == 1:
                half = LANES // 2
                sides.append(jnp.where(left[:half], tiles[0][:half], tiles[0][half:]))
            else:
                sides.append(jnp.where(left, tiles[0], tiles[1]))
        encode_columns(jnp.concatenate(sides, axis=0), coded_ref)
        return
    own_ref = refs[0]
    step = own_ref.shape[1]
    steps = length // step
    bin_count = length // lax.axis_size("freq")
    first = lax.rem(freq_rank * bin_count + length - REACH, length) // step

    def bring(j, carry):
        values = own_ref[pl.ds(lax.rem(first + j, steps), 1)][0]
        to = pl.multiple_of(REACH + j * step, step)
        wide[pl.ds(to, step), 0:LANES] = values
        wide[pl.ds(pl.multiple_of(to - LANES, step), step), LANES:] = values
        return carry

    lax.fori_loop(0, (wide.shape[0] - REACH) // step, bring, 0)
    for a in range(0, places, 2):
        at = REACH + a * LANES
        made = jnp.dot(u_ref[...], wide[at : at + length, :], preferred_element_type=jnp.float32)
        made = made[:LANES] + made[LANES:]
        for half in range(min(2, places - a)):
            piece = made[:, half * LANES : (half + 1) * LANES].T
            g_ref[:, (a + half) * LANES : (a + half + 1) * LANES] = piece[:components] + piece[components:]


def block_place(apart, freq_count):
    return (apart >> 2) + ((apart >> 1) & 1) * (freq_count // 4)


def partial_model(gathered, u, bin_count, components):
    length = u.shape[1]
    places = -(-(bin_count + REACH) // LANES)
    planes = len(gathered) == 2
    if planes:
        own = gathered[0]
        wide_rows = 2 * own.shape[0] * (-(-2 * (own.shape[1] - 16) // LANES) * LANES)
    else:
        wide_rows = REACH + length + 2 * LANES * ((places - 1) // 2)
    outs = [jax.ShapeDtypeStruct((components, places * LANES), jnp.float32)]
    if planes:
        outs.append(jax.ShapeDtypeStruct((places * LANES // 2 + 16, LANES), jnp.int16))
    return pl.pallas_call(
        functools.partial(model_kernel, places, planes),
        out_shape=tuple(outs),
        in_specs=vmem(len(gathered) + 1),
        out_specs=tuple(vmem(len(outs))),
        scratch_shapes=[pltpu.VMEM((wide_rows, 2 * LANES), jnp.bfloat16)],
        compiler_params=pltpu.CompilerParams(vmem_limit_bytes=24 * MIB),
        cost_estimate=pl.CostEstimate(flops=2_000_000_000, bytes_accessed=4 * MIB, transcendentals=0),
        name="partial_model",
    )(*gathered, u)


def shifted_terms(x, amps, lags, bin_count, terms):
    for piece in shift_pieces(x, amps, lags, bin_count, terms, range(amps.shape[1])):
        piece()


def shift_pieces(x, amps, lags, bin_count, terms, runs):
    components = x.shape[0]
    out_count = -(-bin_count // LANES)
    x = pltpu.roll(x, x.shape[1] - 1, 1)
    height = 16
    lane = lax.broadcasted_iota(jnp.int32, (height, LANES), 1)

    def piece(at, k):
        vectors = [x[at : at + height, v * LANES : (v + 1) * LANES] for v in range(out_count + 2)]
        left = REACH - 1 - jnp.broadcast_to(lags[at : at + height, k : k + 1], lane.shape)
        amp = jnp.broadcast_to(amps[at : at + height, k : k + 1], lane.shape)
        inside = left & (LANES - 1)
        index = (lane + inside) & (LANES - 1)
        far, same = left >= LANES, lane >= inside
        near = [jnp.where(far, vectors[v + 1], vectors[v]) for v in range(out_count + 1)]
        for v in range(out_count):
            joined = jnp.where(same, near[v], near[v + 1])
            turned = jnp.take_along_axis(joined, index, axis=1, mode="promise_in_bounds")
            high, low = two_terms(amp * turned)
            width = min(LANES, bin_count - v * LANES)
            to = slice(k * bin_count + v * LANES, k * bin_count + v * LANES + width)
            terms[at : at + height, to] = high[:, :width]
            terms[components + at : components + at + height, to] = low[:, :width]

    return [functools.partial(piece, at, k) for k in runs for at in range(0, components, height)]


def pair_kernel(mine_ref, came_ref, o_ref):
    rows = mine_ref.shape[0]
    freq_count = 2 * came_ref.shape[0]
    freq_rank = lax.axis_index("freq")
    apart = lax.bitwise_xor((freq_rank - 1) & (freq_count - 1), freq_rank)
    o_ref[0:rows, :] = came_ref[pl.ds(block_place(apart, freq_count), 1)][0]
    o_ref[rows:, :] = mine_ref[...]


def window_pair(mine, came):
    return pl.pallas_call(
        pair_kernel,
        out_shape=jax.ShapeDtypeStruct((2 * mine.shape[0], mine.shape[1]), mine.dtype),
        in_specs=vmem(2),
        out_specs=vmem(1)[0],
        compiler_params=pltpu.CompilerParams(vmem_limit_bytes=8 * MIB),
        name="window_pair",
    )(mine, came)


def elution_kernel(planes, *refs):
    amp_ref, lag_ref, terms, window = refs[-4:]
    components = amp_ref.shape[1]
    bin_count = terms.shape[1] // amp_ref.shape[0]
    freq_rank = lax.axis_index("freq")
    if planes:
        pair_ref, other_ref = refs[:2]
        mz_rank = lax.axis_index("mz")
        coded = pair_ref.shape[0] // 2
        rows = 2 * (coded - 16)
        skip = bin_count - REACH
        for ref, half in ((pair_ref, mz_rank), (other_ref, 1 - mz_rank)):
            for block in range(2):
                to = pl.multiple_of((2 * block + half) * rows, 64)
                values = decoded(ref[block * coded : (block + 1) * coded, :])
                half_rows = rows // 2
                window[pl.ds(to, half_rows), :] = values
                window[pl.ds(pl.multiple_of(to + half_rows, 32), half_rows), :] = pltpu.roll(values, LANES // 2, 1)
    else:
        own_ref = refs[0]
        step = own_ref.shape[1]
        steps = own_ref.shape[0]
        first = lax.rem(freq_rank * bin_count + steps * step - REACH, steps * step) // step
        skip = 0
        for j in range(window.shape[0] // step):
            window[j * step : (j + 1) * step, :] = own_ref[pl.ds(lax.rem(first + j, steps), 1)][0]
    pieces = []
    for at in range(skip, window.shape[0], LANES):
        piece = window[at : at + LANES, :].astype(jnp.float32).T
        pieces.append(piece[:components] if planes else piece[:components] + piece[components:])
    shifted_terms(jnp.concatenate(pieces, axis=1), amp_ref[...].T, lag_ref[...].T, bin_count, terms)


def elution_terms(elutions, loadings, shifts, bin_count):
    run_count, components = loadings.shape
    places = -(-(bin_count + REACH) // LANES)
    planes = len(elutions) > 1
    return pl.pallas_call(
        functools.partial(elution_kernel, planes),
        out_shape=jax.ShapeDtypeStruct((2 * components, run_count * bin_count), jnp.bfloat16),
        in_specs=vmem(len(elutions) + 2),
        out_specs=vmem(1)[0],
        scratch_shapes=[
            pltpu.VMEM((2 * bin_count, LANES), jnp.float32)
            if planes
            else pltpu.VMEM((places * LANES, LANES), jnp.bfloat16)
        ],
        compiler_params=pltpu.CompilerParams(vmem_limit_bytes=12 * MIB),
        cost_estimate=pl.CostEstimate(flops=1_000_000_000, bytes_accessed=2 * MIB, transcendentals=0),
        name="elution_terms",
    )(*elutions, loadings, shifts)


def product_kernel(parts, planes, *refs):
    i_ref = refs[0]
    g_refs = refs[1 : 1 + parts]
    elution_ref, amp_ref, lag_ref, num_ref, other_ref, terms, partial = refs[1 + parts :]
    run_count, bin_count, local_mz = i_ref.shape
    components = amp_ref.shape[1]
    chunk = 2 * LANES
    chunks = local_mz // chunk
    g = g_refs[0][...]
    if planes:
        period = bin_count // LANES
        x = decoded(g_refs[1][...])
        first, second, at = [], [], 0
        for a in range(period):
            if a + period < g.shape[1] // LANES:
                tile = x[at : at + LANES].T
                second.append(tile[components:])
                at += LANES
            else:
                half = x[at : at + LANES // 2]
                tile = jnp.concatenate([half, pltpu.roll(half, components, 1)], axis=0).T
                at += LANES // 2
            first.append(tile[:components])
        g = g + jnp.concatenate(first + second, axis=1)
    amps, lags = amp_ref[...].T, lag_ref[...].T
    middle = run_count // 2
    for piece in shift_pieces(g, amps, lags, bin_count, terms, range(middle)):
        piece()
    waiting = shift_pieces(g, amps, lags, bin_count, terms, range(middle, run_count))

    def multiply(n, first, last):
        data = i_ref[first:last, :, n * chunk : (n + 1) * chunk].reshape((last - first) * bin_count, chunk)
        made = jnp.dot(
            terms[:, first * bin_count : last * bin_count], data, preferred_element_type=jnp.float32
        )
        return made[:components] + made[components:]

    share = -(-len(waiting) // chunks)
    for n in range(chunks):
        partial[n] = multiply(n, 0, middle)
        for piece in waiting[n * share : (n + 1) * share]:
            piece()
    gram = lax.dot_general(
        terms[...], elution_ref[...], (((1,), (1,)), ((), ())), preferred_element_type=jnp.float32
    )
    gram = gram[:components] + gram[components:]
    gram = gram[:, :components] + gram[:, components:]
    if planes:
        keep_ref, send_ref = num_ref, other_ref
        half = components // 2
        gram = jnp.concatenate([gram[:half], gram[half:]], axis=1)
        keep_ref[chunks * components :, :] = gram
        send_ref[chunks * components :, :] = gram
    else:
        other_ref[...] = gram

    for n in range(chunks):
        made = partial[n] + multiply(n, middle, run_count)
        if planes:
            freq_rank = lax.axis_index("freq")
            core = freq_rank & 1
            place = block_place(lax.bitwise_xor(freq_rank, 2 * n + core), 2 * chunks)
            at = pl.ds(pl.multiple_of(place * components, components), components)
            even, odd = made[:, :LANES], made[:, LANES:]
            keep_ref[at, :] = jnp.where(core == 0, even, odd)
            send_ref[at, :] = jnp.where(core == 0, odd, even)
        else:
            num_ref[:, n * chunk : (n + 1) * chunk] = made


def product(intensity, models, elution, loadings, shifts, planes):
    run_count, bin_count, local_mz = intensity.shape
    components = loadings.shape[1]
    chunk = 2 * LANES
    chunks = local_mz // chunk
    if planes:
        out_shapes = [(chunks * components + components // 2, LANES)] * 2
    else:
        out_shapes = [(components, local_mz), (components, components)]
    return pl.pallas_call(
        functools.partial(product_kernel, len(models), planes),
        out_shape=tuple(jax.ShapeDtypeStruct(shape, jnp.float32) for shape in out_shapes),
        in_specs=vmem(len(models) + 4),
        out_specs=tuple(vmem(2)),
        scratch_shapes=[
            pltpu.VMEM((2 * components, run_count * bin_count), jnp.bfloat16),
            pltpu.VMEM((chunks, components, chunk), jnp.float32),
        ],
        compiler_params=pltpu.CompilerParams(vmem_limit_bytes=24 * MIB),
        cost_estimate=pl.CostEstimate(
            flops=8_000_000_000, bytes_accessed=2 * intensity.size, transcendentals=0
        ),
        name="model_products",
    )(intensity, *models, elution, loadings, shifts)


def inverse2(a, b, d):
    scale = 1.0 / (a * d - b * b)
    return d * scale, -b * scale, a * scale


def eliminate(gram, right):
    components = gram.shape[0]
    height = 8
    shape = (height, gram.shape[1])
    row_id = lax.broadcasted_iota(jnp.int32, shape, 0)
    starts = range(0, components, height)
    gram = [gram[at : at + height] for at in starts]
    right = [right[at : at + height] for at in starts]
    for j in range(0, components, 4):
        here, r = j // height, j % height
        columns = [[jnp.broadcast_to(tile[:, j + n : j + n + 1], shape) for tile in gram] for n in range(4)]
        pivot = [[columns[n][here][r + m : r + m + 1] for n in range(4)] for m in range(4)]
        a00, a01, a11 = inverse2(pivot[0][0], pivot[0][1], pivot[1][1])
        b00, b01, b10, b11 = pivot[0][2], pivot[0][3], pivot[1][2], pivot[1][3]
        w00, w01 = a00 * b00 + a01 * b10, a00 * b01 + a01 * b11
        w10, w11 = a01 * b00 + a11 * b10, a01 * b01 + a11 * b11
        s00, s01, s11 = inverse2(
            pivot[2][2] - (b00 * w00 + b10 * w10),
            pivot[2][3] - (b00 * w01 + b10 * w11),
            pivot[3][3] - (b01 * w01 + b11 * w11),
        )
        away = (row_id < r) | (row_id >= r + 4)
        for n in range(4):
            columns[n][here] = jnp.where(away, columns[n][here], jnp.where(row_id == r + n, -1.0, 0.0))
        gram_rows = [gram[here][r + n : r + n + 1] for n in range(4)]
        right_rows = [right[here][r + n : r + n + 1] for n in range(4)]
        gram[here] = jnp.where(away, gram[here], 0.0)
        right[here] = jnp.where(away[:, : right[here].shape[1]], right[here], 0.0)
        for t in range(len(gram)):
            c0, c1, c2, c3 = (columns[n][t] for n in range(4))
            t2, t3 = c2 - c0 * w00 - c1 * w10, c3 - c0 * w01 - c1 * w11
            f2, f3 = t2 * s00 + t3 * s01, t2 * s01 + t3 * s11
            f0 = c0 * a00 + c1 * a01 - f2 * w00 - f3 * w01
            f1 = c0 * a01 + c1 * a11 - f2 * w10 - f3 * w11
            for n, factor in enumerate((f0, f1, f2, f3)):
                gram[t] = gram[t] - factor * gram_rows[n]
                right[t] = right[t] - factor[:, : right[t].shape[1]] * right_rows[n]
    return jnp.concatenate(right, axis=0)


def total_of(refs, at, rows):
    total = refs[0][at : at + rows]
    for ref in refs[1:]:
        total = total + ref[at : at + rows]
    return total


def fixed_point(x, full):
    return jnp.clip(jnp.floor(x + 0.5), -full, full)


def as_int16(x):
    return x.astype(jnp.int32).astype(jnp.int16)


def row_level(x):
    peak = jnp.maximum(jnp.max(jnp.abs(x), axis=1, keepdims=True), 1e-30)
    return jnp.floor(256.0 / math.log(2.0) * jnp.log(peak)) + 1.0


def diagonal(x, rows):
    shape = (rows, LANES)
    on = lax.broadcasted_iota(jnp.int32, shape, 0) == lax.broadcasted_iota(jnp.int32, shape, 1)
    return jnp.where(on, jnp.broadcast_to(x, shape), 0.0)


def encode_rows(x, gram, o_ref):
    rows, tail = x.shape[0], gram.shape[0]
    parts = [x[at : at + LANES] for at in range(0, rows, LANES)]
    levels = [row_level(part) for part in parts] + [row_level(gram)]
    at = 0
    for part, level in zip(parts, levels):
        o_ref[at : at + part.shape[0], :] = as_int16(fixed_point(part * (FULL / scale_of(level)), FULL))
        at += part.shape[0]
    scaled = gram * (FULL / scale_of(levels[-1]))
    high = fixed_point(scaled, FULL)
    o_ref[at : at + tail, :] = as_int16(high)
    o_ref[at + tail : at + 2 * tail, :] = as_int16(fixed_point((scaled - high) * (2 * FULL), FULL))
    row_id = lax.broadcasted_iota(jnp.int32, (16, LANES), 0)
    block = jnp.zeros((16, LANES), jnp.float32)
    for n, level in enumerate(levels):
        lanes = jnp.sum(diagonal(level, level.shape[0]), axis=0, keepdims=True)
        block = jnp.where(row_id == n, lanes, block)
    o_ref[at + 2 * tail :, :] = as_int16(block)


def decode_rows(ref, tail):
    rows = ref.shape[0] - 2 * tail - 16
    x = ref[...].astype(jnp.int32).astype(jnp.float32)

    def scale(n, count):
        at = rows + 2 * tail + n
        return scale_of(jnp.sum(diagonal(x[at : at + 1], count), axis=1, keepdims=True)) * (1.0 / FULL)

    parts = []
    for n, at in enumerate(range(0, rows, LANES)):
        count = min(LANES, rows - at)
        parts.append(x[at : at + count] * scale(n, count))
    gram = x[rows : rows + tail] + x[rows + tail : rows + 2 * tail] * (0.5 / FULL)
    return jnp.concatenate(parts, axis=0), gram * scale(len(parts), tail)


def halve_kernel(tail, a_ref, b_ref, o_ref):
    rows = o_ref.shape[0] - 2 * tail - 16
    total = total_of((a_ref, b_ref), rows, rows + tail)
    encode_rows(total[:rows], total[rows:], o_ref)


def spread_kernel(tail, a_ref, b_ref, c_ref, own_ref, *outs):
    rows = own_ref.shape[0] - tail
    count = len(outs) + 1
    total, gram = decode_rows(c_ref, tail)
    total = total + total_of((a_ref, b_ref), 0, count * rows)
    gram = gram + total_of((a_ref, b_ref), 2 * count * rows, tail)
    own_ref[0:rows, :] = total[:rows]
    own_ref[rows:, :] = gram
    for n, o_ref in enumerate(outs):
        encode_rows(total[(n + 1) * rows : (n + 2) * rows], gram, o_ref)


def solve_planes_kernel(own_ref, *refs):
    o_ref = refs[-1]
    components = o_ref.shape[0]
    total, gram = own_ref[:components], own_ref[components:]
    for ref in refs[:-1]:
        part, gram_part = decode_rows(ref, gram.shape[0])
        total, gram = total + part, gram + gram_part
    gram = jnp.concatenate([gram, pltpu.roll(gram, gram.shape[1] // 2, 1)], axis=0)
    o_ref[...] = eliminate(gram, total)


def solve_kernel(g_ref, n_ref, o_ref):
    components = o_ref.shape[0]
    gram = jnp.concatenate([g_ref[...], jnp.zeros((components, LANES - components), jnp.float32)], axis=1)
    o_ref[...] = eliminate(gram, n_ref[...])


def small_call(kernel, outs, name, *args):
    return pl.pallas_call(
        kernel,
        out_shape=tuple(jax.ShapeDtypeStruct(shape, dtype) for shape, dtype in outs),
        in_specs=vmem(len(args)),
        out_specs=tuple(vmem(len(outs))),
        compiler_params=pltpu.CompilerParams(vmem_limit_bytes=8 * MIB),
        name=name,
    )(*args)


def swap(x, axes, count, value):
    return lax.ppermute(x, axes, [(i, i ^ value) for i in range(count)])


def on_device(intensity, elution, loadings, shifts, bin_weight):
    freq_count = lax.axis_size("freq")
    mz_count = lax.axis_size("mz")
    components = loadings.shape[1]
    bin_count = intensity.shape[1]
    axes = ("freq", "mz")
    own = intensity.shape[2] // freq_count
    planes = (
        own == LANES
        and 2 * components == LANES
        and mz_count == 2
        and freq_count & (freq_count - 1) == 0
        and freq_count >= 8
        and elution.shape[0] % 64 == 0
        and bin_count % LANES == 0
        and bin_count >= REACH
    )
    if not planes:
        mine = pack(elution)
        gathered = lax.all_gather(mine, axes, axis=0).reshape(-1, math.gcd(bin_count, LANES), LANES)
        (g,) = partial_model((gathered,), circulant(bin_weight.reshape(LANES, -1), 0), bin_count, components)
        shifted = elution_terms((gathered,), loadings, shifts, bin_count)
        numerator, gram = product(intensity, (g,), shifted, loadings, shifts, planes)
        gram = lax.psum(gram, "freq")
        owned = lax.psum_scatter(numerator, "freq", scatter_dimension=1, tiled=True)
        return small_call(solve_kernel, [((components, own), jnp.float32)], "solve", gram, owned)[0]
    mine = encode(elution)
    z_steps = range(4, freq_count, 4)
    held = jnp.stack([mine] + [swap(mine, "freq", freq_count, step) for step in z_steps])
    weights = bin_weight.reshape(LANES, -1)
    held, weights = lax.optimization_barrier((held, weights))
    held = jnp.concatenate([held, swap(held, "freq", freq_count, 2)], axis=0)
    u = circulant(weights, elution.shape[0])
    held, u = lax.optimization_barrier((held, u))
    came = swap(held, "freq", freq_count, 1)
    pair = window_pair(mine, came)
    other = swap(pair, "mz", mz_count, 1)
    g, coded = partial_model((held, came), u, bin_count, components)
    coded, other = lax.optimization_barrier((coded, other))
    models = (g, swap(coded, "mz", mz_count, 1))
    shifted = elution_terms((pair, other), loadings, shifts, bin_count)
    keep, send = product(intensity, models, shifted, loadings, shifts, planes)
    tail = components // 2
    chips = freq_count // 4
    came = swap(send, "freq", freq_count, 1)
    coded = 2 * tail + 16
    (send,) = small_call(
        functools.partial(halve_kernel, tail),
        [((chips * components + coded, LANES), jnp.int16)],
        "reduce_cores",
        keep,
        came,
    )
    across = swap(send, "freq", freq_count, 2)
    own_part, *sends = small_call(
        functools.partial(spread_kernel, tail),
        [((components + tail, LANES), jnp.float32)] + [((components + coded, LANES), jnp.int16)] * (chips - 1),
        "reduce_x",
        keep,
        came,
        across,
    )
    parts = [swap(send, "freq", freq_count, step) for send, step in zip(sends, z_steps)][::-1]
    return small_call(
        solve_planes_kernel, [((components, own), jnp.float32)], "solve", own_part, *parts
    )[0]


def solution(mesh):
    in_specs = (P(None, "freq", "mz"), P(("freq", "mz"), None), P(), P(), P())
    out_specs = P(None, ("mz", "freq"))
    return jax.shard_map(on_device, mesh=mesh, in_specs=in_specs, out_specs=out_specs, check_vma=False)
```

```python
import functools
import math

import jax
import jax.numpy as jnp
import numpy as np
from jax import lax
from jax.experimental import pallas as pl
from jax.experimental.pallas import tpu as pltpu
from jax.sharding import PartitionSpec as P

PRECISE = lax.Precision.HIGHEST
LANES = 128
REACH = 256
MIB = 1024 * 1024
FULL = 32767.0


def f32_dot(a, b, dims=(((1,), (0,)), ((), ()))):
    return lax.dot_general(a, b, dims, precision=PRECISE, preferred_element_type=jnp.float32)


def two_terms(x):
    high = x.astype(jnp.bfloat16)
    low = (x - high.astype(jnp.float32)).astype(jnp.bfloat16)
    return high, low


def vmem(count):
    return [pl.BlockSpec(memory_space=pltpu.VMEM)] * count


def pack_kernel(x_ref, o_ref):
    x = x_ref[...]
    components, rows = x.shape
    pad = -rows % LANES
    if pad:
        x = jnp.concatenate([x, jnp.zeros((components, pad), x.dtype)], axis=1)
    high, low = two_terms(x.T[:rows])
    o_ref[...] = jnp.concatenate([high, low], axis=1)


def pack(elution):
    rows, components = elution.shape
    return pl.pallas_call(
        pack_kernel,
        out_shape=jax.ShapeDtypeStruct((rows, 2 * components), jnp.bfloat16),
        in_specs=vmem(1),
        out_specs=vmem(1)[0],
        compiler_params=pltpu.CompilerParams(vmem_limit_bytes=8 * MIB),
        name="pack_elution",
    )(elution.T)


def encode_kernel(x_ref, o_ref):
    components, rows = x_ref.shape
    half = rows // 2
    x = x_ref[...]
    pad = -rows % LANES
    x = jnp.concatenate([x, jnp.zeros((components, pad), x.dtype)], axis=1).T[:rows]
    peak = jnp.maximum(jnp.max(jnp.abs(x), axis=0, keepdims=True), 1e-30)
    level = jnp.floor(256.0 / math.log(2.0) * jnp.log(peak)) + 1.0
    x = x * (FULL / scale_of(level))
    x = jnp.clip(jnp.floor(x + 0.5), -FULL, FULL).astype(jnp.int32).astype(jnp.int16)
    o_ref[0:half, :] = jnp.concatenate([x[:half], x[half:]], axis=1)
    level = jnp.broadcast_to(level, (16, components)).astype(jnp.int32).astype(jnp.int16)
    o_ref[half:, :] = jnp.concatenate([level, level], axis=1)


def encode_columns(x, o_ref):
    rows = x.shape[0]
    peak = jnp.maximum(jnp.max(jnp.abs(x), axis=0, keepdims=True), 1e-30)
    level = jnp.floor(256.0 / math.log(2.0) * jnp.log(peak)) + 1.0
    x = jnp.clip(jnp.floor(x * (FULL / scale_of(level)) + 0.5), -FULL, FULL)
    o_ref[0:rows, :] = x.astype(jnp.int32).astype(jnp.int16)
    o_ref[rows:, :] = jnp.broadcast_to(level, (16, x.shape[1])).astype(jnp.int32).astype(jnp.int16)


def scale_of(level):
    return jnp.exp(math.log(2.0) / 256.0 * level)


def decoded(x):
    half = x.shape[0] - 16
    x = x.astype(jnp.int32).astype(jnp.float32)
    return x[:half] * (scale_of(x[half : half + 1]) * (1.0 / FULL))


def decoded_terms(x):
    x = decoded(x)
    high = x.astype(jnp.bfloat16).astype(jnp.float32)
    low = x - high
    left = lax.broadcasted_iota(jnp.int32, x.shape, 1) < LANES // 2
    top = jnp.where(left, high, pltpu.roll(low, LANES // 2, 1))
    bottom = jnp.where(left, pltpu.roll(high, LANES // 2, 1), low)
    return jnp.concatenate([top, bottom], axis=0).astype(jnp.bfloat16)


def encode(elution):
    rows, components = elution.shape
    return pl.pallas_call(
        encode_kernel,
        out_shape=jax.ShapeDtypeStruct((rows // 2 + 16, 2 * components), jnp.int16),
        in_specs=vmem(1),
        out_specs=vmem(1)[0],
        compiler_params=pltpu.CompilerParams(vmem_limit_bytes=8 * MIB),
        name="encode_elution",
    )(elution.T)


def circulant_kernel(turn, w_ref, table_ref, u_ref):
    rows = w_ref.shape[1]
    w = w_ref[...]
    over_lanes = (((0,), (0,)), ((), ()))

    def table(at, height, width):
        return table_ref[at : at + height, :width], table_ref[at + height : at + 2 * height, :width]

    lane_cos, lane_sin = table(0, LANES, LANES)
    twid_cos, twid_sin = table(2 * LANES, rows, LANES)
    row_cos, row_sin = table(2 * LANES + 2 * rows, rows, rows)
    a_re = f32_dot(w, lane_cos, over_lanes)
    a_im = -f32_dot(w, lane_sin, over_lanes)
    b_re = a_re * twid_cos + a_im * twid_sin
    b_im = a_im * twid_cos - a_re * twid_sin
    c = f32_dot(row_cos, b_re) + f32_dot(row_sin, b_im)
    sub = lax.broadcasted_iota(jnp.int32, (LANES, LANES), 0)
    lane = lax.broadcasted_iota(jnp.int32, (LANES, LANES), 1)

    if turn:
        part = LANES - turn % LANES
        near, after = (
            pltpu.roll(jnp.concatenate([c[n:], c[:n]], axis=0), part % LANES, 1)
            for n in (turn // LANES, turn // LANES + 1)
        )
        moved = jnp.where(lax.broadcasted_iota(jnp.int32, c.shape, 1) < part, near, after)
        c = jnp.where(lax.axis_index("mz") == 1, moved, c)

    def turned(row):
        return pltpu.roll(jnp.broadcast_to(c[row : row + 1], (LANES, LANES)), 0, 1, stride=1, stride_axis=0)

    before = turned(rows - 1)
    for row in range(rows):
        now = turned(row)
        high, low = two_terms(jnp.where(lane >= sub, now, before))
        u_ref[0:LANES, row * LANES : (row + 1) * LANES] = high
        u_ref[LANES:, row * LANES : (row + 1) * LANES] = low
        before = now


def circulant(weights, turn):
    length = weights.size
    rows = length // LANES

    def tables(a, b, period):
        angle = 2.0 * math.pi / period * ((a[:, None] * b[None, :]) % period)
        return np.pad(np.concatenate([np.cos(angle), np.sin(angle)]), ((0, 0), (0, LANES - b.size)))

    lane_ids, row_ids = np.arange(LANES), np.arange(rows)
    table = np.concatenate(
        [
            tables(lane_ids, lane_ids, LANES),
            tables(row_ids, lane_ids, length),
            tables(row_ids, row_ids, rows) / length,
        ]
    ).astype(np.float32)
    return pl.pallas_call(
        functools.partial(circulant_kernel, turn),
        out_shape=jax.ShapeDtypeStruct((2 * LANES, length), jnp.bfloat16),
        in_specs=vmem(2),
        out_specs=vmem(1)[0],
        compiler_params=pltpu.CompilerParams(vmem_limit_bytes=16 * MIB),
        cost_estimate=pl.CostEstimate(flops=2_000_000_000, bytes_accessed=4 * MIB, transcendentals=0),
        name="circulant_block",
    )(weights, table)


def model_kernel(places, planes, *refs):
    if planes:
        u_ref, g_ref, coded_ref, wide = refs[-4:]
    else:
        u_ref, g_ref, wide = refs[-3:]
    length = u_ref.shape[1]
    components = g_ref.shape[0]
    freq_rank = lax.axis_index("freq")
    if planes:
        own_ref, came_ref = refs[:2]
        freq_count = 2 * own_ref.shape[0]
        rows = 2 * (own_ref.shape[1] - 16)
        padded = wide.shape[0] // freq_count
        for block in range(freq_count):
            apart = lax.bitwise_xor((freq_rank + block) & (freq_count - 1), freq_rank)
            ref = came_ref if block % 2 else own_ref
            values = decoded_terms(ref[pl.ds(block_place(apart, freq_count), 1)][0])
            at, before = block * padded, (block - 1) % freq_count * padded
            wide[at : at + rows, 0:LANES] = values
            wide[before : before + rows, LANES:] = values
            wide[at + rows : at + padded, :] = jnp.zeros((padded - rows, 2 * LANES), jnp.bfloat16)
        period = length // freq_count // LANES
        left = lax.broadcasted_iota(jnp.int32, (LANES, LANES), 1) < components
        sides = []
        for a in range(period):
            columns = []
            for block in range(freq_count):
                first = REACH // LANES + period * block - a
                for n in range(first, first + padded // LANES):
                    at = n % (length // LANES) * LANES
                    columns.append(u_ref[:, at : at + LANES])
            width = 2 * LANES if a + period < places else LANES
            made = jnp.dot(
                jnp.concatenate(columns, axis=1), wide[:, :width], preferred_element_type=jnp.float32
            )
            made = made[:LANES] + made[LANES:]
            tiles = []
            for half in range(width // LANES):
                tile = made[:, half * LANES : (half + 1) * LANES]
                tiles.append(tile + pltpu.roll(tile, components, 1))
                to = (a + half * period) * LANES
                g_ref[:, to : to + LANES] = tiles[-1].T[:components]
            if len(tiles) == 1:
                half = LANES // 2
                sides.append(jnp.where(left[:half], tiles[0][:half], tiles[0][half:]))
            else:
                sides.append(jnp.where(left, tiles[0], tiles[1]))
        encode_columns(jnp.concatenate(sides, axis=0), coded_ref)
        return
    own_ref = refs[0]
    step = own_ref.shape[1]
    steps = length // step
    bin_count = length // lax.axis_size("freq")
    first = lax.rem(freq_rank * bin_count + length - REACH, length) // step

    def bring(j, carry):
        values = own_ref[pl.ds(lax.rem(first + j, steps), 1)][0]
        to = pl.multiple_of(REACH + j * step, step)
        wide[pl.ds(to, step), 0:LANES] = values
        wide[pl.ds(pl.multiple_of(to - LANES, step), step), LANES:] = values
        return carry

    lax.fori_loop(0, (wide.shape[0] - REACH) // step, bring, 0)
    for a in range(0, places, 2):
        at = REACH + a * LANES
        made = jnp.dot(u_ref[...], wide[at : at + length, :], preferred_element_type=jnp.float32)
        made = made[:LANES] + made[LANES:]
        for half in range(min(2, places - a)):
            piece = made[:, half * LANES : (half + 1) * LANES].T
            g_ref[:, (a + half) * LANES : (a + half + 1) * LANES] = piece[:components] + piece[components:]


def block_place(apart, freq_count):
    return (apart >> 2) + ((apart >> 1) & 1) * (freq_count // 4)


def partial_model(gathered, u, bin_count, components):
    length = u.shape[1]
    places = -(-(bin_count + REACH) // LANES)
    planes = len(gathered) == 2
    if planes:
        own = gathered[0]
        wide_rows = 2 * own.shape[0] * (-(-2 * (own.shape[1] - 16) // LANES) * LANES)
    else:
        wide_rows = REACH + length + 2 * LANES * ((places - 1) // 2)
    outs = [jax.ShapeDtypeStruct((components, places * LANES), jnp.float32)]
    if planes:
        outs.append(jax.ShapeDtypeStruct((places * LANES // 2 + 16, LANES), jnp.int16))
    return pl.pallas_call(
        functools.partial(model_kernel, places, planes),
        out_shape=tuple(outs),
        in_specs=vmem(len(gathered) + 1),
        out_specs=tuple(vmem(len(outs))),
        scratch_shapes=[pltpu.VMEM((wide_rows, 2 * LANES), jnp.bfloat16)],
        compiler_params=pltpu.CompilerParams(vmem_limit_bytes=24 * MIB),
        cost_estimate=pl.CostEstimate(flops=2_000_000_000, bytes_accessed=4 * MIB, transcendentals=0),
        name="partial_model",
    )(*gathered, u)


def shifted_terms(x, amps, lags, bin_count, terms):
    for piece in shift_pieces(x, amps, lags, bin_count, terms, range(amps.shape[1])):
        piece()


def shift_pieces(x, amps, lags, bin_count, terms, runs):
    components = x.shape[0]
    out_count = -(-bin_count // LANES)
    x = pltpu.roll(x, x.shape[1] - 1, 1)
    height = 16
    lane = lax.broadcasted_iota(jnp.int32, (height, LANES), 1)

    def piece(at, k):
        vectors = [x[at : at + height, v * LANES : (v + 1) * LANES] for v in range(out_count + 2)]
        left = REACH - 1 - jnp.broadcast_to(lags[at : at + height, k : k + 1], lane.shape)
        amp = jnp.broadcast_to(amps[at : at + height, k : k + 1], lane.shape)
        inside = left & (LANES - 1)
        index = (lane + inside) & (LANES - 1)
        far, same = left >= LANES, lane >= inside
        near = [jnp.where(far, vectors[v + 1], vectors[v]) for v in range(out_count + 1)]
        for v in range(out_count):
            joined = jnp.where(same, near[v], near[v + 1])
            turned = jnp.take_along_axis(joined, index, axis=1, mode="promise_in_bounds")
            high, low = two_terms(amp * turned)
            width = min(LANES, bin_count - v * LANES)
            to = slice(k * bin_count + v * LANES, k * bin_count + v * LANES + width)
            terms[at : at + height, to] = high[:, :width]
            terms[components + at : components + at + height, to] = low[:, :width]

    return [functools.partial(piece, at, k) for k in runs for at in range(0, components, height)]


def pair_kernel(mine_ref, came_ref, o_ref):
    rows = mine_ref.shape[0]
    freq_count = 2 * came_ref.shape[0]
    freq_rank = lax.axis_index("freq")
    apart = lax.bitwise_xor((freq_rank - 1) & (freq_count - 1), freq_rank)
    o_ref[0:rows, :] = came_ref[pl.ds(block_place(apart, freq_count), 1)][0]
    o_ref[rows:, :] = mine_ref[...]


def window_pair(mine, came):
    return pl.pallas_call(
        pair_kernel,
        out_shape=jax.ShapeDtypeStruct((2 * mine.shape[0], mine.shape[1]), mine.dtype),
        in_specs=vmem(2),
        out_specs=vmem(1)[0],
        compiler_params=pltpu.CompilerParams(vmem_limit_bytes=8 * MIB),
        name="window_pair",
    )(mine, came)


def elution_kernel(planes, *refs):
    amp_ref, lag_ref, terms, window = refs[-4:]
    components = amp_ref.shape[1]
    bin_count = terms.shape[1] // amp_ref.shape[0]
    freq_rank = lax.axis_index("freq")
    if planes:
        pair_ref, other_ref = refs[:2]
        mz_rank = lax.axis_index("mz")
        coded = pair_ref.shape[0] // 2
        rows = 2 * (coded - 16)
        skip = bin_count - REACH
        for ref, half in ((pair_ref, mz_rank), (other_ref, 1 - mz_rank)):
            for block in range(2):
                to = pl.multiple_of((2 * block + half) * rows, 64)
                values = decoded(ref[block * coded : (block + 1) * coded, :])
                half_rows = rows // 2
                window[pl.ds(to, half_rows), :] = values
                window[pl.ds(pl.multiple_of(to + half_rows, 32), half_rows), :] = pltpu.roll(values, LANES // 2, 1)
    else:
        own_ref = refs[0]
        step = own_ref.shape[1]
        steps = own_ref.shape[0]
        first = lax.rem(freq_rank * bin_count + steps * step - REACH, steps * step) // step
        skip = 0
        for j in range(window.shape[0] // step):
            window[j * step : (j + 1) * step, :] = own_ref[pl.ds(lax.rem(first + j, steps), 1)][0]
    pieces = []
    for at in range(skip, window.shape[0], LANES):
        piece = window[at : at + LANES, :].astype(jnp.float32).T
        pieces.append(piece[:components] if planes else piece[:components] + piece[components:])
    shifted_terms(jnp.concatenate(pieces, axis=1), amp_ref[...].T, lag_ref[...].T, bin_count, terms)


def elution_terms(elutions, loadings, shifts, bin_count):
    run_count, components = loadings.shape
    places = -(-(bin_count + REACH) // LANES)
    planes = len(elutions) > 1
    return pl.pallas_call(
        functools.partial(elution_kernel, planes),
        out_shape=jax.ShapeDtypeStruct((2 * components, run_count * bin_count), jnp.bfloat16),
        in_specs=vmem(len(elutions) + 2),
        out_specs=vmem(1)[0],
        scratch_shapes=[
            pltpu.VMEM((2 * bin_count, LANES), jnp.float32)
            if planes
            else pltpu.VMEM((places * LANES, LANES), jnp.bfloat16)
        ],
        compiler_params=pltpu.CompilerParams(vmem_limit_bytes=12 * MIB),
        cost_estimate=pl.CostEstimate(flops=1_000_000_000, bytes_accessed=2 * MIB, transcendentals=0),
        name="elution_terms",
    )(*elutions, loadings, shifts)


def product_kernel(parts, planes, *refs):
    i_ref = refs[0]
    g_refs = refs[1 : 1 + parts]
    elution_ref, amp_ref, lag_ref, num_ref, other_ref, terms, partial = refs[1 + parts :]
    run_count, bin_count, local_mz = i_ref.shape
    components = amp_ref.shape[1]
    chunk = 2 * LANES
    chunks = local_mz // chunk
    g = g_refs[0][...]
    if planes:
        period = bin_count // LANES
        x = decoded(g_refs[1][...])
        first, second, at = [], [], 0
        for a in range(period):
            if a + period < g.shape[1] // LANES:
                tile = x[at : at + LANES].T
                second.append(tile[components:])
                at += LANES
            else:
                half = x[at : at + LANES // 2]
                tile = jnp.concatenate([half, pltpu.roll(half, components, 1)], axis=0).T
                at += LANES // 2
            first.append(tile[:components])
        g = g + jnp.concatenate(first + second, axis=1)
    amps, lags = amp_ref[...].T, lag_ref[...].T
    group = max(run_count // 4, 1)
    firsts = range(0, run_count, group)

    def shifts(first):
        return shift_pieces(g, amps, lags, bin_count, terms, range(first, first + group))

    for piece in shifts(0):
        piece()

    def multiply(n, first, last):
        data = i_ref[first:last, :, n * chunk : (n + 1) * chunk].reshape((last - first) * bin_count, chunk)
        made = jnp.dot(
            terms[:, first * bin_count : last * bin_count], data, preferred_element_type=jnp.float32
        )
        return made[:components] + made[components:]

    for first in firsts[:-1]:
        waiting = shifts(first + group)
        share = -(-len(waiting) // chunks)
        for n in range(chunks):
            made = multiply(n, first, first + group)
            partial[n] = made if first == 0 else partial[n] + made
            for piece in waiting[n * share : (n + 1) * share]:
                piece()
    gram = lax.dot_general(
        terms[...], elution_ref[...], (((1,), (1,)), ((), ())), preferred_element_type=jnp.float32
    )
    gram = gram[:components] + gram[components:]
    gram = gram[:, :components] + gram[:, components:]
    if planes:
        keep_ref, send_ref = num_ref, other_ref
        half = components // 2
        gram = jnp.concatenate([gram[:half], gram[half:]], axis=1)
        keep_ref[chunks * components :, :] = gram
        send_ref[chunks * components :, :] = gram
    else:
        other_ref[...] = gram

    for n in range(chunks):
        made = partial[n] + multiply(n, firsts[-1], run_count)
        if planes:
            freq_rank = lax.axis_index("freq")
            core = freq_rank & 1
            place = block_place(lax.bitwise_xor(freq_rank, 2 * n + core), 2 * chunks)
            at = pl.ds(pl.multiple_of(place * components, components), components)
            even, odd = made[:, :LANES], made[:, LANES:]
            keep_ref[at, :] = jnp.where(core == 0, even, odd)
            send_ref[at, :] = jnp.where(core == 0, odd, even)
        else:
            num_ref[:, n * chunk : (n + 1) * chunk] = made


def product(intensity, models, elution, loadings, shifts, planes):
    run_count, bin_count, local_mz = intensity.shape
    components = loadings.shape[1]
    chunk = 2 * LANES
    chunks = local_mz // chunk
    if planes:
        out_shapes = [(chunks * components + components // 2, LANES)] * 2
    else:
        out_shapes = [(components, local_mz), (components, components)]
    return pl.pallas_call(
        functools.partial(product_kernel, len(models), planes),
        out_shape=tuple(jax.ShapeDtypeStruct(shape, jnp.float32) for shape in out_shapes),
        in_specs=vmem(len(models) + 4),
        out_specs=tuple(vmem(2)),
        scratch_shapes=[
            pltpu.VMEM((2 * components, run_count * bin_count), jnp.bfloat16),
            pltpu.VMEM((chunks, components, chunk), jnp.float32),
        ],
        compiler_params=pltpu.CompilerParams(vmem_limit_bytes=24 * MIB),
        cost_estimate=pl.CostEstimate(
            flops=8_000_000_000, bytes_accessed=2 * intensity.size, transcendentals=0
        ),
        name="model_products",
    )(intensity, *models, elution, loadings, shifts)


def inverse2(a, b, d):
    scale = 1.0 / (a * d - b * b)
    return d * scale, -b * scale, a * scale


def eliminate(gram, right):
    components = gram.shape[0]
    height = 8
    shape = (height, gram.shape[1])
    row_id = lax.broadcasted_iota(jnp.int32, shape, 0)
    starts = range(0, components, height)
    gram = [gram[at : at + height] for at in starts]
    right = [right[at : at + height] for at in starts]
    for j in range(0, components, 4):
        here, r = j // height, j % height
        columns = [[jnp.broadcast_to(tile[:, j + n : j + n + 1], shape) for tile in gram] for n in range(4)]
        pivot = [[columns[n][here][r + m : r + m + 1] for n in range(4)] for m in range(4)]
        a00, a01, a11 = inverse2(pivot[0][0], pivot[0][1], pivot[1][1])
        b00, b01, b10, b11 = pivot[0][2], pivot[0][3], pivot[1][2], pivot[1][3]
        w00, w01 = a00 * b00 + a01 * b10, a00 * b01 + a01 * b11
        w10, w11 = a01 * b00 + a11 * b10, a01 * b01 + a11 * b11
        s00, s01, s11 = inverse2(
            pivot[2][2] - (b00 * w00 + b10 * w10),
            pivot[2][3] - (b00 * w01 + b10 * w11),
            pivot[3][3] - (b01 * w01 + b11 * w11),
        )
        away = (row_id < r) | (row_id >= r + 4)
        for n in range(4):
            columns[n][here] = jnp.where(away, columns[n][here], jnp.where(row_id == r + n, -1.0, 0.0))
        gram_rows = [gram[here][r + n : r + n + 1] for n in range(4)]
        right_rows = [right[here][r + n : r + n + 1] for n in range(4)]
        gram[here] = jnp.where(away, gram[here], 0.0)
        right[here] = jnp.where(away[:, : right[here].shape[1]], right[here], 0.0)
        for t in range(len(gram)):
            c0, c1, c2, c3 = (columns[n][t] for n in range(4))
            t2, t3 = c2 - c0 * w00 - c1 * w10, c3 - c0 * w01 - c1 * w11
            f2, f3 = t2 * s00 + t3 * s01, t2 * s01 + t3 * s11
            f0 = c0 * a00 + c1 * a01 - f2 * w00 - f3 * w01
            f1 = c0 * a01 + c1 * a11 - f2 * w10 - f3 * w11
            for n, factor in enumerate((f0, f1, f2, f3)):
                gram[t] = gram[t] - factor * gram_rows[n]
                right[t] = right[t] - factor[:, : right[t].shape[1]] * right_rows[n]
    return jnp.concatenate(right, axis=0)


def total_of(refs, at, rows):
    total = refs[0][at : at + rows]
    for ref in refs[1:]:
        total = total + ref[at : at + rows]
    return total


def fixed_point(x, full):
    return jnp.clip(jnp.floor(x + 0.5), -full, full)


def as_int16(x):
    return x.astype(jnp.int32).astype(jnp.int16)


def row_level(x):
    peak = jnp.maximum(jnp.max(jnp.abs(x), axis=1, keepdims=True), 1e-30)
    return jnp.floor(256.0 / math.log(2.0) * jnp.log(peak)) + 1.0


def diagonal(x, rows):
    shape = (rows, LANES)
    on = lax.broadcasted_iota(jnp.int32, shape, 0) == lax.broadcasted_iota(jnp.int32, shape, 1)
    return jnp.where(on, jnp.broadcast_to(x, shape), 0.0)


def encode_rows(x, gram, o_ref):
    rows, tail = x.shape[0], gram.shape[0]
    parts = [x[at : at + LANES] for at in range(0, rows, LANES)]
    levels = [row_level(part) for part in parts] + [row_level(gram)]
    at = 0
    for part, level in zip(parts, levels):
        o_ref[at : at + part.shape[0], :] = as_int16(fixed_point(part * (FULL / scale_of(level)), FULL))
        at += part.shape[0]
    scaled = gram * (FULL / scale_of(levels[-1]))
    high = fixed_point(scaled, FULL)
    o_ref[at : at + tail, :] = as_int16(high)
    o_ref[at + tail : at + 2 * tail, :] = as_int16(fixed_point((scaled - high) * (2 * FULL), FULL))
    row_id = lax.broadcasted_iota(jnp.int32, (16, LANES), 0)
    block = jnp.zeros((16, LANES), jnp.float32)
    for n, level in enumerate(levels):
        lanes = jnp.sum(diagonal(level, level.shape[0]), axis=0, keepdims=True)
        block = jnp.where(row_id == n, lanes, block)
    o_ref[at + 2 * tail :, :] = as_int16(block)


def decode_rows(ref, tail):
    rows = ref.shape[0] - 2 * tail - 16
    x = ref[...].astype(jnp.int32).astype(jnp.float32)

    def scale(n, count):
        at = rows + 2 * tail + n
        return scale_of(jnp.sum(diagonal(x[at : at + 1], count), axis=1, keepdims=True)) * (1.0 / FULL)

    parts = []
    for n, at in enumerate(range(0, rows, LANES)):
        count = min(LANES, rows - at)
        parts.append(x[at : at + count] * scale(n, count))
    gram = x[rows : rows + tail] + x[rows + tail : rows + 2 * tail] * (0.5 / FULL)
    return jnp.concatenate(parts, axis=0), gram * scale(len(parts), tail)


def halve_kernel(tail, a_ref, b_ref, o_ref):
    rows = o_ref.shape[0] - 2 * tail - 16
    total = total_of((a_ref, b_ref), rows, rows + tail)
    encode_rows(total[:rows], total[rows:], o_ref)


def spread_kernel(tail, a_ref, b_ref, c_ref, own_ref, *outs):
    rows = own_ref.shape[0] - tail
    count = len(outs) + 1
    total, gram = decode_rows(c_ref, tail)
    total = total + total_of((a_ref, b_ref), 0, count * rows)
    gram = gram + total_of((a_ref, b_ref), 2 * count * rows, tail)
    own_ref[0:rows, :] = total[:rows]
    own_ref[rows:, :] = gram
    for n, o_ref in enumerate(outs):
        encode_rows(total[(n + 1) * rows : (n + 2) * rows], gram, o_ref)


def solve_planes_kernel(own_ref, *refs):
    o_ref = refs[-1]
    components = o_ref.shape[0]
    total, gram = own_ref[:components], own_ref[components:]
    for ref in refs[:-1]:
        part, gram_part = decode_rows(ref, gram.shape[0])
        total, gram = total + part, gram + gram_part
    gram = jnp.concatenate([gram, pltpu.roll(gram, gram.shape[1] // 2, 1)], axis=0)
    o_ref[...] = eliminate(gram, total)


def solve_kernel(g_ref, n_ref, o_ref):
    components = o_ref.shape[0]
    gram = jnp.concatenate([g_ref[...], jnp.zeros((components, LANES - components), jnp.float32)], axis=1)
    o_ref[...] = eliminate(gram, n_ref[...])


def small_call(kernel, outs, name, *args):
    return pl.pallas_call(
        kernel,
        out_shape=tuple(jax.ShapeDtypeStruct(shape, dtype) for shape, dtype in outs),
        in_specs=vmem(len(args)),
        out_specs=tuple(vmem(len(outs))),
        compiler_params=pltpu.CompilerParams(vmem_limit_bytes=8 * MIB),
        name=name,
    )(*args)


def swap(x, axes, count, value):
    return lax.ppermute(x, axes, [(i, i ^ value) for i in range(count)])


def on_device(intensity, elution, loadings, shifts, bin_weight):
    freq_count = lax.axis_size("freq")
    mz_count = lax.axis_size("mz")
    components = loadings.shape[1]
    bin_count = intensity.shape[1]
    axes = ("freq", "mz")
    own = intensity.shape[2] // freq_count
    planes = (
        own == LANES
        and 2 * components == LANES
        and mz_count == 2
        and freq_count & (freq_count - 1) == 0
        and freq_count >= 8
        and elution.shape[0] % 64 == 0
        and bin_count % LANES == 0
        and bin_count >= REACH
    )
    if not planes:
        mine = pack(elution)
        gathered = lax.all_gather(mine, axes, axis=0).reshape(-1, math.gcd(bin_count, LANES), LANES)
        (g,) = partial_model((gathered,), circulant(bin_weight.reshape(LANES, -1), 0), bin_count, components)
        shifted = elution_terms((gathered,), loadings, shifts, bin_count)
        numerator, gram = product(intensity, (g,), shifted, loadings, shifts, planes)
        gram = lax.psum(gram, "freq")
        owned = lax.psum_scatter(numerator, "freq", scatter_dimension=1, tiled=True)
        return small_call(solve_kernel, [((components, own), jnp.float32)], "solve", gram, owned)[0]
    mine = encode(elution)
    z_steps = range(4, freq_count, 4)
    held = jnp.stack([mine] + [swap(mine, "freq", freq_count, step) for step in z_steps])
    weights = bin_weight.reshape(LANES, -1)
    held, weights = lax.optimization_barrier((held, weights))
    held = jnp.concatenate([held, swap(held, "freq", freq_count, 2)], axis=0)
    u = circulant(weights, elution.shape[0])
    held, u = lax.optimization_barrier((held, u))
    came = swap(held, "freq", freq_count, 1)
    pair = window_pair(mine, came)
    other = swap(pair, "mz", mz_count, 1)
    g, coded = partial_model((held, came), u, bin_count, components)
    coded, other = lax.optimization_barrier((coded, other))
    models = (g, swap(coded, "mz", mz_count, 1))
    shifted = elution_terms((pair, other), loadings, shifts, bin_count)
    keep, send = product(intensity, models, shifted, loadings, shifts, planes)
    tail = components // 2
    chips = freq_count // 4
    came = swap(send, "freq", freq_count, 1)
    coded = 2 * tail + 16
    (send,) = small_call(
        functools.partial(halve_kernel, tail),
        [((chips * components + coded, LANES), jnp.int16)],
        "reduce_cores",
        keep,
        came,
    )
    across = swap(send, "freq", freq_count, 2)
    own_part, *sends = small_call(
        functools.partial(spread_kernel, tail),
        [((components + tail, LANES), jnp.float32)] + [((components + coded, LANES), jnp.int16)] * (chips - 1),
        "reduce_x",
        keep,
        came,
        across,
    )
    parts = [swap(send, "freq", freq_count, step) for send, step in zip(sends, z_steps)][::-1]
    return small_call(
        solve_planes_kernel, [((components, own), jnp.float32)], "solve", own_part, *parts
    )[0]


def solution(mesh):
    in_specs = (P(None, "freq", "mz"), P(("freq", "mz"), None), P(), P(), P())
    out_specs = P(None, ("mz", "freq"))
    return jax.shard_map(on_device, mesh=mesh, in_specs=in_specs, out_specs=out_specs, check_vma=False)
```

```python
import functools
import math

import jax
import jax.numpy as jnp
import numpy as np
from jax import lax
from jax.experimental import pallas as pl
from jax.experimental.pallas import tpu as pltpu
from jax.sharding import PartitionSpec as P

PRECISE = lax.Precision.HIGHEST
LANES = 128
REACH = 256
MIB = 1024 * 1024
FULL = 32767.0


def f32_dot(a, b, dims=(((1,), (0,)), ((), ()))):
    return lax.dot_general(a, b, dims, precision=PRECISE, preferred_element_type=jnp.float32)


def two_terms(x):
    high = x.astype(jnp.bfloat16)
    low = (x - high.astype(jnp.float32)).astype(jnp.bfloat16)
    return high, low


def vmem(count):
    return [pl.BlockSpec(memory_space=pltpu.VMEM)] * count


def pack_kernel(x_ref, o_ref):
    x = x_ref[...]
    components, rows = x.shape
    pad = -rows % LANES
    if pad:
        x = jnp.concatenate([x, jnp.zeros((components, pad), x.dtype)], axis=1)
    high, low = two_terms(x.T[:rows])
    o_ref[...] = jnp.concatenate([high, low], axis=1)


def pack(elution):
    rows, components = elution.shape
    return pl.pallas_call(
        pack_kernel,
        out_shape=jax.ShapeDtypeStruct((rows, 2 * components), jnp.bfloat16),
        in_specs=vmem(1),
        out_specs=vmem(1)[0],
        compiler_params=pltpu.CompilerParams(vmem_limit_bytes=8 * MIB),
        name="pack_elution",
    )(elution.T)


def encode_kernel(x_ref, o_ref):
    components, rows = x_ref.shape
    half = rows // 2
    x = x_ref[...]
    pad = -rows % LANES
    x = jnp.concatenate([x, jnp.zeros((components, pad), x.dtype)], axis=1).T[:rows]
    peak = jnp.maximum(jnp.max(jnp.abs(x), axis=0, keepdims=True), 1e-30)
    level = jnp.floor(256.0 / math.log(2.0) * jnp.log(peak)) + 1.0
    x = x * (FULL / scale_of(level))
    x = jnp.clip(jnp.floor(x + 0.5), -FULL, FULL).astype(jnp.int32).astype(jnp.int16)
    o_ref[0:half, :] = jnp.concatenate([x[:half], x[half:]], axis=1)
    level = jnp.broadcast_to(level, (16, components)).astype(jnp.int32).astype(jnp.int16)
    o_ref[half:, :] = jnp.concatenate([level, level], axis=1)


def encode_columns(x, o_ref):
    rows = x.shape[0]
    peak = jnp.maximum(jnp.max(jnp.abs(x), axis=0, keepdims=True), 1e-30)
    level = jnp.floor(256.0 / math.log(2.0) * jnp.log(peak)) + 1.0
    x = jnp.clip(jnp.floor(x * (FULL / scale_of(level)) + 0.5), -FULL, FULL)
    o_ref[0:rows, :] = x.astype(jnp.int32).astype(jnp.int16)
    o_ref[rows:, :] = jnp.broadcast_to(level, (16, x.shape[1])).astype(jnp.int32).astype(jnp.int16)


def scale_of(level):
    return jnp.exp(math.log(2.0) / 256.0 * level)


def decoded(x):
    half = x.shape[0] - 16
    x = x.astype(jnp.int32).astype(jnp.float32)
    return x[:half] * (scale_of(x[half : half + 1]) * (1.0 / FULL))


def decoded_terms(x):
    x = decoded(x)
    high = x.astype(jnp.bfloat16).astype(jnp.float32)
    low = x - high
    left = lax.broadcasted_iota(jnp.int32, x.shape, 1) < LANES // 2
    top = jnp.where(left, high, pltpu.roll(low, LANES // 2, 1))
    bottom = jnp.where(left, pltpu.roll(high, LANES // 2, 1), low)
    return jnp.concatenate([top, bottom], axis=0).astype(jnp.bfloat16)


def encode(elution):
    rows, components = elution.shape
    return pl.pallas_call(
        encode_kernel,
        out_shape=jax.ShapeDtypeStruct((rows // 2 + 16, 2 * components), jnp.int16),
        in_specs=vmem(1),
        out_specs=vmem(1)[0],
        compiler_params=pltpu.CompilerParams(vmem_limit_bytes=8 * MIB),
        name="encode_elution",
    )(elution.T)


def circulant_kernel(turn, w_ref, table_ref, u_ref):
    rows = w_ref.shape[1]
    w = w_ref[...]
    over_lanes = (((0,), (0,)), ((), ()))

    def table(at, height, width):
        return table_ref[at : at + height, :width], table_ref[at + height : at + 2 * height, :width]

    lane_cos, lane_sin = table(0, LANES, LANES)
    twid_cos, twid_sin = table(2 * LANES, rows, LANES)
    row_cos, row_sin = table(2 * LANES + 2 * rows, rows, rows)
    a_re = f32_dot(w, lane_cos, over_lanes)
    a_im = -f32_dot(w, lane_sin, over_lanes)
    b_re = a_re * twid_cos + a_im * twid_sin
    b_im = a_im * twid_cos - a_re * twid_sin
    c = f32_dot(row_cos, b_re) + f32_dot(row_sin, b_im)
    sub = lax.broadcasted_iota(jnp.int32, (LANES, LANES), 0)
    lane = lax.broadcasted_iota(jnp.int32, (LANES, LANES), 1)

    if turn:
        part = LANES - turn % LANES
        near, after = (
            pltpu.roll(jnp.concatenate([c[n:], c[:n]], axis=0), part % LANES, 1)
            for n in (turn // LANES, turn // LANES + 1)
        )
        moved = jnp.where(lax.broadcasted_iota(jnp.int32, c.shape, 1) < part, near, after)
        c = jnp.where(lax.axis_index("mz") == 1, moved, c)

    def turned(row):
        return pltpu.roll(jnp.broadcast_to(c[row : row + 1], (LANES, LANES)), 0, 1, stride=1, stride_axis=0)

    before = turned(rows - 1)
    for row in range(rows):
        now = turned(row)
        high, low = two_terms(jnp.where(lane >= sub, now, before))
        u_ref[0:LANES, row * LANES : (row + 1) * LANES] = high
        u_ref[LANES:, row * LANES : (row + 1) * LANES] = low
        before = now


def circulant(weights, turn):
    length = weights.size
    rows = length // LANES

    def tables(a, b, period):
        angle = 2.0 * math.pi / period * ((a[:, None] * b[None, :]) % period)
        return np.pad(np.concatenate([np.cos(angle), np.sin(angle)]), ((0, 0), (0, LANES - b.size)))

    lane_ids, row_ids = np.arange(LANES), np.arange(rows)
    table = np.concatenate(
        [
            tables(lane_ids, lane_ids, LANES),
            tables(row_ids, lane_ids, length),
            tables(row_ids, row_ids, rows) / length,
        ]
    ).astype(np.float32)
    return pl.pallas_call(
        functools.partial(circulant_kernel, turn),
        out_shape=jax.ShapeDtypeStruct((2 * LANES, length), jnp.bfloat16),
        in_specs=vmem(2),
        out_specs=vmem(1)[0],
        compiler_params=pltpu.CompilerParams(vmem_limit_bytes=16 * MIB),
        cost_estimate=pl.CostEstimate(flops=2_000_000_000, bytes_accessed=4 * MIB, transcendentals=0),
        name="circulant_block",
    )(weights, table)


def model_kernel(places, planes, *refs):
    if planes:
        u_ref, g_ref, coded_ref, wide = refs[-4:]
    else:
        u_ref, g_ref, wide = refs[-3:]
    length = u_ref.shape[1]
    components = g_ref.shape[0]
    freq_rank = lax.axis_index("freq")
    if planes:
        own_ref, came_ref = refs[:2]
        freq_count = 2 * own_ref.shape[0]
        rows = 2 * (own_ref.shape[1] - 16)
        padded = wide.shape[0] // freq_count
        for block in range(freq_count):
            apart = lax.bitwise_xor((freq_rank + block) & (freq_count - 1), freq_rank)
            ref = came_ref if block % 2 else own_ref
            values = decoded_terms(ref[pl.ds(block_place(apart, freq_count), 1)][0])
            at, before = block * padded, (block - 1) % freq_count * padded
            wide[at : at + rows, 0:LANES] = values
            wide[before : before + rows, LANES:] = values
            wide[at + rows : at + padded, :] = jnp.zeros((padded - rows, 2 * LANES), jnp.bfloat16)
        period = length // freq_count // LANES
        left = lax.broadcasted_iota(jnp.int32, (LANES, LANES), 1) < components
        sides = []
        for a in range(period):
            columns = []
            for block in range(freq_count):
                first = REACH // LANES + period * block - a
                for n in range(first, first + padded // LANES):
                    at = n % (length // LANES) * LANES
                    columns.append(u_ref[:, at : at + LANES])
            width = 2 * LANES if a + period < places else LANES
            made = jnp.dot(
                jnp.concatenate(columns, axis=1), wide[:, :width], preferred_element_type=jnp.float32
            )
            made = made[:LANES] + made[LANES:]
            tiles = []
            for half in range(width // LANES):
                tile = made[:, half * LANES : (half + 1) * LANES]
                tiles.append(tile + pltpu.roll(tile, components, 1))
                to = (a + half * period) * LANES
                g_ref[:, to : to + LANES] = tiles[-1].T[:components]
            if len(tiles) == 1:
                half = LANES // 2
                sides.append(jnp.where(left[:half], tiles[0][:half], tiles[0][half:]))
            else:
                sides.append(jnp.where(left, tiles[0], tiles[1]))
        encode_columns(jnp.concatenate(sides, axis=0), coded_ref)
        return
    own_ref = refs[0]
    step = own_ref.shape[1]
    steps = length // step
    bin_count = length // lax.axis_size("freq")
    first = lax.rem(freq_rank * bin_count + length - REACH, length) // step

    def bring(j, carry):
        values = own_ref[pl.ds(lax.rem(first + j, steps), 1)][0]
        to = pl.multiple_of(REACH + j * step, step)
        wide[pl.ds(to, step), 0:LANES] = values
        wide[pl.ds(pl.multiple_of(to - LANES, step), step), LANES:] = values
        return carry

    lax.fori_loop(0, (wide.shape[0] - REACH) // step, bring, 0)
    for a in range(0, places, 2):
        at = REACH + a * LANES
        made = jnp.dot(u_ref[...], wide[at : at + length, :], preferred_element_type=jnp.float32)
        made = made[:LANES] + made[LANES:]
        for half in range(min(2, places - a)):
            piece = made[:, half * LANES : (half + 1) * LANES].T
            g_ref[:, (a + half) * LANES : (a + half + 1) * LANES] = piece[:components] + piece[components:]


def block_place(apart, freq_count):
    return (apart >> 2) + ((apart >> 1) & 1) * (freq_count // 4)


def partial_model(gathered, u, bin_count, components):
    length = u.shape[1]
    places = -(-(bin_count + REACH) // LANES)
    planes = len(gathered) == 2
    if planes:
        own = gathered[0]
        wide_rows = 2 * own.shape[0] * (-(-2 * (own.shape[1] - 16) // LANES) * LANES)
    else:
        wide_rows = REACH + length + 2 * LANES * ((places - 1) // 2)
    outs = [jax.ShapeDtypeStruct((components, places * LANES), jnp.float32)]
    if planes:
        outs.append(jax.ShapeDtypeStruct((places * LANES // 2 + 16, LANES), jnp.int16))
    return pl.pallas_call(
        functools.partial(model_kernel, places, planes),
        out_shape=tuple(outs),
        in_specs=vmem(len(gathered) + 1),
        out_specs=tuple(vmem(len(outs))),
        scratch_shapes=[pltpu.VMEM((wide_rows, 2 * LANES), jnp.bfloat16)],
        compiler_params=pltpu.CompilerParams(vmem_limit_bytes=24 * MIB),
        cost_estimate=pl.CostEstimate(flops=2_000_000_000, bytes_accessed=4 * MIB, transcendentals=0),
        name="partial_model",
    )(*gathered, u)


def shifted_terms(x, amps, lags, bin_count, terms):
    for piece in shift_pieces(x, amps, lags, bin_count, terms, range(amps.shape[1])):
        piece()


def shift_pieces(x, amps, lags, bin_count, terms, runs):
    components = x.shape[0]
    out_count = -(-bin_count // LANES)
    x = pltpu.roll(x, x.shape[1] - 1, 1)
    height = 16
    lane = lax.broadcasted_iota(jnp.int32, (height, LANES), 1)

    def piece(at, k):
        vectors = [x[at : at + height, v * LANES : (v + 1) * LANES] for v in range(out_count + 2)]
        left = REACH - 1 - jnp.broadcast_to(lags[at : at + height, k : k + 1], lane.shape)
        amp = jnp.broadcast_to(amps[at : at + height, k : k + 1], lane.shape)
        inside = left & (LANES - 1)
        index = (lane + inside) & (LANES - 1)
        far, same = left >= LANES, lane >= inside
        near = [jnp.where(far, vectors[v + 1], vectors[v]) for v in range(out_count + 1)]
        for v in range(out_count):
            joined = jnp.where(same, near[v], near[v + 1])
            turned = jnp.take_along_axis(joined, index, axis=1, mode="promise_in_bounds")
            high, low = two_terms(amp * turned)
            width = min(LANES, bin_count - v * LANES)
            to = slice(k * bin_count + v * LANES, k * bin_count + v * LANES + width)
            terms[at : at + height, to] = high[:, :width]
            terms[components + at : components + at + height, to] = low[:, :width]

    return [functools.partial(piece, at, k) for k in runs for at in range(0, components, height)]


def pair_kernel(mine_ref, came_ref, o_ref):
    rows = mine_ref.shape[0]
    freq_count = 2 * came_ref.shape[0]
    freq_rank = lax.axis_index("freq")
    apart = lax.bitwise_xor((freq_rank - 1) & (freq_count - 1), freq_rank)
    o_ref[0:rows, :] = came_ref[pl.ds(block_place(apart, freq_count), 1)][0]
    o_ref[rows:, :] = mine_ref[...]


def window_pair(mine, came):
    return pl.pallas_call(
        pair_kernel,
        out_shape=jax.ShapeDtypeStruct((2 * mine.shape[0], mine.shape[1]), mine.dtype),
        in_specs=vmem(2),
        out_specs=vmem(1)[0],
        compiler_params=pltpu.CompilerParams(vmem_limit_bytes=8 * MIB),
        name="window_pair",
    )(mine, came)


def elution_kernel(planes, *refs):
    amp_ref, lag_ref, terms, window = refs[-4:]
    components = amp_ref.shape[1]
    bin_count = terms.shape[1] // amp_ref.shape[0]
    freq_rank = lax.axis_index("freq")
    if planes:
        pair_ref, other_ref = refs[:2]
        mz_rank = lax.axis_index("mz")
        coded = pair_ref.shape[0] // 2
        rows = 2 * (coded - 16)
        skip = bin_count - REACH
        for block in range(2):
            part = slice(block * coded, (block + 1) * coded)
            pair, other = decoded(pair_ref[part, :]), decoded(other_ref[part, :])
            for half, values in enumerate(
                (jnp.where(mz_rank == 0, pair, other), jnp.where(mz_rank == 0, other, pair))
            ):
                to = (2 * block + half) * rows
                window[to : to + rows // 2, :] = values
                window[to + rows // 2 : to + rows, :] = pltpu.roll(values, LANES // 2, 1)
    else:
        own_ref = refs[0]
        step = own_ref.shape[1]
        steps = own_ref.shape[0]
        first = lax.rem(freq_rank * bin_count + steps * step - REACH, steps * step) // step
        skip = 0
        for j in range(window.shape[0] // step):
            window[j * step : (j + 1) * step, :] = own_ref[pl.ds(lax.rem(first + j, steps), 1)][0]
    pieces = []
    for at in range(skip, window.shape[0], LANES):
        piece = window[at : at + LANES, :].astype(jnp.float32).T
        pieces.append(piece[:components] if planes else piece[:components] + piece[components:])
    shifted_terms(jnp.concatenate(pieces, axis=1), amp_ref[...].T, lag_ref[...].T, bin_count, terms)


def elution_terms(elutions, loadings, shifts, bin_count):
    run_count, components = loadings.shape
    places = -(-(bin_count + REACH) // LANES)
    planes = len(elutions) > 1
    return pl.pallas_call(
        functools.partial(elution_kernel, planes),
        out_shape=jax.ShapeDtypeStruct((2 * components, run_count * bin_count), jnp.bfloat16),
        in_specs=vmem(len(elutions) + 2),
        out_specs=vmem(1)[0],
        scratch_shapes=[
            pltpu.VMEM((2 * bin_count, LANES), jnp.float32)
            if planes
            else pltpu.VMEM((places * LANES, LANES), jnp.bfloat16)
        ],
        compiler_params=pltpu.CompilerParams(vmem_limit_bytes=12 * MIB),
        cost_estimate=pl.CostEstimate(flops=1_000_000_000, bytes_accessed=2 * MIB, transcendentals=0),
        name="elution_terms",
    )(*elutions, loadings, shifts)


def product_kernel(parts, planes, *refs):
    i_ref = refs[0]
    g_refs = refs[1 : 1 + parts]
    elution_ref, amp_ref, lag_ref, num_ref, other_ref, terms, partial = refs[1 + parts :]
    run_count, bin_count, local_mz = i_ref.shape
    components = amp_ref.shape[1]
    chunk = 2 * LANES
    chunks = local_mz // chunk
    g = g_refs[0][...]
    if planes:
        period = bin_count // LANES
        x = decoded(g_refs[1][...])
        first, second, at = [], [], 0
        for a in range(period):
            if a + period < g.shape[1] // LANES:
                tile = x[at : at + LANES].T
                second.append(tile[components:])
                at += LANES
            else:
                half = x[at : at + LANES // 2]
                tile = jnp.concatenate([half, pltpu.roll(half, components, 1)], axis=0).T
                at += LANES // 2
            first.append(tile[:components])
        g = g + jnp.concatenate(first + second, axis=1)
    amps, lags = amp_ref[...].T, lag_ref[...].T
    middle = run_count // 2
    for piece in shift_pieces(g, amps, lags, bin_count, terms, range(middle)):
        piece()
    waiting = shift_pieces(g, amps, lags, bin_count, terms, range(middle, run_count))

    def multiply(n, first, last):
        data = i_ref[first:last, :, n * chunk : (n + 1) * chunk].reshape((last - first) * bin_count, chunk)
        made = jnp.dot(
            terms[:, first * bin_count : last * bin_count], data, preferred_element_type=jnp.float32
        )
        return made[:components] + made[components:]

    share = -(-len(waiting) // chunks)
    for n in range(chunks):
        partial[n] = multiply(n, 0, middle)
        for piece in waiting[n * share : (n + 1) * share]:
            piece()
    gram = lax.dot_general(
        terms[...], elution_ref[...], (((1,), (1,)), ((), ())), preferred_element_type=jnp.float32
    )
    gram = gram[:components] + gram[components:]
    gram = gram[:, :components] + gram[:, components:]
    if planes:
        keep_ref, send_ref = num_ref, other_ref
        half = components // 2
        gram = jnp.concatenate([gram[:half], gram[half:]], axis=1)
        keep_ref[chunks * components :, :] = gram
        send_ref[chunks * components :, :] = gram
    else:
        other_ref[...] = gram

    for n in range(chunks):
        made = partial[n] + multiply(n, middle, run_count)
        if planes:
            freq_rank = lax.axis_index("freq")
            core = freq_rank & 1
            place = block_place(lax.bitwise_xor(freq_rank, 2 * n + core), 2 * chunks)
            at = pl.ds(pl.multiple_of(place * components, components), components)
            even, odd = made[:, :LANES], made[:, LANES:]
            keep_ref[at, :] = jnp.where(core == 0, even, odd)
            send_ref[at, :] = jnp.where(core == 0, odd, even)
        else:
            num_ref[:, n * chunk : (n + 1) * chunk] = made


def product(intensity, models, elution, loadings, shifts, planes):
    run_count, bin_count, local_mz = intensity.shape
    components = loadings.shape[1]
    chunk = 2 * LANES
    chunks = local_mz // chunk
    if planes:
        out_shapes = [(chunks * components + components // 2, LANES)] * 2
    else:
        out_shapes = [(components, local_mz), (components, components)]
    return pl.pallas_call(
        functools.partial(product_kernel, len(models), planes),
        out_shape=tuple(jax.ShapeDtypeStruct(shape, jnp.float32) for shape in out_shapes),
        in_specs=vmem(len(models) + 4),
        out_specs=tuple(vmem(2)),
        scratch_shapes=[
            pltpu.VMEM((2 * components, run_count * bin_count), jnp.bfloat16),
            pltpu.VMEM((chunks, components, chunk), jnp.float32),
        ],
        compiler_params=pltpu.CompilerParams(vmem_limit_bytes=24 * MIB),
        cost_estimate=pl.CostEstimate(
            flops=8_000_000_000, bytes_accessed=2 * intensity.size, transcendentals=0
        ),
        name="model_products",
    )(intensity, *models, elution, loadings, shifts)


def inverse2(a, b, d):
    scale = 1.0 / (a * d - b * b)
    return d * scale, -b * scale, a * scale


def eliminate(gram, right):
    components = gram.shape[0]
    height = 8
    shape = (height, gram.shape[1])
    row_id = lax.broadcasted_iota(jnp.int32, shape, 0)
    starts = range(0, components, height)
    gram = [gram[at : at + height] for at in starts]
    right = [right[at : at + height] for at in starts]
    for j in range(0, components, 4):
        here, r = j // height, j % height
        columns = [[jnp.broadcast_to(tile[:, j + n : j + n + 1], shape) for tile in gram] for n in range(4)]
        pivot = [[columns[n][here][r + m : r + m + 1] for n in range(4)] for m in range(4)]
        a00, a01, a11 = inverse2(pivot[0][0], pivot[0][1], pivot[1][1])
        b00, b01, b10, b11 = pivot[0][2], pivot[0][3], pivot[1][2], pivot[1][3]
        w00, w01 = a00 * b00 + a01 * b10, a00 * b01 + a01 * b11
        w10, w11 = a01 * b00 + a11 * b10, a01 * b01 + a11 * b11
        s00, s01, s11 = inverse2(
            pivot[2][2] - (b00 * w00 + b10 * w10),
            pivot[2][3] - (b00 * w01 + b10 * w11),
            pivot[3][3] - (b01 * w01 + b11 * w11),
        )
        away = (row_id < r) | (row_id >= r + 4)
        for n in range(4):
            columns[n][here] = jnp.where(away, columns[n][here], jnp.where(row_id == r + n, -1.0, 0.0))
        gram_rows = [gram[here][r + n : r + n + 1] for n in range(4)]
        right_rows = [right[here][r + n : r + n + 1] for n in range(4)]
        gram[here] = jnp.where(away, gram[here], 0.0)
        right[here] = jnp.where(away[:, : right[here].shape[1]], right[here], 0.0)
        for t in range(len(gram)):
            c0, c1, c2, c3 = (columns[n][t] for n in range(4))
            t2, t3 = c2 - c0 * w00 - c1 * w10, c3 - c0 * w01 - c1 * w11
            f2, f3 = t2 * s00 + t3 * s01, t2 * s01 + t3 * s11
            f0 = c0 * a00 + c1 * a01 - f2 * w00 - f3 * w01
            f1 = c0 * a01 + c1 * a11 - f2 * w10 - f3 * w11
            for n, factor in enumerate((f0, f1, f2, f3)):
                gram[t] = gram[t] - factor * gram_rows[n]
                right[t] = right[t] - factor[:, : right[t].shape[1]] * right_rows[n]
    return jnp.concatenate(right, axis=0)


def total_of(refs, at, rows):
    total = refs[0][at : at + rows]
    for ref in refs[1:]:
        total = total + ref[at : at + rows]
    return total


def fixed_point(x, full):
    return jnp.clip(jnp.floor(x + 0.5), -full, full)


def as_int16(x):
    return x.astype(jnp.int32).astype(jnp.int16)


def row_level(x):
    peak = jnp.maximum(jnp.max(jnp.abs(x), axis=1, keepdims=True), 1e-30)
    return jnp.floor(256.0 / math.log(2.0) * jnp.log(peak)) + 1.0


def diagonal(x, rows):
    shape = (rows, LANES)
    on = lax.broadcasted_iota(jnp.int32, shape, 0) == lax.broadcasted_iota(jnp.int32, shape, 1)
    return jnp.where(on, jnp.broadcast_to(x, shape), 0.0)


def encode_rows(x, gram, o_ref):
    rows, tail = x.shape[0], gram.shape[0]
    parts = [x[at : at + LANES] for at in range(0, rows, LANES)]
    levels = [row_level(part) for part in parts] + [row_level(gram)]
    at = 0
    for part, level in zip(parts, levels):
        o_ref[at : at + part.shape[0], :] = as_int16(fixed_point(part * (FULL / scale_of(level)), FULL))
        at += part.shape[0]
    scaled = gram * (FULL / scale_of(levels[-1]))
    high = fixed_point(scaled, FULL)
    o_ref[at : at + tail, :] = as_int16(high)
    o_ref[at + tail : at + 2 * tail, :] = as_int16(fixed_point((scaled - high) * (2 * FULL), FULL))
    row_id = lax.broadcasted_iota(jnp.int32, (16, LANES), 0)
    block = jnp.zeros((16, LANES), jnp.float32)
    for n, level in enumerate(levels):
        lanes = jnp.sum(diagonal(level, level.shape[0]), axis=0, keepdims=True)
        block = jnp.where(row_id == n, lanes, block)
    o_ref[at + 2 * tail :, :] = as_int16(block)


def decode_rows(ref, tail):
    rows = ref.shape[0] - 2 * tail - 16
    x = ref[...].astype(jnp.int32).astype(jnp.float32)

    def scale(n, count):
        at = rows + 2 * tail + n
        return scale_of(jnp.sum(diagonal(x[at : at + 1], count), axis=1, keepdims=True)) * (1.0 / FULL)

    parts = []
    for n, at in enumerate(range(0, rows, LANES)):
        count = min(LANES, rows - at)
        parts.append(x[at : at + count] * scale(n, count))
    gram = x[rows : rows + tail] + x[rows + tail : rows + 2 * tail] * (0.5 / FULL)
    return jnp.concatenate(parts, axis=0), gram * scale(len(parts), tail)


def halve_kernel(tail, a_ref, b_ref, o_ref):
    rows = o_ref.shape[0] - 2 * tail - 16
    total = total_of((a_ref, b_ref), rows, rows + tail)
    encode_rows(total[:rows], total[rows:], o_ref)


def spread_kernel(tail, a_ref, b_ref, c_ref, own_ref, *outs):
    rows = own_ref.shape[0] - tail
    count = len(outs) + 1
    total, gram = decode_rows(c_ref, tail)
    total = total + total_of((a_ref, b_ref), 0, count * rows)
    gram = gram + total_of((a_ref, b_ref), 2 * count * rows, tail)
    own_ref[0:rows, :] = total[:rows]
    own_ref[rows:, :] = gram
    for n, o_ref in enumerate(outs):
        encode_rows(total[(n + 1) * rows : (n + 2) * rows], gram, o_ref)


def solve_planes_kernel(own_ref, *refs):
    o_ref = refs[-1]
    components = o_ref.shape[0]
    total, gram = own_ref[:components], own_ref[components:]
    for ref in refs[:-1]:
        part, gram_part = decode_rows(ref, gram.shape[0])
        total, gram = total + part, gram + gram_part
    gram = jnp.concatenate([gram, pltpu.roll(gram, gram.shape[1] // 2, 1)], axis=0)
    o_ref[...] = eliminate(gram, total)


def solve_kernel(g_ref, n_ref, o_ref):
    components = o_ref.shape[0]
    gram = jnp.concatenate([g_ref[...], jnp.zeros((components, LANES - components), jnp.float32)], axis=1)
    o_ref[...] = eliminate(gram, n_ref[...])


def small_call(kernel, outs, name, *args):
    return pl.pallas_call(
        kernel,
        out_shape=tuple(jax.ShapeDtypeStruct(shape, dtype) for shape, dtype in outs),
        in_specs=vmem(len(args)),
        out_specs=tuple(vmem(len(outs))),
        compiler_params=pltpu.CompilerParams(vmem_limit_bytes=8 * MIB),
        name=name,
    )(*args)


def swap(x, axes, count, value):
    return lax.ppermute(x, axes, [(i, i ^ value) for i in range(count)])


def on_device(intensity, elution, loadings, shifts, bin_weight):
    freq_count = lax.axis_size("freq")
    mz_count = lax.axis_size("mz")
    components = loadings.shape[1]
    bin_count = intensity.shape[1]
    axes = ("freq", "mz")
    own = intensity.shape[2] // freq_count
    planes = (
        own == LANES
        and 2 * components == LANES
        and mz_count == 2
        and freq_count & (freq_count - 1) == 0
        and freq_count >= 8
        and elution.shape[0] % 64 == 0
        and bin_count % LANES == 0
        and bin_count >= REACH
    )
    if not planes:
        mine = pack(elution)
        gathered = lax.all_gather(mine, axes, axis=0).reshape(-1, math.gcd(bin_count, LANES), LANES)
        (g,) = partial_model((gathered,), circulant(bin_weight.reshape(LANES, -1), 0), bin_count, components)
        shifted = elution_terms((gathered,), loadings, shifts, bin_count)
        numerator, gram = product(intensity, (g,), shifted, loadings, shifts, planes)
        gram = lax.psum(gram, "freq")
        owned = lax.psum_scatter(numerator, "freq", scatter_dimension=1, tiled=True)
        return small_call(solve_kernel, [((components, own), jnp.float32)], "solve", gram, owned)[0]
    mine = encode(elution)
    z_steps = range(4, freq_count, 4)
    held = jnp.stack([mine] + [swap(mine, "freq", freq_count, step) for step in z_steps])
    weights = bin_weight.reshape(LANES, -1)
    held, weights = lax.optimization_barrier((held, weights))
    held = jnp.concatenate([held, swap(held, "freq", freq_count, 2)], axis=0)
    u = circulant(weights, elution.shape[0])
    held, u = lax.optimization_barrier((held, u))
    came = swap(held, "freq", freq_count, 1)
    pair = window_pair(mine, came)
    other = swap(pair, "mz", mz_count, 1)
    g, coded = partial_model((held, came), u, bin_count, components)
    coded, other = lax.optimization_barrier((coded, other))
    models = (g, swap(coded, "mz", mz_count, 1))
    shifted = elution_terms((pair, other), loadings, shifts, bin_count)
    keep, send = product(intensity, models, shifted, loadings, shifts, planes)
    tail = components // 2
    chips = freq_count // 4
    came = swap(send, "freq", freq_count, 1)
    coded = 2 * tail + 16
    (send,) = small_call(
        functools.partial(halve_kernel, tail),
        [((chips * components + coded, LANES), jnp.int16)],
        "reduce_cores",
        keep,
        came,
    )
    across = swap(send, "freq", freq_count, 2)
    own_part, *sends = small_call(
        functools.partial(spread_kernel, tail),
        [((components + tail, LANES), jnp.float32)] + [((components + coded, LANES), jnp.int16)] * (chips - 1),
        "reduce_x",
        keep,
        came,
        across,
    )
    parts = [swap(send, "freq", freq_count, step) for send, step in zip(sends, z_steps)][::-1]
    return small_call(
        solve_planes_kernel, [((components, own), jnp.float32)], "solve", own_part, *parts
    )[0]


def solution(mesh):
    in_specs = (P(None, "freq", "mz"), P(("freq", "mz"), None), P(), P(), P())
    out_specs = P(None, ("mz", "freq"))
    return jax.shard_map(on_device, mesh=mesh, in_specs=in_specs, out_specs=out_specs, check_vma=False)
```

```python
import functools
import math

import jax
import jax.numpy as jnp
import numpy as np
from jax import lax
from jax.experimental import pallas as pl
from jax.experimental.pallas import tpu as pltpu
from jax.sharding import PartitionSpec as P

PRECISE = lax.Precision.HIGHEST
LANES = 128
REACH = 256
MIB = 1024 * 1024
FULL = 32767.0


def f32_dot(a, b, dims=(((1,), (0,)), ((), ()))):
    return lax.dot_general(a, b, dims, precision=PRECISE, preferred_element_type=jnp.float32)


def two_terms(x):
    high = x.astype(jnp.bfloat16)
    low = (x - high.astype(jnp.float32)).astype(jnp.bfloat16)
    return high, low


def vmem(count):
    return [pl.BlockSpec(memory_space=pltpu.VMEM)] * count


def pack_kernel(x_ref, o_ref):
    x = x_ref[...]
    components, rows = x.shape
    pad = -rows % LANES
    if pad:
        x = jnp.concatenate([x, jnp.zeros((components, pad), x.dtype)], axis=1)
    high, low = two_terms(x.T[:rows])
    o_ref[...] = jnp.concatenate([high, low], axis=1)


def pack(elution):
    rows, components = elution.shape
    return pl.pallas_call(
        pack_kernel,
        out_shape=jax.ShapeDtypeStruct((rows, 2 * components), jnp.bfloat16),
        in_specs=vmem(1),
        out_specs=vmem(1)[0],
        compiler_params=pltpu.CompilerParams(vmem_limit_bytes=8 * MIB),
        name="pack_elution",
    )(elution.T)


def encode_kernel(x_ref, o_ref):
    components, rows = x_ref.shape
    half = rows // 2
    x = x_ref[...]
    pad = -rows % LANES
    x = jnp.concatenate([x, jnp.zeros((components, pad), x.dtype)], axis=1).T[:rows]
    peak = jnp.maximum(jnp.max(jnp.abs(x), axis=0, keepdims=True), 1e-30)
    level = jnp.floor(256.0 / math.log(2.0) * jnp.log(peak)) + 1.0
    x = x * (FULL / scale_of(level))
    x = jnp.clip(jnp.floor(x + 0.5), -FULL, FULL).astype(jnp.int32).astype(jnp.int16)
    o_ref[0:half, :] = jnp.concatenate([x[:half], x[half:]], axis=1)
    level = jnp.broadcast_to(level, (16, components)).astype(jnp.int32).astype(jnp.int16)
    o_ref[half:, :] = jnp.concatenate([level, level], axis=1)


def encode_columns(x, o_ref):
    rows = x.shape[0]
    peak = jnp.maximum(jnp.max(jnp.abs(x), axis=0, keepdims=True), 1e-30)
    level = jnp.floor(256.0 / math.log(2.0) * jnp.log(peak)) + 1.0
    x = jnp.clip(jnp.floor(x * (FULL / scale_of(level)) + 0.5), -FULL, FULL)
    o_ref[0:rows, :] = x.astype(jnp.int32).astype(jnp.int16)
    o_ref[rows:, :] = jnp.broadcast_to(level, (16, x.shape[1])).astype(jnp.int32).astype(jnp.int16)


def scale_of(level):
    return jnp.exp(math.log(2.0) / 256.0 * level)


def decoded(x):
    half = x.shape[0] - 16
    x = x.astype(jnp.int32).astype(jnp.float32)
    return x[:half] * (scale_of(x[half : half + 1]) * (1.0 / FULL))


def decoded_terms(x):
    x = decoded(x)
    high = x.astype(jnp.bfloat16).astype(jnp.float32)
    low = x - high
    left = lax.broadcasted_iota(jnp.int32, x.shape, 1) < LANES // 2
    top = jnp.where(left, high, pltpu.roll(low, LANES // 2, 1))
    bottom = jnp.where(left, pltpu.roll(high, LANES // 2, 1), low)
    return jnp.concatenate([top, bottom], axis=0).astype(jnp.bfloat16)


def encode(elution):
    rows, components = elution.shape
    return pl.pallas_call(
        encode_kernel,
        out_shape=jax.ShapeDtypeStruct((rows // 2 + 16, 2 * components), jnp.int16),
        in_specs=vmem(1),
        out_specs=vmem(1)[0],
        compiler_params=pltpu.CompilerParams(vmem_limit_bytes=8 * MIB),
        name="encode_elution",
    )(elution.T)


def circulant_kernel(turn, w_ref, table_ref, u_ref):
    rows = w_ref.shape[1]
    w = w_ref[...]
    over_lanes = (((0,), (0,)), ((), ()))

    def table(at, height, width):
        return table_ref[at : at + height, :width], table_ref[at + height : at + 2 * height, :width]

    lane_cos, lane_sin = table(0, LANES, LANES)
    twid_cos, twid_sin = table(2 * LANES, rows, LANES)
    row_cos, row_sin = table(2 * LANES + 2 * rows, rows, rows)
    a_re = f32_dot(w, lane_cos, over_lanes)
    a_im = -f32_dot(w, lane_sin, over_lanes)
    b_re = a_re * twid_cos + a_im * twid_sin
    b_im = a_im * twid_cos - a_re * twid_sin
    c = f32_dot(row_cos, b_re) + f32_dot(row_sin, b_im)
    sub = lax.broadcasted_iota(jnp.int32, (LANES, LANES), 0)
    lane = lax.broadcasted_iota(jnp.int32, (LANES, LANES), 1)

    if turn:
        part = LANES - turn % LANES
        near, after = (
            pltpu.roll(jnp.concatenate([c[n:], c[:n]], axis=0), part % LANES, 1)
            for n in (turn // LANES, turn // LANES + 1)
        )
        moved = jnp.where(lax.broadcasted_iota(jnp.int32, c.shape, 1) < part, near, after)
        c = jnp.where(lax.axis_index("mz") == 1, moved, c)

    def turned(row):
        return pltpu.roll(jnp.broadcast_to(c[row : row + 1], (LANES, LANES)), 0, 1, stride=1, stride_axis=0)

    before = turned(rows - 1)
    for row in range(rows):
        now = turned(row)
        high, low = two_terms(jnp.where(lane >= sub, now, before))
        u_ref[0:LANES, row * LANES : (row + 1) * LANES] = high
        u_ref[LANES:, row * LANES : (row + 1) * LANES] = low
        before = now


def circulant(weights, turn):
    length = weights.size
    rows = length // LANES

    def tables(a, b, period):
        angle = 2.0 * math.pi / period * ((a[:, None] * b[None, :]) % period)
        return np.pad(np.concatenate([np.cos(angle), np.sin(angle)]), ((0, 0), (0, LANES - b.size)))

    lane_ids, row_ids = np.arange(LANES), np.arange(rows)
    table = np.concatenate(
        [
            tables(lane_ids, lane_ids, LANES),
            tables(row_ids, lane_ids, length),
            tables(row_ids, row_ids, rows) / length,
        ]
    ).astype(np.float32)
    return pl.pallas_call(
        functools.partial(circulant_kernel, turn),
        out_shape=jax.ShapeDtypeStruct((2 * LANES, length), jnp.bfloat16),
        in_specs=vmem(2),
        out_specs=vmem(1)[0],
        compiler_params=pltpu.CompilerParams(vmem_limit_bytes=16 * MIB),
        cost_estimate=pl.CostEstimate(flops=2_000_000_000, bytes_accessed=4 * MIB, transcendentals=0),
        name="circulant_block",
    )(weights, table)


def model_kernel(places, planes, *refs):
    if planes:
        u_ref, g_ref, coded_ref, wide = refs[-4:]
    else:
        u_ref, g_ref, wide = refs[-3:]
    length = u_ref.shape[1]
    components = g_ref.shape[0]
    freq_rank = lax.axis_index("freq")
    if planes:
        own_ref, came_ref = refs[:2]
        freq_count = 2 * own_ref.shape[0]
        rows = 2 * (own_ref.shape[1] - 16)
        padded = wide.shape[0] // freq_count
        for block in range(freq_count):
            apart = lax.bitwise_xor((freq_rank + block) & (freq_count - 1), freq_rank)
            ref = came_ref if block % 2 else own_ref
            values = decoded_terms(ref[pl.ds(block_place(apart, freq_count), 1)][0])
            at, before = block * padded, (block - 1) % freq_count * padded
            wide[at : at + rows, 0:LANES] = values
            wide[before : before + rows, LANES:] = values
            wide[at + rows : at + padded, :] = jnp.zeros((padded - rows, 2 * LANES), jnp.bfloat16)
        period = length // freq_count // LANES
        left = lax.broadcasted_iota(jnp.int32, (LANES, LANES), 1) < components
        sides = []
        for a in range(period):
            columns = []
            for block in range(freq_count):
                first = REACH // LANES + period * block - a
                for n in range(first, first + padded // LANES):
                    at = n % (length // LANES) * LANES
                    columns.append(u_ref[:, at : at + LANES])
            width = 2 * LANES if a + period < places else LANES
            made = jnp.dot(
                jnp.concatenate(columns, axis=1), wide[:, :width], preferred_element_type=jnp.float32
            )
            made = made[:LANES] + made[LANES:]
            tiles = []
            for half in range(width // LANES):
                tile = made[:, half * LANES : (half + 1) * LANES]
                tiles.append(tile + pltpu.roll(tile, components, 1))
                to = (a + half * period) * LANES
                g_ref[:, to : to + LANES] = tiles[-1].T[:components]
            if len(tiles) == 1:
                half = LANES // 2
                sides.append(jnp.where(left[:half], tiles[0][:half], tiles[0][half:]))
            else:
                sides.append(jnp.where(left, tiles[0], tiles[1]))
        encode_columns(jnp.concatenate(sides, axis=0), coded_ref)
        return
    own_ref = refs[0]
    step = own_ref.shape[1]
    steps = length // step
    bin_count = length // lax.axis_size("freq")
    first = lax.rem(freq_rank * bin_count + length - REACH, length) // step

    def bring(j, carry):
        values = own_ref[pl.ds(lax.rem(first + j, steps), 1)][0]
        to = pl.multiple_of(REACH + j * step, step)
        wide[pl.ds(to, step), 0:LANES] = values
        wide[pl.ds(pl.multiple_of(to - LANES, step), step), LANES:] = values
        return carry

    lax.fori_loop(0, (wide.shape[0] - REACH) // step, bring, 0)
    for a in range(0, places, 2):
        at = REACH + a * LANES
        made = jnp.dot(u_ref[...], wide[at : at + length, :], preferred_element_type=jnp.float32)
        made = made[:LANES] + made[LANES:]
        for half in range(min(2, places - a)):
            piece = made[:, half * LANES : (half + 1) * LANES].T
            g_ref[:, (a + half) * LANES : (a + half + 1) * LANES] = piece[:components] + piece[components:]


def block_place(apart, freq_count):
    return (apart >> 2) + ((apart >> 1) & 1) * (freq_count // 4)


def partial_model(gathered, u, bin_count, components):
    length = u.shape[1]
    places = -(-(bin_count + REACH) // LANES)
    planes = len(gathered) == 2
    if planes:
        own = gathered[0]
        wide_rows = 2 * own.shape[0] * (-(-2 * (own.shape[1] - 16) // LANES) * LANES)
    else:
        wide_rows = REACH + length + 2 * LANES * ((places - 1) // 2)
    outs = [jax.ShapeDtypeStruct((components, places * LANES), jnp.float32)]
    if planes:
        outs.append(jax.ShapeDtypeStruct((places * LANES // 2 + 16, LANES), jnp.int16))
    return pl.pallas_call(
        functools.partial(model_kernel, places, planes),
        out_shape=tuple(outs),
        in_specs=vmem(len(gathered) + 1),
        out_specs=tuple(vmem(len(outs))),
        scratch_shapes=[pltpu.VMEM((wide_rows, 2 * LANES), jnp.bfloat16)],
        compiler_params=pltpu.CompilerParams(vmem_limit_bytes=24 * MIB),
        cost_estimate=pl.CostEstimate(flops=2_000_000_000, bytes_accessed=4 * MIB, transcendentals=0),
        name="partial_model",
    )(*gathered, u)


def shifted_terms(x, amps, lags, bin_count, terms):
    for piece in shift_pieces(x, amps, lags, bin_count, terms, range(amps.shape[1])):
        piece()


def shift_pieces(x, amps, lags, bin_count, terms, runs):
    components = x.shape[0]
    out_count = -(-bin_count // LANES)
    x = pltpu.roll(x, x.shape[1] - 1, 1)
    height = 16
    lane = lax.broadcasted_iota(jnp.int32, (height, LANES), 1)

    def piece(at, k):
        vectors = [x[at : at + height, v * LANES : (v + 1) * LANES] for v in range(out_count + 2)]
        left = REACH - 1 - jnp.broadcast_to(lags[at : at + height, k : k + 1], lane.shape)
        amp = jnp.broadcast_to(amps[at : at + height, k : k + 1], lane.shape)
        inside = left & (LANES - 1)
        index = (lane + inside) & (LANES - 1)
        far, same = left >= LANES, lane >= inside
        near = [jnp.where(far, vectors[v + 1], vectors[v]) for v in range(out_count + 1)]
        for v in range(out_count):
            joined = jnp.where(same, near[v], near[v + 1])
            turned = jnp.take_along_axis(joined, index, axis=1, mode="promise_in_bounds")
            high, low = two_terms(amp * turned)
            width = min(LANES, bin_count - v * LANES)
            to = slice(k * bin_count + v * LANES, k * bin_count + v * LANES + width)
            terms[at : at + height, to] = high[:, :width]
            terms[components + at : components + at + height, to] = low[:, :width]

    return [functools.partial(piece, at, k) for k in runs for at in range(0, components, height)]


def pair_kernel(mine_ref, came_ref, o_ref):
    rows = mine_ref.shape[0]
    freq_count = 2 * came_ref.shape[0]
    freq_rank = lax.axis_index("freq")
    apart = lax.bitwise_xor((freq_rank - 1) & (freq_count - 1), freq_rank)
    o_ref[0:rows, :] = came_ref[pl.ds(block_place(apart, freq_count), 1)][0]
    o_ref[rows:, :] = mine_ref[...]


def window_pair(mine, came):
    return pl.pallas_call(
        pair_kernel,
        out_shape=jax.ShapeDtypeStruct((2 * mine.shape[0], mine.shape[1]), mine.dtype),
        in_specs=vmem(2),
        out_specs=vmem(1)[0],
        compiler_params=pltpu.CompilerParams(vmem_limit_bytes=8 * MIB),
        name="window_pair",
    )(mine, came)


def elution_kernel(planes, *refs):
    amp_ref, lag_ref, terms, window = refs[-4:]
    components = amp_ref.shape[1]
    bin_count = terms.shape[1] // amp_ref.shape[0]
    freq_rank = lax.axis_index("freq")
    if planes:
        pair_ref, other_ref = refs[:2]
        mz_rank = lax.axis_index("mz")
        coded = pair_ref.shape[0] // 2
        rows = 2 * (coded - 16)
        skip = bin_count - REACH
        for ref, half in ((pair_ref, mz_rank), (other_ref, 1 - mz_rank)):
            for block in range(2):
                to = pl.multiple_of((2 * block + half) * rows, 64)
                values = decoded(ref[block * coded : (block + 1) * coded, :])
                half_rows = rows // 2
                window[pl.ds(to, half_rows), :] = values
                window[pl.ds(pl.multiple_of(to + half_rows, 32), half_rows), :] = pltpu.roll(values, LANES // 2, 1)
    else:
        own_ref = refs[0]
        step = own_ref.shape[1]
        steps = own_ref.shape[0]
        first = lax.rem(freq_rank * bin_count + steps * step - REACH, steps * step) // step
        skip = 0
        for j in range(window.shape[0] // step):
            window[j * step : (j + 1) * step, :] = own_ref[pl.ds(lax.rem(first + j, steps), 1)][0]
    pieces = []
    for at in range(skip, window.shape[0], LANES):
        piece = window[at : at + LANES, :].astype(jnp.float32).T
        pieces.append(piece[:components] if planes else piece[:components] + piece[components:])
    shifted_terms(jnp.concatenate(pieces, axis=1), amp_ref[...].T, lag_ref[...].T, bin_count, terms)


def elution_terms(elutions, loadings, shifts, bin_count):
    run_count, components = loadings.shape
    places = -(-(bin_count + REACH) // LANES)
    planes = len(elutions) > 1
    return pl.pallas_call(
        functools.partial(elution_kernel, planes),
        out_shape=jax.ShapeDtypeStruct((2 * components, run_count * bin_count), jnp.bfloat16),
        in_specs=vmem(len(elutions) + 2),
        out_specs=vmem(1)[0],
        scratch_shapes=[
            pltpu.VMEM((2 * bin_count, LANES), jnp.float32)
            if planes
            else pltpu.VMEM((places * LANES, LANES), jnp.bfloat16)
        ],
        compiler_params=pltpu.CompilerParams(vmem_limit_bytes=12 * MIB),
        cost_estimate=pl.CostEstimate(flops=1_000_000_000, bytes_accessed=2 * MIB, transcendentals=0),
        name="elution_terms",
    )(*elutions, loadings, shifts)


def product_kernel(parts, planes, *refs):
    i_ref = refs[0]
    g_refs = refs[1 : 1 + parts]
    elution_ref, amp_ref, lag_ref, num_ref, other_ref, terms, partial = refs[1 + parts :]
    run_count, bin_count, local_mz = i_ref.shape
    components = amp_ref.shape[1]
    chunk = 2 * LANES
    chunks = local_mz // chunk
    g = g_refs[0][...]
    if planes:
        period = bin_count // LANES
        x = decoded(g_refs[1][...])
        first, second, at = [], [], 0
        for a in range(period):
            if a + period < g.shape[1] // LANES:
                tile = x[at : at + LANES].T
                second.append(tile[components:])
                at += LANES
            else:
                half = x[at : at + LANES // 2]
                tile = jnp.concatenate([half, pltpu.roll(half, components, 1)], axis=0).T
                at += LANES // 2
            first.append(tile[:components])
        g = g + jnp.concatenate(first + second, axis=1)
    amps, lags = amp_ref[...].T, lag_ref[...].T
    middle = run_count // 2
    for piece in shift_pieces(g, amps, lags, bin_count, terms, range(middle)):
        piece()
    waiting = shift_pieces(g, amps, lags, bin_count, terms, range(middle, run_count))

    def multiply(n, first, last):
        data = i_ref[first:last, :, n * chunk : (n + 1) * chunk].reshape((last - first) * bin_count, chunk)
        made = jnp.dot(
            terms[:, first * bin_count : last * bin_count], data, preferred_element_type=jnp.float32
        )
        return made[:components] + made[components:]

    share = -(-len(waiting) // chunks)
    for n in range(chunks):
        partial[n] = multiply(n, 0, middle)
        for piece in waiting[n * share : (n + 1) * share]:
            piece()
    gram = lax.dot_general(
        terms[...], elution_ref[...], (((1,), (1,)), ((), ())), preferred_element_type=jnp.float32
    )
    gram = gram[:components] + gram[components:]
    gram = gram[:, :components] + gram[:, components:]
    if planes:
        keep_ref, send_ref = num_ref, other_ref
        half = components // 2
        gram = jnp.concatenate([gram[:half], gram[half:]], axis=1)
        keep_ref[chunks * components :, :] = gram
        send_ref[chunks * components :, :] = gram
    else:
        other_ref[...] = gram

    for n in range(chunks):
        made = partial[n] + multiply(n, middle, run_count)
        if planes:
            freq_rank = lax.axis_index("freq")
            core = freq_rank & 1
            place = block_place(lax.bitwise_xor(freq_rank, 2 * n + core), 2 * chunks)
            at = pl.ds(pl.multiple_of(place * components, components), components)
            even, odd = made[:, :LANES], made[:, LANES:]
            keep_ref[at, :] = jnp.where(core == 0, even, odd)
            send_ref[at, :] = jnp.where(core == 0, odd, even)
        else:
            num_ref[:, n * chunk : (n + 1) * chunk] = made


def product(intensity, models, elution, loadings, shifts, planes):
    run_count, bin_count, local_mz = intensity.shape
    components = loadings.shape[1]
    chunk = 2 * LANES
    chunks = local_mz // chunk
    if planes:
        out_shapes = [(chunks * components + components // 2, LANES)] * 2
    else:
        out_shapes = [(components, local_mz), (components, components)]
    return pl.pallas_call(
        functools.partial(product_kernel, len(models), planes),
        out_shape=tuple(jax.ShapeDtypeStruct(shape, jnp.float32) for shape in out_shapes),
        in_specs=vmem(len(models) + 4),
        out_specs=tuple(vmem(2)),
        scratch_shapes=[
            pltpu.VMEM((2 * components, run_count * bin_count), jnp.bfloat16),
            pltpu.VMEM((chunks, components, chunk), jnp.float32),
        ],
        compiler_params=pltpu.CompilerParams(vmem_limit_bytes=24 * MIB),
        cost_estimate=pl.CostEstimate(
            flops=8_000_000_000, bytes_accessed=2 * intensity.size, transcendentals=0
        ),
        name="model_products",
    )(intensity, *models, elution, loadings, shifts)


def inverse2(a, b, d):
    scale = 1.0 / (a * d - b * b)
    return d * scale, -b * scale, a * scale


def eliminate(gram, right):
    components = gram.shape[0]
    height = 8
    shape = (height, gram.shape[1])
    row_id = lax.broadcasted_iota(jnp.int32, shape, 0)
    starts = range(0, components, height)
    gram = [gram[at : at + height] for at in starts]
    right = [right[at : at + height] for at in starts]
    for j in range(0, components, 4):
        here, r = j // height, j % height
        columns = [[jnp.broadcast_to(tile[:, j + n : j + n + 1], shape) for tile in gram] for n in range(4)]
        pivot = [[columns[n][here][r + m : r + m + 1] for n in range(4)] for m in range(4)]
        a00, a01, a11 = inverse2(pivot[0][0], pivot[0][1], pivot[1][1])
        b00, b01, b10, b11 = pivot[0][2], pivot[0][3], pivot[1][2], pivot[1][3]
        w00, w01 = a00 * b00 + a01 * b10, a00 * b01 + a01 * b11
        w10, w11 = a01 * b00 + a11 * b10, a01 * b01 + a11 * b11
        s00, s01, s11 = inverse2(
            pivot[2][2] - (b00 * w00 + b10 * w10),
            pivot[2][3] - (b00 * w01 + b10 * w11),
            pivot[3][3] - (b01 * w01 + b11 * w11),
        )
        away = (row_id < r) | (row_id >= r + 4)
        for n in range(4):
            columns[n][here] = jnp.where(away, columns[n][here], jnp.where(row_id == r + n, -1.0, 0.0))
        gram_rows = [gram[here][r + n : r + n + 1] for n in range(4)]
        right_rows = [right[here][r + n : r + n + 1] for n in range(4)]
        gram[here] = jnp.where(away, gram[here], 0.0)
        right[here] = jnp.where(away[:, : right[here].shape[1]], right[here], 0.0)
        for t in range(len(gram)):
            c0, c1, c2, c3 = (columns[n][t] for n in range(4))
            t2, t3 = c2 - c0 * w00 - c1 * w10, c3 - c0 * w01 - c1 * w11
            f2, f3 = t2 * s00 + t3 * s01, t2 * s01 + t3 * s11
            f0 = c0 * a00 + c1 * a01 - f2 * w00 - f3 * w01
            f1 = c0 * a01 + c1 * a11 - f2 * w10 - f3 * w11
            for n, factor in enumerate((f0, f1, f2, f3)):
                gram[t] = gram[t] - factor * gram_rows[n]
                right[t] = right[t] - factor[:, : right[t].shape[1]] * right_rows[n]
    return jnp.concatenate(right, axis=0)


def total_of(refs, at, rows):
    total = refs[0][at : at + rows]
    for ref in refs[1:]:
        total = total + ref[at : at + rows]
    return total


def fixed_point(x, full):
    return jnp.clip(jnp.floor(x + 0.5), -full, full)


def as_int16(x):
    return x.astype(jnp.int32).astype(jnp.int16)


def row_level(x):
    peak = jnp.maximum(jnp.max(jnp.abs(x), axis=1, keepdims=True), 1e-30)
    return jnp.floor(256.0 / math.log(2.0) * jnp.log(peak)) + 1.0


def diagonal(x, rows):
    shape = (rows, LANES)
    on = lax.broadcasted_iota(jnp.int32, shape, 0) == lax.broadcasted_iota(jnp.int32, shape, 1)
    return jnp.where(on, jnp.broadcast_to(x, shape), 0.0)


def encode_rows(x, gram, o_ref):
    rows, tail = x.shape[0], gram.shape[0]
    parts = [x[at : at + LANES] for at in range(0, rows, LANES)]
    levels = [row_level(part) for part in parts] + [row_level(gram)]
    at = 0
    for part, level in zip(parts, levels):
        o_ref[at : at + part.shape[0], :] = as_int16(fixed_point(part * (FULL / scale_of(level)), FULL))
        at += part.shape[0]
    scaled = gram * (FULL / scale_of(levels[-1]))
    high = fixed_point(scaled, FULL)
    o_ref[at : at + tail, :] = as_int16(high)
    o_ref[at + tail : at + 2 * tail, :] = as_int16(fixed_point((scaled - high) * (2 * FULL), FULL))
    row_id = lax.broadcasted_iota(jnp.int32, (16, LANES), 0)
    block = jnp.zeros((16, LANES), jnp.float32)
    for n, level in enumerate(levels):
        lanes = jnp.sum(diagonal(level, level.shape[0]), axis=0, keepdims=True)
        block = jnp.where(row_id == n, lanes, block)
    o_ref[at + 2 * tail :, :] = as_int16(block)


def decode_rows(ref, tail):
    rows = ref.shape[0] - 2 * tail - 16
    x = ref[...].astype(jnp.int32).astype(jnp.float32)

    def scale(n, count):
        at = rows + 2 * tail + n
        return scale_of(jnp.sum(diagonal(x[at : at + 1], count), axis=1, keepdims=True)) * (1.0 / FULL)

    parts = []
    for n, at in enumerate(range(0, rows, LANES)):
        count = min(LANES, rows - at)
        parts.append(x[at : at + count] * scale(n, count))
    gram = x[rows : rows + tail] + x[rows + tail : rows + 2 * tail] * (0.5 / FULL)
    return jnp.concatenate(parts, axis=0), gram * scale(len(parts), tail)


def halve_kernel(tail, a_ref, b_ref, o_ref):
    rows = o_ref.shape[0] - 2 * tail - 16
    total = total_of((a_ref, b_ref), rows, rows + tail)
    encode_rows(total[:rows], total[rows:], o_ref)


def spread_kernel(tail, a_ref, b_ref, c_ref, own_ref, *outs):
    rows = own_ref.shape[0] - tail
    count = len(outs) + 1
    total, gram = decode_rows(c_ref, tail)
    total = total + total_of((a_ref, b_ref), 0, count * rows)
    gram = gram + total_of((a_ref, b_ref), 2 * count * rows, tail)
    own_ref[0:rows, :] = total[:rows]
    own_ref[rows:, :] = gram
    for n, o_ref in enumerate(outs):
        encode_rows(total[(n + 1) * rows : (n + 2) * rows], gram, o_ref)


def solve_planes_kernel(own_ref, *refs):
    o_ref = refs[-1]
    components = o_ref.shape[0]
    total, gram = own_ref[:components], own_ref[components:]
    for ref in refs[:-1]:
        part, gram_part = decode_rows(ref, gram.shape[0])
        total, gram = total + part, gram + gram_part
    gram = jnp.concatenate([gram, pltpu.roll(gram, gram.shape[1] // 2, 1)], axis=0)
    o_ref[...] = eliminate(gram, total)


def solve_kernel(g_ref, n_ref, o_ref):
    components = o_ref.shape[0]
    gram = jnp.concatenate([g_ref[...], jnp.zeros((components, LANES - components), jnp.float32)], axis=1)
    o_ref[...] = eliminate(gram, n_ref[...])


def small_call(kernel, outs, name, *args):
    return pl.pallas_call(
        kernel,
        out_shape=tuple(jax.ShapeDtypeStruct(shape, dtype) for shape, dtype in outs),
        in_specs=vmem(len(args)),
        out_specs=tuple(vmem(len(outs))),
        compiler_params=pltpu.CompilerParams(vmem_limit_bytes=8 * MIB),
        name=name,
    )(*args)


def swap(x, axes, count, value):
    return lax.ppermute(x, axes, [(i, i ^ value) for i in range(count)])


def on_device(intensity, elution, loadings, shifts, bin_weight):
    freq_count = lax.axis_size("freq")
    mz_count = lax.axis_size("mz")
    components = loadings.shape[1]
    bin_count = intensity.shape[1]
    axes = ("freq", "mz")
    own = intensity.shape[2] // freq_count
    planes = (
        own == LANES
        and 2 * components == LANES
        and mz_count == 2
        and freq_count & (freq_count - 1) == 0
        and freq_count >= 8
        and elution.shape[0] % 64 == 0
        and bin_count % LANES == 0
        and bin_count >= REACH
    )
    if not planes:
        mine = pack(elution)
        gathered = lax.all_gather(mine, axes, axis=0).reshape(-1, math.gcd(bin_count, LANES), LANES)
        (g,) = partial_model((gathered,), circulant(bin_weight.reshape(LANES, -1), 0), bin_count, components)
        shifted = elution_terms((gathered,), loadings, shifts, bin_count)
        numerator, gram = product(intensity, (g,), shifted, loadings, shifts, planes)
        gram = lax.psum(gram, "freq")
        owned = lax.psum_scatter(numerator, "freq", scatter_dimension=1, tiled=True)
        return small_call(solve_kernel, [((components, own), jnp.float32)], "solve", gram, owned)[0]
    mine = encode(elution)
    z_steps = range(4, freq_count, 4)
    held = jnp.stack([mine] + [swap(mine, "freq", freq_count, step) for step in z_steps])
    weights = bin_weight.reshape(LANES, -1)
    held, weights = lax.optimization_barrier((held, weights))
    held = jnp.concatenate([held, swap(held, "freq", freq_count, 2)], axis=0)
    u = circulant(weights, elution.shape[0])
    held, u = lax.optimization_barrier((held, u))
    came = swap(held, "freq", freq_count, 1)
    pair = window_pair(mine, came)
    other = swap(pair, "mz", mz_count, 1)
    g, coded = partial_model((held, came), u, bin_count, components)
    coded, other = lax.optimization_barrier((coded, other))
    models = (g, swap(coded, "mz", mz_count, 1))
    shifted = elution_terms((pair, other), loadings, shifts, bin_count)
    keep, send = product(intensity, models, shifted, loadings, shifts, planes)
    tail = components // 2
    chips = freq_count // 4
    came = swap(send, "freq", freq_count, 1)
    coded = 2 * tail + 16
    (send,) = small_call(
        functools.partial(halve_kernel, tail),
        [((chips * components + coded, LANES), jnp.int16)],
        "reduce_cores",
        keep,
        came,
    )
    across = swap(send, "freq", freq_count, 2)
    own_part, *sends = small_call(
        functools.partial(spread_kernel, tail),
        [((components + tail, LANES), jnp.float32)] + [((components + coded, LANES), jnp.int16)] * (chips - 1),
        "reduce_x",
        keep,
        came,
        across,
    )
    parts = [swap(send, "freq", freq_count, step) for send, step in zip(sends, z_steps)]
    parts = parts[1:] + parts[:1]
    return small_call(
        solve_planes_kernel, [((components, own), jnp.float32)], "solve", own_part, *parts
    )[0]


def solution(mesh):
    in_specs = (P(None, "freq", "mz"), P(("freq", "mz"), None), P(), P(), P())
    out_specs = P(None, ("mz", "freq"))
    return jax.shard_map(on_device, mesh=mesh, in_specs=in_specs, out_specs=out_specs, check_vma=False)
```
